32 devices in a mesh: parts: 2 (over x), vocab: 16 (over z, y, core).
Axes of the slice: x: 2, y: 2, z: 4, core: 2. Of those that a mesh axis runs over, the one named last changes fastest.
Arguments:
- emission: bfloat16 [8192, 4096], P(None, 'vocab'), may hold values from 0 to 0.9765625
- transition: bfloat16 [8192, 8192], P(None, 'vocab'), may hold values from 0 to 0.30517578
- beta_start: float32 [8192, 16], replicated, may hold values from 0.1 to 1
- allow_list: int32 [16, 8], replicated, may hold values from 0 to 15, as said below
- trans_table: int32 [16, 16], replicated, may hold values from 0 to 15
- last_token: int32 [32], P('parts'), parts along dimension 0, may hold values from 0 to 4095, as said below
- prompt_state: int32 [32], P('parts'), parts along dimension 0, may hold values from 0 to 15
- prior_msg: float32 [32, 8192], P(('parts', 'vocab')), parts along dimension 0, may hold values from 0 to 125
- lm_logits: bfloat16 [32, 4096], P('parts', 'vocab'), parts along dimension 0, may hold values from -12 to 275
Outputs:
- beta_end: float32 [16384, 16], P(('parts', 'vocab')), parts along dimension 0
- constrained: float32 [32, 4096], P('parts', 'vocab'), parts along dimension 0
The draws below stay inside these ranges and needn't reach their ends.
There are 2 independent parts, one for each index of `parts`. The reference program is written for one: setup_inputs(seed, part) draws one part's arguments, and reference() takes and returns one part's arrays. A program takes and returns all parts, laid end to end along the dimension named above; an argument that names none is the same for every part. Nothing has to cross between parts.
Inputs may be any that keep to these rules, and one draw needn't show every extreme that they name: `allow_list`: each row lists 8 different blocks. `last_token`: each prompt's last token may be any token of the vocabulary.
All inputs are finite; a program needn't handle non-finite values.
Results may differ from the reference program's by a relative error of at most 0.00052.
Values may be sent and summed in bfloat16 or wider, within the bound.
No kernel may reach another device: no remote copies, remote signals or barrier semaphores. Data moves between devices by JAX's collectives and lax.ppermute only.
A program may use at most 64 MiB of HBM per device.

```python
import math
import jax
import jax.numpy as jnp
from jax import lax

H = 8192
S = 16
BLK = 256
STEPS = 3
PDEV = 1
NBLK = 16
VOCAB = 4096
NALLOW = 8
P_SIZE = 16


def draw_emission(key, part):
    key = jax.random.fold_in(key, 5)
    key_level, key_token = jax.random.split(key, 2)
    width = 1.5 * jnp.ones((H, 1, 1), jnp.float32)
    level = jnp.clip(jax.random.normal(key_level, (H, NBLK, 1), jnp.float32), -4.0, 4.0)
    token = jnp.clip(jax.random.normal(key_token, (H, NBLK, BLK), jnp.float32), -4.0, 4.0)
    logs = width * level - 0.5 * width * width + 0.7 * token - 0.245
    return (jnp.exp(logs) / VOCAB).reshape(H, VOCAB).astype(jnp.bfloat16)


def draw_transition(key, part):
    key = jax.random.fold_in(key, 7)
    key_noise = jax.random.fold_in(key, 0)
    width = 2.2 * jnp.ones((H, 1), jnp.float32)
    noise = jnp.clip(jax.random.normal(key_noise, (H, H), jnp.float32), -4.0, 4.0)
    values = 2.0 * jnp.exp(width * noise - 0.5 * width * width) / H
    return values.astype(jnp.bfloat16)


def draw_prior_msg(key, part):
    key = jax.random.fold_in(key, 13)
    key_noise = jax.random.fold_in(key, 0)
    noise = jnp.clip(jax.random.normal(key_noise, (P_SIZE, H), jnp.float32), -4.0, 4.0)
    return jnp.exp(noise)


def draw_last_token(key, part):
    key = jax.random.fold_in(key, 17)
    key_pop, key_score, key_pair, key_first, key_second = jax.random.split(key, 5)
    popular = jax.random.randint(key_pop, (NBLK,), 0, 4)
    cols = jnp.arange(NBLK, dtype=jnp.int32)
    score = jax.random.randint(key_score, (NBLK, NBLK), 0, 1024) + 1024 * popular[None, :] * popular[None, :]
    score = score * NBLK + cols[None, :]
    ignored, picked = jax.lax.top_k(score, PDEV)
    slot = jnp.arange(PDEV, dtype=jnp.int32)
    groups = jnp.arange(NBLK, dtype=jnp.int32)
    paired = jax.random.randint(key_pair, (NBLK, PDEV), 0, 2)
    paired = jnp.where((groups[:, None] == 0) & (slot[None, :] == 1), 1, paired)
    odd = (slot % 2 == 1)[None, :] & (paired == 1)
    previous = jnp.roll(picked, 1, axis=1)
    blocks = jnp.where(odd, previous, picked)
    offset = jnp.minimum(jax.random.randint(key_first, (NBLK, PDEV), 0, BLK), jax.random.randint(key_second, (NBLK, PDEV), 0, BLK))
    return (blocks * BLK + offset).reshape(P_SIZE).astype(jnp.int32)


def draw_allow_list(key, part):
    key = jax.random.fold_in(key, 11)
    key_pop, key_noise = jax.random.split(key)
    popular = jax.random.randint(key_pop, (NBLK,), 0, 4)
    noise = jax.random.randint(key_noise, (S, NBLK), 0, 1024)
    score = noise + 1024 * popular[None, :] * popular[None, :]
    rows = jnp.arange(S, dtype=jnp.int32)[:, None]
    cols = jnp.arange(NBLK, dtype=jnp.int32)[None, :]
    forced = (rows == 0) & ((cols == 0) | (cols == NBLK - 1))
    score = jnp.where(forced, 100000, score)
    score = score * NBLK + cols
    ignored, picked = jax.lax.top_k(score, NALLOW)
    return picked.astype(jnp.int32)


def draw_lm_logits(key, part):
    key = jax.random.fold_in(key, 23)
    key_base = jax.random.fold_in(key, 0)
    base = jnp.clip(3.0 * jax.random.normal(key_base, (P_SIZE, VOCAB), jnp.float32), -12.0, 12.0)
    return base.astype(jnp.bfloat16)


def with_ends(array, rng, low, high):
    extent = array.shape
    spot = [jax.random.randint(jax.random.fold_in(rng, axis), (), 0, extent[axis]) for axis in range(len(extent))]
    array = array.at[tuple(spot)].set(low)
    longest = extent.index(max(extent))
    spot[longest] = (spot[longest] + 1) % extent[longest]
    return array.at[tuple(spot)].set(high)


def setup_inputs(seed: int = 0, part: int = 0) -> dict:
    keys = jax.random.split(jax.random.key(seed), 10)
    part_keys = jax.random.split(jax.random.fold_in(keys[9], part), 10)
    emission = draw_emission(jax.random.fold_in(keys[9], 71), part)
    transition = draw_transition(jax.random.fold_in(keys[9], 71), part)
    beta_start = jnp.clip(jnp.exp(jax.random.uniform(keys[2], (H, S), jnp.float32, math.log(0.1), math.log(1.0))), 0.1, 1.0)
    allow_list = draw_allow_list(jax.random.fold_in(keys[9], 71), part)
    trans_table = with_ends(jax.random.randint(keys[4], (S, NBLK), 0, S), jax.random.fold_in(keys[4], 1), 0, S - 1).astype(jnp.int32)
    last_token = draw_last_token(jax.random.fold_in(jax.random.fold_in(keys[9], part), 71), part)
    prompt_state = with_ends(jax.random.randint(part_keys[6], (P_SIZE,), 0, S), jax.random.fold_in(part_keys[6], 1), 0, S - 1).astype(jnp.int32)
    prior_msg = draw_prior_msg(jax.random.fold_in(jax.random.fold_in(keys[9], part), 71), part)
    lm_logits = draw_lm_logits(jax.random.fold_in(jax.random.fold_in(keys[9], part), 71), part)
    return {"emission": emission, "transition": transition, "beta_start": beta_start, "allow_list": allow_list, "trans_table": trans_table, "last_token": last_token, "prompt_state": prompt_state, "prior_msg": prior_msg, "lm_logits": lm_logits}


def reference(emission, transition, beta_start, allow_list, trans_table, last_token, prompt_state, prior_msg, lm_logits):
    block_sums = jnp.sum(emission.reshape(H, NBLK, BLK), axis=2, dtype=jnp.float32)
    blocks = jnp.arange(NBLK, dtype=jnp.int32)
    allowed = jnp.any(allow_list[:, :, None] == blocks[None, None, :], axis=1).astype(jnp.float32)
    messages = beta_start
    for window_step in range(STEPS):
        selected = messages[:, trans_table]
        emitted = jnp.sum((allowed[None, :, :] * block_sums[:, None, :]) * selected, axis=2)
        messages = jnp.dot(transition.astype(jnp.float32), emitted, precision=lax.Precision.HIGHEST)
    columns = emission[:, last_token].T.astype(jnp.float32)
    unnormal = prior_msg * columns
    forward_msg = (unnormal / jnp.sum(unnormal, axis=1, keepdims=True)).astype(jnp.bfloat16)

    def per_block(block):
        dests = trans_table[prompt_state, block]
        chosen = messages[:, dests].T
        scaled = (forward_msg.astype(jnp.float32) * chosen).astype(jnp.bfloat16)
        tile = lax.dynamic_slice_in_dim(emission, (block * BLK).astype(jnp.int32), BLK, 1)
        weights = jnp.dot(scaled, tile, preferred_element_type=jnp.float32)
        return weights * allowed[prompt_state, block][:, None]

    weights = lax.map(per_block, blocks)
    weights = jnp.transpose(weights, (1, 0, 2)).reshape(P_SIZE, VOCAB)
    logits = lm_logits.astype(jnp.float32)
    top = jnp.max(logits, axis=1)
    raised = jnp.exp(logits - top[:, None]) * weights
    total = jnp.sum(raised, axis=1)
    constrained = VOCAB * raised / total[:, None]
    return messages, constrained
```

```python
import jax
import jax.numpy as jnp
from jax import lax
from jax.sharding import PartitionSpec as P

BLK = 256
STEPS = 3


def exchange(blocks):
    return lax.all_to_all(blocks, "vocab", split_axis=0, concat_axis=0, tiled=True)


def spread(own, devices):
    return exchange(jnp.broadcast_to(own[None], (devices,) + own.shape))


def split_wide(wide):
    high = wide.astype(jnp.bfloat16)
    low = (wide - high.astype(jnp.float32)).astype(jnp.bfloat16)
    return high, low


def per_device(
    emission,
    transition,
    beta_start,
    allow_list,
    trans_table,
    last_token,
    prompt_state,
    prior_msg,
    lm_logits,
):
    devices = lax.axis_size("vocab")
    device = lax.axis_index("vocab")
    hidden = emission.shape[0]
    states = beta_start.shape[1]
    own_rows = transition.shape[1]
    local_rows = prior_msg.shape[0]
    prompts = prompt_state.shape[0]
    state_ids = jnp.arange(states, dtype=jnp.int32)
    block_ids = jnp.arange(devices, dtype=jnp.int32)
    block_sums = jnp.sum(emission, axis=1, dtype=jnp.float32)
    own_sums = exchange(block_sums.reshape(devices, own_rows))
    allowed = jnp.any(allow_list[:, :, None] == block_ids, axis=1)
    route = allowed.T[:, :, None] & (trans_table.T[:, :, None] == state_ids)
    route = route.astype(jnp.float32).reshape(devices * states, states)
    messages = lax.dynamic_slice_in_dim(beta_start, device * own_rows, own_rows, 0).T
    by_owner = transition.reshape(devices, own_rows, own_rows)
    for window_step in range(STEPS):
        selected = jnp.dot(route, messages, precision=lax.Precision.HIGHEST)
        selected = selected.reshape(devices, states, own_rows)
        emitted = jnp.sum(selected * own_sums[:, None, :], axis=0)
        halves = jnp.concatenate(split_wide(emitted), axis=0)
        partial = jnp.einsum("dzy,sy->dsz", by_owner, halves, preferred_element_type=jnp.float32)
        partial = partial[:, :states] + partial[:, states:]
        if window_step < STEPS - 1:
            partial = partial.astype(jnp.bfloat16)
        messages = jnp.sum(exchange(partial), axis=0, dtype=jnp.float32)
    beta_end = messages.T
    token_ids = jnp.arange(BLK, dtype=jnp.int32)
    tokens = last_token - device * BLK
    onehot = (tokens[:, None] == token_ids[None, :]).astype(jnp.bfloat16)
    owned = lax.dot_general(
        onehot, emission, (((1,), (1,)), ((), ())), preferred_element_type=jnp.float32
    )
    owned = owned.astype(jnp.bfloat16).reshape(devices, local_rows, hidden)
    columns = jnp.sum(exchange(owned), axis=0, dtype=jnp.float32)
    unnormal = prior_msg * columns
    forward_msg = (unnormal / jnp.sum(unnormal, axis=1, keepdims=True)).astype(jnp.bfloat16)
    forward_all = spread(forward_msg, devices).reshape(prompts, devices, own_rows)
    everywhere = spread(messages, devices)
    dest_here = lax.dynamic_index_in_dim(trans_table, device, axis=1, keepdims=False)
    allow_here = jnp.any(allow_list == device, axis=1).astype(jnp.float32)
    state_onehot = (prompt_state[:, None] == state_ids[None, :]).astype(jnp.float32)
    allowed_rows = jnp.sum(state_onehot * allow_here, axis=1)
    dest_rows = jnp.sum(jnp.where(prompt_state[:, None] == state_ids, dest_here, 0), axis=1)
    dest_onehot = (dest_rows[:, None] == state_ids).astype(jnp.float32)
    chosen = jnp.einsum("ps,dsz->pdz", dest_onehot, everywhere, precision=lax.Precision.HIGHEST)
    scaled = (forward_all.astype(jnp.float32) * chosen).astype(jnp.bfloat16)
    scaled = scaled.reshape(prompts, hidden)
    tile_out = jnp.dot(scaled, emission, preferred_element_type=jnp.float32)
    weights = tile_out * allowed_rows[:, None]
    logits = lm_logits.astype(jnp.float32)
    top_here = jnp.max(logits, axis=1)
    raised = jnp.exp(logits - top_here[:, None]) * weights
    pair = jnp.stack([top_here, jnp.sum(raised, axis=1)])
    pairs = spread(pair, devices)
    tops, totals = pairs[:, 0], pairs[:, 1]
    top = jnp.max(tops, axis=0)
    total = jnp.sum(totals * jnp.exp(tops - top), axis=0)
    raised = raised * jnp.exp(top_here - top)[:, None]
    return (beta_end, BLK * devices * raised / total[:, None])


def solution(mesh):
    return jax.shard_map(
        per_device,
        mesh=mesh,
        in_specs=(
            P(None, "vocab"),
            P(None, "vocab"),
            P(),
            P(),
            P(),
            P("parts"),
            P("parts"),
            P(("parts", "vocab"), None),
            P("parts", "vocab"),
        ),
        out_specs=(P(("parts", "vocab"), None), P("parts", "vocab")),
        check_vma=False,
    )
```

```python
import functools

import jax
import jax.numpy as jnp
from jax import lax
from jax.experimental import pallas as pl
from jax.experimental.pallas import tpu as pltpu
from jax.sharding import PartitionSpec as P

BLK = 256
STEPS = 3
DIRECT = 16
LIMIT = 40 * 1024 * 1024
VMEM = pl.BlockSpec(memory_space=pltpu.VMEM)
ANY = pl.BlockSpec(memory_space=pl.ANY)


def exchange(blocks):
    return lax.all_to_all(blocks, "vocab", split_axis=0, concat_axis=0, tiled=True)


def spread(own, devices):
    return exchange(jnp.broadcast_to(own[None], (devices,) + own.shape))


def swap(block, offset, devices):
    pairs = [(i, i ^ offset) for i in range(devices)]
    return lax.ppermute(block, "vocab", pairs)


def swap_all(blocks):
    devices = len(blocks)
    return [blocks[0]] + [swap(blocks[i], i, devices) for i in range(1, devices)]


def fan_out(block, devices):
    return [block] + [swap(block, i, devices) for i in range(1, devices)]


def split_wide(wide):
    high = wide.astype(jnp.bfloat16)
    low = (wide - high.astype(jnp.float32)).astype(jnp.bfloat16)
    return high, low


def split_three(wide):
    high = wide.astype(jnp.bfloat16)
    rest = wide - high.astype(jnp.float32)
    middle = rest.astype(jnp.bfloat16)
    low = (rest - middle.astype(jnp.float32)).astype(jnp.bfloat16)
    return high, middle, low


def copy_chunk(source, buffer, sems, partner, slot, rows):
    start = pl.multiple_of(partner * rows, rows)
    return pltpu.make_async_copy(
        source.at[pl.ds(start, rows)], buffer.at[pl.ds(slot * rows, rows)], sems.at[slot]
    )


def start_chunks(source, buffer, sems, devices):
    device = lax.axis_index("vocab")
    rows = source.shape[0] // devices
    copies = [copy_chunk(source, buffer, sems, device ^ i, i, rows) for i in range(devices)]
    for copy in copies:
        copy.start()
    return copies


def dot_rows(left, right):
    return lax.dot_general(left, right, (((1,), (1,)), ((), ())), preferred_element_type=jnp.float32)


def sums_kernel(devices, emission_ref, *refs):
    outs, (buffer, sems) = refs[:devices], refs[devices:]
    copies = start_chunks(emission_ref, buffer, sems, devices)
    rows = emission_ref.shape[0] // devices
    ones = jnp.ones((16, emission_ref.shape[1]), jnp.bfloat16)
    for i in range(devices):
        copies[i].wait()
        outs[i][...] = dot_rows(ones, buffer[pl.ds(i * rows, rows)])[:1]


def block_sums(emission, devices):
    hidden = emission.shape[0]
    return pl.pallas_call(
        functools.partial(sums_kernel, devices),
        out_shape=[jax.ShapeDtypeStruct((1, hidden // devices), jnp.float32)] * devices,
        in_specs=[ANY],
        out_specs=[VMEM] * devices,
        scratch_shapes=[
            pltpu.VMEM(emission.shape, emission.dtype),
            pltpu.SemaphoreType.DMA((devices,)),
        ],
        compiler_params=pltpu.CompilerParams(vmem_limit_bytes=LIMIT),
        name="block_sums",
    )(emission)


def step_kernel(devices, received, transition_ref, route_ref, sums_ref, *refs):
    parts, refs = refs[:received], refs[received:]
    outs, (buffer, sems) = refs[:devices], refs[devices:]
    copies = start_chunks(transition_ref, buffer, sems, devices)
    rows = transition_ref.shape[0] // devices
    messages = parts[0][...].astype(jnp.float32)
    for part in parts[1:]:
        messages += part[...].astype(jnp.float32)
    states = messages.shape[0]
    selected = jnp.dot(
        route_ref[...],
        jnp.concatenate(split_three(messages), axis=0),
        preferred_element_type=jnp.float32,
    )
    emitted = selected[:states] * sums_ref[pl.ds(0, 1)]
    for b in range(1, devices):
        emitted += selected[b * states : (b + 1) * states] * sums_ref[pl.ds(b, 1)]
    halves = jnp.concatenate(split_wide(emitted), axis=0)
    for i in range(devices):
        copies[i].wait()
        product = dot_rows(halves, buffer[pl.ds(i * rows, rows)])
        outs[i][...] = (product[:states] + product[states:]).astype(outs[i].dtype)


def step(transition, route, sums, parts, dtype, devices):
    hidden = transition.shape[0]
    shape = (parts[0].shape[0], hidden // devices)
    return pl.pallas_call(
        functools.partial(step_kernel, devices, len(parts)),
        out_shape=[jax.ShapeDtypeStruct(shape, dtype)] * devices,
        in_specs=[ANY] + [VMEM] * (2 + len(parts)),
        out_specs=[VMEM] * devices,
        scratch_shapes=[
            pltpu.VMEM(transition.shape, transition.dtype),
            pltpu.SemaphoreType.DMA((devices,)),
        ],
        compiler_params=pltpu.CompilerParams(vmem_limit_bytes=LIMIT),
        name="backward_step",
    )(transition, route, sums, *parts)


def weigh_kernel(devices, emission_ref, forward_ref, chooser_ref, logits_ref, *refs):
    parts = refs[:devices]
    raised_ref, pair_ref, buffer, sems = refs[devices:]
    copies = start_chunks(emission_ref, buffer, sems, devices)
    device = lax.axis_index("vocab")
    rows = emission_ref.shape[0] // devices
    chooser = chooser_ref[...]
    logits = logits_ref[...].astype(jnp.float32)
    top = jnp.max(logits, axis=1, keepdims=True)
    weights = jnp.zeros(logits.shape, jnp.float32)
    for i in range(devices):
        pieces = jnp.concatenate(split_three(parts[i][...]), axis=0)
        chosen = jnp.dot(chooser, pieces, preferred_element_type=jnp.float32)
        start = pl.multiple_of((device ^ i) * rows, rows)
        forward = forward_ref[:, pl.ds(start, rows)].astype(jnp.float32)
        scaled = (forward * chosen).astype(jnp.bfloat16)
        copies[i].wait()
        weights += jnp.dot(
            scaled, buffer[pl.ds(i * rows, rows)], preferred_element_type=jnp.float32
        )
    allowed = jnp.sum(chooser.astype(jnp.float32), axis=1, keepdims=True) > 0
    raised = jnp.where(allowed, jnp.exp(logits - top) * weights, 0.0)
    raised_ref[...] = raised
    total = jnp.sum(raised, axis=1, keepdims=True)
    lane = lax.broadcasted_iota(jnp.int32, (logits.shape[0], 128), 1)
    pair_ref[...] = jnp.where(lane == 0, top, total)


def weigh(emission, forward, chooser, logits, parts, devices):
    return pl.pallas_call(
        functools.partial(weigh_kernel, devices),
        out_shape=[
            jax.ShapeDtypeStruct(logits.shape, jnp.float32),
            jax.ShapeDtypeStruct((logits.shape[0], 128), jnp.float32),
        ],
        in_specs=[ANY] + [VMEM] * (3 + devices),
        out_specs=[VMEM] * 2,
        scratch_shapes=[
            pltpu.VMEM(emission.shape, emission.dtype),
            pltpu.SemaphoreType.DMA((devices,)),
        ],
        compiler_params=pltpu.CompilerParams(vmem_limit_bytes=LIMIT),
        name="weigh_tokens",
    )(emission, forward, chooser, logits, *parts)


def finish_kernel(devices, raised_ref, *refs):
    pairs, out_ref = refs[:devices], refs[devices]
    own_top = pairs[0][:, :1]
    top = own_top
    for pair in pairs[1:]:
        top = jnp.maximum(top, pair[:, :1])
    total = jnp.zeros_like(top)
    for pair in pairs:
        total += pair[:, 1:2] * jnp.exp(pair[:, :1] - top)
    raised = raised_ref[...] * jnp.exp(own_top - top)
    out_ref[...] = BLK * devices * raised / total


def finish(raised, pairs):
    return pl.pallas_call(
        functools.partial(finish_kernel, len(pairs)),
        out_shape=jax.ShapeDtypeStruct(raised.shape, jnp.float32),
        in_specs=[VMEM] * (1 + len(pairs)),
        out_specs=VMEM,
        name="normalise",
    )(raised, *pairs)


def forward_messages(emission, last_token, prior_msg, devices, device):
    hidden = emission.shape[0]
    local_rows = prior_msg.shape[0]
    token_ids = jnp.arange(BLK, dtype=jnp.int32)
    tokens = last_token - device * BLK
    onehot = (tokens[:, None] == token_ids[None, :]).astype(jnp.bfloat16)
    owned = dot_rows(onehot, emission)
    owned = owned.astype(jnp.bfloat16).reshape(devices, local_rows, hidden)
    columns = jnp.sum(exchange(owned), axis=0, dtype=jnp.float32)
    unnormal = prior_msg * columns
    forward_msg = (unnormal / jnp.sum(unnormal, axis=1, keepdims=True)).astype(jnp.bfloat16)
    return spread(forward_msg, devices).reshape(devices * local_rows, hidden)


def per_device(
    emission,
    transition,
    beta_start,
    allow_list,
    trans_table,
    last_token,
    prompt_state,
    prior_msg,
    lm_logits,
):
    devices = lax.axis_size("vocab")
    device = lax.axis_index("vocab")
    hidden = emission.shape[0]
    states = beta_start.shape[1]
    own_rows = transition.shape[1]
    prompts = prompt_state.shape[0]
    state_ids = jnp.arange(states, dtype=jnp.int32)
    block_ids = jnp.arange(devices, dtype=jnp.int32)
    allowed = jnp.any(allow_list[:, :, None] == block_ids, axis=1)
    forward_all = forward_messages(emission, last_token, prior_msg, devices, device)
    dest_here = lax.dynamic_index_in_dim(trans_table, device, axis=1, keepdims=False)
    allow_here = jnp.any(allow_list == device, axis=1)
    dest_rows = jnp.sum(jnp.where(prompt_state[:, None] == state_ids, dest_here, 0), axis=1)
    allow_rows = jnp.any((prompt_state[:, None] == state_ids) & allow_here, axis=1)
    chooser = (dest_rows[:, None] == state_ids) & allow_rows[:, None]
    messages = lax.dynamic_slice_in_dim(beta_start, device * own_rows, own_rows, 0).T
    if devices <= DIRECT:
        partners = device ^ block_ids
        order = (partners[:, None] == block_ids).astype(jnp.int32)
        dests = jnp.sum(order[:, None, :] * trans_table[None], axis=2)
        allowed_to = jnp.sum(order[:, None, :] * allowed[None], axis=2) > 0
        route = (dests[:, :, None] == state_ids) & allowed_to[:, :, None]
        route = route.reshape(devices * states, states).astype(jnp.bfloat16)
        route = jnp.concatenate([route] * 3, axis=1)
        sums = jnp.concatenate(swap_all(block_sums(emission, devices)), axis=0)
        parts = [messages]
        for window_step in range(STEPS):
            dtype = jnp.bfloat16 if window_step < STEPS - 1 else jnp.float32
            parts = swap_all(step(transition, route, sums, parts, dtype, devices))
        messages = functools.reduce(jnp.add, parts)
        everywhere = fan_out(messages, devices)
        chooser = jnp.concatenate([chooser.astype(jnp.bfloat16)] * 3, axis=1)
        raised, pair = weigh(emission, forward_all, chooser, lm_logits, everywhere, devices)
        constrained = finish(raised, fan_out(pair, devices))
        return messages.T, constrained
    own_sums = exchange(jnp.sum(emission, axis=1, dtype=jnp.float32).reshape(devices, own_rows))
    route = allowed.T[:, :, None] & (trans_table.T[:, :, None] == state_ids)
    route = route.astype(jnp.float32).reshape(devices * states, states)
    by_owner = transition.reshape(devices, own_rows, own_rows)
    for window_step in range(STEPS):
        selected = jnp.dot(route, messages, precision=lax.Precision.HIGHEST)
        selected = selected.reshape(devices, states, own_rows)
        emitted = jnp.sum(selected * own_sums[:, None, :], axis=0)
        halves = jnp.concatenate(split_wide(emitted), axis=0)
        partial = jnp.einsum("dzy,sy->dsz", by_owner, halves, preferred_element_type=jnp.float32)
        partial = partial[:, :states] + partial[:, states:]
        if window_step < STEPS - 1:
            partial = partial.astype(jnp.bfloat16)
        messages = jnp.sum(exchange(partial), axis=0, dtype=jnp.float32)
    everywhere = spread(messages, devices)
    chosen = jnp.einsum(
        "ps,dsz->pdz", chooser.astype(jnp.float32), everywhere, precision=lax.Precision.HIGHEST
    )
    forward_all = forward_all.reshape(prompts, devices, own_rows).astype(jnp.float32)
    scaled = (forward_all * chosen).astype(jnp.bfloat16).reshape(prompts, hidden)
    weights = jnp.dot(scaled, emission, preferred_element_type=jnp.float32)
    weights = jnp.where(allow_rows[:, None], weights, 0.0)
    logits = lm_logits.astype(jnp.float32)
    top_here = jnp.max(logits, axis=1)
    raised = jnp.exp(logits - top_here[:, None]) * weights
    pairs = spread(jnp.stack([top_here, jnp.sum(raised, axis=1)]), devices)
    tops, totals = pairs[:, 0], pairs[:, 1]
    top = jnp.max(tops, axis=0)
    total = jnp.sum(totals * jnp.exp(tops - top), axis=0)
    raised = raised * jnp.exp(top_here - top)[:, None]
    return (messages.T, BLK * devices * raised / total[:, None])


def solution(mesh):
    return jax.shard_map(
        per_device,
        mesh=mesh,
        in_specs=(
            P(None, "vocab"),
            P(None, "vocab"),
            P(),
            P(),
            P(),
            P("parts"),
            P("parts"),
            P(("parts", "vocab"), None),
            P("parts", "vocab"),
        ),
        out_specs=(P(("parts", "vocab"), None), P("parts", "vocab")),
        check_vma=False,
    )
```

```python
import functools

import jax
import jax.numpy as jnp
import numpy as np
from jax import lax
from jax.experimental import pallas as pl
from jax.experimental.pallas import tpu as pltpu
from jax.sharding import Mesh
from jax.sharding import PartitionSpec as P

BLK = 256
STEPS = 3
LIMIT = 16 * 1024 * 1024
VMEM = pl.BlockSpec(memory_space=pltpu.VMEM)
ANY = pl.BlockSpec(memory_space=pl.ANY)


AXES = ("outer", "inner")


def exchange(blocks, axes=AXES):
    return lax.all_to_all(blocks, axes, split_axis=0, concat_axis=0, tiled=True)


def copies_of(own, number):
    return jnp.broadcast_to(own[None], (number,) + own.shape)


def spread(own, devices):
    return exchange(copies_of(own, devices))


def scatter_sum(blocks, dtype):
    near = jnp.sum(exchange(blocks, "inner"), axis=0, dtype=jnp.float32)
    return exchange(near.astype(dtype), "outer")


def two_stage_spread(own, outer, inner):
    far = exchange(copies_of(own, outer), "outer")
    return exchange(copies_of(far, inner), "inner")


def split_wide(wide):
    high = wide.astype(jnp.bfloat16)
    low = (wide - high.astype(jnp.float32)).astype(jnp.bfloat16)
    return high, low


def split_three(wide):
    high = wide.astype(jnp.bfloat16)
    rest = wide - high.astype(jnp.float32)
    middle = rest.astype(jnp.bfloat16)
    low = (rest - middle.astype(jnp.float32)).astype(jnp.bfloat16)
    return high, middle, low


def dot_rows(left, right):
    return lax.dot_general(left, right, (((1,), (1,)), ((), ())), preferred_element_type=jnp.float32)


def resident(array):
    return pltpu.with_memory_space_constraint(array, pltpu.VMEM)


def device_order(outer, inner):
    return [(i, o, o * inner + i) for i in range(inner) for o in range(outer)]


def sums_kernel(outer, inner, emission_ref, out_ref, buffer, sems):
    devices = outer * inner
    rows = emission_ref.shape[0] // devices
    copies = []
    for k in range(devices):
        span = pl.ds(k * rows, rows)
        copies.append(pltpu.make_async_copy(emission_ref.at[span], buffer.at[span], sems.at[k]))
        copies[-1].start()
    ones = jnp.ones((16, emission_ref.shape[1]), jnp.bfloat16)
    for i, o, k in sorted(device_order(outer, inner), key=lambda entry: entry[2]):
        copies[k].wait()
        out_ref[i, pl.ds(o, 1), :] = dot_rows(ones, buffer[pl.ds(k * rows, rows)])[:1]


def block_sums(emission, outer, inner):
    hidden = emission.shape[0]
    devices = outer * inner
    return pl.pallas_call(
        functools.partial(sums_kernel, outer, inner),
        out_shape=jax.ShapeDtypeStruct((inner, outer, hidden // devices), jnp.float32),
        in_specs=[ANY],
        out_specs=VMEM,
        scratch_shapes=[
            pltpu.VMEM(emission.shape, emission.dtype),
            pltpu.SemaphoreType.DMA((devices,)),
        ],
        compiler_params=pltpu.CompilerParams(vmem_limit_bytes=LIMIT),
        name="block_sums",
    )(emission)


def step_kernel(outer, inner, transition_ref, route_ref, sums_ref, parts_ref, out_ref):
    rows = transition_ref.shape[0] // (outer * inner)
    messages = parts_ref[0].astype(jnp.float32)
    for k in range(1, parts_ref.shape[0]):
        messages += parts_ref[k].astype(jnp.float32)
    states = messages.shape[0]
    selected = jnp.dot(
        route_ref[...],
        jnp.concatenate(split_three(messages), axis=0),
        preferred_element_type=jnp.float32,
    )
    emitted = selected[:states] * sums_ref[pl.ds(0, 1)]
    for b in range(1, outer * inner):
        emitted += selected[b * states : (b + 1) * states] * sums_ref[pl.ds(b, 1)]
    halves = jnp.concatenate(split_wide(emitted), axis=0)
    for i, o, k in device_order(outer, inner):
        product = dot_rows(halves, transition_ref[pl.ds(k * rows, rows)])
        out_ref[i, o] = (product[:states] + product[states:]).astype(out_ref.dtype)


def step(transition, route, sums, parts, dtype, outer, inner):
    return pl.pallas_call(
        functools.partial(step_kernel, outer, inner),
        out_shape=jax.ShapeDtypeStruct((inner, outer) + parts.shape[1:], dtype),
        in_specs=[VMEM] * 4,
        out_specs=VMEM,
        compiler_params=pltpu.CompilerParams(vmem_limit_bytes=LIMIT),
        name="backward_step",
    )(resident(transition), route, sums, parts)


def weigh_kernel(outer, inner, emission_ref, forward_ref, chooser_ref, logits_ref, parts_ref, raised_ref, pair_ref):
    rows = emission_ref.shape[0] // (outer * inner)
    chooser = chooser_ref[...]
    logits = logits_ref[...].astype(jnp.float32)
    top = jnp.max(logits, axis=1, keepdims=True)
    weights = jnp.zeros(logits.shape, jnp.float32)
    for i, o, k in device_order(outer, inner):
        span = pl.ds(k * rows, rows)
        pieces = jnp.concatenate(split_three(parts_ref[i, o]), axis=0)
        chosen = jnp.dot(chooser, pieces, preferred_element_type=jnp.float32)
        forward = forward_ref[:, span].astype(jnp.float32)
        scaled = (forward * chosen).astype(jnp.bfloat16)
        weights += jnp.dot(scaled, emission_ref[span], preferred_element_type=jnp.float32)
    allowed = jnp.sum(chooser.astype(jnp.float32), axis=1, keepdims=True) > 0
    raised = jnp.where(allowed, jnp.exp(logits - top) * weights, 0.0)
    raised_ref[...] = raised
    total = jnp.sum(raised, axis=1, keepdims=True)
    lane = lax.broadcasted_iota(jnp.int32, pair_ref.shape, 1)
    pair_ref[...] = jnp.where(lane == 0, top, total)


def weigh(emission, forward, chooser, logits, parts, outer, inner):
    return pl.pallas_call(
        functools.partial(weigh_kernel, outer, inner),
        out_shape=[
            jax.ShapeDtypeStruct(logits.shape, jnp.float32),
            jax.ShapeDtypeStruct((logits.shape[0], 128), jnp.float32),
        ],
        in_specs=[VMEM] * 5,
        out_specs=[VMEM] * 2,
        compiler_params=pltpu.CompilerParams(vmem_limit_bytes=LIMIT),
        name="weigh_tokens",
    )(resident(emission), forward, chooser, logits, parts)


def finish_kernel(devices, raised_ref, pair_ref, pairs_ref, out_ref):
    own_top = pair_ref[:, :1]
    top = own_top
    for k in range(pairs_ref.shape[0]):
        top = jnp.maximum(top, pairs_ref[k, :, :1])
    total = jnp.zeros_like(top)
    for k in range(pairs_ref.shape[0]):
        total += pairs_ref[k, :, 1:2] * jnp.exp(pairs_ref[k, :, :1] - top)
    raised = raised_ref[...] * jnp.exp(own_top - top)
    out_ref[...] = BLK * devices * raised / total


def finish(raised, pair, pairs):
    return pl.pallas_call(
        functools.partial(finish_kernel, pairs.shape[0]),
        out_shape=jax.ShapeDtypeStruct(raised.shape, jnp.float32),
        in_specs=[VMEM] * 3,
        out_specs=VMEM,
        name="normalise",
    )(raised, pair, pairs)


def forward_messages(emission, last_token, prior_msg, devices, device):
    hidden = emission.shape[0]
    local_rows = prior_msg.shape[0]
    token_ids = jnp.arange(BLK, dtype=jnp.int32)
    tokens = last_token - device * BLK
    onehot = (tokens[:, None] == token_ids[None, :]).astype(jnp.bfloat16)
    owned = dot_rows(onehot, emission)
    owned = owned.astype(jnp.bfloat16).reshape(devices, local_rows, hidden)
    columns = jnp.sum(exchange(owned), axis=0, dtype=jnp.float32)
    unnormal = prior_msg * columns
    forward_msg = (unnormal / jnp.sum(unnormal, axis=1, keepdims=True)).astype(jnp.bfloat16)
    return spread(forward_msg, devices).reshape(devices * local_rows, hidden)


def per_device(
    emission,
    transition,
    beta_start,
    allow_list,
    trans_table,
    last_token,
    prompt_state,
    prior_msg,
    lm_logits,
):
    outer, inner = lax.axis_size("outer"), lax.axis_size("inner")
    devices = outer * inner
    device = lax.axis_index(AXES)
    hidden = emission.shape[0]
    states = beta_start.shape[1]
    own_rows = transition.shape[1]
    prompts = prompt_state.shape[0]
    state_ids = jnp.arange(states, dtype=jnp.int32)
    block_ids = jnp.arange(devices, dtype=jnp.int32)
    allowed = jnp.any(allow_list[:, :, None] == block_ids, axis=1)
    forward_all = forward_messages(emission, last_token, prior_msg, devices, device)
    dest_here = lax.dynamic_index_in_dim(trans_table, device, axis=1, keepdims=False)
    allow_here = jnp.any(allow_list == device, axis=1)
    dest_rows = jnp.sum(jnp.where(prompt_state[:, None] == state_ids, dest_here, 0), axis=1)
    allow_rows = jnp.any((prompt_state[:, None] == state_ids) & allow_here, axis=1)
    chooser = (dest_rows[:, None] == state_ids) & allow_rows[:, None]
    messages = lax.dynamic_slice_in_dim(beta_start, device * own_rows, own_rows, 0).T
    if own_rows % 128 == 0:
        dests, allowed_to = trans_table.T, allowed.T
        route = (dests[:, :, None] == state_ids) & allowed_to[:, :, None]
        route = route.reshape(devices * states, states).astype(jnp.bfloat16)
        route = jnp.concatenate([route] * 3, axis=1)
        near = exchange(block_sums(emission, outer, inner), "inner")
        sums = exchange(near.transpose(1, 0, 2), "outer").reshape(devices, own_rows)
        parts = messages[None]
        for window_step in range(STEPS):
            dtype = jnp.bfloat16 if window_step < STEPS - 1 else jnp.float32
            blocks = step(transition, route, sums, parts, dtype, outer, inner)
            parts = scatter_sum(blocks, dtype)
        messages = jnp.sum(parts, axis=0)
        everywhere = two_stage_spread(messages, outer, inner)
        chooser = jnp.concatenate([chooser.astype(jnp.bfloat16)] * 3, axis=1)
        raised, pair = weigh(emission, forward_all, chooser, lm_logits, everywhere, outer, inner)
        pairs = two_stage_spread(pair, outer, inner).reshape((devices,) + pair.shape)
        return messages.T, finish(raised, pair, pairs)
    own_sums = exchange(jnp.sum(emission, axis=1, dtype=jnp.float32).reshape(devices, own_rows))
    route = allowed.T[:, :, None] & (trans_table.T[:, :, None] == state_ids)
    route = route.astype(jnp.float32).reshape(devices * states, states)
    by_owner = transition.reshape(devices, own_rows, own_rows)
    for window_step in range(STEPS):
        selected = jnp.dot(route, messages, precision=lax.Precision.HIGHEST)
        selected = selected.reshape(devices, states, own_rows)
        emitted = jnp.sum(selected * own_sums[:, None, :], axis=0)
        halves = jnp.concatenate(split_wide(emitted), axis=0)
        partial = jnp.einsum("dzy,sy->dsz", by_owner, halves, preferred_element_type=jnp.float32)
        partial = partial[:, :states] + partial[:, states:]
        if window_step < STEPS - 1:
            partial = partial.astype(jnp.bfloat16)
        messages = jnp.sum(exchange(partial), axis=0, dtype=jnp.float32)
    everywhere = spread(messages, devices)
    chosen = jnp.einsum(
        "ps,dsz->pdz", chooser.astype(jnp.float32), everywhere, precision=lax.Precision.HIGHEST
    )
    forward_all = forward_all.reshape(prompts, devices, own_rows).astype(jnp.float32)
    scaled = (forward_all * chosen).astype(jnp.bfloat16).reshape(prompts, hidden)
    weights = jnp.dot(scaled, emission, preferred_element_type=jnp.float32)
    weights = jnp.where(allow_rows[:, None], weights, 0.0)
    logits = lm_logits.astype(jnp.float32)
    top_here = jnp.max(logits, axis=1)
    raised = jnp.exp(logits - top_here[:, None]) * weights
    pairs = spread(jnp.stack([top_here, jnp.sum(raised, axis=1)]), devices)
    tops, totals = pairs[:, 0], pairs[:, 1]
    top = jnp.max(tops, axis=0)
    total = jnp.sum(totals * jnp.exp(tops - top), axis=0)
    raised = raised * jnp.exp(top_here - top)[:, None]
    return (messages.T, BLK * devices * raised / total[:, None])


def solution(mesh):
    parts, devices = mesh.devices.shape
    inner = 1
    while inner * inner < devices:
        inner *= 2
    staged = Mesh(np.reshape(mesh.devices, (parts, devices // inner, inner)), ("parts",) + AXES)
    return jax.shard_map(
        per_device,
        mesh=staged,
        in_specs=(
            P(None, AXES),
            P(None, AXES),
            P(),
            P(),
            P(),
            P("parts"),
            P("parts"),
            P(("parts",) + AXES, None),
            P("parts", AXES),
        ),
        out_specs=(P(("parts",) + AXES, None), P("parts", AXES)),
        check_vma=False,
    )
```

```python
import functools

import jax
import jax.numpy as jnp
from jax import lax
from jax.experimental import pallas as pl
from jax.experimental.pallas import tpu as pltpu
from jax.sharding import PartitionSpec as P

BLK = 256
STEPS = 3
LIMIT = 16 * 1024 * 1024
VMEM = pl.BlockSpec(memory_space=pltpu.VMEM)
HBM = pl.BlockSpec(memory_space=pltpu.HBM)


def exchange(blocks):
    return lax.all_to_all(blocks, "vocab", split_axis=0, concat_axis=0, tiled=True)


def spread(own, devices):
    return exchange(jnp.broadcast_to(own[None], (devices,) + own.shape))


def swap(block, bit, devices):
    pairs = [(i, i ^ (1 << bit)) for i in range(devices)]
    return lax.ppermute(block, "vocab", pairs)


def split_wide(wide):
    high = wide.astype(jnp.bfloat16)
    low = (wide - high.astype(jnp.float32)).astype(jnp.bfloat16)
    return high, low


def split_three(wide):
    high = wide.astype(jnp.bfloat16)
    rest = wide - high.astype(jnp.float32)
    middle = rest.astype(jnp.bfloat16)
    low = (rest - middle.astype(jnp.float32)).astype(jnp.bfloat16)
    return high, middle, low


def dot_rows(left, right):
    return lax.dot_general(left, right, (((1,), (1,)), ((), ())), preferred_element_type=jnp.float32)


def bit_places(count, low_bit=0):
    places = []
    for i in range(1 << count):
        bits = [(i >> b) & 1 for b in range(count)]
        places.append((tuple(bits), i << low_bit))
    return sorted(places)


def partner_rows(i, rows):
    owner = lax.axis_index("vocab") ^ i
    return pl.ds(pl.multiple_of(owner * rows, rows), rows)


def scatter_blocks(blocks, devices, count):
    own = blocks
    for bit in range(count):
        kept = lax.index_in_dim(own, 0, axis=bit, keepdims=False)
        sent = lax.index_in_dim(own, 1, axis=bit, keepdims=False)
        own = jnp.stack([kept, swap(sent, bit, devices)])
    return own


def reduce_blocks(kept, received, dtype, devices, count):
    for bit in range(1, count):
        total = kept + received.astype(jnp.float32)
        received = swap(total[1].astype(dtype), bit, devices)
        kept = total[0]
    return kept, received


def gather_blocks(own, devices, count):
    for bit in range(count - 1, 0, -1):
        own = jnp.stack([own, swap(own, bit, devices)])
    return own, swap(own, 0, devices)


def sums_kernel(count, emission_ref, out_ref, held_ref, sems):
    devices = 1 << count
    rows = emission_ref.shape[0] // devices
    copies = {}
    for bits, i in bit_places(count):
        span = partner_rows(i, rows)
        copies[i] = pltpu.make_async_copy(emission_ref.at[span], held_ref.at[span], sems.at[i])
        copies[i].start()
    ones = jnp.ones((16, emission_ref.shape[1]), jnp.bfloat16)
    for bits, i in bit_places(count):
        copies[i].wait()
        place = bits[:-1] + (pl.ds(bits[-1], 1),)
        out_ref[place] = dot_rows(ones, held_ref[partner_rows(i, rows)])[:1]


def block_sums(emission, count):
    hidden = emission.shape[0]
    shape = (2,) * count + (hidden >> count,)
    return pl.pallas_call(
        functools.partial(sums_kernel, count),
        out_shape=[
            jax.ShapeDtypeStruct(shape, jnp.float32),
            pltpu.VMEM(emission.shape, emission.dtype),
        ],
        in_specs=[HBM],
        out_specs=[VMEM] * 2,
        scratch_shapes=[pltpu.SemaphoreType.DMA((1 << count,))],
        compiler_params=pltpu.CompilerParams(vmem_limit_bytes=LIMIT),
        name="block_sums",
    )(emission)


def hold_kernel(pieces, source_ref, after_ref, held_ref, sems):
    rows = source_ref.shape[0] // pieces
    copies = []
    for k in range(pieces):
        span = pl.ds(k * rows, rows)
        copies.append(pltpu.make_async_copy(source_ref.at[span], held_ref.at[span], sems.at[k]))
        copies[k].start()
    for copy in copies:
        copy.wait()


def hold(source, after, pieces=8):
    return pl.pallas_call(
        functools.partial(hold_kernel, pieces),
        out_shape=pltpu.VMEM(source.shape, source.dtype),
        in_specs=[HBM, pl.BlockSpec(memory_space=pl.ANY)],
        out_specs=VMEM,
        scratch_shapes=[pltpu.SemaphoreType.DMA((pieces,))],
        compiler_params=pltpu.CompilerParams(vmem_limit_bytes=LIMIT),
        name="hold_transition",
    )(source, after)


def half_products(halves, transition_ref, out_ref, count, first):
    states = halves.shape[0] // 2
    rows = transition_ref.shape[0] >> count
    for bits, i in bit_places(count - 1, 1):
        product = dot_rows(halves, transition_ref[partner_rows(i + first, rows)])
        out_ref[bits] = (product[:states] + product[states:]).astype(out_ref.dtype)


def send_kernel(count, transition_ref, route_ref, sums_ref, *refs):
    parts, (halves_ref, out_ref) = refs[:-2], refs[-2:]
    messages = parts[0][...].astype(jnp.float32)
    for part in parts[1:]:
        messages += part[...].astype(jnp.float32)
    states = messages.shape[0]
    selected = jnp.dot(
        route_ref[...],
        jnp.concatenate(split_three(messages), axis=0),
        preferred_element_type=jnp.float32,
    )
    emitted = selected[:states] * sums_ref[pl.ds(0, 1)]
    for b in range(1, 1 << count):
        emitted += selected[b * states : (b + 1) * states] * sums_ref[pl.ds(b, 1)]
    halves = jnp.concatenate(split_wide(emitted), axis=0)
    halves_ref[...] = halves
    half_products(halves, transition_ref, out_ref, count, 1)


def keep_kernel(count, transition_ref, halves_ref, out_ref):
    half_products(halves_ref[...], transition_ref, out_ref, count, 0)


def step(transition, route, sums, parts, dtype, devices, count):
    states, rows = parts[0].shape
    shape = (2,) * (count - 1) + (states, rows)
    params = pltpu.CompilerParams(vmem_limit_bytes=LIMIT)
    halves, sent = pl.pallas_call(
        functools.partial(send_kernel, count),
        out_shape=[
            pltpu.VMEM((2 * states, rows), jnp.bfloat16),
            pltpu.VMEM(shape, dtype),
        ],
        in_specs=[VMEM] * (3 + len(parts)),
        out_specs=[VMEM] * 2,
        compiler_params=params,
        name="step_sent_half",
    )(transition, route, sums, *parts)
    received = swap(sent, 0, devices)
    kept = pl.pallas_call(
        functools.partial(keep_kernel, count),
        out_shape=pltpu.VMEM(shape, jnp.float32),
        in_specs=[VMEM] * 2,
        out_specs=VMEM,
        compiler_params=params,
        name="step_kept_half",
    )(transition, halves)
    return reduce_blocks(kept, received, dtype, devices, count)


def weigh_half(emission_ref, forward_ref, chooser, parts_ref, count, first):
    rows = emission_ref.shape[0] >> count
    weights = jnp.zeros((chooser.shape[0], emission_ref.shape[1]), jnp.float32)
    for bits, i in bit_places(count - 1, 1):
        pieces = jnp.concatenate(split_three(parts_ref[bits]), axis=0)
        chosen = jnp.dot(chooser, pieces, preferred_element_type=jnp.float32)
        forward = forward_ref[i + first].astype(jnp.float32)
        scaled = (forward * chosen).astype(jnp.bfloat16)
        tile = emission_ref[partner_rows(i + first, rows)]
        weights += jnp.dot(scaled, tile, preferred_element_type=jnp.float32)
    return weights


def near_kernel(count, emission_ref, forward_ref, chooser_ref, parts_ref, out_ref):
    out_ref[...] = weigh_half(emission_ref, forward_ref, chooser_ref[...], parts_ref, count, 0)


def far_kernel(count, emission_ref, forward_ref, chooser_ref, logits_ref, near_ref, parts_ref, raised_ref, pair_ref):
    chooser = chooser_ref[...]
    logits = logits_ref[...].astype(jnp.float32)
    top = jnp.max(logits, axis=1, keepdims=True)
    weights = near_ref[...] + weigh_half(emission_ref, forward_ref, chooser, parts_ref, count, 1)
    allowed = jnp.sum(chooser.astype(jnp.float32), axis=1, keepdims=True) > 0
    raised = jnp.where(allowed, jnp.exp(logits - top) * weights, 0.0)
    raised_ref[...] = raised
    total = jnp.sum(raised, axis=1, keepdims=True)
    lane = lax.broadcasted_iota(jnp.int32, pair_ref.shape, 1)
    pair_ref[...] = jnp.where(lane == 0, top, total)


def weigh(emission, forward, chooser, logits, near, far, count):
    params = pltpu.CompilerParams(vmem_limit_bytes=LIMIT)
    half = pl.pallas_call(
        functools.partial(near_kernel, count),
        out_shape=pltpu.VMEM(logits.shape, jnp.float32),
        in_specs=[VMEM] * 4,
        out_specs=VMEM,
        compiler_params=params,
        name="weigh_near",
    )(emission, forward, chooser, near)
    return pl.pallas_call(
        functools.partial(far_kernel, count),
        out_shape=[
            pltpu.VMEM(logits.shape, jnp.float32),
            pltpu.VMEM((logits.shape[0], 128), jnp.float32),
        ],
        in_specs=[VMEM] * 6,
        out_specs=[VMEM] * 2,
        compiler_params=params,
        name="weigh_far",
    )(emission, forward, chooser, logits, half, far)


def normalise(raised, pair, devices, count):
    own_top = top = pair[:, :1]
    total = pair[:, 1:2]
    for bit in range(count):
        other = swap(jnp.concatenate([top, total], axis=1).T, bit, devices).T
        other_top, other_total = other[:, :1], other[:, 1:]
        both = jnp.maximum(top, other_top)
        total = total * jnp.exp(top - both) + other_total * jnp.exp(other_top - both)
        top = both
    return BLK * devices * (raised * jnp.exp(own_top - top)) / total


def owned_kernel(count, tokens_ref, emission_ref, out_ref):
    rows = emission_ref.shape[0] >> count
    tokens = tokens_ref[...] - lax.axis_index("vocab") * BLK
    ids = lax.broadcasted_iota(jnp.int32, (tokens.shape[0], BLK), 1)
    onehot = (tokens == ids).astype(jnp.bfloat16)
    for k in range(1 << count):
        product = dot_rows(onehot, emission_ref[pl.ds(k * rows, rows)])
        out_ref[:, k, :] = product.astype(jnp.bfloat16)


def forward_kernel(prior_ref, routed_ref, out_ref):
    columns = routed_ref[0].astype(jnp.float32)
    for k in range(1, routed_ref.shape[0]):
        columns += routed_ref[k].astype(jnp.float32)
    unnormal = prior_ref[...] * columns
    forward = unnormal / jnp.sum(unnormal)
    for d in range(out_ref.shape[0]):
        for i in range(out_ref.shape[1]):
            out_ref[d, pl.ds(i, 1), :] = forward[d ^ i : (d ^ i) + 1].astype(jnp.bfloat16)


def forward_blocks(emission, last_token, prior_msg, devices, count):
    hidden = emission.shape[0]
    shape = (devices, devices, hidden // devices)
    params = pltpu.CompilerParams(vmem_limit_bytes=LIMIT)
    owned = pl.pallas_call(
        functools.partial(owned_kernel, count),
        out_shape=jax.ShapeDtypeStruct(shape, jnp.bfloat16),
        in_specs=[VMEM] * 2,
        out_specs=VMEM,
        compiler_params=params,
        name="owned_columns",
    )(last_token[:, None], emission)
    copies = pl.pallas_call(
        forward_kernel,
        out_shape=jax.ShapeDtypeStruct(shape, jnp.bfloat16),
        in_specs=[VMEM] * 2,
        out_specs=VMEM,
        compiler_params=params,
        name="forward_messages",
    )(prior_msg.reshape(shape[1:]), exchange(owned))
    return exchange(copies).transpose(1, 0, 2)


def forward_messages(emission, last_token, prior_msg, devices, device):
    hidden = emission.shape[0]
    local_rows = prior_msg.shape[0]
    token_ids = jnp.arange(BLK, dtype=jnp.int32)
    tokens = last_token - device * BLK
    onehot = (tokens[:, None] == token_ids[None, :]).astype(jnp.bfloat16)
    owned = dot_rows(onehot, emission)
    owned = owned.astype(jnp.bfloat16).reshape(devices, local_rows, hidden)
    columns = jnp.sum(exchange(owned), axis=0, dtype=jnp.float32)
    unnormal = prior_msg * columns
    forward_msg = (unnormal / jnp.sum(unnormal, axis=1, keepdims=True)).astype(jnp.bfloat16)
    return spread(forward_msg, devices).reshape(devices * local_rows, hidden)


def per_device(
    emission,
    transition,
    beta_start,
    allow_list,
    trans_table,
    last_token,
    prompt_state,
    prior_msg,
    lm_logits,
):
    devices = lax.axis_size("vocab")
    device = lax.axis_index("vocab")
    hidden = emission.shape[0]
    states = beta_start.shape[1]
    own_rows = transition.shape[1]
    prompts = prompt_state.shape[0]
    state_ids = jnp.arange(states, dtype=jnp.int32)
    block_ids = jnp.arange(devices, dtype=jnp.int32)
    allowed = jnp.any(allow_list[:, :, None] == block_ids, axis=1)
    dest_here = lax.dynamic_index_in_dim(trans_table, device, axis=1, keepdims=False)
    allow_here = jnp.any(allow_list == device, axis=1)
    dest_rows = jnp.sum(jnp.where(prompt_state[:, None] == state_ids, dest_here, 0), axis=1)
    allow_rows = jnp.any((prompt_state[:, None] == state_ids) & allow_here, axis=1)
    chooser = (dest_rows[:, None] == state_ids) & allow_rows[:, None]
    messages = lax.dynamic_slice_in_dim(beta_start, device * own_rows, own_rows, 0).T
    count = devices.bit_length() - 1
    if devices == 1 << count and own_rows % 128 == 0 and prompts == devices:
        partners = device ^ block_ids
        order = (partners[:, None] == block_ids).astype(jnp.int32)
        dests = jnp.sum(order[:, None, :] * trans_table[None], axis=2)
        allowed_to = jnp.sum(order[:, None, :] * allowed[None], axis=2) > 0
        route = (dests[:, :, None] == state_ids) & allowed_to[:, :, None]
        route = route.reshape(devices * states, states).astype(jnp.bfloat16)
        route = jnp.concatenate([route] * 3, axis=1)
        sums, held_emission = block_sums(emission, count)
        held_transition = hold(transition, sums)
        sums = scatter_blocks(sums, devices, count).reshape(devices, own_rows)
        forward = forward_blocks(held_emission, last_token, prior_msg, devices, count)
        parts = (messages,)
        for window_step in range(STEPS):
            dtype = jnp.bfloat16 if window_step < STEPS - 1 else jnp.float32
            parts = step(held_transition, route, sums, parts, dtype, devices, count)
        messages = parts[0] + parts[1]
        near, far = gather_blocks(messages, devices, count)
        chooser = jnp.concatenate([chooser.astype(jnp.bfloat16)] * 3, axis=1)
        raised, pair = weigh(held_emission, forward, chooser, lm_logits, near, far, count)
        return messages.T, normalise(raised, pair, devices, count)
    forward_all = forward_messages(emission, last_token, prior_msg, devices, device)
    own_sums = exchange(jnp.sum(emission, axis=1, dtype=jnp.float32).reshape(devices, own_rows))
    route = allowed.T[:, :, None] & (trans_table.T[:, :, None] == state_ids)
    route = route.astype(jnp.float32).reshape(devices * states, states)
    by_owner = transition.reshape(devices, own_rows, own_rows)
    for window_step in range(STEPS):
        selected = jnp.dot(route, messages, precision=lax.Precision.HIGHEST)
        selected = selected.reshape(devices, states, own_rows)
        emitted = jnp.sum(selected * own_sums[:, None, :], axis=0)
        halves = jnp.concatenate(split_wide(emitted), axis=0)
        partial = jnp.einsum("dzy,sy->dsz", by_owner, halves, preferred_element_type=jnp.float32)
        partial = partial[:, :states] + partial[:, states:]
        if window_step < STEPS - 1:
            partial = partial.astype(jnp.bfloat16)
        messages = jnp.sum(exchange(partial), axis=0, dtype=jnp.float32)
    everywhere = spread(messages, devices)
    chosen = jnp.einsum(
        "ps,dsz->pdz", chooser.astype(jnp.float32), everywhere, precision=lax.Precision.HIGHEST
    )
    forward_all = forward_all.reshape(prompts, devices, own_rows).astype(jnp.float32)
    scaled = (forward_all * chosen).astype(jnp.bfloat16).reshape(prompts, hidden)
    weights = jnp.dot(scaled, emission, preferred_element_type=jnp.float32)
    weights = jnp.where(allow_rows[:, None], weights, 0.0)
    logits = lm_logits.astype(jnp.float32)
    top_here = jnp.max(logits, axis=1)
    raised = jnp.exp(logits - top_here[:, None]) * weights
    pairs = spread(jnp.stack([top_here, jnp.sum(raised, axis=1)]), devices)
    tops, totals = pairs[:, 0], pairs[:, 1]
    top = jnp.max(tops, axis=0)
    total = jnp.sum(totals * jnp.exp(tops - top), axis=0)
    raised = raised * jnp.exp(top_here - top)[:, None]
    return (messages.T, BLK * devices * raised / total[:, None])


def solution(mesh):
    return jax.shard_map(
        per_device,
        mesh=mesh,
        in_specs=(
            P(None, "vocab"),
            P(None, "vocab"),
            P(),
            P(),
            P(),
            P("parts"),
            P("parts"),
            P(("parts", "vocab"), None),
            P("parts", "vocab"),
        ),
        out_specs=(P(("parts", "vocab"), None), P("parts", "vocab")),
        check_vma=False,
    )
```

```python
import functools

import jax
import jax.numpy as jnp
from jax import lax
from jax.experimental import pallas as pl
from jax.experimental.pallas import tpu as pltpu
from jax.sharding import PartitionSpec as P

BLK = 256
STEPS = 3
LIMIT = 16 * 1024 * 1024
VMEM = pl.BlockSpec(memory_space=pltpu.VMEM)
ANY = pl.BlockSpec(memory_space=pl.ANY)
PARAMS = pltpu.CompilerParams(vmem_limit_bytes=LIMIT)


def exchange(blocks):
    return lax.all_to_all(blocks, "vocab", split_axis=0, concat_axis=0, tiled=True)


def spread(own, devices):
    return exchange(jnp.broadcast_to(own[None], (devices,) + own.shape))


def basis(count):
    return [1] + [1 | (1 << bit) for bit in range(1, count)]


def swap(block, bit, devices):
    offset = basis(bit + 1)[bit]
    pairs = [(i, i ^ offset) for i in range(devices)]
    return lax.ppermute(block, "vocab", pairs)


def split_wide(wide):
    high = wide.astype(jnp.bfloat16)
    low = (wide - high.astype(jnp.float32)).astype(jnp.bfloat16)
    return high, low


def split_three(wide):
    high = wide.astype(jnp.bfloat16)
    rest = wide - high.astype(jnp.float32)
    middle = rest.astype(jnp.bfloat16)
    low = (rest - middle.astype(jnp.float32)).astype(jnp.bfloat16)
    return high, middle, low


def dot_rows(left, right):
    return lax.dot_general(left, right, (((1,), (1,)), ((), ())), preferred_element_type=jnp.float32)


def partner_of(bits):
    partner = 0
    for bit, offset in zip(bits, basis(len(bits))):
        partner ^= bit * offset
    return partner


def all_bits(count):
    return [tuple((k >> (count - 1 - b)) & 1 for b in range(count)) for k in range(1 << count)]


def partner_rows(i, rows):
    owner = lax.axis_index("vocab") ^ i
    return pl.ds(pl.multiple_of(owner * rows, rows), rows)


def scatter_blocks(blocks, devices, count):
    own = blocks
    for bit in range(count):
        kept = lax.index_in_dim(own, 0, axis=bit, keepdims=False)
        sent = lax.index_in_dim(own, 1, axis=bit, keepdims=False)
        own = jnp.stack([kept, swap(sent, bit, devices)])
    return own


def reduce_blocks(kept, received, dtype, devices, count):
    for bit in range(1, count):
        total = kept + received.astype(jnp.float32)
        received = swap(total[1].astype(dtype), bit, devices)
        kept = total[0]
    return kept, received


def gather_blocks(own, devices, count):
    for bit in range(count - 1, 0, -1):
        own = jnp.stack([own, swap(own, bit, devices)])
    return own, swap(own, 0, devices)


def sums_kernel(count, emission_ref, out_ref):
    rows = emission_ref.shape[0] >> count
    ones = jnp.ones((16, emission_ref.shape[1]), jnp.bfloat16)
    for bits in all_bits(count):
        tile = emission_ref[partner_rows(partner_of(bits), rows)]
        out_ref[bits[:-1] + (pl.ds(bits[-1], 1),)] = dot_rows(ones, tile)[:1]


def block_sums(emission, count):
    shape = (2,) * count + (emission.shape[0] >> count,)
    return pl.pallas_call(
        functools.partial(sums_kernel, count),
        out_shape=pltpu.VMEM(shape, jnp.float32),
        in_specs=[VMEM],
        out_specs=VMEM,
        compiler_params=PARAMS,
        name="block_sums",
    )(emission)


def owned_kernel(count, tokens_ref, emission_ref, after_ref, kept_ref, sent_ref, wide_ref):
    rows = emission_ref.shape[0] >> count
    device = lax.axis_index("vocab")
    tokens = tokens_ref[...] - device * BLK
    ids = lax.broadcasted_iota(jnp.int32, (tokens.shape[0], BLK), 1)
    onehot = (tokens == ids).astype(jnp.bfloat16)
    for k in range(1 << count):
        wide_ref[:, k, :] = dot_rows(onehot, emission_ref[pl.ds(k * rows, rows)])
    for bits in all_bits(count):
        out_ref = sent_ref if bits[0] else kept_ref
        out_ref[bits[1:]] = wide_ref[device ^ partner_of(bits)].astype(jnp.bfloat16)


def owned_columns(last_token, emission, after, count):
    prompts, rows = last_token.shape[0], emission.shape[0] >> count
    half = pltpu.VMEM((2,) * (count - 1) + (prompts, rows), jnp.bfloat16)
    return pl.pallas_call(
        functools.partial(owned_kernel, count),
        out_shape=[half, half],
        in_specs=[VMEM, VMEM, ANY],
        out_specs=[VMEM] * 2,
        scratch_shapes=[pltpu.VMEM((prompts, prompts, rows), jnp.float32)],
        compiler_params=PARAMS,
        name="owned_columns",
    )(last_token[:, None], emission, after)


def forward_kernel(prior_ref, kept_ref, received_ref, out_ref):
    unnormal = prior_ref[...] * (kept_ref[...] + received_ref[...].astype(jnp.float32))
    out_ref[...] = (unnormal / jnp.sum(unnormal)).astype(jnp.bfloat16)


def forward_messages_here(prior, kept, received):
    return pl.pallas_call(
        forward_kernel,
        out_shape=pltpu.VMEM(prior.shape, jnp.bfloat16),
        in_specs=[VMEM] * 3,
        out_specs=VMEM,
        compiler_params=PARAMS,
        name="forward_messages",
    )(prior, kept, received)


def order_kernel(count, near_ref, far_ref, out_ref):
    size = 1 << count
    device = lax.axis_index("vocab")

    def partner(place):
        number = jnp.zeros_like(place)
        for bit, offset in enumerate(basis(count)):
            number = number ^ (((place >> (count - 1 - bit)) & 1) * offset)
        return device ^ number

    shape = (size * size, size * size)
    to, source = (lax.broadcasted_iota(jnp.int32, shape, axis) for axis in (0, 1))
    same_block = partner(to >> count) == (source & (size - 1))
    same_prompt = (to & (size - 1)) == partner(source >> count)
    onehot = (same_block & same_prompt).astype(jnp.bfloat16)
    half = size * size // 2
    rows = out_ref.shape[1]
    near = near_ref[...].reshape(half, rows)
    far = far_ref[...].reshape(half, rows)
    ordered = jnp.dot(onehot[:, :half], near, preferred_element_type=jnp.float32)
    ordered += jnp.dot(onehot[:, half:], far, preferred_element_type=jnp.float32)
    out_ref[...] = ordered.astype(jnp.bfloat16)


def order_forward(near, far, count):
    rows = near.shape[-1]
    return pl.pallas_call(
        functools.partial(order_kernel, count),
        out_shape=pltpu.VMEM((1 << (2 * count), rows), jnp.bfloat16),
        in_specs=[VMEM] * 2,
        out_specs=VMEM,
        compiler_params=PARAMS,
        name="order_forward",
    )(near, far)


def last_kernel(kept_ref, received_ref, after_ref, out_ref):
    out_ref[...] = kept_ref[...] + received_ref[...]


def last_sum(kept, received, after):
    return pl.pallas_call(
        last_kernel,
        out_shape=pltpu.VMEM(kept.shape, jnp.float32),
        in_specs=[VMEM, VMEM, ANY],
        out_specs=VMEM,
        compiler_params=PARAMS,
        name="last_messages",
    )(kept, received, after)


def half_products(halves, transition_ref, out_ref, count, first):
    states = halves.shape[0] // 2
    rows = transition_ref.shape[0] >> count
    for bits in all_bits(count - 1):
        partner = partner_of((first,) + bits)
        product = dot_rows(halves, transition_ref[partner_rows(partner, rows)])
        out_ref[bits] = (product[:states] + product[states:]).astype(out_ref.dtype)


def send_kernel(count, number, transition_ref, route_ref, sums_ref, *refs):
    parts, (halves_ref, out_ref) = refs[:number], refs[-2:]
    messages = parts[0][...].astype(jnp.float32)
    for part in parts[1:]:
        messages += part[...].astype(jnp.float32)
    states = messages.shape[0]
    selected = jnp.dot(
        route_ref[...],
        jnp.concatenate(split_three(messages), axis=0),
        preferred_element_type=jnp.float32,
    )
    emitted = selected[:states] * sums_ref[pl.ds(0, 1)]
    for b in range(1, 1 << count):
        emitted += selected[b * states : (b + 1) * states] * sums_ref[pl.ds(b, 1)]
    halves = jnp.concatenate(split_wide(emitted), axis=0)
    halves_ref[...] = halves
    half_products(halves, transition_ref, out_ref, count, 1)


def keep_kernel(count, transition_ref, halves_ref, out_ref):
    half_products(halves_ref[...], transition_ref, out_ref, count, 0)


def step(transition, route, sums, parts, after, dtype, devices, count):
    states, rows = parts[0].shape
    shape = (2,) * (count - 1) + (states, rows)
    halves, sent = pl.pallas_call(
        functools.partial(send_kernel, count, len(parts)),
        out_shape=[
            pltpu.VMEM((2 * states, rows), jnp.bfloat16),
            pltpu.VMEM(shape, dtype),
        ],
        in_specs=[VMEM] * (3 + len(parts)) + [ANY] * len(after),
        out_specs=[VMEM] * 2,
        compiler_params=PARAMS,
        name="step_sent_half",
    )(transition, route, sums, *parts, *after)
    received = swap(sent, 0, devices)
    kept = pl.pallas_call(
        functools.partial(keep_kernel, count),
        out_shape=pltpu.VMEM(shape, jnp.float32),
        in_specs=[VMEM] * 2,
        out_specs=VMEM,
        compiler_params=PARAMS,
        name="step_kept_half",
    )(transition, halves)
    return kept, received


def weigh_half(emission_ref, forward_ref, chooser, parts_ref, count, first):
    rows = emission_ref.shape[0] >> count
    prompts = chooser.shape[0]
    weights = jnp.zeros((prompts, emission_ref.shape[1]), jnp.float32)
    for place, bits in enumerate(all_bits(count - 1)):
        pieces = jnp.concatenate(split_three(parts_ref[bits]), axis=0)
        chosen = jnp.dot(chooser, pieces, preferred_element_type=jnp.float32)
        block = place + (first << (count - 1))
        forward = forward_ref[pl.ds(block * prompts, prompts)].astype(jnp.float32)
        scaled = (forward * chosen).astype(jnp.bfloat16)
        tile = emission_ref[partner_rows(partner_of((first,) + bits), rows)]
        weights += jnp.dot(scaled, tile, preferred_element_type=jnp.float32)
    return weights


def near_kernel(count, emission_ref, forward_ref, chooser_ref, parts_ref, out_ref):
    out_ref[...] = weigh_half(emission_ref, forward_ref, chooser_ref[...], parts_ref, count, 0)


def far_kernel(count, emission_ref, forward_ref, chooser_ref, logits_ref, near_ref, parts_ref, raised_ref, pair_ref):
    chooser = chooser_ref[...]
    logits = logits_ref[...].astype(jnp.float32)
    top = jnp.max(logits, axis=1, keepdims=True)
    weights = near_ref[...] + weigh_half(emission_ref, forward_ref, chooser, parts_ref, count, 1)
    allowed = jnp.sum(chooser.astype(jnp.float32), axis=1, keepdims=True) > 0
    raised = jnp.where(allowed, jnp.exp(logits - top) * weights, 0.0)
    raised_ref[...] = raised
    total = jnp.sum(raised, axis=1, keepdims=True)
    lane = lax.broadcasted_iota(jnp.int32, pair_ref.shape, 1)
    pair_ref[...] = jnp.where(lane == 0, top, total)


def weigh(emission, forward, chooser, logits, near, far, count):
    half = pl.pallas_call(
        functools.partial(near_kernel, count),
        out_shape=pltpu.VMEM(logits.shape, jnp.float32),
        in_specs=[VMEM] * 4,
        out_specs=VMEM,
        compiler_params=PARAMS,
        name="weigh_near",
    )(emission, forward, chooser, near)
    return pl.pallas_call(
        functools.partial(far_kernel, count),
        out_shape=[
            pltpu.VMEM(logits.shape, jnp.float32),
            pltpu.VMEM((logits.shape[0], 128), jnp.float32),
        ],
        in_specs=[VMEM] * 6,
        out_specs=[VMEM] * 2,
        compiler_params=PARAMS,
        name="weigh_far",
    )(emission, forward, chooser, logits, half, far)


def normalise(raised, pair, devices):
    pairs = spread(pair[:, :2].T, devices)
    own_top = pair[:, :1]
    tops, totals = pairs[:, 0], pairs[:, 1]
    top = jnp.max(tops, axis=0)
    total = jnp.sum(totals * jnp.exp(tops - top), axis=0)
    return BLK * devices * (raised * jnp.exp(own_top - top[:, None])) / total[:, None]


def forward_messages(emission, last_token, prior_msg, devices, device):
    hidden = emission.shape[0]
    local_rows = prior_msg.shape[0]
    token_ids = jnp.arange(BLK, dtype=jnp.int32)
    tokens = last_token - device * BLK
    onehot = (tokens[:, None] == token_ids[None, :]).astype(jnp.bfloat16)
    owned = dot_rows(onehot, emission)
    owned = owned.astype(jnp.bfloat16).reshape(devices, local_rows, hidden)
    columns = jnp.sum(exchange(owned), axis=0, dtype=jnp.float32)
    unnormal = prior_msg * columns
    forward_msg = (unnormal / jnp.sum(unnormal, axis=1, keepdims=True)).astype(jnp.bfloat16)
    return spread(forward_msg, devices).reshape(devices * local_rows, hidden)


def per_device(
    emission,
    transition,
    beta_start,
    allow_list,
    trans_table,
    last_token,
    prompt_state,
    prior_msg,
    lm_logits,
):
    devices = lax.axis_size("vocab")
    device = lax.axis_index("vocab")
    hidden = emission.shape[0]
    states = beta_start.shape[1]
    own_rows = transition.shape[1]
    prompts = prompt_state.shape[0]
    state_ids = jnp.arange(states, dtype=jnp.int32)
    block_ids = jnp.arange(devices, dtype=jnp.int32)
    allowed = jnp.any(allow_list[:, :, None] == block_ids, axis=1)
    dest_here = lax.dynamic_index_in_dim(trans_table, device, axis=1, keepdims=False)
    allow_here = jnp.any(allow_list == device, axis=1)
    dest_rows = jnp.sum(jnp.where(prompt_state[:, None] == state_ids, dest_here, 0), axis=1)
    allow_rows = jnp.any((prompt_state[:, None] == state_ids) & allow_here, axis=1)
    chooser = (dest_rows[:, None] == state_ids) & allow_rows[:, None]
    messages = lax.dynamic_slice_in_dim(beta_start, device * own_rows, own_rows, 0).T
    count = devices.bit_length() - 1
    if devices == 1 << count and own_rows % 128 == 0 and prompts == devices:
        sources = [partner_of(bits[::-1]) for bits in all_bits(count)]
        partners = device ^ jnp.asarray(sources, jnp.int32)
        order = (partners[:, None] == block_ids).astype(jnp.int32)
        dests = jnp.sum(order[:, None, :] * trans_table[None], axis=2)
        allowed_to = jnp.sum(order[:, None, :] * allowed[None], axis=2) > 0
        route = (dests[:, :, None] == state_ids) & allowed_to[:, :, None]
        route = route.reshape(devices * states, states).astype(jnp.bfloat16)
        route = jnp.concatenate([route] * 3, axis=1)
        sums = block_sums(emission, count)
        columns, sent = owned_columns(last_token, emission, sums, count)
        columns_in = swap(sent, 0, devices)
        sums = scatter_blocks(sums, devices, count).reshape(devices, own_rows)
        parts, after = (messages,), (columns_in,)
        for window_step in range(STEPS):
            dtype = jnp.bfloat16 if window_step < STEPS - 1 else jnp.float32
            kept, received = step(transition, route, sums, parts, after, dtype, devices, count)
            if window_step == 0:
                kept = jnp.concatenate([kept, columns.astype(jnp.float32)], axis=-2)
                received = jnp.concatenate([received, columns_in], axis=-2)
            parts = reduce_blocks(kept, received, dtype, devices, count)
            after = ()
            if window_step == 0:
                prior = prior_msg.reshape(devices, own_rows)
                forward = forward_messages_here(prior, parts[0][states:], parts[1][states:])
                forward_near, forward_far = gather_blocks(forward, devices, count)
                parts = (parts[0][:states], parts[1][:states])
            if window_step == 1:
                after = (forward_near,)
        forward = order_forward(forward_near, forward_far, count)
        messages = last_sum(*parts, forward)
        near, far = gather_blocks(messages, devices, count)
        chooser = jnp.concatenate([chooser.astype(jnp.bfloat16)] * 3, axis=1)
        raised, pair = weigh(emission, forward, chooser, lm_logits, near, far, count)
        return messages.T, normalise(raised, pair, devices)
    forward_all = forward_messages(emission, last_token, prior_msg, devices, device)
    own_sums = exchange(jnp.sum(emission, axis=1, dtype=jnp.float32).reshape(devices, own_rows))
    route = allowed.T[:, :, None] & (trans_table.T[:, :, None] == state_ids)
    route = route.astype(jnp.float32).reshape(devices * states, states)
    by_owner = transition.reshape(devices, own_rows, own_rows)
    for window_step in range(STEPS):
        selected = jnp.dot(route, messages, precision=lax.Precision.HIGHEST)
        selected = selected.reshape(devices, states, own_rows)
        emitted = jnp.sum(selected * own_sums[:, None, :], axis=0)
        halves = jnp.concatenate(split_wide(emitted), axis=0)
        partial = jnp.einsum("dzy,sy->dsz", by_owner, halves, preferred_element_type=jnp.float32)
        partial = partial[:, :states] + partial[:, states:]
        if window_step < STEPS - 1:
            partial = partial.astype(jnp.bfloat16)
        messages = jnp.sum(exchange(partial), axis=0, dtype=jnp.float32)
    everywhere = spread(messages, devices)
    chosen = jnp.einsum(
        "ps,dsz->pdz", chooser.astype(jnp.float32), everywhere, precision=lax.Precision.HIGHEST
    )
    forward_all = forward_all.reshape(prompts, devices, own_rows).astype(jnp.float32)
    scaled = (forward_all * chosen).astype(jnp.bfloat16).reshape(prompts, hidden)
    weights = jnp.dot(scaled, emission, preferred_element_type=jnp.float32)
    weights = jnp.where(allow_rows[:, None], weights, 0.0)
    logits = lm_logits.astype(jnp.float32)
    top_here = jnp.max(logits, axis=1)
    raised = jnp.exp(logits - top_here[:, None]) * weights
    pairs = spread(jnp.stack([top_here, jnp.sum(raised, axis=1)]), devices)
    tops, totals = pairs[:, 0], pairs[:, 1]
    top = jnp.max(tops, axis=0)
    total = jnp.sum(totals * jnp.exp(tops - top), axis=0)
    raised = raised * jnp.exp(top_here - top)[:, None]
    return (messages.T, BLK * devices * raised / total[:, None])


def solution(mesh):
    return jax.shard_map(
        per_device,
        mesh=mesh,
        in_specs=(
            P(None, "vocab"),
            P(None, "vocab"),
            P(),
            P(),
            P(),
            P("parts"),
            P("parts"),
            P(("parts", "vocab"), None),
            P("parts", "vocab"),
        ),
        out_specs=(P(("parts", "vocab"), None), P("parts", "vocab")),
        check_vma=False,
    )
```

```python
import functools

import jax
import jax.numpy as jnp
from jax import lax
from jax.experimental import pallas as pl
from jax.experimental.pallas import tpu as pltpu
from jax.sharding import PartitionSpec as P

BLK = 256
STEPS = 3
LIMIT = 16 * 1024 * 1024
VMEM = pl.BlockSpec(memory_space=pltpu.VMEM)
SMEM = pl.BlockSpec(memory_space=pltpu.SMEM)
ANY = pl.BlockSpec(memory_space=pl.ANY)
PARAMS = pltpu.CompilerParams(vmem_limit_bytes=LIMIT)


def exchange(blocks):
    return lax.all_to_all(blocks, "vocab", split_axis=0, concat_axis=0, tiled=True)


def spread(own, devices):
    return exchange(jnp.broadcast_to(own[None], (devices,) + own.shape))


def basis(count):
    return [1] + [1 | (1 << bit) for bit in range(1, count)]


def swap(block, offset, devices):
    pairs = [(i, i ^ offset) for i in range(devices)]
    return lax.ppermute(block, "vocab", pairs)


def split_wide(wide):
    high = wide.astype(jnp.bfloat16)
    low = (wide - high.astype(jnp.float32)).astype(jnp.bfloat16)
    return high, low


def split_three(wide):
    high = wide.astype(jnp.bfloat16)
    rest = wide - high.astype(jnp.float32)
    middle = rest.astype(jnp.bfloat16)
    low = (rest - middle.astype(jnp.float32)).astype(jnp.bfloat16)
    return high, middle, low


def dot_rows(left, right):
    return lax.dot_general(left, right, (((1,), (1,)), ((), ())), preferred_element_type=jnp.float32)


def partner_of(bits):
    partner = 0
    for bit, offset in zip(bits, basis(len(bits))):
        partner ^= bit * offset
    return partner


def all_bits(count):
    return [tuple((k >> (count - 1 - b)) & 1 for b in range(count)) for k in range(1 << count)]


def far_partners(count):
    return [partner_of((0, 0) + bits) for bits in all_bits(count - 2)]


def half_places(count, first):
    far = far_partners(count)
    return [
        ((bit, k), partner_of((first, bit)) ^ offset)
        for bit in range(2)
        for k, offset in enumerate(far)
    ]


def partner_rows(i, rows):
    owner = lax.axis_index("vocab") ^ i
    return pl.ds(pl.multiple_of(owner * rows, rows), rows)


def reduce_blocks(kept, received, dtype, devices, count):
    total = kept + received.astype(jnp.float32)
    middle = swap(total[1].astype(dtype), basis(2)[1], devices)
    near = total[0] + middle.astype(jnp.float32)
    blocks = [near[0]]
    for k, offset in enumerate(far_partners(count)):
        if k:
            blocks.append(swap(near[k].astype(dtype), offset, devices))
    return total, blocks


def gather_far(own, devices, count):
    return jnp.stack([own] + [swap(own, offset, devices) for offset in far_partners(count)[1:]])


def gather_near(own, devices):
    near = jnp.stack([own, swap(own, basis(2)[1], devices)])
    return near, swap(near, basis(1)[0], devices)


def sums_kernel(emission_ref, out_ref):
    rows = out_ref.shape[2]
    ones = jnp.ones((16, emission_ref.shape[1]), jnp.bfloat16)
    for k in range(out_ref.shape[0]):
        out_ref[k] = dot_rows(ones, emission_ref[pl.ds(k * rows, rows)])[:1]


def block_sums(emission, devices):
    return pl.pallas_call(
        sums_kernel,
        out_shape=pltpu.VMEM((devices, 1, emission.shape[0] // devices), jnp.float32),
        in_specs=[VMEM],
        out_specs=VMEM,
        compiler_params=PARAMS,
        name="block_sums",
    )(emission)


def column_of(scalars_ref, shape):
    row = lax.broadcasted_iota(jnp.int32, shape, 0)
    column = jnp.zeros(shape, jnp.int32)
    for k in range(shape[0]):
        column = jnp.where(row == k, scalars_ref[k], column)
    return column


def setup_kernel(
    count, token_ref, state_ref, allow_ref, table_ref, start_ref, emission_ref, after_ref,
    kept_ref, sent_ref, route_ref, chooser_ref, messages_ref, wide_ref,
):
    device = lax.axis_index("vocab")
    devices = 1 << count
    rows = emission_ref.shape[0] >> count
    states = table_ref.shape[0]
    messages_ref[...] = start_ref[:, pl.ds(pl.multiple_of(device * rows, rows), rows)]
    shape = (devices, BLK)
    tokens = column_of(token_ref, shape) - device * BLK
    onehot = (tokens == lax.broadcasted_iota(jnp.int32, shape, 1)).astype(jnp.bfloat16)
    for k in range(devices):
        wide_ref[:, k, :] = dot_rows(onehot, emission_ref[pl.ds(k * rows, rows)])
    for first, out_ref in ((0, kept_ref), (1, sent_ref)):
        for place, partner in half_places(count, first):
            out_ref[place] = wide_ref[device ^ partner].astype(jnp.bfloat16)
    allow, table = allow_ref[...], table_ref[...]
    shape = (states, states)
    ids = lax.broadcasted_iota(jnp.int32, shape, 1)
    own = jnp.zeros(shape, jnp.float32)
    for b in range(devices):
        allowed = jnp.max((allow == b).astype(jnp.float32), axis=1, keepdims=True)
        step = jnp.where(table[:, b : b + 1] == ids, allowed, 0.0)
        own = jnp.where(device == b, step, own)
        step = step.astype(jnp.bfloat16)
        route_ref[pl.ds(b * states, states)] = jnp.concatenate([step] * 3, axis=1)
    shape = (devices, states)
    prompts = column_of(state_ref, shape) == lax.broadcasted_iota(jnp.int32, shape, 1)
    chooser = jnp.dot(
        prompts.astype(jnp.bfloat16), own.astype(jnp.bfloat16), preferred_element_type=jnp.float32
    ).astype(jnp.bfloat16)
    chooser_ref[...] = jnp.concatenate([chooser] * 3, axis=1)


def setup(last_token, prompt_state, allow_list, trans_table, beta_start, emission, after, count):
    devices, states = 1 << count, trans_table.shape[0]
    rows = emission.shape[0] >> count
    half = pltpu.VMEM((2, devices // 4, devices, rows), jnp.bfloat16)
    return pl.pallas_call(
        functools.partial(setup_kernel, count),
        out_shape=[
            half,
            half,
            pltpu.VMEM((devices * states, 3 * states), jnp.bfloat16),
            pltpu.VMEM((devices, 3 * states), jnp.bfloat16),
            pltpu.VMEM((states, rows), jnp.float32),
        ],
        in_specs=[SMEM] * 2 + [VMEM] * 4 + [ANY],
        out_specs=[VMEM] * 5,
        scratch_shapes=[pltpu.VMEM((devices, devices, rows), jnp.float32)],
        compiler_params=PARAMS,
        name="setup_tables",
    )(last_token, prompt_state, allow_list, trans_table, beta_start.T, emission, after)


def forward_kernel(prior_ref, *refs):
    blocks, out_ref = refs[:-2], refs[-1]
    columns = blocks[0][...]
    for block in blocks[1:]:
        columns += block[...].astype(jnp.float32)
    devices, rows = columns.shape
    prior = jnp.concatenate([prior_ref[:, pl.ds(k * rows, rows)] for k in range(devices)], axis=0)
    unnormal = prior * columns
    out_ref[...] = (unnormal / jnp.sum(unnormal)).astype(jnp.bfloat16)


def forward_messages_here(prior, blocks, after):
    return pl.pallas_call(
        forward_kernel,
        out_shape=pltpu.VMEM(blocks[0].shape, jnp.bfloat16),
        in_specs=[VMEM] * (1 + len(blocks)) + [ANY],
        out_specs=VMEM,
        compiler_params=PARAMS,
        name="forward_messages",
    )(prior, *blocks, after)


def order_kernel(count, near_ref, far_ref, out_ref):
    size = 1 << count
    device = lax.axis_index("vocab")

    def partner(place):
        number = jnp.zeros_like(place)
        for bit, offset in enumerate(basis(count)):
            number = number ^ (((place >> (count - 1 - bit)) & 1) * offset)
        return device ^ number

    shape = (size * size, size * size)
    to, source = (lax.broadcasted_iota(jnp.int32, shape, axis) for axis in (0, 1))
    same_block = partner(to >> count) == (source & (size - 1))
    same_prompt = (to & (size - 1)) == partner(source >> count)
    onehot = (same_block & same_prompt).astype(jnp.bfloat16)
    half = size * size // 2
    rows = out_ref.shape[1]
    near = near_ref[...].reshape(half, rows)
    far = far_ref[...].reshape(half, rows)
    ordered = jnp.dot(onehot[:, :half], near, preferred_element_type=jnp.float32)
    ordered += jnp.dot(onehot[:, half:], far, preferred_element_type=jnp.float32)
    out_ref[...] = ordered.astype(jnp.bfloat16)


def order_forward(near, far, count):
    rows = near.shape[-1]
    return pl.pallas_call(
        functools.partial(order_kernel, count),
        out_shape=pltpu.VMEM((1 << (2 * count), rows), jnp.bfloat16),
        in_specs=[VMEM] * 2,
        out_specs=VMEM,
        compiler_params=PARAMS,
        name="order_forward",
    )(near, far)


def last_kernel(*refs):
    blocks, out_ref = refs[:-2], refs[-1]
    messages = blocks[0][...]
    for block in blocks[1:]:
        messages += block[...]
    out_ref[...] = messages


def last_sum(blocks, after):
    return pl.pallas_call(
        last_kernel,
        out_shape=pltpu.VMEM(blocks[0].shape, jnp.float32),
        in_specs=[VMEM] * len(blocks) + [ANY],
        out_specs=VMEM,
        compiler_params=PARAMS,
        name="last_messages",
    )(*blocks, after)


def half_products(halves, transition_ref, out_ref, count, first):
    states = halves.shape[0] // 2
    rows = transition_ref.shape[0] >> count
    for place, partner in half_places(count, first):
        product = dot_rows(halves, transition_ref[partner_rows(partner, rows)])
        out_ref[place] = (product[:states] + product[states:]).astype(out_ref.dtype)


def send_kernel(count, number, transition_ref, route_ref, sums_ref, *refs):
    parts, (halves_ref, out_ref) = refs[:number], refs[-2:]
    messages = parts[0][...].astype(jnp.float32)
    for part in parts[1:]:
        messages += part[...].astype(jnp.float32)
    states = messages.shape[0]
    selected = jnp.dot(
        route_ref[...],
        jnp.concatenate(split_three(messages), axis=0),
        preferred_element_type=jnp.float32,
    )
    emitted = selected[:states] * sums_ref[0]
    for b in range(1, 1 << count):
        emitted += selected[b * states : (b + 1) * states] * sums_ref[b]
    halves = jnp.concatenate(split_wide(emitted), axis=0)
    halves_ref[...] = halves
    half_products(halves, transition_ref, out_ref, count, 1)


def keep_kernel(count, transition_ref, halves_ref, out_ref):
    half_products(halves_ref[...], transition_ref, out_ref, count, 0)


def step(transition, route, sums, parts, after, dtype, devices, count):
    states, rows = parts[0].shape
    shape = (2, devices // 4, states, rows)
    halves, sent = pl.pallas_call(
        functools.partial(send_kernel, count, len(parts)),
        out_shape=[
            pltpu.VMEM((2 * states, rows), jnp.bfloat16),
            pltpu.VMEM(shape, dtype),
        ],
        in_specs=[VMEM] * (3 + len(parts)) + [ANY] * len(after),
        out_specs=[VMEM] * 2,
        compiler_params=PARAMS,
        name="step_sent_half",
    )(transition, route, sums, *parts, *after)
    received = swap(sent, basis(1)[0], devices)
    kept = pl.pallas_call(
        functools.partial(keep_kernel, count),
        out_shape=pltpu.VMEM(shape, jnp.float32),
        in_specs=[VMEM] * 2,
        out_specs=VMEM,
        compiler_params=PARAMS,
        name="step_kept_half",
    )(transition, halves)
    return kept, received


def weigh_half(emission_ref, forward_ref, chooser, parts_ref, count, first):
    rows = emission_ref.shape[0] >> count
    prompts = chooser.shape[0]
    weights = jnp.zeros((prompts, emission_ref.shape[1]), jnp.float32)
    for order, (place, partner) in enumerate(half_places(count, first)):
        pieces = jnp.concatenate(split_three(parts_ref[place]), axis=0)
        chosen = jnp.dot(chooser, pieces, preferred_element_type=jnp.float32)
        block = order + (first << (count - 1))
        forward = forward_ref[pl.ds(block * prompts, prompts)].astype(jnp.float32)
        scaled = (forward * chosen).astype(jnp.bfloat16)
        tile = emission_ref[partner_rows(partner, rows)]
        weights += jnp.dot(scaled, tile, preferred_element_type=jnp.float32)
    return weights


def near_kernel(count, emission_ref, forward_ref, chooser_ref, parts_ref, out_ref):
    out_ref[...] = weigh_half(emission_ref, forward_ref, chooser_ref[...], parts_ref, count, 0)


def far_kernel(count, emission_ref, forward_ref, chooser_ref, logits_ref, near_ref, parts_ref, raised_ref, pair_ref):
    chooser = chooser_ref[...]
    logits = logits_ref[...].astype(jnp.float32)
    top = jnp.max(logits, axis=1, keepdims=True)
    weights = near_ref[...] + weigh_half(emission_ref, forward_ref, chooser, parts_ref, count, 1)
    allowed = jnp.sum(chooser.astype(jnp.float32), axis=1, keepdims=True) > 0
    raised = jnp.where(allowed, jnp.exp(logits - top) * weights, 0.0)
    raised_ref[...] = raised
    total = jnp.sum(raised, axis=1, keepdims=True)
    lane = lax.broadcasted_iota(jnp.int32, pair_ref.shape, 1)
    pair_ref[...] = jnp.where(lane == 0, top, total)


def weigh(emission, forward, chooser, logits, near, far, count):
    half = pl.pallas_call(
        functools.partial(near_kernel, count),
        out_shape=pltpu.VMEM(logits.shape, jnp.float32),
        in_specs=[VMEM] * 4,
        out_specs=VMEM,
        compiler_params=PARAMS,
        name="weigh_near",
    )(emission, forward, chooser, near)
    return pl.pallas_call(
        functools.partial(far_kernel, count),
        out_shape=[
            pltpu.VMEM(logits.shape, jnp.float32),
            pltpu.VMEM((logits.shape[0], 128), jnp.float32),
        ],
        in_specs=[VMEM] * 6,
        out_specs=[VMEM] * 2,
        compiler_params=PARAMS,
        name="weigh_far",
    )(emission, forward, chooser, logits, half, far)


def normalise(raised, pair, devices):
    pairs = spread(pair[:, :2].T, devices)
    own_top = pair[:, :1]
    tops, totals = pairs[:, 0], pairs[:, 1]
    top = jnp.max(tops, axis=0)
    total = jnp.sum(totals * jnp.exp(tops - top), axis=0)
    return BLK * devices * (raised * jnp.exp(own_top - top[:, None])) / total[:, None]


def forward_messages(emission, last_token, prior_msg, devices, device):
    hidden = emission.shape[0]
    local_rows = prior_msg.shape[0]
    token_ids = jnp.arange(BLK, dtype=jnp.int32)
    tokens = last_token - device * BLK
    onehot = (tokens[:, None] == token_ids[None, :]).astype(jnp.bfloat16)
    owned = dot_rows(onehot, emission)
    owned = owned.astype(jnp.bfloat16).reshape(devices, local_rows, hidden)
    columns = jnp.sum(exchange(owned), axis=0, dtype=jnp.float32)
    unnormal = prior_msg * columns
    forward_msg = (unnormal / jnp.sum(unnormal, axis=1, keepdims=True)).astype(jnp.bfloat16)
    return spread(forward_msg, devices).reshape(devices * local_rows, hidden)


def per_device(
    emission,
    transition,
    beta_start,
    allow_list,
    trans_table,
    last_token,
    prompt_state,
    prior_msg,
    lm_logits,
):
    devices = lax.axis_size("vocab")
    device = lax.axis_index("vocab")
    hidden = emission.shape[0]
    states = beta_start.shape[1]
    own_rows = transition.shape[1]
    prompts = prompt_state.shape[0]
    count = devices.bit_length() - 1
    if devices == 1 << count and count > 2 and own_rows % 128 == 0 and prompts == devices:
        sums = block_sums(emission, devices)
        columns, columns_out, route, chooser, messages = setup(
            last_token, prompt_state, allow_list, trans_table, beta_start, emission, sums, count
        )
        columns_in = swap(columns_out, basis(1)[0], devices)
        sums = exchange(sums)
        parts, after = [messages], (columns_in,)
        for window_step in range(STEPS):
            dtype = jnp.bfloat16 if window_step < STEPS - 1 else jnp.float32
            kept, received = step(transition, route, sums, parts, after, dtype, devices, count)
            if window_step == 0:
                kept = jnp.concatenate([kept, columns.astype(jnp.float32)], axis=-2)
                received = jnp.concatenate([received, columns_in], axis=-2)
            total, parts = reduce_blocks(kept, received, dtype, devices, count)
            if window_step == 0:
                columns = [part[states:] for part in parts]
                parts = [part[:states] for part in parts]
                after = ()
            if window_step == 1:
                forward = forward_messages_here(prior_msg, columns, total)
                forward = gather_far(forward, devices, count)
                after = (forward,)
        forward = order_forward(*gather_near(forward, devices), count)
        messages = last_sum(parts, forward)
        near, far = gather_near(gather_far(messages, devices, count), devices)
        raised, pair = weigh(emission, forward, chooser, lm_logits, near, far, count)
        return messages.T, normalise(raised, pair, devices)
    state_ids = jnp.arange(states, dtype=jnp.int32)
    block_ids = jnp.arange(devices, dtype=jnp.int32)
    allowed = jnp.any(allow_list[:, :, None] == block_ids, axis=1)
    dest_here = lax.dynamic_index_in_dim(trans_table, device, axis=1, keepdims=False)
    allow_here = jnp.any(allow_list == device, axis=1)
    dest_rows = jnp.sum(jnp.where(prompt_state[:, None] == state_ids, dest_here, 0), axis=1)
    allow_rows = jnp.any((prompt_state[:, None] == state_ids) & allow_here, axis=1)
    chooser = (dest_rows[:, None] == state_ids) & allow_rows[:, None]
    messages = lax.dynamic_slice_in_dim(beta_start, device * own_rows, own_rows, 0).T
    forward_all = forward_messages(emission, last_token, prior_msg, devices, device)
    own_sums = exchange(jnp.sum(emission, axis=1, dtype=jnp.float32).reshape(devices, own_rows))
    route = allowed.T[:, :, None] & (trans_table.T[:, :, None] == state_ids)
    route = route.astype(jnp.float32).reshape(devices * states, states)
    by_owner = transition.reshape(devices, own_rows, own_rows)
    for window_step in range(STEPS):
        selected = jnp.dot(route, messages, precision=lax.Precision.HIGHEST)
        selected = selected.reshape(devices, states, own_rows)
        emitted = jnp.sum(selected * own_sums[:, None, :], axis=0)
        halves = jnp.concatenate(split_wide(emitted), axis=0)
        partial = jnp.einsum("dzy,sy->dsz", by_owner, halves, preferred_element_type=jnp.float32)
        partial = partial[:, :states] + partial[:, states:]
        if window_step < STEPS - 1:
            partial = partial.astype(jnp.bfloat16)
        messages = jnp.sum(exchange(partial), axis=0, dtype=jnp.float32)
    everywhere = spread(messages, devices)
    chosen = jnp.einsum(
        "ps,dsz->pdz", chooser.astype(jnp.float32), everywhere, precision=lax.Precision.HIGHEST
    )
    forward_all = forward_all.reshape(prompts, devices, own_rows).astype(jnp.float32)
    scaled = (forward_all * chosen).astype(jnp.bfloat16).reshape(prompts, hidden)
    weights = jnp.dot(scaled, emission, preferred_element_type=jnp.float32)
    weights = jnp.where(allow_rows[:, None], weights, 0.0)
    logits = lm_logits.astype(jnp.float32)
    top_here = jnp.max(logits, axis=1)
    raised = jnp.exp(logits - top_here[:, None]) * weights
    pairs = spread(jnp.stack([top_here, jnp.sum(raised, axis=1)]), devices)
    tops, totals = pairs[:, 0], pairs[:, 1]
    top = jnp.max(tops, axis=0)
    total = jnp.sum(totals * jnp.exp(tops - top), axis=0)
    raised = raised * jnp.exp(top_here - top)[:, None]
    return (messages.T, BLK * devices * raised / total[:, None])


def solution(mesh):
    return jax.shard_map(
        per_device,
        mesh=mesh,
        in_specs=(
            P(None, "vocab"),
            P(None, "vocab"),
            P(),
            P(),
            P(),
            P("parts"),
            P("parts"),
            P(("parts", "vocab"), None),
            P("parts", "vocab"),
        ),
        out_specs=(P(("parts", "vocab"), None), P("parts", "vocab")),
        check_vma=False,
    )
```

```python
import functools

import jax
import jax.numpy as jnp
from jax import lax
from jax.experimental import pallas as pl
from jax.experimental.pallas import tpu as pltpu
from jax.sharding import PartitionSpec as P

BLK = 256
STEPS = 3
LIMIT = 16 * 1024 * 1024
VMEM = pl.BlockSpec(memory_space=pltpu.VMEM)
SMEM = pl.BlockSpec(memory_space=pltpu.SMEM)
ANY = pl.BlockSpec(memory_space=pl.ANY)
PARAMS = pltpu.CompilerParams(vmem_limit_bytes=LIMIT)


def exchange(blocks):
    return lax.all_to_all(blocks, "vocab", split_axis=0, concat_axis=0, tiled=True)


def spread(own, devices):
    return exchange(jnp.broadcast_to(own[None], (devices,) + own.shape))


def basis(count):
    return [1] + [1 | (1 << bit) for bit in range(1, count)]


def swap(block, offset, devices):
    pairs = [(i, i ^ offset) for i in range(devices)]
    return lax.ppermute(block, "vocab", pairs)


def split_wide(wide):
    high = wide.astype(jnp.bfloat16)
    low = (wide - high.astype(jnp.float32)).astype(jnp.bfloat16)
    return high, low


def split_three(wide):
    high = wide.astype(jnp.bfloat16)
    rest = wide - high.astype(jnp.float32)
    middle = rest.astype(jnp.bfloat16)
    low = (rest - middle.astype(jnp.float32)).astype(jnp.bfloat16)
    return high, middle, low


def dot_rows(left, right):
    return lax.dot_general(left, right, (((1,), (1,)), ((), ())), preferred_element_type=jnp.float32)


def partner_of(bits):
    partner = 0
    for bit, offset in zip(bits, basis(len(bits))):
        partner ^= bit * offset
    return partner


def all_bits(count):
    return [tuple((k >> (count - 1 - b)) & 1 for b in range(count)) for k in range(1 << count)]


def far_partners(count):
    return [partner_of((0, 0) + bits) for bits in all_bits(count - 2)]


def half_places(count, first):
    far = far_partners(count)
    return [
        ((bit, k), partner_of((first, bit)) ^ offset)
        for bit in range(2)
        for k, offset in enumerate(far)
    ]


def partner_rows(i, rows):
    owner = lax.axis_index("vocab") ^ i
    return pl.ds(pl.multiple_of(owner * rows, rows), rows)


def reduce_blocks(kept, received, dtype, devices, count, extra=()):
    total = kept + received.astype(jnp.float32)
    middle = swap(total[1].astype(dtype), basis(2)[1], devices)
    near = total[0] + middle.astype(jnp.float32)
    blocks = [near[0]]
    for k, offset in enumerate(far_partners(count)):
        if k:
            block = jnp.concatenate((near[k].astype(dtype),) + extra, axis=0)
            blocks.append(swap(block, offset, devices))
    return blocks


def gather_far(own, devices, count):
    return jnp.stack([own] + [swap(own, offset, devices) for offset in far_partners(count)[1:]])


def gather_near(own, devices):
    near = jnp.stack([own, swap(own, basis(2)[1], devices)])
    return near, swap(near, basis(1)[0], devices)


def sums_kernel(emission_ref, out_ref):
    rows = out_ref.shape[2]
    ones = jnp.ones((16, emission_ref.shape[1]), jnp.bfloat16)
    for k in range(out_ref.shape[0]):
        out_ref[k] = dot_rows(ones, emission_ref[pl.ds(k * rows, rows)])[:1]


def block_sums(emission, devices):
    return pl.pallas_call(
        sums_kernel,
        out_shape=pltpu.VMEM((devices, 1, emission.shape[0] // devices), jnp.float32),
        in_specs=[VMEM],
        out_specs=VMEM,
        compiler_params=PARAMS,
        name="block_sums",
    )(emission)


def column_of(scalars_ref, shape):
    row = lax.broadcasted_iota(jnp.int32, shape, 0)
    column = jnp.zeros(shape, jnp.int32)
    for k in range(shape[0]):
        column = jnp.where(row == k, scalars_ref[k], column)
    return column


def setup_kernel(
    count, token_ref, state_ref, allow_ref, table_ref, start_ref, emission_ref, after_ref,
    kept_ref, sent_ref, route_ref, chooser_ref, messages_ref, wide_ref,
):
    device = lax.axis_index("vocab")
    devices = 1 << count
    rows = emission_ref.shape[0] >> count
    states = table_ref.shape[0]
    messages_ref[...] = start_ref[:, pl.ds(pl.multiple_of(device * rows, rows), rows)]
    shape = (devices, BLK)
    tokens = column_of(token_ref, shape) - device * BLK
    onehot = (tokens == lax.broadcasted_iota(jnp.int32, shape, 1)).astype(jnp.bfloat16)
    for k in range(devices):
        wide_ref[:, k, :] = dot_rows(onehot, emission_ref[pl.ds(k * rows, rows)])
    for first, out_ref in ((0, kept_ref), (1, sent_ref)):
        for place, partner in half_places(count, first):
            out_ref[place] = wide_ref[device ^ partner].astype(jnp.bfloat16)
    allow, table = allow_ref[...], table_ref[...]
    hits = [jnp.max((allow == b).astype(jnp.float32), axis=0, keepdims=True) for b in range(devices)]
    shape = (states, states)
    diagonal = [lax.broadcasted_iota(jnp.int32, shape, axis) for axis in (0, 1)]
    diagonal = (diagonal[0] == diagonal[1]).astype(jnp.bfloat16)
    hits = dot_rows(diagonal, jnp.concatenate(hits, axis=0).astype(jnp.bfloat16))
    ids = lax.broadcasted_iota(jnp.int32, shape, 1)
    own = jnp.zeros(shape, jnp.float32)
    for b in range(devices):
        step = jnp.where(table[:, b : b + 1] == ids, hits[:, b : b + 1], 0.0)
        own = jnp.where(device == b, step, own)
        step = step.astype(jnp.bfloat16)
        route_ref[pl.ds(b * states, states)] = jnp.concatenate([step] * 3, axis=1)
    shape = (devices, states)
    prompts = column_of(state_ref, shape) == lax.broadcasted_iota(jnp.int32, shape, 1)
    chooser = jnp.dot(
        prompts.astype(jnp.bfloat16), own.astype(jnp.bfloat16), preferred_element_type=jnp.float32
    ).astype(jnp.bfloat16)
    chooser_ref[...] = jnp.concatenate([chooser] * 3, axis=1)


def setup(last_token, prompt_state, allow_list, trans_table, beta_start, emission, after, count):
    devices, states = 1 << count, trans_table.shape[0]
    rows = emission.shape[0] >> count
    half = pltpu.VMEM((2, devices // 4, devices, rows), jnp.bfloat16)
    return pl.pallas_call(
        functools.partial(setup_kernel, count),
        out_shape=[
            half,
            half,
            pltpu.VMEM((devices * states, 3 * states), jnp.bfloat16),
            pltpu.VMEM((devices, 3 * states), jnp.bfloat16),
            pltpu.VMEM((states, rows), jnp.float32),
        ],
        in_specs=[SMEM] * 2 + [VMEM] * 4 + [ANY],
        out_specs=[VMEM] * 5,
        scratch_shapes=[pltpu.VMEM((devices, devices, rows), jnp.float32)],
        compiler_params=PARAMS,
        name="setup_tables",
    )(last_token, prompt_state, allow_list.T, trans_table, beta_start.T, emission, after)


def forward_kernel(prior_ref, *refs):
    blocks, out_ref = refs[:-1], refs[-1]
    devices, rows = out_ref.shape
    columns = blocks[0][-devices:]
    for block in blocks[1:]:
        columns += block[-devices:].astype(jnp.float32)
    prior = jnp.concatenate([prior_ref[:, pl.ds(k * rows, rows)] for k in range(devices)], axis=0)
    unnormal = prior * columns
    out_ref[...] = (unnormal / jnp.sum(unnormal)).astype(jnp.bfloat16)


def forward_messages_here(prior, blocks, devices):
    return pl.pallas_call(
        forward_kernel,
        out_shape=pltpu.VMEM((devices, blocks[0].shape[1]), jnp.bfloat16),
        in_specs=[VMEM] * (1 + len(blocks)),
        out_specs=VMEM,
        compiler_params=PARAMS,
        name="forward_messages",
    )(prior, *blocks)


def order_kernel(count, near_ref, far_ref, out_ref):
    size = 1 << count
    device = lax.axis_index("vocab")

    def partner(place):
        number = jnp.zeros_like(place)
        for bit, offset in enumerate(basis(count)):
            number = number ^ (((place >> (count - 1 - bit)) & 1) * offset)
        return device ^ number

    shape = (size * size, size * size)
    to, source = (lax.broadcasted_iota(jnp.int32, shape, axis) for axis in (0, 1))
    same_block = partner(to >> count) == (source & (size - 1))
    same_prompt = (to & (size - 1)) == partner(source >> count)
    onehot = (same_block & same_prompt).astype(jnp.bfloat16)
    half = size * size // 2
    rows = out_ref.shape[1]
    near = near_ref[...].reshape(half, rows)
    far = far_ref[...].reshape(half, rows)
    ordered = jnp.dot(onehot[:, :half], near, preferred_element_type=jnp.float32)
    ordered += jnp.dot(onehot[:, half:], far, preferred_element_type=jnp.float32)
    out_ref[...] = ordered.astype(jnp.bfloat16)


def order_forward(near, far, count):
    rows = near.shape[-1]
    return pl.pallas_call(
        functools.partial(order_kernel, count),
        out_shape=pltpu.VMEM((1 << (2 * count), rows), jnp.bfloat16),
        in_specs=[VMEM] * 2,
        out_specs=VMEM,
        compiler_params=PARAMS,
        name="order_forward",
    )(near, far)


def last_kernel(*refs):
    blocks, out_ref = refs[:-2], refs[-1]
    messages = blocks[0][...]
    for block in blocks[1:]:
        messages += block[...]
    out_ref[...] = messages


def last_sum(blocks, after):
    return pl.pallas_call(
        last_kernel,
        out_shape=pltpu.VMEM(blocks[0].shape, jnp.float32),
        in_specs=[VMEM] * len(blocks) + [ANY],
        out_specs=VMEM,
        compiler_params=PARAMS,
        name="last_messages",
    )(*blocks, after)


def half_products(halves, transition_ref, out_ref, count, first):
    states = halves.shape[0] // 2
    rows = transition_ref.shape[0] >> count
    for place, partner in half_places(count, first):
        product = dot_rows(halves, transition_ref[partner_rows(partner, rows)])
        product = product[:states] + product[states:]
        out_ref[place + (pl.ds(0, states),)] = product.astype(out_ref.dtype)


def add_rows(out_ref, states, extra):
    for ref in extra:
        rows = pl.ds(states, ref.shape[2])
        for place in ((y, k) for y in range(ref.shape[0]) for k in range(ref.shape[1])):
            out_ref[place + (rows,)] = ref[place].astype(out_ref.dtype)


def send_kernel(count, number, transition_ref, route_ref, sums_ref, *refs):
    parts, extra, (halves_ref, out_ref) = refs[:number], refs[number:-2], refs[-2:]
    states = halves_ref.shape[0] // 2
    messages = parts[0][:states].astype(jnp.float32)
    for part in parts[1:]:
        messages += part[:states].astype(jnp.float32)
    selected = jnp.dot(
        route_ref[...],
        jnp.concatenate(split_three(messages), axis=0),
        preferred_element_type=jnp.float32,
    )
    emitted = selected[:states] * sums_ref[0]
    for b in range(1, 1 << count):
        emitted += selected[b * states : (b + 1) * states] * sums_ref[b]
    halves = jnp.concatenate(split_wide(emitted), axis=0)
    halves_ref[...] = halves
    half_products(halves, transition_ref, out_ref, count, 1)
    add_rows(out_ref, states, extra)


def keep_kernel(count, transition_ref, halves_ref, *refs):
    extra, out_ref = refs[:-1], refs[-1]
    half_products(halves_ref[...], transition_ref, out_ref, count, 0)
    add_rows(out_ref, halves_ref.shape[0] // 2, extra)


def step(transition, route, sums, parts, dtype, devices, count, kept_rows=(), sent_rows=()):
    states, rows = route.shape[0] // devices, parts[0].shape[1]
    total = states + sum(block.shape[2] for block in kept_rows)
    shape = (2, devices // 4, total, rows)
    halves, sent = pl.pallas_call(
        functools.partial(send_kernel, count, len(parts)),
        out_shape=[
            pltpu.VMEM((2 * states, rows), jnp.bfloat16),
            pltpu.VMEM(shape, dtype),
        ],
        in_specs=[VMEM] * (3 + len(parts) + len(sent_rows)),
        out_specs=[VMEM] * 2,
        compiler_params=PARAMS,
        name="step_sent_half",
    )(transition, route, sums, *parts, *sent_rows)
    received = swap(sent, basis(1)[0], devices)
    kept = pl.pallas_call(
        functools.partial(keep_kernel, count),
        out_shape=pltpu.VMEM(shape, jnp.float32),
        in_specs=[VMEM] * (2 + len(kept_rows)),
        out_specs=VMEM,
        compiler_params=PARAMS,
        name="step_kept_half",
    )(transition, halves, *kept_rows)
    return kept, received


def weigh_half(emission_ref, forward_ref, chooser, parts_ref, count, first):
    rows = emission_ref.shape[0] >> count
    prompts = chooser.shape[0]
    weights = jnp.zeros((prompts, emission_ref.shape[1]), jnp.float32)
    for order, (place, partner) in enumerate(half_places(count, first)):
        pieces = jnp.concatenate(split_three(parts_ref[place]), axis=0)
        chosen = jnp.dot(chooser, pieces, preferred_element_type=jnp.float32)
        block = order + (first << (count - 1))
        forward = forward_ref[pl.ds(block * prompts, prompts)].astype(jnp.float32)
        scaled = (forward * chosen).astype(jnp.bfloat16)
        tile = emission_ref[partner_rows(partner, rows)]
        weights += jnp.dot(scaled, tile, preferred_element_type=jnp.float32)
    return weights


def near_kernel(count, emission_ref, forward_ref, chooser_ref, parts_ref, out_ref):
    out_ref[...] = weigh_half(emission_ref, forward_ref, chooser_ref[...], parts_ref, count, 0)


def far_kernel(count, emission_ref, forward_ref, chooser_ref, logits_ref, near_ref, parts_ref, raised_ref, pair_ref):
    chooser = chooser_ref[...]
    logits = logits_ref[...].astype(jnp.float32)
    top = jnp.max(logits, axis=1, keepdims=True)
    weights = near_ref[...] + weigh_half(emission_ref, forward_ref, chooser, parts_ref, count, 1)
    allowed = jnp.sum(chooser.astype(jnp.float32), axis=1, keepdims=True) > 0
    raised = jnp.where(allowed, jnp.exp(logits - top) * weights, 0.0)
    raised_ref[...] = raised
    total = jnp.sum(raised, axis=1, keepdims=True)
    lane = lax.broadcasted_iota(jnp.int32, pair_ref.shape, 1)
    pair_ref[...] = jnp.where(lane == 0, top, total)


def weigh(emission, forward, chooser, logits, near, far, count):
    half = pl.pallas_call(
        functools.partial(near_kernel, count),
        out_shape=pltpu.VMEM(logits.shape, jnp.float32),
        in_specs=[VMEM] * 4,
        out_specs=VMEM,
        compiler_params=PARAMS,
        name="weigh_near",
    )(emission, forward, chooser, near)
    return pl.pallas_call(
        functools.partial(far_kernel, count),
        out_shape=[
            pltpu.VMEM(logits.shape, jnp.float32),
            pltpu.VMEM((logits.shape[0], 128), jnp.float32),
        ],
        in_specs=[VMEM] * 6,
        out_specs=[VMEM] * 2,
        compiler_params=PARAMS,
        name="weigh_far",
    )(emission, forward, chooser, logits, half, far)


def normalise(raised, pair, devices):
    pairs = spread(pair[:, :2].T, devices)
    own_top = pair[:, :1]
    tops, totals = pairs[:, 0], pairs[:, 1]
    top = jnp.max(tops, axis=0)
    total = jnp.sum(totals * jnp.exp(tops - top), axis=0)
    return BLK * devices * (raised * jnp.exp(own_top - top[:, None])) / total[:, None]


def forward_messages(emission, last_token, prior_msg, devices, device):
    hidden = emission.shape[0]
    local_rows = prior_msg.shape[0]
    token_ids = jnp.arange(BLK, dtype=jnp.int32)
    tokens = last_token - device * BLK
    onehot = (tokens[:, None] == token_ids[None, :]).astype(jnp.bfloat16)
    owned = dot_rows(onehot, emission)
    owned = owned.astype(jnp.bfloat16).reshape(devices, local_rows, hidden)
    columns = jnp.sum(exchange(owned), axis=0, dtype=jnp.float32)
    unnormal = prior_msg * columns
    forward_msg = (unnormal / jnp.sum(unnormal, axis=1, keepdims=True)).astype(jnp.bfloat16)
    return spread(forward_msg, devices).reshape(devices * local_rows, hidden)


def per_device(
    emission,
    transition,
    beta_start,
    allow_list,
    trans_table,
    last_token,
    prompt_state,
    prior_msg,
    lm_logits,
):
    devices = lax.axis_size("vocab")
    device = lax.axis_index("vocab")
    hidden = emission.shape[0]
    states = beta_start.shape[1]
    own_rows = transition.shape[1]
    prompts = prompt_state.shape[0]
    count = devices.bit_length() - 1
    if devices == 1 << count and count > 2 and own_rows % 128 == 0 and prompts == devices:
        sums = block_sums(emission, devices)
        columns, columns_out, route, chooser, messages = setup(
            last_token, prompt_state, allow_list, trans_table, beta_start, emission, sums, count
        )
        sums = exchange(sums)
        parts, kept_rows, sent_rows, extra = [messages], (columns,), (columns_out,), ()
        for window_step in range(STEPS):
            dtype = jnp.bfloat16 if window_step < STEPS - 1 else jnp.float32
            kept, received = step(
                transition, route, sums, parts, dtype, devices, count, kept_rows, sent_rows
            )
            if window_step == 1:
                forward = forward_messages_here(prior_msg, parts, devices)
                extra = (forward,)
            parts = reduce_blocks(kept, received, dtype, devices, count, extra)
            if window_step == 1:
                forward = jnp.stack([forward] + [part[states:] for part in parts[1:]])
            kept_rows, sent_rows, extra = (), (), ()
        forward = order_forward(*gather_near(forward, devices), count)
        messages = last_sum(parts, forward)
        near, far = gather_near(gather_far(messages, devices, count), devices)
        raised, pair = weigh(emission, forward, chooser, lm_logits, near, far, count)
        return messages.T, normalise(raised, pair, devices)
    state_ids = jnp.arange(states, dtype=jnp.int32)
    block_ids = jnp.arange(devices, dtype=jnp.int32)
    allowed = jnp.any(allow_list[:, :, None] == block_ids, axis=1)
    dest_here = lax.dynamic_index_in_dim(trans_table, device, axis=1, keepdims=False)
    allow_here = jnp.any(allow_list == device, axis=1)
    dest_rows = jnp.sum(jnp.where(prompt_state[:, None] == state_ids, dest_here, 0), axis=1)
    allow_rows = jnp.any((prompt_state[:, None] == state_ids) & allow_here, axis=1)
    chooser = (dest_rows[:, None] == state_ids) & allow_rows[:, None]
    messages = lax.dynamic_slice_in_dim(beta_start, device * own_rows, own_rows, 0).T
    forward_all = forward_messages(emission, last_token, prior_msg, devices, device)
    own_sums = exchange(jnp.sum(emission, axis=1, dtype=jnp.float32).reshape(devices, own_rows))
    route = allowed.T[:, :, None] & (trans_table.T[:, :, None] == state_ids)
    route = route.astype(jnp.float32).reshape(devices * states, states)
    by_owner = transition.reshape(devices, own_rows, own_rows)
    for window_step in range(STEPS):
        selected = jnp.dot(route, messages, precision=lax.Precision.HIGHEST)
        selected = selected.reshape(devices, states, own_rows)
        emitted = jnp.sum(selected * own_sums[:, None, :], axis=0)
        halves = jnp.concatenate(split_wide(emitted), axis=0)
        partial = jnp.einsum("dzy,sy->dsz", by_owner, halves, preferred_element_type=jnp.float32)
        partial = partial[:, :states] + partial[:, states:]
        if window_step < STEPS - 1:
            partial = partial.astype(jnp.bfloat16)
        messages = jnp.sum(exchange(partial), axis=0, dtype=jnp.float32)
    everywhere = spread(messages, devices)
    chosen = jnp.einsum(
        "ps,dsz->pdz", chooser.astype(jnp.float32), everywhere, precision=lax.Precision.HIGHEST
    )
    forward_all = forward_all.reshape(prompts, devices, own_rows).astype(jnp.float32)
    scaled = (forward_all * chosen).astype(jnp.bfloat16).reshape(prompts, hidden)
    weights = jnp.dot(scaled, emission, preferred_element_type=jnp.float32)
    weights = jnp.where(allow_rows[:, None], weights, 0.0)
    logits = lm_logits.astype(jnp.float32)
    top_here = jnp.max(logits, axis=1)
    raised = jnp.exp(logits - top_here[:, None]) * weights
    pairs = spread(jnp.stack([top_here, jnp.sum(raised, axis=1)]), devices)
    tops, totals = pairs[:, 0], pairs[:, 1]
    top = jnp.max(tops, axis=0)
    total = jnp.sum(totals * jnp.exp(tops - top), axis=0)
    raised = raised * jnp.exp(top_here - top)[:, None]
    return (messages.T, BLK * devices * raised / total[:, None])


def solution(mesh):
    return jax.shard_map(
        per_device,
        mesh=mesh,
        in_specs=(
            P(None, "vocab"),
            P(None, "vocab"),
            P(),
            P(),
            P(),
            P("parts"),
            P("parts"),
            P(("parts", "vocab"), None),
            P("parts", "vocab"),
        ),
        out_specs=(P(("parts", "vocab"), None), P("parts", "vocab")),
        check_vma=False,
    )
```

```python
import functools

import jax
import jax.numpy as jnp
from jax import lax
from jax.experimental import pallas as pl
from jax.experimental.pallas import tpu as pltpu
from jax.sharding import PartitionSpec as P

BLK = 256
STEPS = 3
LIMIT = 16 * 1024 * 1024
VMEM = pl.BlockSpec(memory_space=pltpu.VMEM)
SMEM = pl.BlockSpec(memory_space=pltpu.SMEM)
ANY = pl.BlockSpec(memory_space=pl.ANY)
PARAMS = pltpu.CompilerParams(vmem_limit_bytes=LIMIT)


def exchange(blocks):
    return lax.all_to_all(blocks, "vocab", split_axis=0, concat_axis=0, tiled=True)


def spread(own, devices):
    return exchange(jnp.broadcast_to(own[None], (devices,) + own.shape))


def basis(count):
    return [1] + [(1 << bit) | (bit != 2) for bit in range(1, count)]


def swap(block, offset, devices):
    pairs = [(i, i ^ offset) for i in range(devices)]
    return lax.ppermute(block, "vocab", pairs)


def split_wide(wide):
    high = wide.astype(jnp.bfloat16)
    low = (wide - high.astype(jnp.float32)).astype(jnp.bfloat16)
    return high, low


def split_three(wide):
    high = wide.astype(jnp.bfloat16)
    rest = wide - high.astype(jnp.float32)
    middle = rest.astype(jnp.bfloat16)
    low = (rest - middle.astype(jnp.float32)).astype(jnp.bfloat16)
    return high, middle, low


def dot_rows(left, right):
    return lax.dot_general(left, right, (((1,), (1,)), ((), ())), preferred_element_type=jnp.float32)


def partner_of(bits):
    partner = 0
    for bit, offset in zip(bits, basis(len(bits))):
        partner ^= bit * offset
    return partner


def all_bits(count):
    return [tuple((k >> (count - 1 - b)) & 1 for b in range(count)) for k in range(1 << count)]


def far_partners(count):
    return [partner_of((0, 0) + bits) for bits in all_bits(count - 2)]


def half_places(count, first):
    far = far_partners(count)
    return [
        ((bit, k), partner_of((first, bit)) ^ offset)
        for bit in range(2)
        for k, offset in enumerate(far)
    ]


def partner_rows(i, rows):
    owner = lax.axis_index("vocab") ^ i
    return pl.ds(pl.multiple_of(owner * rows, rows), rows)


def reduce_blocks(kept, received, dtype, devices, count, extra=()):
    total = kept + received.astype(jnp.float32)
    middle = swap(total[1].astype(dtype), basis(2)[1], devices)
    near = total[0] + middle.astype(jnp.float32)
    blocks = [near[0]]
    for k, offset in enumerate(far_partners(count)):
        if k:
            block = jnp.concatenate((near[k].astype(dtype),) + extra, axis=0)
            blocks.append(swap(block, offset, devices))
    return blocks


def gather_far(own, devices, count):
    return jnp.stack([own] + [swap(own, offset, devices) for offset in far_partners(count)[1:]])


def gather_near(own, devices):
    near = jnp.stack([own, swap(own, basis(2)[1], devices)])
    return near, swap(near, basis(1)[0], devices)


def column_of(scalars_ref, shape):
    row = lax.broadcasted_iota(jnp.int32, shape, 0)
    column = jnp.zeros(shape, jnp.int32)
    for k in range(shape[0]):
        column = jnp.where(row == k, scalars_ref[k], column)
    return column


def tables_kernel(
    count, token_hbm, state_hbm, allow_hbm, table_hbm, start_hbm, emission_ref, sums_in_ref,
    route_ref, chooser_ref, messages_ref, kept_ref, sent_ref, sums_ref,
    token_ref, state_ref, allow_ref, table_ref, wide_ref, sems,
):
    device = lax.axis_index("vocab")
    devices = 1 << count
    states, rows = messages_ref.shape
    own = pl.ds(pl.multiple_of(device * rows, rows), rows)
    pairs = [
        (token_hbm, token_ref), (state_hbm, state_ref), (allow_hbm, allow_ref),
        (table_hbm, table_ref), (start_hbm.at[:, own], messages_ref),
    ]
    copies = [
        pltpu.make_async_copy(source, to, sems.at[k]) for k, (source, to) in enumerate(pairs)
    ]
    for copy in copies:
        copy.start()
    sums_ref[...] = sums_in_ref[...]
    copies[0].wait()
    shape = (devices, BLK)
    tokens = column_of(token_ref, shape) - device * BLK
    onehot = (tokens == lax.broadcasted_iota(jnp.int32, shape, 1)).astype(jnp.bfloat16)
    for k in range(devices):
        wide_ref[:, k, :] = dot_rows(onehot, emission_ref[pl.ds(k * rows, rows)])
    for first, out_ref in ((0, kept_ref), (1, sent_ref)):
        for place, partner in half_places(count, first):
            out_ref[place] = wide_ref[device ^ partner].astype(jnp.bfloat16)
    for copy in copies[1:]:
        copy.wait()
    allow, table = allow_ref[...], table_ref[...]
    hits = [jnp.max((allow == b).astype(jnp.float32), axis=0, keepdims=True) for b in range(devices)]
    shape = (states, states)
    diagonal = [lax.broadcasted_iota(jnp.int32, shape, axis) for axis in (0, 1)]
    diagonal = (diagonal[0] == diagonal[1]).astype(jnp.bfloat16)
    hits = dot_rows(diagonal, jnp.concatenate(hits, axis=0).astype(jnp.bfloat16))
    ids = lax.broadcasted_iota(jnp.int32, shape, 1)
    own_step = jnp.zeros(shape, jnp.float32)
    for b in range(devices):
        step = jnp.where(table[:, b : b + 1] == ids, hits[:, b : b + 1], 0.0)
        own_step = jnp.where(device == b, step, own_step)
        step = step.astype(jnp.bfloat16)
        route_ref[pl.ds(b * states, states)] = jnp.concatenate([step] * 3, axis=1)
    shape = (devices, states)
    prompts = column_of(state_ref, shape) == lax.broadcasted_iota(jnp.int32, shape, 1)
    chooser = jnp.dot(
        prompts.astype(jnp.bfloat16),
        own_step.astype(jnp.bfloat16),
        preferred_element_type=jnp.float32,
    ).astype(jnp.bfloat16)
    chooser_ref[...] = jnp.concatenate([chooser] * 3, axis=1)


def tables(last_token, prompt_state, allow_list, trans_table, beta_start, emission, after, count):
    devices, states = 1 << count, trans_table.shape[0]
    rows = emission.shape[0] >> count
    half = pltpu.VMEM((2, devices // 4, devices, rows), jnp.bfloat16)
    operands = (last_token, prompt_state, allow_list.T, trans_table, beta_start.T)
    return pl.pallas_call(
        functools.partial(tables_kernel, count),
        out_shape=[
            pltpu.VMEM((devices * states, 3 * states), jnp.bfloat16),
            pltpu.VMEM((devices, 3 * states), jnp.bfloat16),
            pltpu.VMEM((states, rows), jnp.float32),
            half,
            half,
            jax.ShapeDtypeStruct(after.shape, after.dtype),
        ],
        in_specs=[ANY] * len(operands) + [VMEM] * 2,
        out_specs=[VMEM] * 6,
        scratch_shapes=[
            pltpu.SMEM(last_token.shape, jnp.int32),
            pltpu.SMEM(prompt_state.shape, jnp.int32),
            pltpu.VMEM(allow_list.shape[::-1], jnp.int32),
            pltpu.VMEM(trans_table.shape, jnp.int32),
            pltpu.VMEM((devices, devices, rows), jnp.float32),
            pltpu.SemaphoreType.DMA((len(operands),)),
        ],
        compiler_params=PARAMS,
        name="tables",
    )(*(in_hbm(operand) for operand in operands), emission, after)


def sums_kernel(emission_ref, out_ref):
    rows = out_ref.shape[2]
    ones = jnp.ones((16, emission_ref.shape[1]), jnp.bfloat16)
    for k in range(out_ref.shape[0]):
        out_ref[k] = dot_rows(ones, emission_ref[pl.ds(k * rows, rows)])[:1]


def block_sums(emission, devices):
    return pl.pallas_call(
        sums_kernel,
        out_shape=jax.ShapeDtypeStruct((devices, 1, emission.shape[0] // devices), jnp.float32),
        in_specs=[VMEM],
        out_specs=VMEM,
        compiler_params=PARAMS,
        name="block_sums",
    )(emission)


def in_hbm(array):
    return pltpu.with_memory_space_constraint(array, pltpu.HBM)


def forward_kernel(prior_ref, *refs):
    blocks, out_ref = refs[:-1], refs[-1]
    devices, rows = out_ref.shape
    columns = blocks[0][-devices:]
    for block in blocks[1:]:
        columns += block[-devices:].astype(jnp.float32)
    prior = jnp.concatenate([prior_ref[:, pl.ds(k * rows, rows)] for k in range(devices)], axis=0)
    unnormal = prior * columns
    out_ref[...] = (unnormal / jnp.sum(unnormal)).astype(jnp.bfloat16)


def forward_messages_here(prior, blocks, devices):
    return pl.pallas_call(
        forward_kernel,
        out_shape=pltpu.VMEM((devices, blocks[0].shape[1]), jnp.bfloat16),
        in_specs=[VMEM] * (1 + len(blocks)),
        out_specs=VMEM,
        compiler_params=PARAMS,
        name="forward_messages",
    )(prior, *blocks)


def order_kernel(count, near_ref, far_ref, out_ref):
    size = 1 << count
    device = lax.axis_index("vocab")

    def partner(place):
        number = jnp.zeros_like(place)
        for bit, offset in enumerate(basis(count)):
            number = number ^ (((place >> (count - 1 - bit)) & 1) * offset)
        return device ^ number

    shape = (size * size, size * size)
    to, source = (lax.broadcasted_iota(jnp.int32, shape, axis) for axis in (0, 1))
    same_block = partner(to >> count) == (source & (size - 1))
    same_prompt = (to & (size - 1)) == partner(source >> count)
    onehot = (same_block & same_prompt).astype(jnp.bfloat16)
    half = size * size // 2
    rows = out_ref.shape[1]
    near = near_ref[...].reshape(half, rows)
    far = far_ref[...].reshape(half, rows)
    ordered = jnp.dot(onehot[:, :half], near, preferred_element_type=jnp.float32)
    ordered += jnp.dot(onehot[:, half:], far, preferred_element_type=jnp.float32)
    out_ref[...] = ordered.astype(jnp.bfloat16)


def order_forward(near, far, count):
    rows = near.shape[-1]
    return pl.pallas_call(
        functools.partial(order_kernel, count),
        out_shape=pltpu.VMEM((1 << (2 * count), rows), jnp.bfloat16),
        in_specs=[VMEM] * 2,
        out_specs=VMEM,
        compiler_params=PARAMS,
        name="order_forward",
    )(near, far)


def last_kernel(*refs):
    blocks, out_ref = refs[:-2], refs[-1]
    messages = blocks[0][...]
    for block in blocks[1:]:
        messages += block[...]
    out_ref[...] = messages


def last_sum(blocks, after):
    return pl.pallas_call(
        last_kernel,
        out_shape=pltpu.VMEM(blocks[0].shape, jnp.float32),
        in_specs=[VMEM] * len(blocks) + [ANY],
        out_specs=VMEM,
        compiler_params=PARAMS,
        name="last_messages",
    )(*blocks, after)


def half_products(halves, transition_ref, out_ref, count, first):
    states = halves.shape[0] // 2
    rows = transition_ref.shape[0] >> count
    for place, partner in half_places(count, first):
        product = dot_rows(halves, transition_ref[partner_rows(partner, rows)])
        product = product[:states] + product[states:]
        out_ref[place + (pl.ds(0, states),)] = product.astype(out_ref.dtype)


def add_rows(out_ref, states, extra):
    for ref in extra:
        rows = pl.ds(states, ref.shape[2])
        for place in ((y, k) for y in range(ref.shape[0]) for k in range(ref.shape[1])):
            out_ref[place + (rows,)] = ref[place].astype(out_ref.dtype)


def send_kernel(count, number, transition_ref, route_ref, sums_ref, *refs):
    parts, extra, (halves_ref, out_ref) = refs[:number], refs[number:-2], refs[-2:]
    states = halves_ref.shape[0] // 2
    messages = parts[0][:states].astype(jnp.float32)
    for part in parts[1:]:
        messages += part[:states].astype(jnp.float32)
    selected = jnp.dot(
        route_ref[...],
        jnp.concatenate(split_three(messages), axis=0),
        preferred_element_type=jnp.float32,
    )
    emitted = selected[:states] * sums_ref[0]
    for b in range(1, 1 << count):
        emitted += selected[b * states : (b + 1) * states] * sums_ref[b]
    halves = jnp.concatenate(split_wide(emitted), axis=0)
    halves_ref[...] = halves
    half_products(halves, transition_ref, out_ref, count, 1)
    add_rows(out_ref, states, extra)


def keep_kernel(count, transition_ref, halves_ref, *refs):
    extra, out_ref = refs[:-1], refs[-1]
    half_products(halves_ref[...], transition_ref, out_ref, count, 0)
    add_rows(out_ref, halves_ref.shape[0] // 2, extra)


def step(transition, route, sums, parts, dtype, devices, count, kept_rows=(), sent_rows=()):
    states, rows = route.shape[0] // devices, parts[0].shape[1]
    total = states + sum(block.shape[2] for block in kept_rows)
    shape = (2, devices // 4, total, rows)
    halves, sent = pl.pallas_call(
        functools.partial(send_kernel, count, len(parts)),
        out_shape=[
            pltpu.VMEM((2 * states, rows), jnp.bfloat16),
            pltpu.VMEM(shape, dtype),
        ],
        in_specs=[VMEM] * (3 + len(parts) + len(sent_rows)),
        out_specs=[VMEM] * 2,
        compiler_params=PARAMS,
        name="step_sent_half",
    )(transition, route, sums, *parts, *sent_rows)
    received = swap(sent, basis(1)[0], devices)
    kept = pl.pallas_call(
        functools.partial(keep_kernel, count),
        out_shape=pltpu.VMEM(shape, jnp.float32),
        in_specs=[VMEM] * (2 + len(kept_rows)),
        out_specs=VMEM,
        compiler_params=PARAMS,
        name="step_kept_half",
    )(transition, halves, *kept_rows)
    return kept, received


def weigh_half(emission_ref, forward_ref, chooser, parts_ref, count, first):
    rows = emission_ref.shape[0] >> count
    prompts = chooser.shape[0]
    weights = jnp.zeros((prompts, emission_ref.shape[1]), jnp.float32)
    for order, (place, partner) in enumerate(half_places(count, first)):
        pieces = jnp.concatenate(split_three(parts_ref[place]), axis=0)
        chosen = jnp.dot(chooser, pieces, preferred_element_type=jnp.float32)
        block = order + (first << (count - 1))
        forward = forward_ref[pl.ds(block * prompts, prompts)].astype(jnp.float32)
        scaled = (forward * chosen).astype(jnp.bfloat16)
        tile = emission_ref[partner_rows(partner, rows)]
        weights += jnp.dot(scaled, tile, preferred_element_type=jnp.float32)
    return weights


def near_kernel(count, emission_ref, forward_ref, chooser_ref, parts_ref, out_ref):
    out_ref[...] = weigh_half(emission_ref, forward_ref, chooser_ref[...], parts_ref, count, 0)


def far_kernel(count, emission_ref, forward_ref, chooser_ref, logits_ref, near_ref, parts_ref, raised_ref, pair_ref):
    chooser = chooser_ref[...]
    logits = logits_ref[...].astype(jnp.float32)
    top = jnp.max(logits, axis=1, keepdims=True)
    weights = near_ref[...] + weigh_half(emission_ref, forward_ref, chooser, parts_ref, count, 1)
    allowed = jnp.sum(chooser.astype(jnp.float32), axis=1, keepdims=True) > 0
    raised = jnp.where(allowed, jnp.exp(logits - top) * weights, 0.0)
    raised_ref[...] = raised
    total = jnp.sum(raised, axis=1, keepdims=True)
    size = raised.shape[0]
    diagonal = [lax.broadcasted_iota(jnp.int32, (size, size), axis) for axis in (0, 1)]
    diagonal = diagonal[0] == diagonal[1]
    ones = jnp.ones((16, size), jnp.bfloat16)
    rows = []
    for column in (top, total):
        parts = split_three(jnp.where(diagonal, column, 0.0))
        row = [jnp.dot(ones, part, preferred_element_type=jnp.float32)[:1] for part in parts]
        rows.append((row[2] + row[1]) + row[0])
    pair_ref[...] = jnp.broadcast_to(jnp.concatenate(rows, axis=0)[None], pair_ref.shape)


def weigh(emission, forward, chooser, logits, near, far, count):
    half = pl.pallas_call(
        functools.partial(near_kernel, count),
        out_shape=pltpu.VMEM(logits.shape, jnp.float32),
        in_specs=[VMEM] * 4,
        out_specs=VMEM,
        compiler_params=PARAMS,
        name="weigh_near",
    )(emission, forward, chooser, near)
    return pl.pallas_call(
        functools.partial(far_kernel, count),
        out_shape=[
            pltpu.VMEM(logits.shape, jnp.float32),
            pltpu.VMEM((1 << count, 2, logits.shape[0]), jnp.float32),
        ],
        in_specs=[VMEM] * 6,
        out_specs=[VMEM] * 2,
        compiler_params=PARAMS,
        name="weigh_far",
    )(emission, forward, chooser, logits, half, far)


def normalise(raised, pair, devices):
    pairs = exchange(pair)
    own_top = pair[0, 0]
    tops, totals = pairs[:, 0], pairs[:, 1]
    top = jnp.max(tops, axis=0)
    total = jnp.sum(totals * jnp.exp(tops - top), axis=0)
    return BLK * devices * (raised * jnp.exp(own_top - top)[:, None]) / total[:, None]


def forward_messages(emission, last_token, prior_msg, devices, device):
    hidden = emission.shape[0]
    local_rows = prior_msg.shape[0]
    token_ids = jnp.arange(BLK, dtype=jnp.int32)
    tokens = last_token - device * BLK
    onehot = (tokens[:, None] == token_ids[None, :]).astype(jnp.bfloat16)
    owned = dot_rows(onehot, emission)
    owned = owned.astype(jnp.bfloat16).reshape(devices, local_rows, hidden)
    columns = jnp.sum(exchange(owned), axis=0, dtype=jnp.float32)
    unnormal = prior_msg * columns
    forward_msg = (unnormal / jnp.sum(unnormal, axis=1, keepdims=True)).astype(jnp.bfloat16)
    return spread(forward_msg, devices).reshape(devices * local_rows, hidden)


def per_device(
    emission,
    transition,
    beta_start,
    allow_list,
    trans_table,
    last_token,
    prompt_state,
    prior_msg,
    lm_logits,
):
    devices = lax.axis_size("vocab")
    device = lax.axis_index("vocab")
    hidden = emission.shape[0]
    states = beta_start.shape[1]
    own_rows = transition.shape[1]
    prompts = prompt_state.shape[0]
    count = devices.bit_length() - 1
    if devices == 1 << count and count > 2 and own_rows % 128 == 0 and prompts == devices:
        sums = block_sums(emission, devices)
        route, chooser, messages, columns, columns_out, sums = tables(
            last_token, prompt_state, allow_list, trans_table, beta_start, emission, sums, count
        )
        sums = exchange(sums)
        parts, kept_rows, sent_rows, extra = [messages], (columns,), (columns_out,), ()
        for window_step in range(STEPS):
            dtype = jnp.bfloat16 if window_step < STEPS - 1 else jnp.float32
            kept, received = step(
                transition, route, sums, parts, dtype, devices, count, kept_rows, sent_rows
            )
            if window_step == 1:
                forward = forward_messages_here(prior_msg, parts, devices)
                extra = (forward,)
            parts = reduce_blocks(kept, received, dtype, devices, count, extra)
            if window_step == 1:
                forward = jnp.stack([forward] + [part[states:] for part in parts[1:]])
            kept_rows, sent_rows, extra = (), (), ()
        forward = order_forward(*gather_near(forward, devices), count)
        messages = last_sum(parts, forward)
        near, far = gather_near(gather_far(messages, devices, count), devices)
        raised, pair = weigh(emission, forward, chooser, lm_logits, near, far, count)
        return messages.T, normalise(raised, pair, devices)
    state_ids = jnp.arange(states, dtype=jnp.int32)
    block_ids = jnp.arange(devices, dtype=jnp.int32)
    allowed = jnp.any(allow_list[:, :, None] == block_ids, axis=1)
    dest_here = lax.dynamic_index_in_dim(trans_table, device, axis=1, keepdims=False)
    allow_here = jnp.any(allow_list == device, axis=1)
    dest_rows = jnp.sum(jnp.where(prompt_state[:, None] == state_ids, dest_here, 0), axis=1)
    allow_rows = jnp.any((prompt_state[:, None] == state_ids) & allow_here, axis=1)
    chooser = (dest_rows[:, None] == state_ids) & allow_rows[:, None]
    messages = lax.dynamic_slice_in_dim(beta_start, device * own_rows, own_rows, 0).T
    forward_all = forward_messages(emission, last_token, prior_msg, devices, device)
    own_sums = exchange(jnp.sum(emission, axis=1, dtype=jnp.float32).reshape(devices, own_rows))
    route = allowed.T[:, :, None] & (trans_table.T[:, :, None] == state_ids)
    route = route.astype(jnp.float32).reshape(devices * states, states)
    by_owner = transition.reshape(devices, own_rows, own_rows)
    for window_step in range(STEPS):
        selected = jnp.dot(route, messages, precision=lax.Precision.HIGHEST)
        selected = selected.reshape(devices, states, own_rows)
        emitted = jnp.sum(selected * own_sums[:, None, :], axis=0)
        halves = jnp.concatenate(split_wide(emitted), axis=0)
        partial = jnp.einsum("dzy,sy->dsz", by_owner, halves, preferred_element_type=jnp.float32)
        partial = partial[:, :states] + partial[:, states:]
        if window_step < STEPS - 1:
            partial = partial.astype(jnp.bfloat16)
        messages = jnp.sum(exchange(partial), axis=0, dtype=jnp.float32)
    everywhere = spread(messages, devices)
    chosen = jnp.einsum(
        "ps,dsz->pdz", chooser.astype(jnp.float32), everywhere, precision=lax.Precision.HIGHEST
    )
    forward_all = forward_all.reshape(prompts, devices, own_rows).astype(jnp.float32)
    scaled = (forward_all * chosen).astype(jnp.bfloat16).reshape(prompts, hidden)
    weights = jnp.dot(scaled, emission, preferred_element_type=jnp.float32)
    weights = jnp.where(allow_rows[:, None], weights, 0.0)
    logits = lm_logits.astype(jnp.float32)
    top_here = jnp.max(logits, axis=1)
    raised = jnp.exp(logits - top_here[:, None]) * weights
    pairs = spread(jnp.stack([top_here, jnp.sum(raised, axis=1)]), devices)
    tops, totals = pairs[:, 0], pairs[:, 1]
    top = jnp.max(tops, axis=0)
    total = jnp.sum(totals * jnp.exp(tops - top), axis=0)
    raised = raised * jnp.exp(top_here - top)[:, None]
    return (messages.T, BLK * devices * raised / total[:, None])


def solution(mesh):
    return jax.shard_map(
        per_device,
        mesh=mesh,
        in_specs=(
            P(None, "vocab"),
            P(None, "vocab"),
            P(),
            P(),
            P(),
            P("parts"),
            P("parts"),
            P(("parts", "vocab"), None),
            P("parts", "vocab"),
        ),
        out_specs=(P(("parts", "vocab"), None), P("parts", "vocab")),
        check_vma=False,
    )
```

```python
import functools

import jax
import jax.numpy as jnp
from jax import lax
from jax.experimental import pallas as pl
from jax.experimental.pallas import tpu as pltpu
from jax.sharding import PartitionSpec as P

BLK = 256
STEPS = 3
BESIDE = 3
LIMIT = 16 * 1024 * 1024
VMEM = pl.BlockSpec(memory_space=pltpu.VMEM)
SMEM = pl.BlockSpec(memory_space=pltpu.SMEM)
ANY = pl.BlockSpec(memory_space=pl.ANY)
PARAMS = pltpu.CompilerParams(vmem_limit_bytes=LIMIT)


def exchange(blocks):
    return lax.all_to_all(blocks, "vocab", split_axis=0, concat_axis=0, tiled=True)


def spread(own, devices):
    return exchange(jnp.broadcast_to(own[None], (devices,) + own.shape))


def basis(count):
    return [1, BESIDE] + [(1 << bit) | (bit != 2) for bit in range(count - 1, 1, -1)]


def swap(block, offset, devices):
    pairs = [(i, i ^ offset) for i in range(devices)]
    return lax.ppermute(block, "vocab", pairs)


def split_wide(wide):
    high = wide.astype(jnp.bfloat16)
    low = (wide - high.astype(jnp.float32)).astype(jnp.bfloat16)
    return high, low


def split_three(wide):
    high = wide.astype(jnp.bfloat16)
    rest = wide - high.astype(jnp.float32)
    middle = rest.astype(jnp.bfloat16)
    low = (rest - middle.astype(jnp.float32)).astype(jnp.bfloat16)
    return high, middle, low


def dot_rows(left, right):
    return lax.dot_general(left, right, (((1,), (1,)), ((), ())), preferred_element_type=jnp.float32)


def partner_of(bits, count):
    partner = 0
    for bit, offset in zip(bits, basis(count)):
        partner ^= bit * offset
    return partner


def all_bits(count):
    return [tuple((k >> (count - 1 - b)) & 1 for b in range(count)) for k in range(1 << count)]


def far_partners(count):
    return [partner_of((0, 0) + bits, count) for bits in all_bits(count - 2)]


def half_places(count, first):
    far = far_partners(count)
    return [
        ((bit, k), partner_of((first, bit), count) ^ offset)
        for bit in range(2)
        for k, offset in enumerate(far)
    ]


def partner_rows(i, rows):
    owner = lax.axis_index("vocab") ^ i
    return pl.ds(pl.multiple_of(owner * rows, rows), rows)


def reduce_blocks(kept, received, dtype, devices, count, extra=()):
    total = kept + received.astype(jnp.float32)
    middle = swap(total[1].astype(dtype), BESIDE, devices)
    near = total[0] + middle.astype(jnp.float32)
    blocks = [near[0]]
    for k, offset in enumerate(far_partners(count)):
        if k:
            block = jnp.concatenate((near[k].astype(dtype),) + extra, axis=0)
            blocks.append(swap(block, offset, devices))
    return blocks


def gather_far(own, devices, count):
    return jnp.stack([own] + [swap(own, offset, devices) for offset in far_partners(count)[1:]])


def gather_near(own, devices):
    near = jnp.stack([own, swap(own, BESIDE, devices)])
    return near, swap(near, 1, devices)


def column_of(scalars_ref, shape):
    row = lax.broadcasted_iota(jnp.int32, shape, 0)
    column = jnp.zeros(shape, jnp.int32)
    for k in range(shape[0]):
        column = jnp.where(row == k, scalars_ref[k], column)
    return column


def tables_kernel(
    count, state_hbm, allow_hbm, table_hbm, start_hbm, emission_ref, sums_in_ref,
    route_ref, chooser_ref, messages_ref, sums_ref, state_ref, allow_ref, table_ref, sems,
):
    device = lax.axis_index("vocab")
    devices = 1 << count
    states, rows = messages_ref.shape
    own = pl.ds(pl.multiple_of(device * rows, rows), rows)
    pairs = [
        (state_hbm, state_ref), (allow_hbm, allow_ref), (table_hbm, table_ref),
        (start_hbm.at[:, own], messages_ref),
    ]
    copies = [
        pltpu.make_async_copy(source, to, sems.at[k]) for k, (source, to) in enumerate(pairs)
    ]
    for copy in copies:
        copy.start()
    sums_ref[...] = sums_in_ref[...]
    for copy in copies:
        copy.wait()
    allow, table = allow_ref[...], table_ref[...]
    hits = [jnp.max((allow == b).astype(jnp.float32), axis=0, keepdims=True) for b in range(devices)]
    shape = (states, states)
    diagonal = [lax.broadcasted_iota(jnp.int32, shape, axis) for axis in (0, 1)]
    diagonal = (diagonal[0] == diagonal[1]).astype(jnp.bfloat16)
    hits = dot_rows(diagonal, jnp.concatenate(hits, axis=0).astype(jnp.bfloat16))
    ids = lax.broadcasted_iota(jnp.int32, shape, 1)
    own_step = jnp.zeros(shape, jnp.float32)
    for b in range(devices):
        step = jnp.where(table[:, b : b + 1] == ids, hits[:, b : b + 1], 0.0)
        own_step = jnp.where(device == b, step, own_step)
        step = step.astype(jnp.bfloat16)
        route_ref[pl.ds(b * states, states)] = jnp.concatenate([step] * 3, axis=1)
    shape = (devices, states)
    prompts = column_of(state_ref, shape) == lax.broadcasted_iota(jnp.int32, shape, 1)
    chooser = jnp.dot(
        prompts.astype(jnp.bfloat16),
        own_step.astype(jnp.bfloat16),
        preferred_element_type=jnp.float32,
    ).astype(jnp.bfloat16)
    chooser_ref[...] = jnp.concatenate([chooser] * 3, axis=1)


def tables(prompt_state, allow_list, trans_table, beta_start, emission, after, count):
    devices, states = 1 << count, trans_table.shape[0]
    rows = emission.shape[0] >> count
    operands = (prompt_state, allow_list.T, trans_table, beta_start.T)
    return pl.pallas_call(
        functools.partial(tables_kernel, count),
        out_shape=[
            pltpu.VMEM((devices * states, 3 * states), jnp.bfloat16),
            pltpu.VMEM((devices, 3 * states), jnp.bfloat16),
            pltpu.VMEM((states, rows), jnp.float32),
            jax.ShapeDtypeStruct(after.shape, after.dtype),
        ],
        in_specs=[ANY] * len(operands) + [VMEM] * 2,
        out_specs=[VMEM] * 4,
        scratch_shapes=[
            pltpu.SMEM(prompt_state.shape, jnp.int32),
            pltpu.VMEM(allow_list.shape[::-1], jnp.int32),
            pltpu.VMEM(trans_table.shape, jnp.int32),
            pltpu.SemaphoreType.DMA((len(operands),)),
        ],
        compiler_params=PARAMS,
        name="tables",
    )(*(in_hbm(operand) for operand in operands), emission, after)


def products_kernel(count, token_hbm, emission_ref, sums_ref, kept_ref, sent_ref, token_ref, wide_ref, sem):
    device = lax.axis_index("vocab")
    devices = 1 << count
    rows = emission_ref.shape[0] >> count
    copy = pltpu.make_async_copy(token_hbm, token_ref, sem)
    copy.start()
    copy.wait()
    shape = (devices, BLK)
    tokens = column_of(token_ref, shape) - device * BLK
    onehot = (tokens == lax.broadcasted_iota(jnp.int32, shape, 1)).astype(jnp.bfloat16)
    left = jnp.concatenate([onehot, jnp.ones((16, BLK), jnp.bfloat16)], axis=0)
    for k in range(devices):
        product = dot_rows(left, emission_ref[pl.ds(k * rows, rows)])
        wide_ref[:, k, :] = product[:devices]
        sums_ref[k] = product[devices : devices + 1]
    for first, out_ref in ((0, kept_ref), (1, sent_ref)):
        for place, partner in half_places(count, first):
            out_ref[place] = wide_ref[device ^ partner].astype(jnp.bfloat16)


def first_products(last_token, emission, count):
    devices, rows = 1 << count, emission.shape[0] >> count
    half = pltpu.VMEM((2, devices // 4, devices, rows), jnp.bfloat16)
    return pl.pallas_call(
        functools.partial(products_kernel, count),
        out_shape=[jax.ShapeDtypeStruct((devices, 1, rows), jnp.float32), half, half],
        in_specs=[ANY, VMEM],
        out_specs=[VMEM] * 3,
        scratch_shapes=[
            pltpu.SMEM(last_token.shape, jnp.int32),
            pltpu.VMEM((devices, devices, rows), jnp.float32),
            pltpu.SemaphoreType.DMA,
        ],
        compiler_params=PARAMS,
        name="first_products",
    )(in_hbm(last_token), emission)


def in_hbm(array):
    return pltpu.with_memory_space_constraint(array, pltpu.HBM)


def forward_kernel(prior_ref, *refs):
    blocks, out_ref = refs[:-1], refs[-1]
    devices, rows = out_ref.shape
    columns = blocks[0][-devices:]
    for block in blocks[1:]:
        columns += block[-devices:].astype(jnp.float32)
    prior = jnp.concatenate([prior_ref[:, pl.ds(k * rows, rows)] for k in range(devices)], axis=0)
    unnormal = prior * columns
    out_ref[...] = (unnormal / jnp.sum(unnormal)).astype(jnp.bfloat16)


def forward_messages_here(prior, blocks, devices):
    return pl.pallas_call(
        forward_kernel,
        out_shape=pltpu.VMEM((devices, blocks[0].shape[1]), jnp.bfloat16),
        in_specs=[VMEM] * (1 + len(blocks)),
        out_specs=VMEM,
        compiler_params=PARAMS,
        name="forward_messages",
    )(prior, *blocks)


def order_kernel(count, near_ref, far_ref, out_ref):
    size = 1 << count
    device = lax.axis_index("vocab")

    def partner(place):
        number = jnp.zeros_like(place)
        for bit, offset in enumerate(basis(count)):
            number = number ^ (((place >> (count - 1 - bit)) & 1) * offset)
        return device ^ number

    shape = (size * size, size * size)
    to, source = (lax.broadcasted_iota(jnp.int32, shape, axis) for axis in (0, 1))
    same_block = partner(to >> count) == (source & (size - 1))
    same_prompt = (to & (size - 1)) == partner(source >> count)
    onehot = (same_block & same_prompt).astype(jnp.bfloat16)
    half = size * size // 2
    rows = out_ref.shape[1]
    near = near_ref[...].reshape(half, rows)
    far = far_ref[...].reshape(half, rows)
    ordered = jnp.dot(onehot[:, :half], near, preferred_element_type=jnp.float32)
    ordered += jnp.dot(onehot[:, half:], far, preferred_element_type=jnp.float32)
    out_ref[...] = ordered.astype(jnp.bfloat16)


def order_forward(near, far, count):
    rows = near.shape[-1]
    return pl.pallas_call(
        functools.partial(order_kernel, count),
        out_shape=pltpu.VMEM((1 << (2 * count), rows), jnp.bfloat16),
        in_specs=[VMEM] * 2,
        out_specs=VMEM,
        compiler_params=PARAMS,
        name="order_forward",
    )(near, far)


def last_kernel(*refs):
    blocks, out_ref = refs[:-2], refs[-1]
    messages = blocks[0][...]
    for block in blocks[1:]:
        messages += block[...]
    out_ref[...] = messages


def last_sum(blocks, after):
    return pl.pallas_call(
        last_kernel,
        out_shape=pltpu.VMEM(blocks[0].shape, jnp.float32),
        in_specs=[VMEM] * len(blocks) + [ANY],
        out_specs=VMEM,
        compiler_params=PARAMS,
        name="last_messages",
    )(*blocks, after)


def half_products(halves, transition_ref, out_ref, count, first):
    states = halves.shape[0] // 2
    rows = transition_ref.shape[0] >> count
    for place, partner in half_places(count, first):
        product = dot_rows(halves, transition_ref[partner_rows(partner, rows)])
        product = product[:states] + product[states:]
        out_ref[place + (pl.ds(0, states),)] = product.astype(out_ref.dtype)


def add_rows(out_ref, states, extra):
    for ref in extra:
        rows = pl.ds(states, ref.shape[2])
        for place in ((y, k) for y in range(ref.shape[0]) for k in range(ref.shape[1])):
            out_ref[place + (rows,)] = ref[place].astype(out_ref.dtype)


def send_kernel(count, number, transition_ref, route_ref, sums_ref, *refs):
    parts, extra, (halves_ref, out_ref) = refs[:number], refs[number:-2], refs[-2:]
    states = halves_ref.shape[0] // 2
    messages = parts[0][:states].astype(jnp.float32)
    for part in parts[1:]:
        messages += part[:states].astype(jnp.float32)
    selected = jnp.dot(
        route_ref[...],
        jnp.concatenate(split_three(messages), axis=0),
        preferred_element_type=jnp.float32,
    )
    emitted = selected[:states] * sums_ref[0]
    for b in range(1, 1 << count):
        emitted += selected[b * states : (b + 1) * states] * sums_ref[b]
    halves = jnp.concatenate(split_wide(emitted), axis=0)
    halves_ref[...] = halves
    half_products(halves, transition_ref, out_ref, count, 1)
    add_rows(out_ref, states, extra)


def keep_kernel(count, transition_ref, halves_ref, *refs):
    extra, out_ref = refs[:-1], refs[-1]
    half_products(halves_ref[...], transition_ref, out_ref, count, 0)
    add_rows(out_ref, halves_ref.shape[0] // 2, extra)


def step(transition, route, sums, parts, dtype, devices, count, kept_rows=(), sent_rows=()):
    states, rows = route.shape[0] // devices, parts[0].shape[1]
    total = states + sum(block.shape[2] for block in kept_rows)
    shape = (2, devices // 4, total, rows)
    halves, sent = pl.pallas_call(
        functools.partial(send_kernel, count, len(parts)),
        out_shape=[
            pltpu.VMEM((2 * states, rows), jnp.bfloat16),
            pltpu.VMEM(shape, dtype),
        ],
        in_specs=[VMEM] * (3 + len(parts) + len(sent_rows)),
        out_specs=[VMEM] * 2,
        compiler_params=PARAMS,
        name="step_sent_half",
    )(transition, route, sums, *parts, *sent_rows)
    received = swap(sent, 1, devices)
    kept = pl.pallas_call(
        functools.partial(keep_kernel, count),
        out_shape=pltpu.VMEM(shape, jnp.float32),
        in_specs=[VMEM] * (2 + len(kept_rows)),
        out_specs=VMEM,
        compiler_params=PARAMS,
        name="step_kept_half",
    )(transition, halves, *kept_rows)
    return kept, received


def weigh_half(emission_ref, forward_ref, chooser, parts_ref, count, first):
    rows = emission_ref.shape[0] >> count
    prompts = chooser.shape[0]
    weights = jnp.zeros((prompts, emission_ref.shape[1]), jnp.float32)
    for order, (place, partner) in enumerate(half_places(count, first)):
        pieces = jnp.concatenate(split_three(parts_ref[place]), axis=0)
        chosen = jnp.dot(chooser, pieces, preferred_element_type=jnp.float32)
        block = order + (first << (count - 1))
        forward = forward_ref[pl.ds(block * prompts, prompts)].astype(jnp.float32)
        scaled = (forward * chosen).astype(jnp.bfloat16)
        tile = emission_ref[partner_rows(partner, rows)]
        weights += jnp.dot(scaled, tile, preferred_element_type=jnp.float32)
    return weights


def near_kernel(count, emission_ref, forward_ref, chooser_ref, parts_ref, out_ref):
    out_ref[...] = weigh_half(emission_ref, forward_ref, chooser_ref[...], parts_ref, count, 0)


def far_kernel(count, emission_ref, forward_ref, chooser_ref, logits_ref, near_ref, parts_ref, raised_ref, pair_ref):
    chooser = chooser_ref[...]
    logits = logits_ref[...].astype(jnp.float32)
    top = jnp.max(logits, axis=1, keepdims=True)
    weights = near_ref[...] + weigh_half(emission_ref, forward_ref, chooser, parts_ref, count, 1)
    allowed = jnp.sum(chooser.astype(jnp.float32), axis=1, keepdims=True) > 0
    raised = jnp.where(allowed, jnp.exp(logits - top) * weights, 0.0)
    raised_ref[...] = raised
    total = jnp.sum(raised, axis=1, keepdims=True)
    size = raised.shape[0]
    diagonal = [lax.broadcasted_iota(jnp.int32, (size, size), axis) for axis in (0, 1)]
    diagonal = diagonal[0] == diagonal[1]
    columns = [
        jnp.concatenate(split_three(jnp.where(diagonal, column, 0.0)), axis=0)
        for column in (top, total)
    ]
    row = jnp.dot(
        jnp.ones((16, 3 * size), jnp.bfloat16),
        jnp.concatenate(columns, axis=1),
        preferred_element_type=jnp.float32,
    )
    for k in range(pair_ref.shape[0]):
        pair_ref[k] = row[:1]


def weigh(emission, forward, chooser, logits, near, far, count):
    half = pl.pallas_call(
        functools.partial(near_kernel, count),
        out_shape=pltpu.VMEM(logits.shape, jnp.float32),
        in_specs=[VMEM] * 4,
        out_specs=VMEM,
        compiler_params=PARAMS,
        name="weigh_near",
    )(emission, forward, chooser, near)
    return pl.pallas_call(
        functools.partial(far_kernel, count),
        out_shape=[
            pltpu.VMEM(logits.shape, jnp.float32),
            pltpu.VMEM((1 << count, 1, 2 * logits.shape[0]), jnp.float32),
        ],
        in_specs=[VMEM] * 6,
        out_specs=[VMEM] * 2,
        compiler_params=PARAMS,
        name="weigh_far",
    )(emission, forward, chooser, logits, half, far)


def finish_kernel(scale, raised_ref, pair_ref, pairs_ref, out_ref):
    size = raised_ref.shape[0]
    tops, totals = pairs_ref[:, 0, :size], pairs_ref[:, 0, size:]
    top = jnp.max(tops, axis=0, keepdims=True)
    total = jnp.sum(totals * jnp.exp(tops - top), axis=0, keepdims=True)
    own = jnp.exp(pair_ref[0, :, :size] - top)
    diagonal = [lax.broadcasted_iota(jnp.int32, (size, size), axis) for axis in (0, 1)]
    diagonal = diagonal[0] == diagonal[1]
    own, total = (
        jnp.sum(jnp.where(diagonal, row, 0.0), axis=1, keepdims=True) for row in (own, total)
    )
    out_ref[...] = scale * (raised_ref[...] * own) / total


def normalise(raised, pair, devices):
    return pl.pallas_call(
        functools.partial(finish_kernel, BLK * devices),
        out_shape=jax.ShapeDtypeStruct(raised.shape, jnp.float32),
        in_specs=[VMEM] * 3,
        out_specs=VMEM,
        compiler_params=PARAMS,
        name="normalise",
    )(raised, pair, exchange(pair))


def forward_messages(emission, last_token, prior_msg, devices, device):
    hidden = emission.shape[0]
    local_rows = prior_msg.shape[0]
    token_ids = jnp.arange(BLK, dtype=jnp.int32)
    tokens = last_token - device * BLK
    onehot = (tokens[:, None] == token_ids[None, :]).astype(jnp.bfloat16)
    owned = dot_rows(onehot, emission)
    owned = owned.astype(jnp.bfloat16).reshape(devices, local_rows, hidden)
    columns = jnp.sum(exchange(owned), axis=0, dtype=jnp.float32)
    unnormal = prior_msg * columns
    forward_msg = (unnormal / jnp.sum(unnormal, axis=1, keepdims=True)).astype(jnp.bfloat16)
    return spread(forward_msg, devices).reshape(devices * local_rows, hidden)


def per_device(
    emission,
    transition,
    beta_start,
    allow_list,
    trans_table,
    last_token,
    prompt_state,
    prior_msg,
    lm_logits,
):
    devices = lax.axis_size("vocab")
    device = lax.axis_index("vocab")
    hidden = emission.shape[0]
    states = beta_start.shape[1]
    own_rows = transition.shape[1]
    prompts = prompt_state.shape[0]
    count = devices.bit_length() - 1
    if devices == 1 << count and count > 2 and own_rows % 128 == 0 and prompts == devices:
        sums, columns, columns_out = first_products(last_token, emission, count)
        route, chooser, messages, sums = tables(
            prompt_state, allow_list, trans_table, beta_start, emission, sums, count
        )
        sums = exchange(sums)
        parts, kept_rows, sent_rows, extra = [messages], (columns,), (columns_out,), ()
        for window_step in range(STEPS):
            dtype = jnp.bfloat16 if window_step < STEPS - 1 else jnp.float32
            kept, received = step(
                transition, route, sums, parts, dtype, devices, count, kept_rows, sent_rows
            )
            if window_step == 1:
                forward = forward_messages_here(prior_msg, parts, devices)
                extra = (forward,)
            parts = reduce_blocks(kept, received, dtype, devices, count, extra)
            if window_step == 1:
                forward = jnp.stack([forward] + [part[states:] for part in parts[1:]])
            kept_rows, sent_rows, extra = (), (), ()
        forward = order_forward(*gather_near(forward, devices), count)
        messages = last_sum(parts, forward)
        near, far = gather_near(gather_far(messages, devices, count), devices)
        raised, pair = weigh(emission, forward, chooser, lm_logits, near, far, count)
        return messages.T, normalise(raised, pair, devices)
    state_ids = jnp.arange(states, dtype=jnp.int32)
    block_ids = jnp.arange(devices, dtype=jnp.int32)
    allowed = jnp.any(allow_list[:, :, None] == block_ids, axis=1)
    dest_here = lax.dynamic_index_in_dim(trans_table, device, axis=1, keepdims=False)
    allow_here = jnp.any(allow_list == device, axis=1)
    dest_rows = jnp.sum(jnp.where(prompt_state[:, None] == state_ids, dest_here, 0), axis=1)
    allow_rows = jnp.any((prompt_state[:, None] == state_ids) & allow_here, axis=1)
    chooser = (dest_rows[:, None] == state_ids) & allow_rows[:, None]
    messages = lax.dynamic_slice_in_dim(beta_start, device * own_rows, own_rows, 0).T
    forward_all = forward_messages(emission, last_token, prior_msg, devices, device)
    own_sums = exchange(jnp.sum(emission, axis=1, dtype=jnp.float32).reshape(devices, own_rows))
    route = allowed.T[:, :, None] & (trans_table.T[:, :, None] == state_ids)
    route = route.astype(jnp.float32).reshape(devices * states, states)
    by_owner = transition.reshape(devices, own_rows, own_rows)
    for window_step in range(STEPS):
        selected = jnp.dot(route, messages, precision=lax.Precision.HIGHEST)
        selected = selected.reshape(devices, states, own_rows)
        emitted = jnp.sum(selected * own_sums[:, None, :], axis=0)
        halves = jnp.concatenate(split_wide(emitted), axis=0)
        partial = jnp.einsum("dzy,sy->dsz", by_owner, halves, preferred_element_type=jnp.float32)
        partial = partial[:, :states] + partial[:, states:]
        if window_step < STEPS - 1:
            partial = partial.astype(jnp.bfloat16)
        messages = jnp.sum(exchange(partial), axis=0, dtype=jnp.float32)
    everywhere = spread(messages, devices)
    chosen = jnp.einsum(
        "ps,dsz->pdz", chooser.astype(jnp.float32), everywhere, precision=lax.Precision.HIGHEST
    )
    forward_all = forward_all.reshape(prompts, devices, own_rows).astype(jnp.float32)
    scaled = (forward_all * chosen).astype(jnp.bfloat16).reshape(prompts, hidden)
    weights = jnp.dot(scaled, emission, preferred_element_type=jnp.float32)
    weights = jnp.where(allow_rows[:, None], weights, 0.0)
    logits = lm_logits.astype(jnp.float32)
    top_here = jnp.max(logits, axis=1)
    raised = jnp.exp(logits - top_here[:, None]) * weights
    pairs = spread(jnp.stack([top_here, jnp.sum(raised, axis=1)]), devices)
    tops, totals = pairs[:, 0], pairs[:, 1]
    top = jnp.max(tops, axis=0)
    total = jnp.sum(totals * jnp.exp(tops - top), axis=0)
    raised = raised * jnp.exp(top_here - top)[:, None]
    return (messages.T, BLK * devices * raised / total[:, None])


def solution(mesh):
    return jax.shard_map(
        per_device,
        mesh=mesh,
        in_specs=(
            P(None, "vocab"),
            P(None, "vocab"),
            P(),
            P(),
            P(),
            P("parts"),
            P("parts"),
            P(("parts", "vocab"), None),
            P("parts", "vocab"),
        ),
        out_specs=(P(("parts", "vocab"), None), P("parts", "vocab")),
        check_vma=False,
    )
```

```python
import functools

import jax
import jax.numpy as jnp
from jax import lax
from jax.experimental import pallas as pl
from jax.experimental.pallas import tpu as pltpu
from jax.sharding import PartitionSpec as P

BLK = 256
STEPS = 3
LIMIT = 16 * 1024 * 1024
VMEM = pl.BlockSpec(memory_space=pltpu.VMEM)
SMEM = pl.BlockSpec(memory_space=pltpu.SMEM)
ANY = pl.BlockSpec(memory_space=pl.ANY)
PARAMS = pltpu.CompilerParams(vmem_limit_bytes=LIMIT)


def exchange(blocks):
    return lax.all_to_all(blocks, "vocab", split_axis=0, concat_axis=0, tiled=True)


def spread(own, devices):
    return exchange(jnp.broadcast_to(own[None], (devices,) + own.shape))


def basis(count):
    return [1, 3, 4] + [(1 << bit) | 1 for bit in range(3, count)]


def swap(block, offset, devices):
    pairs = [(i, i ^ offset) for i in range(devices)]
    return lax.ppermute(block, "vocab", pairs)


def split_wide(wide):
    high = wide.astype(jnp.bfloat16)
    low = (wide - high.astype(jnp.float32)).astype(jnp.bfloat16)
    return high, low


def split_outside(wide):
    high = lax.reduce_precision(wide, exponent_bits=8, mantissa_bits=7)
    return high.astype(jnp.bfloat16), (wide - high).astype(jnp.bfloat16)


def split_three(wide):
    high = wide.astype(jnp.bfloat16)
    rest = wide - high.astype(jnp.float32)
    middle = rest.astype(jnp.bfloat16)
    low = (rest - middle.astype(jnp.float32)).astype(jnp.bfloat16)
    return high, middle, low


def dot_rows(left, right):
    return lax.dot_general(left, right, (((1,), (1,)), ((), ())), preferred_element_type=jnp.float32)


def partner_of(bits, count):
    partner = 0
    for bit, offset in zip(bits, basis(count)):
        partner ^= bit * offset
    return partner


def all_bits(count):
    return [tuple((k >> (count - 1 - b)) & 1 for b in range(count)) for k in range(1 << count)]


def square_partners(count):
    return [partner_of((0,) + bits, count) for bits in all_bits(2)]


def far_partners(count):
    return [partner_of((0, 0, 0) + bits, count) for bits in all_bits(count - 3)]


def half_places(count, first):
    return [
        ((q, h), first ^ near ^ far)
        for q, near in enumerate(square_partners(count))
        for h, far in enumerate(far_partners(count))
    ]


def partner_rows(i, rows):
    owner = lax.axis_index("vocab") ^ i
    return pl.ds(pl.multiple_of(owner * rows, rows), rows)


def pack(blocks, wide, extra):
    rows = blocks.reshape(-1, blocks.shape[-1])
    parts = split_outside(rows) if wide else (rows.astype(jnp.bfloat16),)
    return jnp.concatenate(parts + extra, axis=0)


def unpack(packed, shape, wide):
    size = shape[0] * shape[1]
    rows = packed[:size].astype(jnp.float32)
    if wide:
        rows += packed[size : 2 * size].astype(jnp.float32)
    return rows.reshape(shape)


def reduce_blocks(kept, received, wide, devices, count, near_extra=(), far_extra=()):
    total = kept + received.astype(jnp.float32)
    near, extras = total[0], list(near_extra)
    for q, offset in enumerate(square_partners(count)):
        if q:
            packed = swap(pack(total[q], wide, near_extra), offset, devices)
            near += unpack(packed, total.shape[1:], wide)
            for extra in near_extra:
                extras.append(packed[-extra.shape[0] :])
    blocks = [near[0]]
    for h, offset in enumerate(far_partners(count)):
        if h:
            blocks.append(swap(pack(near[h], wide, far_extra), offset, devices))
    return blocks, extras


def gather_blocks(own, devices, count):
    far = jnp.stack([own] + [swap(own, offset, devices) for offset in far_partners(count)[1:]])
    near = jnp.stack([far] + [swap(far, offset, devices) for offset in square_partners(count)[1:]])
    return near, swap(near, 1, devices)


def column_of(scalars_ref, shape):
    row = lax.broadcasted_iota(jnp.int32, shape, 0)
    column = jnp.zeros(shape, jnp.int32)
    for k in range(shape[0]):
        column = jnp.where(row == k, scalars_ref[k], column)
    return column


def tables_kernel(
    count, state_hbm, allow_hbm, table_hbm, start_hbm, emission_ref, sums_in_ref,
    route_ref, chooser_ref, messages_ref, sums_ref, state_ref, allow_ref, table_ref, sems,
):
    device = lax.axis_index("vocab")
    devices = 1 << count
    states, rows = messages_ref.shape
    own = pl.ds(pl.multiple_of(device * rows, rows), rows)
    pairs = [
        (state_hbm, state_ref), (allow_hbm, allow_ref), (table_hbm, table_ref),
        (start_hbm.at[:, own], messages_ref),
    ]
    copies = [
        pltpu.make_async_copy(source, to, sems.at[k]) for k, (source, to) in enumerate(pairs)
    ]
    for copy in copies:
        copy.start()
    sums_ref[...] = sums_in_ref[...]
    for copy in copies:
        copy.wait()
    allow, table = allow_ref[...], table_ref[...]
    hits = [jnp.max((allow == b).astype(jnp.float32), axis=0, keepdims=True) for b in range(devices)]
    shape = (states, states)
    diagonal = [lax.broadcasted_iota(jnp.int32, shape, axis) for axis in (0, 1)]
    diagonal = (diagonal[0] == diagonal[1]).astype(jnp.bfloat16)
    hits = dot_rows(diagonal, jnp.concatenate(hits, axis=0).astype(jnp.bfloat16))
    ids = lax.broadcasted_iota(jnp.int32, shape, 1)
    own_step = jnp.zeros(shape, jnp.float32)
    for b in range(devices):
        step = jnp.where(table[:, b : b + 1] == ids, hits[:, b : b + 1], 0.0)
        own_step = jnp.where(device == b, step, own_step)
        step = step.astype(jnp.bfloat16)
        route_ref[pl.ds(b * states, states)] = jnp.concatenate([step] * 3, axis=1)
    shape = (devices, states)
    prompts = column_of(state_ref, shape) == lax.broadcasted_iota(jnp.int32, shape, 1)
    chooser = jnp.dot(
        prompts.astype(jnp.bfloat16),
        own_step.astype(jnp.bfloat16),
        preferred_element_type=jnp.float32,
    ).astype(jnp.bfloat16)
    chooser_ref[...] = jnp.concatenate([chooser] * 3, axis=1)


def tables(prompt_state, allow_list, trans_table, beta_start, emission, after, count):
    devices, states = 1 << count, trans_table.shape[0]
    rows = emission.shape[0] >> count
    operands = (prompt_state, allow_list.T, trans_table, beta_start.T)
    return pl.pallas_call(
        functools.partial(tables_kernel, count),
        out_shape=[
            pltpu.VMEM((devices * states, 3 * states), jnp.bfloat16),
            pltpu.VMEM((devices, 3 * states), jnp.bfloat16),
            pltpu.VMEM((states, rows), jnp.float32),
            jax.ShapeDtypeStruct(after.shape, after.dtype),
        ],
        in_specs=[ANY] * len(operands) + [VMEM] * 2,
        out_specs=[VMEM] * 4,
        scratch_shapes=[
            pltpu.SMEM(prompt_state.shape, jnp.int32),
            pltpu.VMEM(allow_list.shape[::-1], jnp.int32),
            pltpu.VMEM(trans_table.shape, jnp.int32),
            pltpu.SemaphoreType.DMA((len(operands),)),
        ],
        compiler_params=PARAMS,
        name="tables",
    )(*(in_hbm(operand) for operand in operands), emission, after)


def products_kernel(count, token_hbm, emission_ref, sums_ref, kept_ref, sent_ref, token_ref, wide_ref, sem):
    device = lax.axis_index("vocab")
    devices = 1 << count
    rows = emission_ref.shape[0] >> count
    copy = pltpu.make_async_copy(token_hbm, token_ref, sem)
    copy.start()
    copy.wait()
    shape = (devices, BLK)
    tokens = column_of(token_ref, shape) - device * BLK
    onehot = (tokens == lax.broadcasted_iota(jnp.int32, shape, 1)).astype(jnp.bfloat16)
    left = jnp.concatenate([onehot, jnp.ones((16, BLK), jnp.bfloat16)], axis=0)
    for k in range(devices):
        product = dot_rows(left, emission_ref[pl.ds(k * rows, rows)])
        wide_ref[:, k, :] = product[:devices]
        sums_ref[k] = product[devices : devices + 1]
    for first, out_ref in ((0, kept_ref), (1, sent_ref)):
        for place, partner in half_places(count, first):
            out_ref[place] = wide_ref[device ^ partner].astype(jnp.bfloat16)


def first_products(last_token, emission, count):
    devices, rows = 1 << count, emission.shape[0] >> count
    half = pltpu.VMEM((4, devices // 8, devices, rows), jnp.bfloat16)
    return pl.pallas_call(
        functools.partial(products_kernel, count),
        out_shape=[jax.ShapeDtypeStruct((devices, 1, rows), jnp.float32), half, half],
        in_specs=[ANY, VMEM],
        out_specs=[VMEM] * 3,
        scratch_shapes=[
            pltpu.SMEM(last_token.shape, jnp.int32),
            pltpu.VMEM((devices, devices, rows), jnp.float32),
            pltpu.SemaphoreType.DMA,
        ],
        compiler_params=PARAMS,
        name="first_products",
    )(in_hbm(last_token), emission)


def in_hbm(array):
    return pltpu.with_memory_space_constraint(array, pltpu.HBM)


def forward_kernel(prior_ref, *refs):
    blocks, out_ref = refs[:-1], refs[-1]
    devices, rows = out_ref.shape
    columns = blocks[0][-devices:]
    for block in blocks[1:]:
        columns += block[-devices:].astype(jnp.float32)
    prior = jnp.concatenate([prior_ref[:, pl.ds(k * rows, rows)] for k in range(devices)], axis=0)
    unnormal = prior * columns
    out_ref[...] = (unnormal / jnp.sum(unnormal)).astype(jnp.bfloat16)


def forward_messages_here(prior, blocks, devices):
    return pl.pallas_call(
        forward_kernel,
        out_shape=pltpu.VMEM((devices, blocks[0].shape[1]), jnp.bfloat16),
        in_specs=[VMEM] * (1 + len(blocks)),
        out_specs=VMEM,
        compiler_params=PARAMS,
        name="forward_messages",
    )(prior, *blocks)


def order_kernel(count, near_ref, far_ref, out_ref):
    size = 1 << count
    device = lax.axis_index("vocab")

    def partner(place):
        number = jnp.zeros_like(place)
        for bit, offset in enumerate(basis(count)):
            number = number ^ (((place >> (count - 1 - bit)) & 1) * offset)
        return device ^ number

    shape = (size * size, size * size)
    to, source = (lax.broadcasted_iota(jnp.int32, shape, axis) for axis in (0, 1))
    same_block = partner(to >> count) == (source & (size - 1))
    same_prompt = (to & (size - 1)) == partner(source >> count)
    onehot = (same_block & same_prompt).astype(jnp.bfloat16)
    half = size * size // 2
    rows = out_ref.shape[1]
    near = near_ref[...].reshape(half, rows)
    far = far_ref[...].reshape(half, rows)
    ordered = jnp.dot(onehot[:, :half], near, preferred_element_type=jnp.float32)
    ordered += jnp.dot(onehot[:, half:], far, preferred_element_type=jnp.float32)
    out_ref[...] = ordered.astype(jnp.bfloat16)


def order_forward(near, far, count):
    rows = near.shape[-1]
    return pl.pallas_call(
        functools.partial(order_kernel, count),
        out_shape=pltpu.VMEM((1 << (2 * count), rows), jnp.bfloat16),
        in_specs=[VMEM] * 2,
        out_specs=VMEM,
        compiler_params=PARAMS,
        name="order_forward",
    )(near, far)


def last_kernel(*refs):
    blocks, out_ref = refs[:-2], refs[-1]
    states = out_ref.shape[0]
    messages = blocks[0][...]
    for block in blocks[1:]:
        for part in range(2):
            messages += block[pl.ds(part * states, states)].astype(jnp.float32)
    out_ref[...] = messages


def last_sum(blocks, after):
    return pl.pallas_call(
        last_kernel,
        out_shape=pltpu.VMEM(blocks[0].shape, jnp.float32),
        in_specs=[VMEM] * len(blocks) + [ANY],
        out_specs=VMEM,
        compiler_params=PARAMS,
        name="last_messages",
    )(*blocks, after)


def half_products(halves, transition_ref, out_ref, count, first):
    states = halves.shape[0] // 2
    rows = transition_ref.shape[0] >> count
    for place, partner in half_places(count, first):
        product = dot_rows(halves, transition_ref[partner_rows(partner, rows)])
        product = product[:states] + product[states:]
        out_ref[place + (pl.ds(0, states),)] = product.astype(out_ref.dtype)


def add_rows(out_ref, states, extra):
    for ref in extra:
        rows = pl.ds(states, ref.shape[2])
        for place in ((y, k) for y in range(ref.shape[0]) for k in range(ref.shape[1])):
            out_ref[place + (rows,)] = ref[place].astype(out_ref.dtype)


def send_kernel(count, number, transition_ref, route_ref, sums_ref, *refs):
    parts, extra, (halves_ref, out_ref) = refs[:number], refs[number:-2], refs[-2:]
    states = halves_ref.shape[0] // 2
    messages = parts[0][:states].astype(jnp.float32)
    for part in parts[1:]:
        messages += part[:states].astype(jnp.float32)
    selected = jnp.dot(
        route_ref[...],
        jnp.concatenate(split_three(messages), axis=0),
        preferred_element_type=jnp.float32,
    )
    emitted = selected[:states] * sums_ref[0]
    for b in range(1, 1 << count):
        emitted += selected[b * states : (b + 1) * states] * sums_ref[b]
    halves = jnp.concatenate(split_wide(emitted), axis=0)
    halves_ref[...] = halves
    half_products(halves, transition_ref, out_ref, count, 1)
    add_rows(out_ref, states, extra)


def keep_kernel(count, transition_ref, halves_ref, *refs):
    extra, out_ref = refs[:-1], refs[-1]
    half_products(halves_ref[...], transition_ref, out_ref, count, 0)
    add_rows(out_ref, halves_ref.shape[0] // 2, extra)


def step(transition, route, sums, parts, dtype, devices, count, kept_rows=(), sent_rows=()):
    states, rows = route.shape[0] // devices, parts[0].shape[1]
    total = states + sum(block.shape[2] for block in kept_rows)
    shape = (4, devices // 8, total, rows)
    halves, sent = pl.pallas_call(
        functools.partial(send_kernel, count, len(parts)),
        out_shape=[
            pltpu.VMEM((2 * states, rows), jnp.bfloat16),
            pltpu.VMEM(shape, dtype),
        ],
        in_specs=[VMEM] * (3 + len(parts) + len(sent_rows)),
        out_specs=[VMEM] * 2,
        compiler_params=PARAMS,
        name="step_sent_half",
    )(transition, route, sums, *parts, *sent_rows)
    received = swap(sent, 1, devices)
    kept = pl.pallas_call(
        functools.partial(keep_kernel, count),
        out_shape=pltpu.VMEM(shape, jnp.float32),
        in_specs=[VMEM] * (2 + len(kept_rows)),
        out_specs=VMEM,
        compiler_params=PARAMS,
        name="step_kept_half",
    )(transition, halves, *kept_rows)
    return kept, received


def weigh_half(emission_ref, forward_ref, chooser, parts_ref, count, first):
    rows = emission_ref.shape[0] >> count
    prompts = chooser.shape[0]
    weights = jnp.zeros((prompts, emission_ref.shape[1]), jnp.float32)
    for order, (place, partner) in enumerate(half_places(count, first)):
        pieces = jnp.concatenate(split_three(parts_ref[place]), axis=0)
        chosen = jnp.dot(chooser, pieces, preferred_element_type=jnp.float32)
        block = order + (first << (count - 1))
        forward = forward_ref[pl.ds(block * prompts, prompts)].astype(jnp.float32)
        scaled = (forward * chosen).astype(jnp.bfloat16)
        tile = emission_ref[partner_rows(partner, rows)]
        weights += jnp.dot(scaled, tile, preferred_element_type=jnp.float32)
    return weights


def near_kernel(count, emission_ref, forward_ref, chooser_ref, parts_ref, out_ref):
    out_ref[...] = weigh_half(emission_ref, forward_ref, chooser_ref[...], parts_ref, count, 0)


def far_kernel(count, emission_ref, forward_ref, chooser_ref, logits_ref, near_ref, parts_ref, raised_ref, pair_ref):
    chooser = chooser_ref[...]
    logits = logits_ref[...].astype(jnp.float32)
    top = jnp.max(logits, axis=1, keepdims=True)
    weights = near_ref[...] + weigh_half(emission_ref, forward_ref, chooser, parts_ref, count, 1)
    allowed = jnp.sum(chooser.astype(jnp.float32), axis=1, keepdims=True) > 0
    raised = jnp.where(allowed, jnp.exp(logits - top) * weights, 0.0)
    raised_ref[...] = raised
    total = jnp.sum(raised, axis=1, keepdims=True)
    size = raised.shape[0]
    diagonal = [lax.broadcasted_iota(jnp.int32, (size, size), axis) for axis in (0, 1)]
    diagonal = diagonal[0] == diagonal[1]
    columns = [
        jnp.concatenate(split_three(jnp.where(diagonal, column, 0.0)), axis=0)
        for column in (top, total)
    ]
    row = jnp.dot(
        jnp.ones((16, 3 * size), jnp.bfloat16),
        jnp.concatenate(columns, axis=1),
        preferred_element_type=jnp.float32,
    )
    for k in range(pair_ref.shape[0]):
        pair_ref[k] = row[:1]


def weigh(emission, forward, chooser, logits, near, far, count):
    half = pl.pallas_call(
        functools.partial(near_kernel, count),
        out_shape=pltpu.VMEM(logits.shape, jnp.float32),
        in_specs=[VMEM] * 4,
        out_specs=VMEM,
        compiler_params=PARAMS,
        name="weigh_near",
    )(emission, forward, chooser, near)
    return pl.pallas_call(
        functools.partial(far_kernel, count),
        out_shape=[
            pltpu.VMEM(logits.shape, jnp.float32),
            pltpu.VMEM((1 << count, 1, 2 * logits.shape[0]), jnp.float32),
        ],
        in_specs=[VMEM] * 6,
        out_specs=[VMEM] * 2,
        compiler_params=PARAMS,
        name="weigh_far",
    )(emission, forward, chooser, logits, half, far)


def finish_kernel(scale, raised_ref, pair_ref, pairs_ref, out_ref):
    size = raised_ref.shape[0]
    tops, totals = pairs_ref[:, 0, :size], pairs_ref[:, 0, size:]
    top = jnp.max(tops, axis=0, keepdims=True)
    total = jnp.sum(totals * jnp.exp(tops - top), axis=0, keepdims=True)
    own = jnp.exp(pair_ref[0, :, :size] - top)
    diagonal = [lax.broadcasted_iota(jnp.int32, (size, size), axis) for axis in (0, 1)]
    diagonal = diagonal[0] == diagonal[1]
    own, total = (
        jnp.sum(jnp.where(diagonal, row, 0.0), axis=1, keepdims=True) for row in (own, total)
    )
    out_ref[...] = scale * (raised_ref[...] * own) / total


def normalise(raised, pair, devices):
    return pl.pallas_call(
        functools.partial(finish_kernel, BLK * devices),
        out_shape=jax.ShapeDtypeStruct(raised.shape, jnp.float32),
        in_specs=[VMEM] * 3,
        out_specs=VMEM,
        compiler_params=PARAMS,
        name="normalise",
    )(raised, pair, exchange(pair))


def forward_messages(emission, last_token, prior_msg, devices, device):
    hidden = emission.shape[0]
    local_rows = prior_msg.shape[0]
    token_ids = jnp.arange(BLK, dtype=jnp.int32)
    tokens = last_token - device * BLK
    onehot = (tokens[:, None] == token_ids[None, :]).astype(jnp.bfloat16)
    owned = dot_rows(onehot, emission)
    owned = owned.astype(jnp.bfloat16).reshape(devices, local_rows, hidden)
    columns = jnp.sum(exchange(owned), axis=0, dtype=jnp.float32)
    unnormal = prior_msg * columns
    forward_msg = (unnormal / jnp.sum(unnormal, axis=1, keepdims=True)).astype(jnp.bfloat16)
    return spread(forward_msg, devices).reshape(devices * local_rows, hidden)


def per_device(
    emission,
    transition,
    beta_start,
    allow_list,
    trans_table,
    last_token,
    prompt_state,
    prior_msg,
    lm_logits,
):
    devices = lax.axis_size("vocab")
    device = lax.axis_index("vocab")
    hidden = emission.shape[0]
    states = beta_start.shape[1]
    own_rows = transition.shape[1]
    prompts = prompt_state.shape[0]
    count = devices.bit_length() - 1
    if devices == 1 << count and count > 2 and own_rows % 128 == 0 and prompts == devices:
        sums, columns, columns_out = first_products(last_token, emission, count)
        route, chooser, messages, sums = tables(
            prompt_state, allow_list, trans_table, beta_start, emission, sums, count
        )
        sums = exchange(sums)
        parts, kept_rows, sent_rows = [messages], (columns,), (columns_out,)
        for window_step in range(STEPS):
            wide = window_step == STEPS - 1
            dtype = jnp.float32 if wide else jnp.bfloat16
            kept, received = step(
                transition, route, sums, parts, dtype, devices, count, kept_rows, sent_rows
            )
            kept_rows, sent_rows, near_extra, far_extra = (), (), (), ()
            if window_step == 1:
                forward = forward_messages_here(prior_msg, parts, devices)
                far_extra = (forward,)
            if window_step == 2:
                near_extra = (forward,)
            parts, extras = reduce_blocks(
                kept, received, wide, devices, count, near_extra, far_extra
            )
            if window_step == 1:
                others = [part[-devices:] for part in parts[1:]]
                forward = jnp.concatenate([forward] + others, axis=0)
        near = jnp.stack(extras).reshape(4, devices // 8, devices, own_rows)
        forward = order_forward(near, swap(near, 1, devices), count)
        messages = last_sum(parts, forward)
        near, far = gather_blocks(messages, devices, count)
        raised, pair = weigh(emission, forward, chooser, lm_logits, near, far, count)
        return messages.T, normalise(raised, pair, devices)
    state_ids = jnp.arange(states, dtype=jnp.int32)
    block_ids = jnp.arange(devices, dtype=jnp.int32)
    allowed = jnp.any(allow_list[:, :, None] == block_ids, axis=1)
    dest_here = lax.dynamic_index_in_dim(trans_table, device, axis=1, keepdims=False)
    allow_here = jnp.any(allow_list == device, axis=1)
    dest_rows = jnp.sum(jnp.where(prompt_state[:, None] == state_ids, dest_here, 0), axis=1)
    allow_rows = jnp.any((prompt_state[:, None] == state_ids) & allow_here, axis=1)
    chooser = (dest_rows[:, None] == state_ids) & allow_rows[:, None]
    messages = lax.dynamic_slice_in_dim(beta_start, device * own_rows, own_rows, 0).T
    forward_all = forward_messages(emission, last_token, prior_msg, devices, device)
    own_sums = exchange(jnp.sum(emission, axis=1, dtype=jnp.float32).reshape(devices, own_rows))
    route = allowed.T[:, :, None] & (trans_table.T[:, :, None] == state_ids)
    route = route.astype(jnp.float32).reshape(devices * states, states)
    by_owner = transition.reshape(devices, own_rows, own_rows)
    for window_step in range(STEPS):
        selected = jnp.dot(route, messages, precision=lax.Precision.HIGHEST)
        selected = selected.reshape(devices, states, own_rows)
        emitted = jnp.sum(selected * own_sums[:, None, :], axis=0)
        halves = jnp.concatenate(split_outside(emitted), axis=0)
        partial = jnp.einsum("dzy,sy->dsz", by_owner, halves, preferred_element_type=jnp.float32)
        partial = partial[:, :states] + partial[:, states:]
        if window_step < STEPS - 1:
            partial = partial.astype(jnp.bfloat16)
        messages = jnp.sum(exchange(partial), axis=0, dtype=jnp.float32)
    everywhere = spread(messages, devices)
    chosen = jnp.einsum(
        "ps,dsz->pdz", chooser.astype(jnp.float32), everywhere, precision=lax.Precision.HIGHEST
    )
    forward_all = forward_all.reshape(prompts, devices, own_rows).astype(jnp.float32)
    scaled = (forward_all * chosen).astype(jnp.bfloat16).reshape(prompts, hidden)
    weights = jnp.dot(scaled, emission, preferred_element_type=jnp.float32)
    weights = jnp.where(allow_rows[:, None], weights, 0.0)
    logits = lm_logits.astype(jnp.float32)
    top_here = jnp.max(logits, axis=1)
    raised = jnp.exp(logits - top_here[:, None]) * weights
    pairs = spread(jnp.stack([top_here, jnp.sum(raised, axis=1)]), devices)
    tops, totals = pairs[:, 0], pairs[:, 1]
    top = jnp.max(tops, axis=0)
    total = jnp.sum(totals * jnp.exp(tops - top), axis=0)
    raised = raised * jnp.exp(top_here - top)[:, None]
    return (messages.T, BLK * devices * raised / total[:, None])


def solution(mesh):
    return jax.shard_map(
        per_device,
        mesh=mesh,
        in_specs=(
            P(None, "vocab"),
            P(None, "vocab"),
            P(),
            P(),
            P(),
            P("parts"),
            P("parts"),
            P(("parts", "vocab"), None),
            P("parts", "vocab"),
        ),
        out_specs=(P(("parts", "vocab"), None), P("parts", "vocab")),
        check_vma=False,
    )
```

```python
import functools

import jax
import jax.numpy as jnp
from jax import lax
from jax.experimental import pallas as pl
from jax.experimental.pallas import tpu as pltpu
from jax.sharding import PartitionSpec as P

BLK = 256
STEPS = 3
LIMIT = 16 * 1024 * 1024
VMEM = pl.BlockSpec(memory_space=pltpu.VMEM)
SMEM = pl.BlockSpec(memory_space=pltpu.SMEM)
ANY = pl.BlockSpec(memory_space=pl.ANY)
PARAMS = pltpu.CompilerParams(vmem_limit_bytes=LIMIT)


def exchange(blocks):
    return lax.all_to_all(blocks, "vocab", split_axis=0, concat_axis=0, tiled=True)


def spread(own, devices):
    return exchange(jnp.broadcast_to(own[None], (devices,) + own.shape))


def basis(count):
    return [1, 3, 4] + [(1 << bit) | 1 for bit in range(3, count)]


def swap(block, offset, devices):
    pairs = [(i, i ^ offset) for i in range(devices)]
    return lax.ppermute(block, "vocab", pairs)


def split_wide(wide):
    high = wide.astype(jnp.bfloat16)
    low = (wide - high.astype(jnp.float32)).astype(jnp.bfloat16)
    return high, low


def split_outside(wide):
    high = lax.reduce_precision(wide, exponent_bits=8, mantissa_bits=7)
    return high.astype(jnp.bfloat16), (wide - high).astype(jnp.bfloat16)


def split_three(wide):
    high = wide.astype(jnp.bfloat16)
    rest = wide - high.astype(jnp.float32)
    middle = rest.astype(jnp.bfloat16)
    low = (rest - middle.astype(jnp.float32)).astype(jnp.bfloat16)
    return high, middle, low


def dot_rows(left, right):
    return lax.dot_general(left, right, (((1,), (1,)), ((), ())), preferred_element_type=jnp.float32)


def partner_of(bits, count):
    partner = 0
    for bit, offset in zip(bits, basis(count)):
        partner ^= bit * offset
    return partner


def all_bits(count):
    return [tuple((k >> (count - 1 - b)) & 1 for b in range(count)) for k in range(1 << count)]


def square_partners(count):
    return [partner_of((0,) + bits, count) for bits in all_bits(2)]


def far_partners(count):
    return [partner_of((0, 0, 0) + bits, count) for bits in all_bits(count - 3)]


def half_places(count, first):
    return [
        ((q, h), first ^ near ^ far)
        for q, near in enumerate(square_partners(count))
        for h, far in enumerate(far_partners(count))
    ]


def partner_rows(i, rows):
    owner = lax.axis_index("vocab") ^ i
    return pl.ds(pl.multiple_of(owner * rows, rows), rows)


def pack(blocks, wide, extra):
    rows = blocks.reshape(-1, blocks.shape[-1])
    parts = split_outside(rows) if wide else (rows.astype(jnp.bfloat16),)
    return jnp.concatenate(parts + extra, axis=0)


def unpack(packed, shape, wide):
    size = shape[0] * shape[1]
    rows = packed[:size].astype(jnp.float32)
    if wide:
        rows += packed[size : 2 * size].astype(jnp.float32)
    return rows.reshape(shape)


def reduce_blocks(kept, received, wide, devices, count, near_extra=(), far_extra=()):
    total = kept + received.astype(jnp.float32)
    near, extras = total[0], list(near_extra)
    for q, offset in enumerate(square_partners(count)):
        if q:
            packed = swap(pack(total[q], wide, near_extra), offset, devices)
            near += unpack(packed, total.shape[1:], wide)
            for extra in near_extra:
                extras.append(packed[-extra.shape[0] :])
    blocks = [near[0]]
    for h, offset in enumerate(far_partners(count)):
        if h:
            blocks.append(swap(pack(near[h], wide, far_extra), offset, devices))
    return blocks, extras


def gather_blocks(own, devices, count):
    far = jnp.stack([own] + [swap(own, offset, devices) for offset in far_partners(count)[1:]])
    near = jnp.stack([far] + [swap(far, offset, devices) for offset in square_partners(count)[1:]])
    return near, swap(near, 1, devices)


def column_of(scalars_ref, shape):
    row = lax.broadcasted_iota(jnp.int32, shape, 0)
    column = jnp.zeros(shape, jnp.int32)
    for k in range(shape[0]):
        column = jnp.where(row == k, scalars_ref[k], column)
    return column


def tables_kernel(
    count, state_ref, allow_ref, table_ref, emission_ref, sums_in_ref,
    route_ref, chooser_ref, sums_ref,
):
    device = lax.axis_index("vocab")
    devices = 1 << count
    states = table_ref.shape[0]
    sums_ref[...] = sums_in_ref[...]
    allow, table = allow_ref[...], table_ref[...]
    hits = [jnp.max((allow == b).astype(jnp.float32), axis=0, keepdims=True) for b in range(devices)]
    shape = (states, states)
    diagonal = [lax.broadcasted_iota(jnp.int32, shape, axis) for axis in (0, 1)]
    diagonal = (diagonal[0] == diagonal[1]).astype(jnp.bfloat16)
    hits = dot_rows(diagonal, jnp.concatenate(hits, axis=0).astype(jnp.bfloat16))
    ids = lax.broadcasted_iota(jnp.int32, shape, 1)
    own_step = jnp.zeros(shape, jnp.float32)
    for b in range(devices):
        step = jnp.where(table[:, b : b + 1] == ids, hits[:, b : b + 1], 0.0)
        own_step = jnp.where(device == b, step, own_step)
        step = step.astype(jnp.bfloat16)
        route_ref[pl.ds(b * states, states)] = jnp.concatenate([step] * 3, axis=1)
    shape = (states, devices)
    prompts = state_ref[...] == lax.broadcasted_iota(jnp.int32, shape, 0)
    chooser = lax.dot_general(
        prompts.astype(jnp.bfloat16),
        own_step.astype(jnp.bfloat16),
        (((0,), (0,)), ((), ())),
        preferred_element_type=jnp.float32,
    ).astype(jnp.bfloat16)
    chooser_ref[...] = jnp.concatenate([chooser] * 3, axis=1)


def tables(state, allow, table, emission, sums, count):
    devices, states = 1 << count, table.shape[0]
    return pl.pallas_call(
        functools.partial(tables_kernel, count),
        out_shape=[
            pltpu.VMEM((devices * states, 3 * states), jnp.bfloat16),
            pltpu.VMEM((devices, 3 * states), jnp.bfloat16),
            jax.ShapeDtypeStruct(sums.shape, sums.dtype),
        ],
        in_specs=[VMEM] * 5,
        out_specs=[VMEM] * 3,
        compiler_params=PARAMS,
        name="tables",
    )(state, allow, table, emission, sums)


def products_kernel(
    count, token_hbm, state_hbm, allow_hbm, table_hbm, start_hbm, emission_ref,
    sums_ref, kept_ref, sent_ref, state_ref, allow_ref, table_ref, messages_ref,
    token_ref, columns_ref, sems,
):
    device = lax.axis_index("vocab")
    devices = 1 << count
    rows = emission_ref.shape[0] >> count
    own = pl.ds(pl.multiple_of(device * rows, rows), rows)
    pairs = [
        (token_hbm, token_ref), (state_hbm, state_ref), (allow_hbm, allow_ref),
        (table_hbm, table_ref), (start_hbm.at[:, own], messages_ref),
    ]
    copies = [
        pltpu.make_async_copy(source, to, sems.at[k]) for k, (source, to) in enumerate(pairs)
    ]
    for copy in copies:
        copy.start()
    shape = (devices * devices // 2, devices * devices)
    to, source = (lax.broadcasted_iota(jnp.int32, shape, axis) for axis in (0, 1))
    same_block = (to & (devices - 1)) == (source >> count)
    orders = []
    for first in range(2):
        prompt = partner_at((to >> count) + first * (devices // 2), count)
        onehot = same_block & ((source & (devices - 1)) == prompt)
        orders.append(onehot.astype(jnp.bfloat16))
    copies[0].wait()
    shape = (devices, BLK)
    tokens = column_of(token_ref, shape) - device * BLK
    onehot = (tokens == lax.broadcasted_iota(jnp.int32, shape, 1)).astype(jnp.bfloat16)
    left = jnp.concatenate([onehot, jnp.ones((16, BLK), jnp.bfloat16)], axis=0)
    for k in range(devices):
        product = dot_rows(left, emission_ref[pl.ds(k * rows, rows)])
        columns_ref[pl.ds(k * devices, devices)] = product[:devices].astype(jnp.bfloat16)
        sums_ref[k] = product[devices : devices + 1]
    for order, out_ref in zip(orders, (kept_ref, sent_ref)):
        ordered = jnp.dot(order, columns_ref[...], preferred_element_type=jnp.float32)
        out_ref[...] = ordered.astype(jnp.bfloat16).reshape(out_ref.shape)
    for copy in copies[1:]:
        copy.wait()


def first_products(last_token, prompt_state, allow_list, trans_table, beta_start, emission, count):
    devices, rows = 1 << count, emission.shape[0] >> count
    half = pltpu.VMEM((4, devices // 8, devices, rows), jnp.bfloat16)
    small = (prompt_state[None], allow_list.T, trans_table)
    operands = (last_token,) + small + (beta_start.T,)
    return pl.pallas_call(
        functools.partial(products_kernel, count),
        out_shape=[jax.ShapeDtypeStruct((devices, 1, rows), jnp.float32), half, half]
        + [pltpu.VMEM(array.shape, array.dtype) for array in small]
        + [pltpu.VMEM((beta_start.shape[1], rows), jnp.float32)],
        in_specs=[ANY] * len(operands) + [VMEM],
        out_specs=[VMEM] * 7,
        scratch_shapes=[
            pltpu.SMEM(last_token.shape, jnp.int32),
            pltpu.VMEM((devices * devices, rows), jnp.bfloat16),
            pltpu.SemaphoreType.DMA((len(operands),)),
        ],
        compiler_params=PARAMS,
        name="first_products",
    )(*(in_hbm(operand) for operand in operands), emission)


def in_hbm(array):
    return pltpu.with_memory_space_constraint(array, pltpu.HBM)


def forward_kernel(prior_ref, *refs):
    blocks, out_ref = refs[:-1], refs[-1]
    devices, rows = out_ref.shape
    columns = blocks[0][-devices:]
    for block in blocks[1:]:
        columns += block[-devices:].astype(jnp.float32)
    prior = jnp.concatenate([prior_ref[:, pl.ds(k * rows, rows)] for k in range(devices)], axis=0)
    unnormal = prior * columns
    out_ref[...] = (unnormal / jnp.sum(unnormal)).astype(jnp.bfloat16)


def forward_messages_here(prior, blocks, devices):
    return pl.pallas_call(
        forward_kernel,
        out_shape=pltpu.VMEM((devices, blocks[0].shape[1]), jnp.bfloat16),
        in_specs=[VMEM] * (1 + len(blocks)),
        out_specs=VMEM,
        compiler_params=PARAMS,
        name="forward_messages",
    )(prior, *blocks)


def partner_at(place, count):
    number = jnp.zeros_like(place)
    for bit, offset in enumerate(basis(count)):
        number = number ^ (((place >> (count - 1 - bit)) & 1) * offset)
    return lax.axis_index("vocab") ^ number


def order_kernel(count, near_ref, far_ref, out_ref):
    size = 1 << count
    shape = (size * size, size * size)
    to, source = (lax.broadcasted_iota(jnp.int32, shape, axis) for axis in (0, 1))
    same_block = partner_at(to >> count, count) == (source & (size - 1))
    same_prompt = (to & (size - 1)) == partner_at(source >> count, count)
    onehot = (same_block & same_prompt).astype(jnp.bfloat16)
    half = size * size // 2
    rows = out_ref.shape[1]
    near = near_ref[...].reshape(half, rows)
    far = far_ref[...].reshape(half, rows)
    ordered = jnp.dot(onehot[:, :half], near, preferred_element_type=jnp.float32)
    ordered += jnp.dot(onehot[:, half:], far, preferred_element_type=jnp.float32)
    out_ref[...] = ordered.astype(jnp.bfloat16)


def order_forward(near, far, count):
    rows = near.shape[-1]
    return pl.pallas_call(
        functools.partial(order_kernel, count),
        out_shape=pltpu.VMEM((1 << (2 * count), rows), jnp.bfloat16),
        in_specs=[VMEM] * 2,
        out_specs=VMEM,
        compiler_params=PARAMS,
        name="order_forward",
    )(near, far)


def last_kernel(*refs):
    blocks, out_ref = refs[:-2], refs[-1]
    states = out_ref.shape[0]
    messages = blocks[0][...]
    for block in blocks[1:]:
        for part in range(2):
            messages += block[pl.ds(part * states, states)].astype(jnp.float32)
    out_ref[...] = messages


def last_sum(blocks, after):
    return pl.pallas_call(
        last_kernel,
        out_shape=pltpu.VMEM(blocks[0].shape, jnp.float32),
        in_specs=[VMEM] * len(blocks) + [ANY],
        out_specs=VMEM,
        compiler_params=PARAMS,
        name="last_messages",
    )(*blocks, after)


def half_products(halves, transition_ref, out_ref, count, first):
    states = halves.shape[0] // 2
    rows = transition_ref.shape[0] >> count
    for place, partner in half_places(count, first):
        product = dot_rows(halves, transition_ref[partner_rows(partner, rows)])
        product = product[:states] + product[states:]
        out_ref[place + (pl.ds(0, states),)] = product.astype(out_ref.dtype)


def add_rows(out_ref, states, extra):
    for ref in extra:
        rows = pl.ds(states, ref.shape[2])
        for place in ((y, k) for y in range(ref.shape[0]) for k in range(ref.shape[1])):
            out_ref[place + (rows,)] = ref[place].astype(out_ref.dtype)


def send_kernel(count, number, transition_ref, route_ref, sums_ref, *refs):
    parts, extra, (halves_ref, out_ref) = refs[:number], refs[number:-2], refs[-2:]
    states = halves_ref.shape[0] // 2
    messages = parts[0][:states].astype(jnp.float32)
    for part in parts[1:]:
        messages += part[:states].astype(jnp.float32)
    selected = jnp.dot(
        route_ref[...],
        jnp.concatenate(split_three(messages), axis=0),
        preferred_element_type=jnp.float32,
    )
    emitted = selected[:states] * sums_ref[0]
    for b in range(1, 1 << count):
        emitted += selected[b * states : (b + 1) * states] * sums_ref[b]
    halves = jnp.concatenate(split_wide(emitted), axis=0)
    halves_ref[...] = halves
    half_products(halves, transition_ref, out_ref, count, 1)
    add_rows(out_ref, states, extra)


def keep_kernel(count, transition_ref, halves_ref, *refs):
    extra, out_ref = refs[:-1], refs[-1]
    half_products(halves_ref[...], transition_ref, out_ref, count, 0)
    add_rows(out_ref, halves_ref.shape[0] // 2, extra)


def step(transition, route, sums, parts, dtype, devices, count, kept_rows=(), sent_rows=()):
    states, rows = route.shape[0] // devices, parts[0].shape[1]
    total = states + sum(block.shape[2] for block in kept_rows)
    shape = (4, devices // 8, total, rows)
    halves, sent = pl.pallas_call(
        functools.partial(send_kernel, count, len(parts)),
        out_shape=[
            pltpu.VMEM((2 * states, rows), jnp.bfloat16),
            pltpu.VMEM(shape, dtype),
        ],
        in_specs=[VMEM] * (3 + len(parts) + len(sent_rows)),
        out_specs=[VMEM] * 2,
        compiler_params=PARAMS,
        name="step_sent_half",
    )(transition, route, sums, *parts, *sent_rows)
    received = swap(sent, 1, devices)
    kept = pl.pallas_call(
        functools.partial(keep_kernel, count),
        out_shape=pltpu.VMEM(shape, jnp.float32),
        in_specs=[VMEM] * (2 + len(kept_rows)),
        out_specs=VMEM,
        compiler_params=PARAMS,
        name="step_kept_half",
    )(transition, halves, *kept_rows)
    return kept, received


def weigh_half(emission_ref, forward_ref, chooser, parts_ref, count, first):
    rows = emission_ref.shape[0] >> count
    prompts = chooser.shape[0]
    weights = jnp.zeros((prompts, emission_ref.shape[1]), jnp.float32)
    for order, (place, partner) in enumerate(half_places(count, first)):
        pieces = jnp.concatenate(split_three(parts_ref[place]), axis=0)
        chosen = jnp.dot(chooser, pieces, preferred_element_type=jnp.float32)
        block = order + (first << (count - 1))
        forward = forward_ref[pl.ds(block * prompts, prompts)].astype(jnp.float32)
        scaled = (forward * chosen).astype(jnp.bfloat16)
        tile = emission_ref[partner_rows(partner, rows)]
        weights += jnp.dot(scaled, tile, preferred_element_type=jnp.float32)
    return weights


def near_kernel(count, emission_ref, forward_ref, chooser_ref, parts_ref, out_ref):
    out_ref[...] = weigh_half(emission_ref, forward_ref, chooser_ref[...], parts_ref, count, 0)


def far_kernel(count, emission_ref, forward_ref, chooser_ref, logits_ref, near_ref, parts_ref, raised_ref, pair_ref):
    chooser = chooser_ref[...]
    logits = logits_ref[...].astype(jnp.float32)
    top = jnp.max(logits, axis=1, keepdims=True)
    weights = near_ref[...] + weigh_half(emission_ref, forward_ref, chooser, parts_ref, count, 1)
    allowed = jnp.sum(chooser.astype(jnp.float32), axis=1, keepdims=True) > 0
    raised = jnp.where(allowed, jnp.exp(logits - top) * weights, 0.0)
    raised_ref[...] = raised
    total = jnp.sum(raised, axis=1, keepdims=True)
    lane = lax.broadcasted_iota(jnp.int32, pair_ref.shape, 1)
    pair_ref[...] = jnp.where(lane == 0, top, total)


def weigh(emission, forward, chooser, logits, near, far, count):
    half = pl.pallas_call(
        functools.partial(near_kernel, count),
        out_shape=pltpu.VMEM(logits.shape, jnp.float32),
        in_specs=[VMEM] * 4,
        out_specs=VMEM,
        compiler_params=PARAMS,
        name="weigh_near",
    )(emission, forward, chooser, near)
    return pl.pallas_call(
        functools.partial(far_kernel, count),
        out_shape=[
            pltpu.VMEM(logits.shape, jnp.float32),
            pltpu.VMEM((logits.shape[0], 128), jnp.float32),
        ],
        in_specs=[VMEM] * 6,
        out_specs=[VMEM] * 2,
        compiler_params=PARAMS,
        name="weigh_far",
    )(emission, forward, chooser, logits, half, far)


def normalise(raised, pair, devices):
    pairs = spread(pair[:, :2].T, devices)
    own_top = pair[:, :1]
    tops, totals = pairs[:, 0], pairs[:, 1]
    top = jnp.max(tops, axis=0)
    total = jnp.sum(totals * jnp.exp(tops - top), axis=0)
    return BLK * devices * (raised * jnp.exp(own_top - top[:, None])) / total[:, None]


def forward_messages(emission, last_token, prior_msg, devices, device):
    hidden = emission.shape[0]
    local_rows = prior_msg.shape[0]
    token_ids = jnp.arange(BLK, dtype=jnp.int32)
    tokens = last_token - device * BLK
    onehot = (tokens[:, None] == token_ids[None, :]).astype(jnp.bfloat16)
    owned = dot_rows(onehot, emission)
    owned = owned.astype(jnp.bfloat16).reshape(devices, local_rows, hidden)
    columns = jnp.sum(exchange(owned), axis=0, dtype=jnp.float32)
    unnormal = prior_msg * columns
    forward_msg = (unnormal / jnp.sum(unnormal, axis=1, keepdims=True)).astype(jnp.bfloat16)
    return spread(forward_msg, devices).reshape(devices * local_rows, hidden)


def per_device(
    emission,
    transition,
    beta_start,
    allow_list,
    trans_table,
    last_token,
    prompt_state,
    prior_msg,
    lm_logits,
):
    devices = lax.axis_size("vocab")
    device = lax.axis_index("vocab")
    hidden = emission.shape[0]
    states = beta_start.shape[1]
    own_rows = transition.shape[1]
    prompts = prompt_state.shape[0]
    count = devices.bit_length() - 1
    if devices == 1 << count and count > 2 and own_rows % 128 == 0 and prompts == devices:
        sums, columns, columns_out, state, allow, table, messages = first_products(
            last_token, prompt_state, allow_list, trans_table, beta_start, emission, count
        )
        route, chooser, sums = tables(state, allow, table, emission, sums, count)
        sums = exchange(sums)
        parts, kept_rows, sent_rows = [messages], (columns,), (columns_out,)
        for window_step in range(STEPS):
            wide = window_step == STEPS - 1
            dtype = jnp.float32 if wide else jnp.bfloat16
            kept, received = step(
                transition, route, sums, parts, dtype, devices, count, kept_rows, sent_rows
            )
            kept_rows, sent_rows, near_extra, far_extra = (), (), (), ()
            if window_step == 1:
                forward = forward_messages_here(prior_msg, parts, devices)
                far_extra = (forward,)
            if window_step == 2:
                near_extra = (forward,)
            parts, extras = reduce_blocks(
                kept, received, wide, devices, count, near_extra, far_extra
            )
            if window_step == 1:
                others = [part[-devices:] for part in parts[1:]]
                forward = jnp.concatenate([forward] + others, axis=0)
        near = jnp.stack(extras).reshape(4, devices // 8, devices, own_rows)
        forward = order_forward(near, swap(near, 1, devices), count)
        messages = last_sum(parts, forward)
        near, far = gather_blocks(messages, devices, count)
        raised, pair = weigh(emission, forward, chooser, lm_logits, near, far, count)
        return messages.T, normalise(raised, pair, devices)
    state_ids = jnp.arange(states, dtype=jnp.int32)
    block_ids = jnp.arange(devices, dtype=jnp.int32)
    allowed = jnp.any(allow_list[:, :, None] == block_ids, axis=1)
    dest_here = lax.dynamic_index_in_dim(trans_table, device, axis=1, keepdims=False)
    allow_here = jnp.any(allow_list == device, axis=1)
    dest_rows = jnp.sum(jnp.where(prompt_state[:, None] == state_ids, dest_here, 0), axis=1)
    allow_rows = jnp.any((prompt_state[:, None] == state_ids) & allow_here, axis=1)
    chooser = (dest_rows[:, None] == state_ids) & allow_rows[:, None]
    messages = lax.dynamic_slice_in_dim(beta_start, device * own_rows, own_rows, 0).T
    forward_all = forward_messages(emission, last_token, prior_msg, devices, device)
    own_sums = exchange(jnp.sum(emission, axis=1, dtype=jnp.float32).reshape(devices, own_rows))
    route = allowed.T[:, :, None] & (trans_table.T[:, :, None] == state_ids)
    route = route.astype(jnp.float32).reshape(devices * states, states)
    by_owner = transition.reshape(devices, own_rows, own_rows)
    for window_step in range(STEPS):
        selected = jnp.dot(route, messages, precision=lax.Precision.HIGHEST)
        selected = selected.reshape(devices, states, own_rows)
        emitted = jnp.sum(selected * own_sums[:, None, :], axis=0)
        halves = jnp.concatenate(split_outside(emitted), axis=0)
        partial = jnp.einsum("dzy,sy->dsz", by_owner, halves, preferred_element_type=jnp.float32)
        partial = partial[:, :states] + partial[:, states:]
        if window_step < STEPS - 1:
            partial = partial.astype(jnp.bfloat16)
        messages = jnp.sum(exchange(partial), axis=0, dtype=jnp.float32)
    everywhere = spread(messages, devices)
    chosen = jnp.einsum(
        "ps,dsz->pdz", chooser.astype(jnp.float32), everywhere, precision=lax.Precision.HIGHEST
    )
    forward_all = forward_all.reshape(prompts, devices, own_rows).astype(jnp.float32)
    scaled = (forward_all * chosen).astype(jnp.bfloat16).reshape(prompts, hidden)
    weights = jnp.dot(scaled, emission, preferred_element_type=jnp.float32)
    weights = jnp.where(allow_rows[:, None], weights, 0.0)
    logits = lm_logits.astype(jnp.float32)
    top_here = jnp.max(logits, axis=1)
    raised = jnp.exp(logits - top_here[:, None]) * weights
    pairs = spread(jnp.stack([top_here, jnp.sum(raised, axis=1)]), devices)
    tops, totals = pairs[:, 0], pairs[:, 1]
    top = jnp.max(tops, axis=0)
    total = jnp.sum(totals * jnp.exp(tops - top), axis=0)
    raised = raised * jnp.exp(top_here - top)[:, None]
    return (messages.T, BLK * devices * raised / total[:, None])


def solution(mesh):
    return jax.shard_map(
        per_device,
        mesh=mesh,
        in_specs=(
            P(None, "vocab"),
            P(None, "vocab"),
            P(),
            P(),
            P(),
            P("parts"),
            P("parts"),
            P(("parts", "vocab"), None),
            P("parts", "vocab"),
        ),
        out_specs=(P(("parts", "vocab"), None), P("parts", "vocab")),
        check_vma=False,
    )
```

```python
import functools

import jax
import jax.numpy as jnp
from jax import lax
from jax.experimental import pallas as pl
from jax.experimental.pallas import tpu as pltpu
from jax.sharding import PartitionSpec as P

BLK = 256
STEPS = 3
LIMIT = 16 * 1024 * 1024
VMEM = pl.BlockSpec(memory_space=pltpu.VMEM)
SMEM = pl.BlockSpec(memory_space=pltpu.SMEM)
ANY = pl.BlockSpec(memory_space=pl.ANY)
PARAMS = pltpu.CompilerParams(vmem_limit_bytes=LIMIT)


def exchange(blocks):
    return lax.all_to_all(blocks, "vocab", split_axis=0, concat_axis=0, tiled=True)


def spread(own, devices):
    return exchange(jnp.broadcast_to(own[None], (devices,) + own.shape))


def basis(count):
    return [1, 3, 4] + [(1 << bit) | 1 for bit in range(3, count)]


def swap(block, offset, devices):
    pairs = [(i, i ^ offset) for i in range(devices)]
    return lax.ppermute(block, "vocab", pairs)


def split_wide(wide):
    high = wide.astype(jnp.bfloat16)
    low = (wide - high.astype(jnp.float32)).astype(jnp.bfloat16)
    return high, low


def split_outside(wide):
    high = lax.reduce_precision(wide, exponent_bits=8, mantissa_bits=7)
    return high.astype(jnp.bfloat16), (wide - high).astype(jnp.bfloat16)


def split_three(wide):
    high = wide.astype(jnp.bfloat16)
    rest = wide - high.astype(jnp.float32)
    middle = rest.astype(jnp.bfloat16)
    low = (rest - middle.astype(jnp.float32)).astype(jnp.bfloat16)
    return high, middle, low


def dot_rows(left, right):
    return lax.dot_general(left, right, (((1,), (1,)), ((), ())), preferred_element_type=jnp.float32)


def partner_of(bits, count):
    partner = 0
    for bit, offset in zip(bits, basis(count)):
        partner ^= bit * offset
    return partner


def all_bits(count):
    return [tuple((k >> (count - 1 - b)) & 1 for b in range(count)) for k in range(1 << count)]


def square_partners(count):
    return [partner_of((0,) + bits, count) for bits in all_bits(2)]


def far_partners(count):
    return [partner_of((0, 0, 0) + bits, count) for bits in all_bits(count - 3)]


def half_places(count, first, squares=range(4)):
    near = square_partners(count)
    return [
        ((q, h), first ^ near[q] ^ far)
        for q in squares
        for h, far in enumerate(far_partners(count))
    ]


def partner_rows(i, rows):
    owner = lax.axis_index("vocab") ^ i
    return pl.ds(pl.multiple_of(owner * rows, rows), rows)


def pack(blocks, wide, extra):
    rows = blocks.reshape(-1, blocks.shape[-1])
    parts = split_outside(rows) if wide else (rows.astype(jnp.bfloat16),)
    return jnp.concatenate(parts + extra, axis=0)


def unpack(packed, shape, wide):
    size = shape[0] * shape[1]
    rows = packed[:size].astype(jnp.float32)
    if wide:
        rows += packed[size : 2 * size].astype(jnp.float32)
    return rows.reshape(shape)


def reduce_blocks(leaving, staying, wide, devices, count, near_extra=(), far_extra=()):
    extras, arrived = list(near_extra), []
    for q, offset in enumerate(square_partners(count)[1:]):
        packed = swap(pack(leaving[q], wide, near_extra), offset, devices)
        arrived.append(unpack(packed, leaving.shape[1:], wide))
        first = packed
        for extra in near_extra:
            extras.append(packed[-extra.shape[0] :])
    near = functools.reduce(jnp.add, arrived, staying(first))
    blocks = [near[0]]
    for h, offset in enumerate(far_partners(count)):
        if h:
            blocks.append(swap(pack(near[h], wide, far_extra), offset, devices))
    return blocks, extras


def gather_blocks(own, devices, count):
    far = jnp.stack([own] + [swap(own, offset, devices) for offset in far_partners(count)[1:]])
    near = jnp.stack([far] + [swap(far, offset, devices) for offset in square_partners(count)[1:]])
    return near, swap(near, 1, devices)


def column_of(scalars_ref, shape):
    row = lax.broadcasted_iota(jnp.int32, shape, 0)
    column = jnp.zeros(shape, jnp.int32)
    for k in range(shape[0]):
        column = jnp.where(row == k, scalars_ref[k], column)
    return column


def tables_kernel(
    count, state_ref, allow_ref, table_ref, emission_ref, sums_in_ref,
    route_ref, chooser_ref, sums_ref,
):
    device = lax.axis_index("vocab")
    devices = 1 << count
    states = table_ref.shape[0]
    sums_ref[...] = sums_in_ref[...]
    allow, table = allow_ref[...], table_ref[...]
    hits = [jnp.max((allow == b).astype(jnp.float32), axis=0, keepdims=True) for b in range(devices)]
    shape = (states, states)
    diagonal = [lax.broadcasted_iota(jnp.int32, shape, axis) for axis in (0, 1)]
    diagonal = (diagonal[0] == diagonal[1]).astype(jnp.bfloat16)
    hits = dot_rows(diagonal, jnp.concatenate(hits, axis=0).astype(jnp.bfloat16))
    ids = lax.broadcasted_iota(jnp.int32, shape, 1)
    own_step = jnp.zeros(shape, jnp.float32)
    for b in range(devices):
        step = jnp.where(table[:, b : b + 1] == ids, hits[:, b : b + 1], 0.0)
        own_step = jnp.where(device == b, step, own_step)
        step = step.astype(jnp.bfloat16)
        route_ref[pl.ds(b * states, states)] = jnp.concatenate([step] * 3, axis=1)
    shape = (states, devices)
    prompts = state_ref[...] == lax.broadcasted_iota(jnp.int32, shape, 0)
    chooser = lax.dot_general(
        prompts.astype(jnp.bfloat16),
        own_step.astype(jnp.bfloat16),
        (((0,), (0,)), ((), ())),
        preferred_element_type=jnp.float32,
    ).astype(jnp.bfloat16)
    chooser_ref[...] = jnp.concatenate([chooser] * 3, axis=1)


def tables(state, allow, table, emission, sums, count):
    devices, states = 1 << count, table.shape[0]
    return pl.pallas_call(
        functools.partial(tables_kernel, count),
        out_shape=[
            pltpu.VMEM((devices * states, 3 * states), jnp.bfloat16),
            pltpu.VMEM((devices, 3 * states), jnp.bfloat16),
            jax.ShapeDtypeStruct(sums.shape, sums.dtype),
        ],
        in_specs=[VMEM] * 5,
        out_specs=[VMEM] * 3,
        compiler_params=PARAMS,
        name="tables",
    )(state, allow, table, emission, sums)


def products_kernel(
    count, token_hbm, state_hbm, allow_hbm, table_hbm, start_hbm, emission_ref,
    sums_ref, kept_ref, sent_ref, state_ref, allow_ref, table_ref, messages_ref,
    token_ref, columns_ref, sems,
):
    device = lax.axis_index("vocab")
    devices = 1 << count
    rows = emission_ref.shape[0] >> count
    own = pl.ds(pl.multiple_of(device * rows, rows), rows)
    pairs = [
        (token_hbm, token_ref), (state_hbm, state_ref), (allow_hbm, allow_ref),
        (table_hbm, table_ref), (start_hbm.at[:, own], messages_ref),
    ]
    copies = [
        pltpu.make_async_copy(source, to, sems.at[k]) for k, (source, to) in enumerate(pairs)
    ]
    for copy in copies:
        copy.start()
    shape = (devices * devices // 2, devices * devices)
    to, source = (lax.broadcasted_iota(jnp.int32, shape, axis) for axis in (0, 1))
    same_block = (to & (devices - 1)) == (source >> count)
    orders = []
    for first in range(2):
        prompt = partner_at((to >> count) + first * (devices // 2), count)
        onehot = same_block & ((source & (devices - 1)) == prompt)
        orders.append(onehot.astype(jnp.bfloat16))
    copies[0].wait()
    shape = (devices, BLK)
    tokens = column_of(token_ref, shape) - device * BLK
    onehot = (tokens == lax.broadcasted_iota(jnp.int32, shape, 1)).astype(jnp.bfloat16)
    left = jnp.concatenate([onehot, jnp.ones((16, BLK), jnp.bfloat16)], axis=0)
    for k in range(devices):
        product = dot_rows(left, emission_ref[pl.ds(k * rows, rows)])
        columns_ref[pl.ds(k * devices, devices)] = product[:devices].astype(jnp.bfloat16)
        sums_ref[k] = product[devices : devices + 1]
    for order, out_ref in zip(orders, (kept_ref, sent_ref)):
        ordered = jnp.dot(order, columns_ref[...], preferred_element_type=jnp.float32)
        out_ref[...] = ordered.astype(jnp.bfloat16).reshape(out_ref.shape)
    for copy in copies[1:]:
        copy.wait()


def first_products(last_token, prompt_state, allow_list, trans_table, beta_start, emission, count):
    devices, rows = 1 << count, emission.shape[0] >> count
    half = pltpu.VMEM((4, devices // 8, devices, rows), jnp.bfloat16)
    small = (prompt_state[None], allow_list.T, trans_table)
    operands = (last_token,) + small + (beta_start.T,)
    return pl.pallas_call(
        functools.partial(products_kernel, count),
        out_shape=[jax.ShapeDtypeStruct((devices, 1, rows), jnp.float32), half, half]
        + [pltpu.VMEM(array.shape, array.dtype) for array in small]
        + [pltpu.VMEM((beta_start.shape[1], rows), jnp.float32)],
        in_specs=[ANY] * len(operands) + [VMEM],
        out_specs=[VMEM] * 7,
        scratch_shapes=[
            pltpu.SMEM(last_token.shape, jnp.int32),
            pltpu.VMEM((devices * devices, rows), jnp.bfloat16),
            pltpu.SemaphoreType.DMA((len(operands),)),
        ],
        compiler_params=PARAMS,
        name="first_products",
    )(*(in_hbm(operand) for operand in operands), emission)


def in_hbm(array):
    return pltpu.with_memory_space_constraint(array, pltpu.HBM)


def forward_kernel(prior_ref, *refs):
    blocks, out_ref = refs[:-1], refs[-1]
    devices, rows = out_ref.shape
    columns = blocks[0][-devices:]
    for block in blocks[1:]:
        columns += block[-devices:].astype(jnp.float32)
    prior = jnp.concatenate([prior_ref[:, pl.ds(k * rows, rows)] for k in range(devices)], axis=0)
    unnormal = prior * columns
    out_ref[...] = (unnormal / jnp.sum(unnormal)).astype(jnp.bfloat16)


def forward_messages_here(prior, blocks, devices):
    return pl.pallas_call(
        forward_kernel,
        out_shape=pltpu.VMEM((devices, blocks[0].shape[1]), jnp.bfloat16),
        in_specs=[VMEM] * (1 + len(blocks)),
        out_specs=VMEM,
        compiler_params=PARAMS,
        name="forward_messages",
    )(prior, *blocks)


def partner_at(place, count):
    number = jnp.zeros_like(place)
    for bit, offset in enumerate(basis(count)):
        number = number ^ (((place >> (count - 1 - bit)) & 1) * offset)
    return lax.axis_index("vocab") ^ number


def order_kernel(count, near_ref, far_ref, out_ref):
    size = 1 << count
    shape = (size * size, size * size)
    to, source = (lax.broadcasted_iota(jnp.int32, shape, axis) for axis in (0, 1))
    same_block = partner_at(to >> count, count) == (source & (size - 1))
    same_prompt = (to & (size - 1)) == partner_at(source >> count, count)
    onehot = (same_block & same_prompt).astype(jnp.bfloat16)
    half = size * size // 2
    rows = out_ref.shape[1]
    near = near_ref[...].reshape(half, rows)
    far = far_ref[...].reshape(half, rows)
    ordered = jnp.dot(onehot[:, :half], near, preferred_element_type=jnp.float32)
    ordered += jnp.dot(onehot[:, half:], far, preferred_element_type=jnp.float32)
    out_ref[...] = ordered.astype(jnp.bfloat16)


def order_forward(near, far, count):
    rows = near.shape[-1]
    return pl.pallas_call(
        functools.partial(order_kernel, count),
        out_shape=pltpu.VMEM((1 << (2 * count), rows), jnp.bfloat16),
        in_specs=[VMEM] * 2,
        out_specs=VMEM,
        compiler_params=PARAMS,
        name="order_forward",
    )(near, far)


def last_kernel(*refs):
    blocks, out_ref = refs[:-2], refs[-1]
    states = out_ref.shape[0]
    messages = blocks[0][...]
    for block in blocks[1:]:
        for part in range(2):
            messages += block[pl.ds(part * states, states)].astype(jnp.float32)
    out_ref[...] = messages


def last_sum(blocks, after):
    return pl.pallas_call(
        last_kernel,
        out_shape=pltpu.VMEM(blocks[0].shape, jnp.float32),
        in_specs=[VMEM] * len(blocks) + [ANY],
        out_specs=VMEM,
        compiler_params=PARAMS,
        name="last_messages",
    )(*blocks, after)


def half_products(halves, transition_ref, out_ref, extra, count, first, squares):
    states = halves.shape[0] // 2
    rows = transition_ref.shape[0] >> count
    for (q, h), partner in half_places(count, first, squares):
        product = dot_rows(halves, transition_ref[partner_rows(partner, rows)])
        product = product[:states] + product[states:]
        place = (q - squares[0], h)
        out_ref[place + (pl.ds(0, states),)] = product.astype(out_ref.dtype)
        for ref in extra:
            rows_after = pl.ds(states, ref.shape[2])
            out_ref[place + (rows_after,)] = ref[q, h].astype(out_ref.dtype)


def send_kernel(count, number, further, squares, transition_ref, route_ref, sums_ref, *refs):
    parts, extra = refs[:number], refs[number : number + further]
    halves_ref, out_ref = refs[number + further :]
    states = halves_ref.shape[0] // 2
    messages = parts[0][:states].astype(jnp.float32)
    for part in parts[1:]:
        messages += part[:states].astype(jnp.float32)
    selected = jnp.dot(
        route_ref[...],
        jnp.concatenate(split_three(messages), axis=0),
        preferred_element_type=jnp.float32,
    )
    emitted = selected[:states] * sums_ref[0]
    for b in range(1, 1 << count):
        emitted += selected[b * states : (b + 1) * states] * sums_ref[b]
    halves = jnp.concatenate(split_wide(emitted), axis=0)
    halves_ref[...] = halves
    half_products(halves, transition_ref, out_ref, extra, count, 1, squares)


def more_kernel(count, first, further, squares, transition_ref, halves_ref, *refs):
    extra, out_ref = refs[:further], refs[-1]
    half_products(halves_ref[...], transition_ref, out_ref, extra, count, first, squares)


def more_products(transition, halves, extra, after, dtype, count, first, squares):
    states, rows = halves.shape[0] // 2, halves.shape[1]
    total = states + sum(block.shape[2] for block in extra)
    shape = (len(squares), 1 << (count - 3), total, rows)
    return pl.pallas_call(
        functools.partial(more_kernel, count, first, len(extra), squares),
        out_shape=pltpu.VMEM(shape, dtype),
        in_specs=[VMEM] * (2 + len(extra)) + [ANY] * len(after),
        out_specs=VMEM,
        compiler_params=PARAMS,
        name="step_sent_half" if first else "step_kept_half",
    )(transition, halves, *extra, *after)


def step(transition, route, sums, parts, dtype, devices, count, kept_rows, sent_rows):
    states, rows = route.shape[0] // devices, parts[0].shape[1]
    total = states + sum(block.shape[2] for block in kept_rows)
    halves, sent = pl.pallas_call(
        functools.partial(send_kernel, count, len(parts), len(sent_rows), range(4)),
        out_shape=[
            pltpu.VMEM((2 * states, rows), jnp.bfloat16),
            pltpu.VMEM((4, devices // 8, total, rows), dtype),
        ],
        in_specs=[VMEM] * (3 + len(parts) + len(sent_rows)),
        out_specs=[VMEM] * 2,
        compiler_params=PARAMS,
        name="step_sent_half",
    )(transition, route, sums, *parts, *sent_rows)
    received = swap(sent, 1, devices)
    kept = more_products(transition, halves, kept_rows, (), jnp.float32, count, 0, range(1, 4))

    def staying(after):
        kept = more_products(transition, halves, kept_rows, (after,), jnp.float32, count, 0, range(1))
        return kept[0] + received[0].astype(jnp.float32)

    return kept + received[1:].astype(jnp.float32), staying


def weigh_half(emission_ref, forward_ref, chooser, parts_ref, count, first):
    rows = emission_ref.shape[0] >> count
    prompts = chooser.shape[0]
    weights = jnp.zeros((prompts, emission_ref.shape[1]), jnp.float32)
    for order, (place, partner) in enumerate(half_places(count, first)):
        pieces = jnp.concatenate(split_three(parts_ref[place]), axis=0)
        chosen = jnp.dot(chooser, pieces, preferred_element_type=jnp.float32)
        block = order + (first << (count - 1))
        forward = forward_ref[pl.ds(block * prompts, prompts)].astype(jnp.float32)
        scaled = (forward * chosen).astype(jnp.bfloat16)
        tile = emission_ref[partner_rows(partner, rows)]
        weights += jnp.dot(scaled, tile, preferred_element_type=jnp.float32)
    return weights


def near_kernel(count, emission_ref, forward_ref, chooser_ref, parts_ref, out_ref):
    out_ref[...] = weigh_half(emission_ref, forward_ref, chooser_ref[...], parts_ref, count, 0)


def far_kernel(count, emission_ref, forward_ref, chooser_ref, logits_ref, near_ref, parts_ref, raised_ref, pair_ref):
    chooser = chooser_ref[...]
    logits = logits_ref[...].astype(jnp.float32)
    top = jnp.max(logits, axis=1, keepdims=True)
    weights = near_ref[...] + weigh_half(emission_ref, forward_ref, chooser, parts_ref, count, 1)
    allowed = jnp.sum(chooser.astype(jnp.float32), axis=1, keepdims=True) > 0
    raised = jnp.where(allowed, jnp.exp(logits - top) * weights, 0.0)
    raised_ref[...] = raised
    total = jnp.sum(raised, axis=1, keepdims=True)
    lane = lax.broadcasted_iota(jnp.int32, pair_ref.shape, 1)
    pair_ref[...] = jnp.where(lane == 0, top, total)


def weigh(emission, forward, chooser, logits, near, far, count):
    half = pl.pallas_call(
        functools.partial(near_kernel, count),
        out_shape=pltpu.VMEM(logits.shape, jnp.float32),
        in_specs=[VMEM] * 4,
        out_specs=VMEM,
        compiler_params=PARAMS,
        name="weigh_near",
    )(emission, forward, chooser, near)
    return pl.pallas_call(
        functools.partial(far_kernel, count),
        out_shape=[
            pltpu.VMEM(logits.shape, jnp.float32),
            pltpu.VMEM((logits.shape[0], 128), jnp.float32),
        ],
        in_specs=[VMEM] * 6,
        out_specs=[VMEM] * 2,
        compiler_params=PARAMS,
        name="weigh_far",
    )(emission, forward, chooser, logits, half, far)


def normalise(raised, pair, devices):
    pairs = spread(pair[:, :2].T, devices)
    own_top = pair[:, :1]
    tops, totals = pairs[:, 0], pairs[:, 1]
    top = jnp.max(tops, axis=0)
    total = jnp.sum(totals * jnp.exp(tops - top), axis=0)
    return BLK * devices * (raised * jnp.exp(own_top - top[:, None])) / total[:, None]


def forward_messages(emission, last_token, prior_msg, devices, device):
    hidden = emission.shape[0]
    local_rows = prior_msg.shape[0]
    token_ids = jnp.arange(BLK, dtype=jnp.int32)
    tokens = last_token - device * BLK
    onehot = (tokens[:, None] == token_ids[None, :]).astype(jnp.bfloat16)
    owned = dot_rows(onehot, emission)
    owned = owned.astype(jnp.bfloat16).reshape(devices, local_rows, hidden)
    columns = jnp.sum(exchange(owned), axis=0, dtype=jnp.float32)
    unnormal = prior_msg * columns
    forward_msg = (unnormal / jnp.sum(unnormal, axis=1, keepdims=True)).astype(jnp.bfloat16)
    return spread(forward_msg, devices).reshape(devices * local_rows, hidden)


def per_device(
    emission,
    transition,
    beta_start,
    allow_list,
    trans_table,
    last_token,
    prompt_state,
    prior_msg,
    lm_logits,
):
    devices = lax.axis_size("vocab")
    device = lax.axis_index("vocab")
    hidden = emission.shape[0]
    states = beta_start.shape[1]
    own_rows = transition.shape[1]
    prompts = prompt_state.shape[0]
    count = devices.bit_length() - 1
    if devices == 1 << count and count > 2 and own_rows % 128 == 0 and prompts == devices:
        sums, columns, columns_out, state, allow, table, messages = first_products(
            last_token, prompt_state, allow_list, trans_table, beta_start, emission, count
        )
        route, chooser, sums = tables(state, allow, table, emission, sums, count)
        sums = exchange(sums)
        parts, kept_rows, sent_rows = [messages], (columns,), (columns_out,)
        for window_step in range(STEPS):
            wide = window_step == STEPS - 1
            dtype = jnp.float32 if wide else jnp.bfloat16
            leaving, staying = step(
                transition, route, sums, parts, dtype, devices, count, kept_rows, sent_rows
            )
            kept_rows, sent_rows, near_extra, far_extra = (), (), (), ()
            if window_step == 1:
                forward = forward_messages_here(prior_msg, parts, devices)
                far_extra = (forward,)
            if window_step == 2:
                near_extra = (forward,)
            parts, extras = reduce_blocks(
                leaving, staying, wide, devices, count, near_extra, far_extra
            )
            if window_step == 1:
                others = [part[-devices:] for part in parts[1:]]
                forward = jnp.concatenate([forward] + others, axis=0)
        near = jnp.stack(extras).reshape(4, devices // 8, devices, own_rows)
        forward = order_forward(near, swap(near, 1, devices), count)
        messages = last_sum(parts, forward)
        near, far = gather_blocks(messages, devices, count)
        raised, pair = weigh(emission, forward, chooser, lm_logits, near, far, count)
        return messages.T, normalise(raised, pair, devices)
    state_ids = jnp.arange(states, dtype=jnp.int32)
    block_ids = jnp.arange(devices, dtype=jnp.int32)
    allowed = jnp.any(allow_list[:, :, None] == block_ids, axis=1)
    dest_here = lax.dynamic_index_in_dim(trans_table, device, axis=1, keepdims=False)
    allow_here = jnp.any(allow_list == device, axis=1)
    dest_rows = jnp.sum(jnp.where(prompt_state[:, None] == state_ids, dest_here, 0), axis=1)
    allow_rows = jnp.any((prompt_state[:, None] == state_ids) & allow_here, axis=1)
    chooser = (dest_rows[:, None] == state_ids) & allow_rows[:, None]
    messages = lax.dynamic_slice_in_dim(beta_start, device * own_rows, own_rows, 0).T
    forward_all = forward_messages(emission, last_token, prior_msg, devices, device)
    own_sums = exchange(jnp.sum(emission, axis=1, dtype=jnp.float32).reshape(devices, own_rows))
    route = allowed.T[:, :, None] & (trans_table.T[:, :, None] == state_ids)
    route = route.astype(jnp.float32).reshape(devices * states, states)
    by_owner = transition.reshape(devices, own_rows, own_rows)
    for window_step in range(STEPS):
        selected = jnp.dot(route, messages, precision=lax.Precision.HIGHEST)
        selected = selected.reshape(devices, states, own_rows)
        emitted = jnp.sum(selected * own_sums[:, None, :], axis=0)
        halves = jnp.concatenate(split_outside(emitted), axis=0)
        partial = jnp.einsum("dzy,sy->dsz", by_owner, halves, preferred_element_type=jnp.float32)
        partial = partial[:, :states] + partial[:, states:]
        if window_step < STEPS - 1:
            partial = partial.astype(jnp.bfloat16)
        messages = jnp.sum(exchange(partial), axis=0, dtype=jnp.float32)
    everywhere = spread(messages, devices)
    chosen = jnp.einsum(
        "ps,dsz->pdz", chooser.astype(jnp.float32), everywhere, precision=lax.Precision.HIGHEST
    )
    forward_all = forward_all.reshape(prompts, devices, own_rows).astype(jnp.float32)
    scaled = (forward_all * chosen).astype(jnp.bfloat16).reshape(prompts, hidden)
    weights = jnp.dot(scaled, emission, preferred_element_type=jnp.float32)
    weights = jnp.where(allow_rows[:, None], weights, 0.0)
    logits = lm_logits.astype(jnp.float32)
    top_here = jnp.max(logits, axis=1)
    raised = jnp.exp(logits - top_here[:, None]) * weights
    pairs = spread(jnp.stack([top_here, jnp.sum(raised, axis=1)]), devices)
    tops, totals = pairs[:, 0], pairs[:, 1]
    top = jnp.max(tops, axis=0)
    total = jnp.sum(totals * jnp.exp(tops - top), axis=0)
    raised = raised * jnp.exp(top_here - top)[:, None]
    return (messages.T, BLK * devices * raised / total[:, None])


def solution(mesh):
    return jax.shard_map(
        per_device,
        mesh=mesh,
        in_specs=(
            P(None, "vocab"),
            P(None, "vocab"),
            P(),
            P(),
            P(),
            P("parts"),
            P("parts"),
            P(("parts", "vocab"), None),
            P("parts", "vocab"),
        ),
        out_specs=(P(("parts", "vocab"), None), P("parts", "vocab")),
        check_vma=False,
    )
```

```python
import functools

import jax
import jax.numpy as jnp
from jax import lax
from jax.experimental import pallas as pl
from jax.experimental.pallas import tpu as pltpu
from jax.sharding import PartitionSpec as P

BLK = 256
STEPS = 3
LIMIT = 16 * 1024 * 1024
VMEM = pl.BlockSpec(memory_space=pltpu.VMEM)
SMEM = pl.BlockSpec(memory_space=pltpu.SMEM)
ANY = pl.BlockSpec(memory_space=pl.ANY)
PARAMS = pltpu.CompilerParams(vmem_limit_bytes=LIMIT)


def exchange(blocks):
    return lax.all_to_all(blocks, "vocab", split_axis=0, concat_axis=0, tiled=True)


def spread(own, devices):
    return exchange(jnp.broadcast_to(own[None], (devices,) + own.shape))


def basis(count):
    return [1, 3, 4] + [(1 << bit) | 1 for bit in range(3, count)]


def swap(block, offset, devices):
    pairs = [(i, i ^ offset) for i in range(devices)]
    return lax.ppermute(block, "vocab", pairs)


def split_wide(wide):
    high = wide.astype(jnp.bfloat16)
    low = (wide - high.astype(jnp.float32)).astype(jnp.bfloat16)
    return high, low


def split_outside(wide):
    high = lax.reduce_precision(wide, exponent_bits=8, mantissa_bits=7)
    return high.astype(jnp.bfloat16), (wide - high).astype(jnp.bfloat16)


def split_three(wide):
    high = wide.astype(jnp.bfloat16)
    rest = wide - high.astype(jnp.float32)
    middle = rest.astype(jnp.bfloat16)
    low = (rest - middle.astype(jnp.float32)).astype(jnp.bfloat16)
    return high, middle, low


def dot_rows(left, right):
    return lax.dot_general(left, right, (((1,), (1,)), ((), ())), preferred_element_type=jnp.float32)


def partner_of(bits, count):
    partner = 0
    for bit, offset in zip(bits, basis(count)):
        partner ^= bit * offset
    return partner


def all_bits(count):
    return [tuple((k >> (count - 1 - b)) & 1 for b in range(count)) for k in range(1 << count)]


def square_partners(count):
    return [partner_of((0,) + bits, count) for bits in all_bits(2)]


def far_partners(count):
    return [partner_of((0, 0, 0) + bits, count) for bits in all_bits(count - 3)]


def half_places(count, first):
    return [
        ((q, h), first ^ near ^ far)
        for q, near in enumerate(square_partners(count))
        for h, far in enumerate(far_partners(count))
    ]


def partner_rows(i, rows):
    owner = lax.axis_index("vocab") ^ i
    return pl.ds(pl.multiple_of(owner * rows, rows), rows)


def pack(blocks, wide, extra):
    rows = blocks.reshape(-1, blocks.shape[-1])
    parts = split_outside(rows) if wide else (rows.astype(jnp.bfloat16),)
    return jnp.concatenate(parts + extra, axis=0)


def unpack(packed, shape, wide):
    size = shape[0] * shape[1]
    rows = packed[:size].astype(jnp.float32)
    if wide:
        rows += packed[size : 2 * size].astype(jnp.float32)
    return rows.reshape(shape)


def reduce_blocks(kept, received, wide, devices, count, near_extra=(), far_extra=()):
    total = kept + received.astype(jnp.float32)
    near, extras = total[0], list(near_extra)
    for q, offset in enumerate(square_partners(count)):
        if q:
            packed = swap(pack(total[q], wide, near_extra), offset, devices)
            near += unpack(packed, total.shape[1:], wide)
            for extra in near_extra:
                extras.append(packed[-extra.shape[0] :])
    blocks = [near[0]]
    for h, offset in enumerate(far_partners(count)):
        if h:
            blocks.append(swap(pack(near[h], wide, far_extra), offset, devices))
    return blocks, extras


def gather_blocks(own, devices, count):
    far = jnp.stack([own] + [swap(own, offset, devices) for offset in far_partners(count)[1:]])
    near = jnp.stack([far] + [swap(far, offset, devices) for offset in square_partners(count)[1:]])
    return near, swap(near, 1, devices)


def column_of(scalars_ref, shape):
    row = lax.broadcasted_iota(jnp.int32, shape, 0)
    column = jnp.zeros(shape, jnp.int32)
    for k in range(shape[0]):
        column = jnp.where(row == k, scalars_ref[k], column)
    return column


def tables_kernel(
    count, state_ref, allow_ref, table_ref, emission_ref, sums_in_ref,
    route_ref, chooser_ref, sums_ref,
):
    device = lax.axis_index("vocab")
    devices = 1 << count
    states = table_ref.shape[0]
    sums_ref[...] = sums_in_ref[...]
    allow, table = allow_ref[...], table_ref[...]
    hits = [jnp.max((allow == b).astype(jnp.float32), axis=0, keepdims=True) for b in range(devices)]
    shape = (states, states)
    diagonal = [lax.broadcasted_iota(jnp.int32, shape, axis) for axis in (0, 1)]
    diagonal = (diagonal[0] == diagonal[1]).astype(jnp.bfloat16)
    hits = dot_rows(diagonal, jnp.concatenate(hits, axis=0).astype(jnp.bfloat16))
    ids = lax.broadcasted_iota(jnp.int32, shape, 1)
    own_step = jnp.zeros(shape, jnp.float32)
    for b in range(devices):
        step = jnp.where(table[:, b : b + 1] == ids, hits[:, b : b + 1], 0.0)
        own_step = jnp.where(device == b, step, own_step)
        step = step.astype(jnp.bfloat16)
        route_ref[pl.ds(b * states, states)] = jnp.concatenate([step] * 3, axis=1)
    shape = (states, devices)
    prompts = state_ref[...] == lax.broadcasted_iota(jnp.int32, shape, 0)
    chooser = lax.dot_general(
        prompts.astype(jnp.bfloat16),
        own_step.astype(jnp.bfloat16),
        (((0,), (0,)), ((), ())),
        preferred_element_type=jnp.float32,
    ).astype(jnp.bfloat16)
    chooser_ref[...] = jnp.concatenate([chooser] * 3, axis=1)


def tables(state, allow, table, emission, sums, count):
    devices, states = 1 << count, table.shape[0]
    return pl.pallas_call(
        functools.partial(tables_kernel, count),
        out_shape=[
            pltpu.VMEM((devices * states, 3 * states), jnp.bfloat16),
            pltpu.VMEM((devices, 3 * states), jnp.bfloat16),
            jax.ShapeDtypeStruct(sums.shape, sums.dtype),
        ],
        in_specs=[VMEM] * 5,
        out_specs=[VMEM] * 3,
        compiler_params=PARAMS,
        name="tables",
    )(state, allow, table, emission, sums)


def products_kernel(
    count, token_hbm, state_hbm, allow_hbm, table_hbm, start_hbm, emission_hbm,
    sums_ref, kept_ref, sent_ref, state_ref, allow_ref, table_ref, messages_ref, emission_ref,
    token_ref, columns_ref, sems, chunk_sems,
):
    device = lax.axis_index("vocab")
    devices = 1 << count
    rows = emission_ref.shape[0] >> count
    own = pl.ds(pl.multiple_of(device * rows, rows), rows)
    pairs = [
        (token_hbm, token_ref), (state_hbm, state_ref), (allow_hbm, allow_ref),
        (table_hbm, table_ref), (start_hbm.at[:, own], messages_ref),
    ]
    copies = [
        pltpu.make_async_copy(source, to, sems.at[k]) for k, (source, to) in enumerate(pairs)
    ]
    chunks = []
    for k in range(devices):
        span = pl.ds(k * rows, rows)
        chunks.append(
            pltpu.make_async_copy(emission_hbm.at[span], emission_ref.at[span], chunk_sems.at[k])
        )
    for copy in copies + chunks:
        copy.start()
    shape = (devices * devices // 2, devices * devices)
    to, source = (lax.broadcasted_iota(jnp.int32, shape, axis) for axis in (0, 1))
    same_block = (to & (devices - 1)) == (source >> count)
    orders = []
    for first in range(2):
        prompt = partner_at((to >> count) + first * (devices // 2), count)
        onehot = same_block & ((source & (devices - 1)) == prompt)
        orders.append(onehot.astype(jnp.bfloat16))
    copies[0].wait()
    shape = (devices, BLK)
    tokens = column_of(token_ref, shape) - device * BLK
    onehot = (tokens == lax.broadcasted_iota(jnp.int32, shape, 1)).astype(jnp.bfloat16)
    left = jnp.concatenate([onehot, jnp.ones((16, BLK), jnp.bfloat16)], axis=0)
    for k in range(devices):
        chunks[k].wait()
        product = dot_rows(left, emission_ref[pl.ds(k * rows, rows)])
        columns_ref[pl.ds(k * devices, devices)] = product[:devices].astype(jnp.bfloat16)
        sums_ref[k] = product[devices : devices + 1]
    for order, out_ref in zip(orders, (kept_ref, sent_ref)):
        ordered = jnp.dot(order, columns_ref[...], preferred_element_type=jnp.float32)
        out_ref[...] = ordered.astype(jnp.bfloat16).reshape(out_ref.shape)
    for copy in copies[1:]:
        copy.wait()


def first_products(last_token, prompt_state, allow_list, trans_table, beta_start, emission, count):
    devices, rows = 1 << count, emission.shape[0] >> count
    half = pltpu.VMEM((4, devices // 8, devices, rows), jnp.bfloat16)
    small = (prompt_state[None], allow_list.T, trans_table)
    operands = (last_token,) + small + (beta_start.T,)
    return pl.pallas_call(
        functools.partial(products_kernel, count),
        out_shape=[jax.ShapeDtypeStruct((devices, 1, rows), jnp.float32), half, half]
        + [pltpu.VMEM(array.shape, array.dtype) for array in small]
        + [pltpu.VMEM((beta_start.shape[1], rows), jnp.float32)]
        + [pltpu.VMEM(emission.shape, emission.dtype)],
        in_specs=[ANY] * (len(operands) + 1),
        out_specs=[VMEM] * 8,
        scratch_shapes=[
            pltpu.SMEM(last_token.shape, jnp.int32),
            pltpu.VMEM((devices * devices, rows), jnp.bfloat16),
            pltpu.SemaphoreType.DMA((len(operands),)),
            pltpu.SemaphoreType.DMA((devices,)),
        ],
        compiler_params=PARAMS,
        name="first_products",
    )(*(in_hbm(operand) for operand in operands + (emission,)))


def in_hbm(array):
    return pltpu.with_memory_space_constraint(array, pltpu.HBM)


def forward_kernel(prior_ref, *refs):
    blocks, out_ref = refs[:-1], refs[-1]
    devices, rows = out_ref.shape
    columns = blocks[0][-devices:]
    for block in blocks[1:]:
        columns += block[-devices:].astype(jnp.float32)
    prior = jnp.concatenate([prior_ref[:, pl.ds(k * rows, rows)] for k in range(devices)], axis=0)
    unnormal = prior * columns
    out_ref[...] = (unnormal / jnp.sum(unnormal)).astype(jnp.bfloat16)


def forward_messages_here(prior, blocks, devices):
    return pl.pallas_call(
        forward_kernel,
        out_shape=pltpu.VMEM((devices, blocks[0].shape[1]), jnp.bfloat16),
        in_specs=[VMEM] * (1 + len(blocks)),
        out_specs=VMEM,
        compiler_params=PARAMS,
        name="forward_messages",
    )(prior, *blocks)


def partner_at(place, count):
    number = jnp.zeros_like(place)
    for bit, offset in enumerate(basis(count)):
        number = number ^ (((place >> (count - 1 - bit)) & 1) * offset)
    return lax.axis_index("vocab") ^ number


def order_kernel(count, near_ref, far_ref, out_ref):
    size = 1 << count
    shape = (size * size, size * size)
    to, source = (lax.broadcasted_iota(jnp.int32, shape, axis) for axis in (0, 1))
    same_block = partner_at(to >> count, count) == (source & (size - 1))
    same_prompt = (to & (size - 1)) == partner_at(source >> count, count)
    onehot = (same_block & same_prompt).astype(jnp.bfloat16)
    half = size * size // 2
    rows = out_ref.shape[1]
    near = near_ref[...].reshape(half, rows)
    far = far_ref[...].reshape(half, rows)
    ordered = jnp.dot(onehot[:, :half], near, preferred_element_type=jnp.float32)
    ordered += jnp.dot(onehot[:, half:], far, preferred_element_type=jnp.float32)
    out_ref[...] = ordered.astype(jnp.bfloat16)


def order_forward(near, far, count):
    rows = near.shape[-1]
    return pl.pallas_call(
        functools.partial(order_kernel, count),
        out_shape=pltpu.VMEM((1 << (2 * count), rows), jnp.bfloat16),
        in_specs=[VMEM] * 2,
        out_specs=VMEM,
        compiler_params=PARAMS,
        name="order_forward",
    )(near, far)


def last_kernel(*refs):
    blocks, out_ref = refs[:-2], refs[-1]
    states = out_ref.shape[0]
    messages = blocks[0][...]
    for block in blocks[1:]:
        for part in range(2):
            messages += block[pl.ds(part * states, states)].astype(jnp.float32)
    out_ref[...] = messages


def last_sum(blocks, after):
    return pl.pallas_call(
        last_kernel,
        out_shape=pltpu.VMEM(blocks[0].shape, jnp.float32),
        in_specs=[VMEM] * len(blocks) + [ANY],
        out_specs=VMEM,
        compiler_params=PARAMS,
        name="last_messages",
    )(*blocks, after)


def half_products(halves, transition_ref, out_ref, count, first):
    states = halves.shape[0] // 2
    rows = transition_ref.shape[0] >> count
    for place, partner in half_places(count, first):
        product = dot_rows(halves, transition_ref[partner_rows(partner, rows)])
        product = product[:states] + product[states:]
        out_ref[place + (pl.ds(0, states),)] = product.astype(out_ref.dtype)


def add_rows(out_ref, states, extra):
    for ref in extra:
        rows = pl.ds(states, ref.shape[2])
        for place in ((y, k) for y in range(ref.shape[0]) for k in range(ref.shape[1])):
            out_ref[place + (rows,)] = ref[place].astype(out_ref.dtype)


def send_kernel(count, number, transition_ref, route_ref, sums_ref, *refs):
    parts, extra, (halves_ref, out_ref) = refs[:number], refs[number:-2], refs[-2:]
    states = halves_ref.shape[0] // 2
    messages = parts[0][:states].astype(jnp.float32)
    for part in parts[1:]:
        messages += part[:states].astype(jnp.float32)
    selected = jnp.dot(
        route_ref[...],
        jnp.concatenate(split_three(messages), axis=0),
        preferred_element_type=jnp.float32,
    )
    emitted = selected[:states] * sums_ref[0]
    for b in range(1, 1 << count):
        emitted += selected[b * states : (b + 1) * states] * sums_ref[b]
    halves = jnp.concatenate(split_wide(emitted), axis=0)
    halves_ref[...] = halves
    half_products(halves, transition_ref, out_ref, count, 1)
    add_rows(out_ref, states, extra)


def keep_kernel(count, transition_ref, halves_ref, *refs):
    extra, out_ref = refs[:-1], refs[-1]
    half_products(halves_ref[...], transition_ref, out_ref, count, 0)
    add_rows(out_ref, halves_ref.shape[0] // 2, extra)


def step(transition, route, sums, parts, dtype, devices, count, kept_rows=(), sent_rows=()):
    states, rows = route.shape[0] // devices, parts[0].shape[1]
    total = states + sum(block.shape[2] for block in kept_rows)
    shape = (4, devices // 8, total, rows)
    halves, sent = pl.pallas_call(
        functools.partial(send_kernel, count, len(parts)),
        out_shape=[
            pltpu.VMEM((2 * states, rows), jnp.bfloat16),
            pltpu.VMEM(shape, dtype),
        ],
        in_specs=[VMEM] * (3 + len(parts) + len(sent_rows)),
        out_specs=[VMEM] * 2,
        compiler_params=PARAMS,
        name="step_sent_half",
    )(transition, route, sums, *parts, *sent_rows)
    received = swap(sent, 1, devices)
    kept = pl.pallas_call(
        functools.partial(keep_kernel, count),
        out_shape=pltpu.VMEM(shape, jnp.float32),
        in_specs=[VMEM] * (2 + len(kept_rows)),
        out_specs=VMEM,
        compiler_params=PARAMS,
        name="step_kept_half",
    )(transition, halves, *kept_rows)
    return kept, received


def weigh_half(emission_ref, forward_ref, chooser, parts_ref, count, first):
    rows = emission_ref.shape[0] >> count
    prompts = chooser.shape[0]
    weights = jnp.zeros((prompts, emission_ref.shape[1]), jnp.float32)
    for order, (place, partner) in enumerate(half_places(count, first)):
        pieces = jnp.concatenate(split_three(parts_ref[place]), axis=0)
        chosen = jnp.dot(chooser, pieces, preferred_element_type=jnp.float32)
        block = order + (first << (count - 1))
        forward = forward_ref[pl.ds(block * prompts, prompts)].astype(jnp.float32)
        scaled = (forward * chosen).astype(jnp.bfloat16)
        tile = emission_ref[partner_rows(partner, rows)]
        weights += jnp.dot(scaled, tile, preferred_element_type=jnp.float32)
    return weights


def near_kernel(count, emission_ref, forward_ref, chooser_ref, parts_ref, out_ref):
    out_ref[...] = weigh_half(emission_ref, forward_ref, chooser_ref[...], parts_ref, count, 0)


def far_kernel(count, emission_ref, forward_ref, chooser_ref, logits_ref, near_ref, parts_ref, raised_ref, pair_ref):
    chooser = chooser_ref[...]
    logits = logits_ref[...].astype(jnp.float32)
    top = jnp.max(logits, axis=1, keepdims=True)
    weights = near_ref[...] + weigh_half(emission_ref, forward_ref, chooser, parts_ref, count, 1)
    allowed = jnp.sum(chooser.astype(jnp.float32), axis=1, keepdims=True) > 0
    raised = jnp.where(allowed, jnp.exp(logits - top) * weights, 0.0)
    raised_ref[...] = raised
    total = jnp.sum(raised, axis=1, keepdims=True)
    lane = lax.broadcasted_iota(jnp.int32, (raised.shape[0], 128), 1)
    rows = jnp.where(lane == 0, top, total).T[:2]
    for k in range(pair_ref.shape[0]):
        pair_ref[k] = rows


def weigh(emission, forward, chooser, logits, near, far, count):
    half = pl.pallas_call(
        functools.partial(near_kernel, count),
        out_shape=pltpu.VMEM(logits.shape, jnp.float32),
        in_specs=[VMEM] * 4,
        out_specs=VMEM,
        compiler_params=PARAMS,
        name="weigh_near",
    )(emission, forward, chooser, near)
    return pl.pallas_call(
        functools.partial(far_kernel, count),
        out_shape=[
            pltpu.VMEM(logits.shape, jnp.float32),
            pltpu.VMEM((1 << count, 2, logits.shape[0]), jnp.float32),
        ],
        in_specs=[VMEM] * 6,
        out_specs=[VMEM] * 2,
        compiler_params=PARAMS,
        name="weigh_far",
    )(emission, forward, chooser, logits, half, far)


def normalise(raised, pair, devices):
    pairs = exchange(pair)
    own_top = pair[0, 0]
    tops, totals = pairs[:, 0], pairs[:, 1]
    top = jnp.max(tops, axis=0)
    total = jnp.sum(totals * jnp.exp(tops - top), axis=0)
    return BLK * devices * (raised * jnp.exp(own_top - top)[:, None]) / total[:, None]


def forward_messages(emission, last_token, prior_msg, devices, device):
    hidden = emission.shape[0]
    local_rows = prior_msg.shape[0]
    token_ids = jnp.arange(BLK, dtype=jnp.int32)
    tokens = last_token - device * BLK
    onehot = (tokens[:, None] == token_ids[None, :]).astype(jnp.bfloat16)
    owned = dot_rows(onehot, emission)
    owned = owned.astype(jnp.bfloat16).reshape(devices, local_rows, hidden)
    columns = jnp.sum(exchange(owned), axis=0, dtype=jnp.float32)
    unnormal = prior_msg * columns
    forward_msg = (unnormal / jnp.sum(unnormal, axis=1, keepdims=True)).astype(jnp.bfloat16)
    return spread(forward_msg, devices).reshape(devices * local_rows, hidden)


def per_device(
    emission,
    transition,
    beta_start,
    allow_list,
    trans_table,
    last_token,
    prompt_state,
    prior_msg,
    lm_logits,
):
    devices = lax.axis_size("vocab")
    device = lax.axis_index("vocab")
    hidden = emission.shape[0]
    states = beta_start.shape[1]
    own_rows = transition.shape[1]
    prompts = prompt_state.shape[0]
    count = devices.bit_length() - 1
    if devices == 1 << count and count > 2 and own_rows % 128 == 0 and prompts == devices:
        sums, columns, columns_out, state, allow, table, messages, held = first_products(
            last_token, prompt_state, allow_list, trans_table, beta_start, emission, count
        )
        route, chooser, sums = tables(state, allow, table, held, sums, count)
        sums = exchange(sums)
        parts, kept_rows, sent_rows = [messages], (columns,), (columns_out,)
        for window_step in range(STEPS):
            wide = window_step == STEPS - 1
            dtype = jnp.float32 if wide else jnp.bfloat16
            kept, received = step(
                transition, route, sums, parts, dtype, devices, count, kept_rows, sent_rows
            )
            kept_rows, sent_rows, near_extra, far_extra = (), (), (), ()
            if window_step == 1:
                forward = forward_messages_here(prior_msg, parts, devices)
                far_extra = (forward,)
            if window_step == 2:
                near_extra = (forward,)
            parts, extras = reduce_blocks(
                kept, received, wide, devices, count, near_extra, far_extra
            )
            if window_step == 1:
                others = [part[-devices:] for part in parts[1:]]
                forward = jnp.concatenate([forward] + others, axis=0)
        near = jnp.stack(extras).reshape(4, devices // 8, devices, own_rows)
        forward = order_forward(near, swap(near, 1, devices), count)
        messages = last_sum(parts, forward)
        near, far = gather_blocks(messages, devices, count)
        raised, pair = weigh(emission, forward, chooser, lm_logits, near, far, count)
        return messages.T, normalise(raised, pair, devices)
    state_ids = jnp.arange(states, dtype=jnp.int32)
    block_ids = jnp.arange(devices, dtype=jnp.int32)
    allowed = jnp.any(allow_list[:, :, None] == block_ids, axis=1)
    dest_here = lax.dynamic_index_in_dim(trans_table, device, axis=1, keepdims=False)
    allow_here = jnp.any(allow_list == device, axis=1)
    dest_rows = jnp.sum(jnp.where(prompt_state[:, None] == state_ids, dest_here, 0), axis=1)
    allow_rows = jnp.any((prompt_state[:, None] == state_ids) & allow_here, axis=1)
    chooser = (dest_rows[:, None] == state_ids) & allow_rows[:, None]
    messages = lax.dynamic_slice_in_dim(beta_start, device * own_rows, own_rows, 0).T
    forward_all = forward_messages(emission, last_token, prior_msg, devices, device)
    own_sums = exchange(jnp.sum(emission, axis=1, dtype=jnp.float32).reshape(devices, own_rows))
    route = allowed.T[:, :, None] & (trans_table.T[:, :, None] == state_ids)
    route = route.astype(jnp.float32).reshape(devices * states, states)
    by_owner = transition.reshape(devices, own_rows, own_rows)
    for window_step in range(STEPS):
        selected = jnp.dot(route, messages, precision=lax.Precision.HIGHEST)
        selected = selected.reshape(devices, states, own_rows)
        emitted = jnp.sum(selected * own_sums[:, None, :], axis=0)
        halves = jnp.concatenate(split_outside(emitted), axis=0)
        partial = jnp.einsum("dzy,sy->dsz", by_owner, halves, preferred_element_type=jnp.float32)
        partial = partial[:, :states] + partial[:, states:]
        if window_step < STEPS - 1:
            partial = partial.astype(jnp.bfloat16)
        messages = jnp.sum(exchange(partial), axis=0, dtype=jnp.float32)
    everywhere = spread(messages, devices)
    chosen = jnp.einsum(
        "ps,dsz->pdz", chooser.astype(jnp.float32), everywhere, precision=lax.Precision.HIGHEST
    )
    forward_all = forward_all.reshape(prompts, devices, own_rows).astype(jnp.float32)
    scaled = (forward_all * chosen).astype(jnp.bfloat16).reshape(prompts, hidden)
    weights = jnp.dot(scaled, emission, preferred_element_type=jnp.float32)
    weights = jnp.where(allow_rows[:, None], weights, 0.0)
    logits = lm_logits.astype(jnp.float32)
    top_here = jnp.max(logits, axis=1)
    raised = jnp.exp(logits - top_here[:, None]) * weights
    pairs = spread(jnp.stack([top_here, jnp.sum(raised, axis=1)]), devices)
    tops, totals = pairs[:, 0], pairs[:, 1]
    top = jnp.max(tops, axis=0)
    total = jnp.sum(totals * jnp.exp(tops - top), axis=0)
    raised = raised * jnp.exp(top_here - top)[:, None]
    return (messages.T, BLK * devices * raised / total[:, None])


def solution(mesh):
    return jax.shard_map(
        per_device,
        mesh=mesh,
        in_specs=(
            P(None, "vocab"),
            P(None, "vocab"),
            P(),
            P(),
            P(),
            P("parts"),
            P("parts"),
            P(("parts", "vocab"), None),
            P("parts", "vocab"),
        ),
        out_specs=(P(("parts", "vocab"), None), P("parts", "vocab")),
        check_vma=False,
    )
```

```python
import functools

import jax
import jax.numpy as jnp
from jax import lax
from jax.experimental import pallas as pl
from jax.experimental.pallas import tpu as pltpu
from jax.sharding import PartitionSpec as P

BLK = 256
STEPS = 3
LIMIT = 16 * 1024 * 1024
VMEM = pl.BlockSpec(memory_space=pltpu.VMEM)
SMEM = pl.BlockSpec(memory_space=pltpu.SMEM)
ANY = pl.BlockSpec(memory_space=pl.ANY)
PARAMS = pltpu.CompilerParams(vmem_limit_bytes=LIMIT)


def exchange(blocks):
    return lax.all_to_all(blocks, "vocab", split_axis=0, concat_axis=0, tiled=True)


def spread(own, devices):
    return exchange(jnp.broadcast_to(own[None], (devices,) + own.shape))


def basis(count):
    return [1, 3, 4] + [(1 << bit) | 1 for bit in range(3, count)]


def swap(block, offset, devices):
    pairs = [(i, i ^ offset) for i in range(devices)]
    return lax.ppermute(block, "vocab", pairs)


def split_wide(wide):
    high = wide.astype(jnp.bfloat16)
    low = (wide - high.astype(jnp.float32)).astype(jnp.bfloat16)
    return high, low


def split_outside(wide):
    high = lax.reduce_precision(wide, exponent_bits=8, mantissa_bits=7)
    return high.astype(jnp.bfloat16), (wide - high).astype(jnp.bfloat16)


def split_three(wide):
    high = wide.astype(jnp.bfloat16)
    rest = wide - high.astype(jnp.float32)
    middle = rest.astype(jnp.bfloat16)
    low = (rest - middle.astype(jnp.float32)).astype(jnp.bfloat16)
    return high, middle, low


def dot_rows(left, right):
    return lax.dot_general(left, right, (((1,), (1,)), ((), ())), preferred_element_type=jnp.float32)


def partner_of(bits, count):
    partner = 0
    for bit, offset in zip(bits, basis(count)):
        partner ^= bit * offset
    return partner


def all_bits(count):
    return [tuple((k >> (count - 1 - b)) & 1 for b in range(count)) for k in range(1 << count)]


def square_partners(count):
    return [partner_of((0,) + bits, count) for bits in all_bits(2)]


def far_partners(count):
    return [partner_of((0, 0, 0) + bits, count) for bits in all_bits(count - 3)]


def half_places(count, first):
    return [
        ((q, h), first ^ near ^ far)
        for q, near in enumerate(square_partners(count))
        for h, far in enumerate(far_partners(count))
    ]


def partner_rows(i, rows):
    owner = lax.axis_index("vocab") ^ i
    return pl.ds(pl.multiple_of(owner * rows, rows), rows)


def pack(blocks, wide, extra):
    rows = blocks.reshape(-1, blocks.shape[-1])
    parts = split_outside(rows) if wide else (rows.astype(jnp.bfloat16),)
    return jnp.concatenate(parts + extra, axis=0)


def unpack(packed, shape, wide):
    size = shape[0] * shape[1]
    rows = packed[:size].astype(jnp.float32)
    if wide:
        rows += packed[size : 2 * size].astype(jnp.float32)
    return rows.reshape(shape)


def reduce_square(kept, received, wide, devices, count, extra=()):
    total = kept + received.astype(jnp.float32)
    near, extras = total[0], list(extra)
    for q, offset in enumerate(square_partners(count)):
        if q:
            packed = swap(pack(total[q], wide, extra), offset, devices)
            near += unpack(packed, total.shape[1:], wide)
            for rows in extra:
                extras.append(packed[-rows.shape[0] :])
    return near, extras


def reduce_far(near, devices, count, extra=()):
    blocks = [near[0]]
    for h, offset in enumerate(far_partners(count)):
        if h:
            blocks.append(swap(pack(near[h], False, extra), offset, devices))
    return blocks


def gather_square(far, devices, count):
    near = jnp.stack([far] + [swap(far, offset, devices) for offset in square_partners(count)[1:]])
    return near, swap(near, 1, devices)


def column_of(scalars_ref, shape):
    row = lax.broadcasted_iota(jnp.int32, shape, 0)
    column = jnp.zeros(shape, jnp.int32)
    for k in range(shape[0]):
        column = jnp.where(row == k, scalars_ref[k], column)
    return column


def tables_kernel(
    count, state_ref, allow_ref, table_ref, emission_ref, sums_in_ref,
    route_ref, chooser_ref, sums_ref,
):
    device = lax.axis_index("vocab")
    devices = 1 << count
    states = table_ref.shape[0]
    sums_ref[...] = sums_in_ref[...]
    allow, table = allow_ref[...], table_ref[...]
    hits = [jnp.max((allow == b).astype(jnp.float32), axis=0, keepdims=True) for b in range(devices)]
    shape = (states, states)
    diagonal = [lax.broadcasted_iota(jnp.int32, shape, axis) for axis in (0, 1)]
    diagonal = (diagonal[0] == diagonal[1]).astype(jnp.bfloat16)
    hits = dot_rows(diagonal, jnp.concatenate(hits, axis=0).astype(jnp.bfloat16))
    ids = lax.broadcasted_iota(jnp.int32, shape, 1)
    own_step = jnp.zeros(shape, jnp.float32)
    for b in range(devices):
        step = jnp.where(table[:, b : b + 1] == ids, hits[:, b : b + 1], 0.0)
        own_step = jnp.where(device == b, step, own_step)
        step = step.astype(jnp.bfloat16)
        route_ref[pl.ds(b * states, states)] = jnp.concatenate([step] * 3, axis=1)
    shape = (states, devices)
    prompts = state_ref[...] == lax.broadcasted_iota(jnp.int32, shape, 0)
    chooser = lax.dot_general(
        prompts.astype(jnp.bfloat16),
        own_step.astype(jnp.bfloat16),
        (((0,), (0,)), ((), ())),
        preferred_element_type=jnp.float32,
    ).astype(jnp.bfloat16)
    chooser_ref[...] = jnp.concatenate([chooser] * 3, axis=1)


def tables(state, allow, table, emission, sums, count):
    devices, states = 1 << count, table.shape[0]
    return pl.pallas_call(
        functools.partial(tables_kernel, count),
        out_shape=[
            pltpu.VMEM((devices * states, 3 * states), jnp.bfloat16),
            pltpu.VMEM((devices, 3 * states), jnp.bfloat16),
            jax.ShapeDtypeStruct(sums.shape, sums.dtype),
        ],
        in_specs=[VMEM] * 5,
        out_specs=[VMEM] * 3,
        compiler_params=PARAMS,
        name="tables",
    )(state, allow, table, emission, sums)


def products_kernel(
    count, token_hbm, state_hbm, allow_hbm, table_hbm, start_hbm, emission_ref,
    sums_ref, kept_ref, sent_ref, state_ref, allow_ref, table_ref, messages_ref,
    token_ref, columns_ref, sems,
):
    device = lax.axis_index("vocab")
    devices = 1 << count
    rows = emission_ref.shape[0] >> count
    own = pl.ds(pl.multiple_of(device * rows, rows), rows)
    pairs = [
        (token_hbm, token_ref), (state_hbm, state_ref), (allow_hbm, allow_ref),
        (table_hbm, table_ref), (start_hbm.at[:, own], messages_ref),
    ]
    copies = [
        pltpu.make_async_copy(source, to, sems.at[k]) for k, (source, to) in enumerate(pairs)
    ]
    for copy in copies:
        copy.start()
    shape = (devices * devices // 2, devices * devices)
    to, source = (lax.broadcasted_iota(jnp.int32, shape, axis) for axis in (0, 1))
    same_block = (to & (devices - 1)) == (source >> count)
    orders = []
    for first in range(2):
        prompt = partner_at((to >> count) + first * (devices // 2), count)
        onehot = same_block & ((source & (devices - 1)) == prompt)
        orders.append(onehot.astype(jnp.bfloat16))
    copies[0].wait()
    shape = (devices, BLK)
    tokens = column_of(token_ref, shape) - device * BLK
    onehot = (tokens == lax.broadcasted_iota(jnp.int32, shape, 1)).astype(jnp.bfloat16)
    left = jnp.concatenate([onehot, jnp.ones((16, BLK), jnp.bfloat16)], axis=0)
    for k in range(devices):
        product = dot_rows(left, emission_ref[pl.ds(k * rows, rows)])
        columns_ref[pl.ds(k * devices, devices)] = product[:devices].astype(jnp.bfloat16)
        sums_ref[k] = product[devices : devices + 1]
    for order, out_ref in zip(orders, (kept_ref, sent_ref)):
        ordered = jnp.dot(order, columns_ref[...], preferred_element_type=jnp.float32)
        out_ref[...] = ordered.astype(jnp.bfloat16).reshape(out_ref.shape)
    for copy in copies[1:]:
        copy.wait()


def first_products(last_token, prompt_state, allow_list, trans_table, beta_start, emission, count):
    devices, rows = 1 << count, emission.shape[0] >> count
    half = pltpu.VMEM((4, devices // 8, devices, rows), jnp.bfloat16)
    small = (prompt_state[None], allow_list.T, trans_table)
    operands = (last_token,) + small + (beta_start.T,)
    return pl.pallas_call(
        functools.partial(products_kernel, count),
        out_shape=[jax.ShapeDtypeStruct((devices, 1, rows), jnp.float32), half, half]
        + [pltpu.VMEM(array.shape, array.dtype) for array in small]
        + [pltpu.VMEM((beta_start.shape[1], rows), jnp.float32)],
        in_specs=[ANY] * len(operands) + [VMEM],
        out_specs=[VMEM] * 7,
        scratch_shapes=[
            pltpu.SMEM(last_token.shape, jnp.int32),
            pltpu.VMEM((devices * devices, rows), jnp.bfloat16),
            pltpu.SemaphoreType.DMA((len(operands),)),
        ],
        compiler_params=PARAMS,
        name="first_products",
    )(*(in_hbm(operand) for operand in operands), emission)


def in_hbm(array):
    return pltpu.with_memory_space_constraint(array, pltpu.HBM)


def forward_kernel(prior_ref, *refs):
    blocks, out_ref = refs[:-1], refs[-1]
    devices, rows = out_ref.shape
    columns = blocks[0][-devices:]
    for block in blocks[1:]:
        columns += block[-devices:].astype(jnp.float32)
    prior = jnp.concatenate([prior_ref[:, pl.ds(k * rows, rows)] for k in range(devices)], axis=0)
    unnormal = prior * columns
    out_ref[...] = (unnormal / jnp.sum(unnormal)).astype(jnp.bfloat16)


def forward_messages_here(prior, blocks, devices):
    return pl.pallas_call(
        forward_kernel,
        out_shape=pltpu.VMEM((devices, blocks[0].shape[1]), jnp.bfloat16),
        in_specs=[VMEM] * (1 + len(blocks)),
        out_specs=VMEM,
        compiler_params=PARAMS,
        name="forward_messages",
    )(prior, *blocks)


def partner_at(place, count):
    number = jnp.zeros_like(place)
    for bit, offset in enumerate(basis(count)):
        number = number ^ (((place >> (count - 1 - bit)) & 1) * offset)
    return lax.axis_index("vocab") ^ number


def order_kernel(count, near_ref, far_ref, out_ref):
    size = 1 << count
    shape = (size * size, size * size)
    to, source = (lax.broadcasted_iota(jnp.int32, shape, axis) for axis in (0, 1))
    same_block = partner_at(to >> count, count) == (source & (size - 1))
    same_prompt = (to & (size - 1)) == partner_at(source >> count, count)
    onehot = (same_block & same_prompt).astype(jnp.bfloat16)
    half = size * size // 2
    rows = out_ref.shape[1]
    near = near_ref[...].reshape(half, rows)
    far = far_ref[...].reshape(half, rows)
    ordered = jnp.dot(onehot[:, :half], near, preferred_element_type=jnp.float32)
    ordered += jnp.dot(onehot[:, half:], far, preferred_element_type=jnp.float32)
    out_ref[...] = ordered.astype(jnp.bfloat16)


def order_forward(near, far, count):
    rows = near.shape[-1]
    return pl.pallas_call(
        functools.partial(order_kernel, count),
        out_shape=pltpu.VMEM((1 << (2 * count), rows), jnp.bfloat16),
        in_specs=[VMEM] * 2,
        out_specs=VMEM,
        compiler_params=PARAMS,
        name="order_forward",
    )(near, far)


def last_kernel(near_ref, *refs):
    blocks, out_ref = refs[:-2], refs[-1]
    count, states, _ = out_ref.shape
    for h in range(count):
        messages = near_ref[h]
        for g, block in enumerate(blocks, 1):
            for part in range(2):
                start = (part * count + (h ^ g)) * states
                messages += block[pl.ds(start, states)].astype(jnp.float32)
        out_ref[h] = messages


def last_sum(near, after, devices, count):
    packed = pack(near, True, ())
    blocks = [swap(packed, offset, devices) for offset in far_partners(count)[1:]]
    return pl.pallas_call(
        last_kernel,
        out_shape=pltpu.VMEM(near.shape, jnp.float32),
        in_specs=[VMEM] * (1 + len(blocks)) + [ANY],
        out_specs=VMEM,
        compiler_params=PARAMS,
        name="last_messages",
    )(near, *blocks, after)


def half_products(halves, transition_ref, out_ref, count, first):
    states = halves.shape[0] // 2
    rows = transition_ref.shape[0] >> count
    for place, partner in half_places(count, first):
        product = dot_rows(halves, transition_ref[partner_rows(partner, rows)])
        product = product[:states] + product[states:]
        out_ref[place + (pl.ds(0, states),)] = product.astype(out_ref.dtype)


def add_rows(out_ref, states, extra):
    for ref in extra:
        rows = pl.ds(states, ref.shape[2])
        for place in ((y, k) for y in range(ref.shape[0]) for k in range(ref.shape[1])):
            out_ref[place + (rows,)] = ref[place].astype(out_ref.dtype)


def send_kernel(count, number, transition_ref, route_ref, sums_ref, *refs):
    parts, extra, (halves_ref, out_ref) = refs[:number], refs[number:-2], refs[-2:]
    states = halves_ref.shape[0] // 2
    messages = parts[0][:states].astype(jnp.float32)
    for part in parts[1:]:
        messages += part[:states].astype(jnp.float32)
    selected = jnp.dot(
        route_ref[...],
        jnp.concatenate(split_three(messages), axis=0),
        preferred_element_type=jnp.float32,
    )
    emitted = selected[:states] * sums_ref[0]
    for b in range(1, 1 << count):
        emitted += selected[b * states : (b + 1) * states] * sums_ref[b]
    halves = jnp.concatenate(split_wide(emitted), axis=0)
    halves_ref[...] = halves
    half_products(halves, transition_ref, out_ref, count, 1)
    add_rows(out_ref, states, extra)


def keep_kernel(count, transition_ref, halves_ref, *refs):
    extra, out_ref = refs[:-1], refs[-1]
    half_products(halves_ref[...], transition_ref, out_ref, count, 0)
    add_rows(out_ref, halves_ref.shape[0] // 2, extra)


def step(transition, route, sums, parts, dtype, devices, count, kept_rows=(), sent_rows=()):
    states, rows = route.shape[0] // devices, parts[0].shape[1]
    total = states + sum(block.shape[2] for block in kept_rows)
    shape = (4, devices // 8, total, rows)
    halves, sent = pl.pallas_call(
        functools.partial(send_kernel, count, len(parts)),
        out_shape=[
            pltpu.VMEM((2 * states, rows), jnp.bfloat16),
            pltpu.VMEM(shape, dtype),
        ],
        in_specs=[VMEM] * (3 + len(parts) + len(sent_rows)),
        out_specs=[VMEM] * 2,
        compiler_params=PARAMS,
        name="step_sent_half",
    )(transition, route, sums, *parts, *sent_rows)
    received = swap(sent, 1, devices)
    kept = pl.pallas_call(
        functools.partial(keep_kernel, count),
        out_shape=pltpu.VMEM(shape, jnp.float32),
        in_specs=[VMEM] * (2 + len(kept_rows)),
        out_specs=VMEM,
        compiler_params=PARAMS,
        name="step_kept_half",
    )(transition, halves, *kept_rows)
    return kept, received


def weigh_half(emission_ref, forward_ref, chooser, parts_ref, count, first):
    rows = emission_ref.shape[0] >> count
    prompts = chooser.shape[0]
    weights = jnp.zeros((prompts, emission_ref.shape[1]), jnp.float32)
    for order, (place, partner) in enumerate(half_places(count, first)):
        pieces = jnp.concatenate(split_three(parts_ref[place]), axis=0)
        chosen = jnp.dot(chooser, pieces, preferred_element_type=jnp.float32)
        block = order + (first << (count - 1))
        forward = forward_ref[pl.ds(block * prompts, prompts)].astype(jnp.float32)
        scaled = (forward * chosen).astype(jnp.bfloat16)
        tile = emission_ref[partner_rows(partner, rows)]
        weights += jnp.dot(scaled, tile, preferred_element_type=jnp.float32)
    return weights


def near_kernel(count, emission_ref, forward_ref, chooser_ref, parts_ref, out_ref):
    out_ref[...] = weigh_half(emission_ref, forward_ref, chooser_ref[...], parts_ref, count, 0)


def far_kernel(count, emission_ref, forward_ref, chooser_ref, logits_ref, near_ref, parts_ref, raised_ref, pair_ref):
    chooser = chooser_ref[...]
    logits = logits_ref[...].astype(jnp.float32)
    top = jnp.max(logits, axis=1, keepdims=True)
    weights = near_ref[...] + weigh_half(emission_ref, forward_ref, chooser, parts_ref, count, 1)
    allowed = jnp.sum(chooser.astype(jnp.float32), axis=1, keepdims=True) > 0
    raised = jnp.where(allowed, jnp.exp(logits - top) * weights, 0.0)
    raised_ref[...] = raised
    total = jnp.sum(raised, axis=1, keepdims=True)
    lane = lax.broadcasted_iota(jnp.int32, pair_ref.shape, 1)
    pair_ref[...] = jnp.where(lane == 0, top, total)


def weigh(emission, forward, chooser, logits, near, far, count):
    half = pl.pallas_call(
        functools.partial(near_kernel, count),
        out_shape=pltpu.VMEM(logits.shape, jnp.float32),
        in_specs=[VMEM] * 4,
        out_specs=VMEM,
        compiler_params=PARAMS,
        name="weigh_near",
    )(emission, forward, chooser, near)
    return pl.pallas_call(
        functools.partial(far_kernel, count),
        out_shape=[
            pltpu.VMEM(logits.shape, jnp.float32),
            pltpu.VMEM((logits.shape[0], 128), jnp.float32),
        ],
        in_specs=[VMEM] * 6,
        out_specs=[VMEM] * 2,
        compiler_params=PARAMS,
        name="weigh_far",
    )(emission, forward, chooser, logits, half, far)


def normalise(raised, pair, devices):
    pairs = spread(pair[:, :2].T, devices)
    own_top = pair[:, :1]
    tops, totals = pairs[:, 0], pairs[:, 1]
    top = jnp.max(tops, axis=0)
    total = jnp.sum(totals * jnp.exp(tops - top), axis=0)
    return BLK * devices * (raised * jnp.exp(own_top - top[:, None])) / total[:, None]


def forward_messages(emission, last_token, prior_msg, devices, device):
    hidden = emission.shape[0]
    local_rows = prior_msg.shape[0]
    token_ids = jnp.arange(BLK, dtype=jnp.int32)
    tokens = last_token - device * BLK
    onehot = (tokens[:, None] == token_ids[None, :]).astype(jnp.bfloat16)
    owned = dot_rows(onehot, emission)
    owned = owned.astype(jnp.bfloat16).reshape(devices, local_rows, hidden)
    columns = jnp.sum(exchange(owned), axis=0, dtype=jnp.float32)
    unnormal = prior_msg * columns
    forward_msg = (unnormal / jnp.sum(unnormal, axis=1, keepdims=True)).astype(jnp.bfloat16)
    return spread(forward_msg, devices).reshape(devices * local_rows, hidden)


def per_device(
    emission,
    transition,
    beta_start,
    allow_list,
    trans_table,
    last_token,
    prompt_state,
    prior_msg,
    lm_logits,
):
    devices = lax.axis_size("vocab")
    device = lax.axis_index("vocab")
    hidden = emission.shape[0]
    states = beta_start.shape[1]
    own_rows = transition.shape[1]
    prompts = prompt_state.shape[0]
    count = devices.bit_length() - 1
    if devices == 1 << count and count > 2 and own_rows % 128 == 0 and prompts == devices:
        sums, columns, columns_out, state, allow, table, messages = first_products(
            last_token, prompt_state, allow_list, trans_table, beta_start, emission, count
        )
        route, chooser, sums = tables(state, allow, table, emission, sums, count)
        sums = exchange(sums)
        parts, kept_rows, sent_rows = [messages], (columns,), (columns_out,)
        for window_step in range(STEPS):
            wide = window_step == STEPS - 1
            dtype = jnp.float32 if wide else jnp.bfloat16
            kept, received = step(
                transition, route, sums, parts, dtype, devices, count, kept_rows, sent_rows
            )
            kept_rows, sent_rows, extra = (), (), ()
            if window_step == 1:
                forward = forward_messages_here(prior_msg, parts, devices)
            if window_step == 2:
                extra = (forward,)
            near, extras = reduce_square(kept, received, wide, devices, count, extra)
            if window_step == 0:
                parts = reduce_far(near, devices, count)
            if window_step == 1:
                parts = reduce_far(near, devices, count, (forward,))
                others = [part[-devices:] for part in parts[1:]]
                forward = jnp.concatenate([forward] + others, axis=0)
        forward = jnp.stack(extras).reshape(4, devices // 8, devices, own_rows)
        forward = order_forward(forward, swap(forward, 1, devices), count)
        messages = last_sum(near, forward, devices, count)
        near, far = gather_square(messages, devices, count)
        messages = messages[0]
        raised, pair = weigh(emission, forward, chooser, lm_logits, near, far, count)
        return messages.T, normalise(raised, pair, devices)
    state_ids = jnp.arange(states, dtype=jnp.int32)
    block_ids = jnp.arange(devices, dtype=jnp.int32)
    allowed = jnp.any(allow_list[:, :, None] == block_ids, axis=1)
    dest_here = lax.dynamic_index_in_dim(trans_table, device, axis=1, keepdims=False)
    allow_here = jnp.any(allow_list == device, axis=1)
    dest_rows = jnp.sum(jnp.where(prompt_state[:, None] == state_ids, dest_here, 0), axis=1)
    allow_rows = jnp.any((prompt_state[:, None] == state_ids) & allow_here, axis=1)
    chooser = (dest_rows[:, None] == state_ids) & allow_rows[:, None]
    messages = lax.dynamic_slice_in_dim(beta_start, device * own_rows, own_rows, 0).T
    forward_all = forward_messages(emission, last_token, prior_msg, devices, device)
    own_sums = exchange(jnp.sum(emission, axis=1, dtype=jnp.float32).reshape(devices, own_rows))
    route = allowed.T[:, :, None] & (trans_table.T[:, :, None] == state_ids)
    route = route.astype(jnp.float32).reshape(devices * states, states)
    by_owner = transition.reshape(devices, own_rows, own_rows)
    for window_step in range(STEPS):
        selected = jnp.dot(route, messages, precision=lax.Precision.HIGHEST)
        selected = selected.reshape(devices, states, own_rows)
        emitted = jnp.sum(selected * own_sums[:, None, :], axis=0)
        halves = jnp.concatenate(split_outside(emitted), axis=0)
        partial = jnp.einsum("dzy,sy->dsz", by_owner, halves, preferred_element_type=jnp.float32)
        partial = partial[:, :states] + partial[:, states:]
        if window_step < STEPS - 1:
            partial = partial.astype(jnp.bfloat16)
        messages = jnp.sum(exchange(partial), axis=0, dtype=jnp.float32)
    everywhere = spread(messages, devices)
    chosen = jnp.einsum(
        "ps,dsz->pdz", chooser.astype(jnp.float32), everywhere, precision=lax.Precision.HIGHEST
    )
    forward_all = forward_all.reshape(prompts, devices, own_rows).astype(jnp.float32)
    scaled = (forward_all * chosen).astype(jnp.bfloat16).reshape(prompts, hidden)
    weights = jnp.dot(scaled, emission, preferred_element_type=jnp.float32)
    weights = jnp.where(allow_rows[:, None], weights, 0.0)
    logits = lm_logits.astype(jnp.float32)
    top_here = jnp.max(logits, axis=1)
    raised = jnp.exp(logits - top_here[:, None]) * weights
    pairs = spread(jnp.stack([top_here, jnp.sum(raised, axis=1)]), devices)
    tops, totals = pairs[:, 0], pairs[:, 1]
    top = jnp.max(tops, axis=0)
    total = jnp.sum(totals * jnp.exp(tops - top), axis=0)
    raised = raised * jnp.exp(top_here - top)[:, None]
    return (messages.T, BLK * devices * raised / total[:, None])


def solution(mesh):
    return jax.shard_map(
        per_device,
        mesh=mesh,
        in_specs=(
            P(None, "vocab"),
            P(None, "vocab"),
            P(),
            P(),
            P(),
            P("parts"),
            P("parts"),
            P(("parts", "vocab"), None),
            P("parts", "vocab"),
        ),
        out_specs=(P(("parts", "vocab"), None), P("parts", "vocab")),
        check_vma=False,
    )
```

```python
import functools

import jax
import jax.numpy as jnp
from jax import lax
from jax.experimental import pallas as pl
from jax.experimental.pallas import tpu as pltpu
from jax.sharding import PartitionSpec as P

BLK = 256
STEPS = 3
LIMIT = 16 * 1024 * 1024
VMEM = pl.BlockSpec(memory_space=pltpu.VMEM)
SMEM = pl.BlockSpec(memory_space=pltpu.SMEM)
ANY = pl.BlockSpec(memory_space=pl.ANY)
PARAMS = pltpu.CompilerParams(vmem_limit_bytes=LIMIT)


def exchange(blocks):
    return lax.all_to_all(blocks, "vocab", split_axis=0, concat_axis=0, tiled=True)


def spread(own, devices):
    return exchange(jnp.broadcast_to(own[None], (devices,) + own.shape))


def basis(count):
    return [1] + [(1 << bit) | 1 for bit in range(1, count)]


def swap(block, offset, devices):
    pairs = [(i, i ^ offset) for i in range(devices)]
    return lax.ppermute(block, "vocab", pairs)


def split_wide(wide):
    high = wide.astype(jnp.bfloat16)
    low = (wide - high.astype(jnp.float32)).astype(jnp.bfloat16)
    return high, low


def split_outside(wide):
    high = lax.reduce_precision(wide, exponent_bits=8, mantissa_bits=7)
    return high.astype(jnp.bfloat16), (wide - high).astype(jnp.bfloat16)


def split_three(wide):
    high = wide.astype(jnp.bfloat16)
    rest = wide - high.astype(jnp.float32)
    middle = rest.astype(jnp.bfloat16)
    low = (rest - middle.astype(jnp.float32)).astype(jnp.bfloat16)
    return high, middle, low


def dot_rows(left, right):
    return lax.dot_general(left, right, (((1,), (1,)), ((), ())), preferred_element_type=jnp.float32)


def partner_of(bits, count):
    partner = 0
    for bit, offset in zip(bits, basis(count)):
        partner ^= bit * offset
    return partner


def all_bits(count):
    return [tuple((k >> (count - 1 - b)) & 1 for b in range(count)) for k in range(1 << count)]


def square_partners(count):
    return [partner_of((0,) + bits, count) for bits in all_bits(2)]


def far_partners(count):
    return [partner_of((0, 0, 0) + bits, count) for bits in all_bits(count - 3)]


def half_places(count, first):
    return [
        ((q, h), first ^ near ^ far)
        for q, near in enumerate(square_partners(count))
        for h, far in enumerate(far_partners(count))
    ]


def partner_rows(i, rows):
    owner = lax.axis_index("vocab") ^ i
    return pl.ds(pl.multiple_of(owner * rows, rows), rows)


def pack(blocks, wide, extra):
    rows = blocks.reshape(-1, blocks.shape[-1])
    parts = split_outside(rows) if wide else (rows.astype(jnp.bfloat16),)
    return jnp.concatenate(parts + extra, axis=0)


def unpack(packed, shape, wide):
    size = shape[0] * shape[1]
    rows = packed[:size].astype(jnp.float32)
    if wide:
        rows += packed[size : 2 * size].astype(jnp.float32)
    return rows.reshape(shape)


def reduce_square(kept, received, wide, devices, count, extra=()):
    total = kept + received.astype(jnp.float32)
    near, extras = total[0], list(extra)
    for q, offset in enumerate(square_partners(count)):
        if q:
            packed = swap(pack(total[q], wide, extra), offset, devices)
            near += unpack(packed, total.shape[1:], wide)
            for rows in extra:
                extras.append(packed[-rows.shape[0] :])
    return near, extras


def reduce_far(near, devices, count, extra=()):
    blocks = [near[0]]
    for h, offset in enumerate(far_partners(count)):
        if h:
            blocks.append(swap(pack(near[h], False, extra), offset, devices))
    return blocks


def gather_square(far, devices, count):
    near = jnp.stack([far] + [swap(far, offset, devices) for offset in square_partners(count)[1:]])
    return near, swap(near, 1, devices)


def column_of(scalars_ref, shape):
    row = lax.broadcasted_iota(jnp.int32, shape, 0)
    column = jnp.zeros(shape, jnp.int32)
    for k in range(shape[0]):
        column = jnp.where(row == k, scalars_ref[k], column)
    return column


def tables_kernel(
    count, state_ref, allow_ref, table_ref, emission_ref, sums_in_ref,
    route_ref, chooser_ref, sums_ref,
):
    device = lax.axis_index("vocab")
    devices = 1 << count
    states = table_ref.shape[0]
    sums_ref[...] = sums_in_ref[...]
    allow, table = allow_ref[...], table_ref[...]
    hits = [jnp.max((allow == b).astype(jnp.float32), axis=0, keepdims=True) for b in range(devices)]
    shape = (states, states)
    diagonal = [lax.broadcasted_iota(jnp.int32, shape, axis) for axis in (0, 1)]
    diagonal = (diagonal[0] == diagonal[1]).astype(jnp.bfloat16)
    hits = dot_rows(diagonal, jnp.concatenate(hits, axis=0).astype(jnp.bfloat16))
    ids = lax.broadcasted_iota(jnp.int32, shape, 1)
    own_step = jnp.zeros(shape, jnp.float32)
    for b in range(devices):
        step = jnp.where(table[:, b : b + 1] == ids, hits[:, b : b + 1], 0.0)
        own_step = jnp.where(device == b, step, own_step)
        step = step.astype(jnp.bfloat16)
        route_ref[pl.ds(b * states, states)] = jnp.concatenate([step] * 3, axis=1)
    shape = (states, devices)
    prompts = state_ref[...] == lax.broadcasted_iota(jnp.int32, shape, 0)
    chooser = lax.dot_general(
        prompts.astype(jnp.bfloat16),
        own_step.astype(jnp.bfloat16),
        (((0,), (0,)), ((), ())),
        preferred_element_type=jnp.float32,
    ).astype(jnp.bfloat16)
    chooser_ref[...] = jnp.concatenate([chooser] * 3, axis=1)


def tables(state, allow, table, emission, sums, count):
    devices, states = 1 << count, table.shape[0]
    return pl.pallas_call(
        functools.partial(tables_kernel, count),
        out_shape=[
            pltpu.VMEM((devices * states, 3 * states), jnp.bfloat16),
            pltpu.VMEM((devices, 3 * states), jnp.bfloat16),
            jax.ShapeDtypeStruct(sums.shape, sums.dtype),
        ],
        in_specs=[VMEM] * 5,
        out_specs=[VMEM] * 3,
        compiler_params=PARAMS,
        name="tables",
    )(state, allow, table, emission, sums)


def products_kernel(
    count, token_hbm, state_hbm, allow_hbm, table_hbm, start_hbm, emission_ref,
    sums_ref, kept_ref, sent_ref, state_ref, allow_ref, table_ref, messages_ref,
    token_ref, columns_ref, sems,
):
    device = lax.axis_index("vocab")
    devices = 1 << count
    rows = emission_ref.shape[0] >> count
    own = pl.ds(pl.multiple_of(device * rows, rows), rows)
    pairs = [
        (token_hbm, token_ref), (state_hbm, state_ref), (allow_hbm, allow_ref),
        (table_hbm, table_ref), (start_hbm.at[:, own], messages_ref),
    ]
    copies = [
        pltpu.make_async_copy(source, to, sems.at[k]) for k, (source, to) in enumerate(pairs)
    ]
    for copy in copies:
        copy.start()
    shape = (devices * devices // 2, devices * devices)
    to, source = (lax.broadcasted_iota(jnp.int32, shape, axis) for axis in (0, 1))
    same_block = (to & (devices - 1)) == (source >> count)
    orders = []
    for first in range(2):
        prompt = partner_at((to >> count) + first * (devices // 2), count)
        onehot = same_block & ((source & (devices - 1)) == prompt)
        orders.append(onehot.astype(jnp.bfloat16))
    copies[0].wait()
    shape = (devices, BLK)
    tokens = column_of(token_ref, shape) - device * BLK
    onehot = (tokens == lax.broadcasted_iota(jnp.int32, shape, 1)).astype(jnp.bfloat16)
    left = jnp.concatenate([onehot, jnp.ones((16, BLK), jnp.bfloat16)], axis=0)
    for k in range(devices):
        product = dot_rows(left, emission_ref[pl.ds(k * rows, rows)])
        columns_ref[pl.ds(k * devices, devices)] = product[:devices].astype(jnp.bfloat16)
        sums_ref[k] = product[devices : devices + 1]
    for order, out_ref in zip(orders, (kept_ref, sent_ref)):
        ordered = jnp.dot(order, columns_ref[...], preferred_element_type=jnp.float32)
        out_ref[...] = ordered.astype(jnp.bfloat16).reshape(out_ref.shape)
    for copy in copies[1:]:
        copy.wait()


def first_products(last_token, prompt_state, allow_list, trans_table, beta_start, emission, count):
    devices, rows = 1 << count, emission.shape[0] >> count
    half = pltpu.VMEM((4, devices // 8, devices, rows), jnp.bfloat16)
    small = (prompt_state[None], allow_list.T, trans_table)
    operands = (last_token,) + small + (beta_start.T,)
    return pl.pallas_call(
        functools.partial(products_kernel, count),
        out_shape=[jax.ShapeDtypeStruct((devices, 1, rows), jnp.float32), half, half]
        + [pltpu.VMEM(array.shape, array.dtype) for array in small]
        + [pltpu.VMEM((beta_start.shape[1], rows), jnp.float32)],
        in_specs=[ANY] * len(operands) + [VMEM],
        out_specs=[VMEM] * 7,
        scratch_shapes=[
            pltpu.SMEM(last_token.shape, jnp.int32),
            pltpu.VMEM((devices * devices, rows), jnp.bfloat16),
            pltpu.SemaphoreType.DMA((len(operands),)),
        ],
        compiler_params=PARAMS,
        name="first_products",
    )(*(in_hbm(operand) for operand in operands), emission)


def in_hbm(array):
    return pltpu.with_memory_space_constraint(array, pltpu.HBM)


def forward_kernel(prior_ref, *refs):
    blocks, out_ref = refs[:-1], refs[-1]
    devices, rows = out_ref.shape
    columns = blocks[0][-devices:]
    for block in blocks[1:]:
        columns += block[-devices:].astype(jnp.float32)
    prior = jnp.concatenate([prior_ref[:, pl.ds(k * rows, rows)] for k in range(devices)], axis=0)
    unnormal = prior * columns
    out_ref[...] = (unnormal / jnp.sum(unnormal)).astype(jnp.bfloat16)


def forward_messages_here(prior, blocks, devices):
    return pl.pallas_call(
        forward_kernel,
        out_shape=pltpu.VMEM((devices, blocks[0].shape[1]), jnp.bfloat16),
        in_specs=[VMEM] * (1 + len(blocks)),
        out_specs=VMEM,
        compiler_params=PARAMS,
        name="forward_messages",
    )(prior, *blocks)


def partner_at(place, count):
    number = jnp.zeros_like(place)
    for bit, offset in enumerate(basis(count)):
        number = number ^ (((place >> (count - 1 - bit)) & 1) * offset)
    return lax.axis_index("vocab") ^ number


def order_kernel(count, near_ref, far_ref, out_ref):
    size = 1 << count
    shape = (size * size, size * size)
    to, source = (lax.broadcasted_iota(jnp.int32, shape, axis) for axis in (0, 1))
    same_block = partner_at(to >> count, count) == (source & (size - 1))
    same_prompt = (to & (size - 1)) == partner_at(source >> count, count)
    onehot = (same_block & same_prompt).astype(jnp.bfloat16)
    half = size * size // 2
    rows = out_ref.shape[1]
    near = near_ref[...].reshape(half, rows)
    far = far_ref[...].reshape(half, rows)
    ordered = jnp.dot(onehot[:, :half], near, preferred_element_type=jnp.float32)
    ordered += jnp.dot(onehot[:, half:], far, preferred_element_type=jnp.float32)
    out_ref[...] = ordered.astype(jnp.bfloat16)


def order_forward(near, far, count):
    rows = near.shape[-1]
    return pl.pallas_call(
        functools.partial(order_kernel, count),
        out_shape=pltpu.VMEM((1 << (2 * count), rows), jnp.bfloat16),
        in_specs=[VMEM] * 2,
        out_specs=VMEM,
        compiler_params=PARAMS,
        name="order_forward",
    )(near, far)


def last_kernel(near_ref, *refs):
    blocks, out_ref = refs[:-2], refs[-1]
    count, states, _ = out_ref.shape
    for h in range(count):
        messages = near_ref[h]
        for g, block in enumerate(blocks, 1):
            for part in range(2):
                start = (part * count + (h ^ g)) * states
                messages += block[pl.ds(start, states)].astype(jnp.float32)
        out_ref[h] = messages


def last_sum(near, after, devices, count):
    packed = pack(near, True, ())
    blocks = [swap(packed, offset, devices) for offset in far_partners(count)[1:]]
    return pl.pallas_call(
        last_kernel,
        out_shape=pltpu.VMEM(near.shape, jnp.float32),
        in_specs=[VMEM] * (1 + len(blocks)) + [ANY],
        out_specs=VMEM,
        compiler_params=PARAMS,
        name="last_messages",
    )(near, *blocks, after)


def half_products(halves, transition_ref, out_ref, count, first):
    states = halves.shape[0] // 2
    rows = transition_ref.shape[0] >> count
    for place, partner in half_places(count, first):
        product = dot_rows(halves, transition_ref[partner_rows(partner, rows)])
        product = product[:states] + product[states:]
        out_ref[place + (pl.ds(0, states),)] = product.astype(out_ref.dtype)


def add_rows(out_ref, states, extra):
    for ref in extra:
        rows = pl.ds(states, ref.shape[2])
        for place in ((y, k) for y in range(ref.shape[0]) for k in range(ref.shape[1])):
            out_ref[place + (rows,)] = ref[place].astype(out_ref.dtype)


def send_kernel(count, number, transition_ref, route_ref, sums_ref, *refs):
    parts, extra, (halves_ref, out_ref) = refs[:number], refs[number:-2], refs[-2:]
    states = halves_ref.shape[0] // 2
    messages = parts[0][:states].astype(jnp.float32)
    for part in parts[1:]:
        messages += part[:states].astype(jnp.float32)
    selected = jnp.dot(
        route_ref[...],
        jnp.concatenate(split_three(messages), axis=0),
        preferred_element_type=jnp.float32,
    )
    emitted = selected[:states] * sums_ref[0]
    for b in range(1, 1 << count):
        emitted += selected[b * states : (b + 1) * states] * sums_ref[b]
    halves = jnp.concatenate(split_wide(emitted), axis=0)
    halves_ref[...] = halves
    half_products(halves, transition_ref, out_ref, count, 1)
    add_rows(out_ref, states, extra)


def keep_kernel(count, transition_ref, halves_ref, *refs):
    extra, out_ref = refs[:-1], refs[-1]
    half_products(halves_ref[...], transition_ref, out_ref, count, 0)
    add_rows(out_ref, halves_ref.shape[0] // 2, extra)


def step(transition, route, sums, parts, dtype, devices, count, kept_rows=(), sent_rows=()):
    states, rows = route.shape[0] // devices, parts[0].shape[1]
    total = states + sum(block.shape[2] for block in kept_rows)
    shape = (4, devices // 8, total, rows)
    halves, sent = pl.pallas_call(
        functools.partial(send_kernel, count, len(parts)),
        out_shape=[
            pltpu.VMEM((2 * states, rows), jnp.bfloat16),
            pltpu.VMEM(shape, dtype),
        ],
        in_specs=[VMEM] * (3 + len(parts) + len(sent_rows)),
        out_specs=[VMEM] * 2,
        compiler_params=PARAMS,
        name="step_sent_half",
    )(transition, route, sums, *parts, *sent_rows)
    received = swap(sent, 1, devices)
    kept = pl.pallas_call(
        functools.partial(keep_kernel, count),
        out_shape=pltpu.VMEM(shape, jnp.float32),
        in_specs=[VMEM] * (2 + len(kept_rows)),
        out_specs=VMEM,
        compiler_params=PARAMS,
        name="step_kept_half",
    )(transition, halves, *kept_rows)
    return kept, received


def weigh_half(emission_ref, forward_ref, chooser, parts_ref, count, first):
    rows = emission_ref.shape[0] >> count
    prompts = chooser.shape[0]
    weights = jnp.zeros((prompts, emission_ref.shape[1]), jnp.float32)
    for order, (place, partner) in enumerate(half_places(count, first)):
        pieces = jnp.concatenate(split_three(parts_ref[place]), axis=0)
        chosen = jnp.dot(chooser, pieces, preferred_element_type=jnp.float32)
        block = order + (first << (count - 1))
        forward = forward_ref[pl.ds(block * prompts, prompts)].astype(jnp.float32)
        scaled = (forward * chosen).astype(jnp.bfloat16)
        tile = emission_ref[partner_rows(partner, rows)]
        weights += jnp.dot(scaled, tile, preferred_element_type=jnp.float32)
    return weights


def near_kernel(count, emission_ref, forward_ref, chooser_ref, parts_ref, out_ref):
    out_ref[...] = weigh_half(emission_ref, forward_ref, chooser_ref[...], parts_ref, count, 0)


def far_kernel(count, emission_ref, forward_ref, chooser_ref, logits_ref, near_ref, parts_ref, raised_ref, pair_ref):
    chooser = chooser_ref[...]
    logits = logits_ref[...].astype(jnp.float32)
    top = jnp.max(logits, axis=1, keepdims=True)
    weights = near_ref[...] + weigh_half(emission_ref, forward_ref, chooser, parts_ref, count, 1)
    allowed = jnp.sum(chooser.astype(jnp.float32), axis=1, keepdims=True) > 0
    raised = jnp.where(allowed, jnp.exp(logits - top) * weights, 0.0)
    raised_ref[...] = raised
    total = jnp.sum(raised, axis=1, keepdims=True)
    lane = lax.broadcasted_iota(jnp.int32, pair_ref.shape, 1)
    pair_ref[...] = jnp.where(lane == 0, top, total)


def weigh(emission, forward, chooser, logits, near, far, count):
    half = pl.pallas_call(
        functools.partial(near_kernel, count),
        out_shape=pltpu.VMEM(logits.shape, jnp.float32),
        in_specs=[VMEM] * 4,
        out_specs=VMEM,
        compiler_params=PARAMS,
        name="weigh_near",
    )(emission, forward, chooser, near)
    return pl.pallas_call(
        functools.partial(far_kernel, count),
        out_shape=[
            pltpu.VMEM(logits.shape, jnp.float32),
            pltpu.VMEM((logits.shape[0], 128), jnp.float32),
        ],
        in_specs=[VMEM] * 6,
        out_specs=[VMEM] * 2,
        compiler_params=PARAMS,
        name="weigh_far",
    )(emission, forward, chooser, logits, half, far)


def normalise(raised, pair, devices):
    pairs = spread(pair[:, :2].T, devices)
    own_top = pair[:, :1]
    tops, totals = pairs[:, 0], pairs[:, 1]
    top = jnp.max(tops, axis=0)
    total = jnp.sum(totals * jnp.exp(tops - top), axis=0)
    return BLK * devices * (raised * jnp.exp(own_top - top[:, None])) / total[:, None]


def forward_messages(emission, last_token, prior_msg, devices, device):
    hidden = emission.shape[0]
    local_rows = prior_msg.shape[0]
    token_ids = jnp.arange(BLK, dtype=jnp.int32)
    tokens = last_token - device * BLK
    onehot = (tokens[:, None] == token_ids[None, :]).astype(jnp.bfloat16)
    owned = dot_rows(onehot, emission)
    owned = owned.astype(jnp.bfloat16).reshape(devices, local_rows, hidden)
    columns = jnp.sum(exchange(owned), axis=0, dtype=jnp.float32)
    unnormal = prior_msg * columns
    forward_msg = (unnormal / jnp.sum(unnormal, axis=1, keepdims=True)).astype(jnp.bfloat16)
    return spread(forward_msg, devices).reshape(devices * local_rows, hidden)


def per_device(
    emission,
    transition,
    beta_start,
    allow_list,
    trans_table,
    last_token,
    prompt_state,
    prior_msg,
    lm_logits,
):
    devices = lax.axis_size("vocab")
    device = lax.axis_index("vocab")
    hidden = emission.shape[0]
    states = beta_start.shape[1]
    own_rows = transition.shape[1]
    prompts = prompt_state.shape[0]
    count = devices.bit_length() - 1
    if devices == 1 << count and count > 2 and own_rows % 128 == 0 and prompts == devices:
        sums, columns, columns_out, state, allow, table, messages = first_products(
            last_token, prompt_state, allow_list, trans_table, beta_start, emission, count
        )
        route, chooser, sums = tables(state, allow, table, emission, sums, count)
        sums = exchange(sums)
        parts, kept_rows, sent_rows = [messages], (columns,), (columns_out,)
        for window_step in range(STEPS):
            wide = window_step == STEPS - 1
            dtype = jnp.float32 if wide else jnp.bfloat16
            kept, received = step(
                transition, route, sums, parts, dtype, devices, count, kept_rows, sent_rows
            )
            kept_rows, sent_rows, extra = (), (), ()
            if window_step == 1:
                forward = forward_messages_here(prior_msg, parts, devices)
            if window_step == 2:
                extra = (forward,)
            near, extras = reduce_square(kept, received, wide, devices, count, extra)
            if window_step == 0:
                parts = reduce_far(near, devices, count)
            if window_step == 1:
                parts = reduce_far(near, devices, count, (forward,))
                others = [part[-devices:] for part in parts[1:]]
                forward = jnp.concatenate([forward] + others, axis=0)
        forward = jnp.stack(extras).reshape(4, devices // 8, devices, own_rows)
        forward = order_forward(forward, swap(forward, 1, devices), count)
        messages = last_sum(near, forward, devices, count)
        near, far = gather_square(messages, devices, count)
        messages = messages[0]
        raised, pair = weigh(emission, forward, chooser, lm_logits, near, far, count)
        return messages.T, normalise(raised, pair, devices)
    state_ids = jnp.arange(states, dtype=jnp.int32)
    block_ids = jnp.arange(devices, dtype=jnp.int32)
    allowed = jnp.any(allow_list[:, :, None] == block_ids, axis=1)
    dest_here = lax.dynamic_index_in_dim(trans_table, device, axis=1, keepdims=False)
    allow_here = jnp.any(allow_list == device, axis=1)
    dest_rows = jnp.sum(jnp.where(prompt_state[:, None] == state_ids, dest_here, 0), axis=1)
    allow_rows = jnp.any((prompt_state[:, None] == state_ids) & allow_here, axis=1)
    chooser = (dest_rows[:, None] == state_ids) & allow_rows[:, None]
    messages = lax.dynamic_slice_in_dim(beta_start, device * own_rows, own_rows, 0).T
    forward_all = forward_messages(emission, last_token, prior_msg, devices, device)
    own_sums = exchange(jnp.sum(emission, axis=1, dtype=jnp.float32).reshape(devices, own_rows))
    route = allowed.T[:, :, None] & (trans_table.T[:, :, None] == state_ids)
    route = route.astype(jnp.float32).reshape(devices * states, states)
    by_owner = transition.reshape(devices, own_rows, own_rows)
    for window_step in range(STEPS):
        selected = jnp.dot(route, messages, precision=lax.Precision.HIGHEST)
        selected = selected.reshape(devices, states, own_rows)
        emitted = jnp.sum(selected * own_sums[:, None, :], axis=0)
        halves = jnp.concatenate(split_outside(emitted), axis=0)
        partial = jnp.einsum("dzy,sy->dsz", by_owner, halves, preferred_element_type=jnp.float32)
        partial = partial[:, :states] + partial[:, states:]
        if window_step < STEPS - 1:
            partial = partial.astype(jnp.bfloat16)
        messages = jnp.sum(exchange(partial), axis=0, dtype=jnp.float32)
    everywhere = spread(messages, devices)
    chosen = jnp.einsum(
        "ps,dsz->pdz", chooser.astype(jnp.float32), everywhere, precision=lax.Precision.HIGHEST
    )
    forward_all = forward_all.reshape(prompts, devices, own_rows).astype(jnp.float32)
    scaled = (forward_all * chosen).astype(jnp.bfloat16).reshape(prompts, hidden)
    weights = jnp.dot(scaled, emission, preferred_element_type=jnp.float32)
    weights = jnp.where(allow_rows[:, None], weights, 0.0)
    logits = lm_logits.astype(jnp.float32)
    top_here = jnp.max(logits, axis=1)
    raised = jnp.exp(logits - top_here[:, None]) * weights
    pairs = spread(jnp.stack([top_here, jnp.sum(raised, axis=1)]), devices)
    tops, totals = pairs[:, 0], pairs[:, 1]
    top = jnp.max(tops, axis=0)
    total = jnp.sum(totals * jnp.exp(tops - top), axis=0)
    raised = raised * jnp.exp(top_here - top)[:, None]
    return (messages.T, BLK * devices * raised / total[:, None])


def solution(mesh):
    return jax.shard_map(
        per_device,
        mesh=mesh,
        in_specs=(
            P(None, "vocab"),
            P(None, "vocab"),
            P(),
            P(),
            P(),
            P("parts"),
            P("parts"),
            P(("parts", "vocab"), None),
            P("parts", "vocab"),
        ),
        out_specs=(P(("parts", "vocab"), None), P("parts", "vocab")),
        check_vma=False,
    )
```

```python
import functools

import jax
import jax.numpy as jnp
from jax import lax
from jax.experimental import pallas as pl
from jax.experimental.pallas import tpu as pltpu
from jax.sharding import PartitionSpec as P

BLK = 256
STEPS = 3
LIMIT = 16 * 1024 * 1024
VMEM = pl.BlockSpec(memory_space=pltpu.VMEM)
SMEM = pl.BlockSpec(memory_space=pltpu.SMEM)
ANY = pl.BlockSpec(memory_space=pl.ANY)
PARAMS = pltpu.CompilerParams(vmem_limit_bytes=LIMIT)


def exchange(blocks):
    return lax.all_to_all(blocks, "vocab", split_axis=0, concat_axis=0, tiled=True)


def spread(own, devices):
    return exchange(jnp.broadcast_to(own[None], (devices,) + own.shape))


def basis(count):
    return [1] + [(1 << bit) | 1 for bit in range(1, count)]


def swap(block, offset, devices):
    pairs = [(i, i ^ offset) for i in range(devices)]
    return lax.ppermute(block, "vocab", pairs)


def split_wide(wide):
    high = wide.astype(jnp.bfloat16)
    low = (wide - high.astype(jnp.float32)).astype(jnp.bfloat16)
    return high, low


def split_outside(wide):
    high = lax.reduce_precision(wide, exponent_bits=8, mantissa_bits=7)
    return high.astype(jnp.bfloat16), (wide - high).astype(jnp.bfloat16)


def split_three(wide):
    high = wide.astype(jnp.bfloat16)
    rest = wide - high.astype(jnp.float32)
    middle = rest.astype(jnp.bfloat16)
    low = (rest - middle.astype(jnp.float32)).astype(jnp.bfloat16)
    return high, middle, low


def dot_rows(left, right):
    return lax.dot_general(left, right, (((1,), (1,)), ((), ())), preferred_element_type=jnp.float32)


def partner_of(bits, count):
    partner = 0
    for bit, offset in zip(bits, basis(count)):
        partner ^= bit * offset
    return partner


def all_bits(count):
    return [tuple((k >> (count - 1 - b)) & 1 for b in range(count)) for k in range(1 << count)]


def square_partners(count):
    return [partner_of((0,) + bits, count) for bits in all_bits(2)]


def far_partners(count):
    return [partner_of((0, 0, 0) + bits, count) for bits in all_bits(count - 3)]


def half_places(count, first):
    return [
        ((q, h), first ^ near ^ far)
        for q, near in enumerate(square_partners(count))
        for h, far in enumerate(far_partners(count))
    ]


def partner_rows(i, rows):
    owner = lax.axis_index("vocab") ^ i
    return pl.ds(pl.multiple_of(owner * rows, rows), rows)


def pack(blocks, wide, extra):
    rows = blocks.reshape(-1, blocks.shape[-1])
    parts = split_outside(rows) if wide else (rows.astype(jnp.bfloat16),)
    return jnp.concatenate(parts + extra, axis=0)


def unpack(packed, shape, wide):
    size = shape[0] * shape[1]
    rows = packed[:size].astype(jnp.float32)
    if wide:
        rows += packed[size : 2 * size].astype(jnp.float32)
    return rows.reshape(shape)


def reduce_square(kept, received, wide, devices, count, extra=()):
    total = kept + received.astype(jnp.float32)
    near, extras = total[0], list(extra)
    for q, offset in enumerate(square_partners(count)):
        if q:
            packed = swap(pack(total[q], wide, extra), offset, devices)
            near += unpack(packed, total.shape[1:], wide)
            for rows in extra:
                extras.append(packed[-rows.shape[0] :])
    return near, extras


def reduce_far(near, devices, count, extra=()):
    blocks = [near[0]]
    for h, offset in enumerate(far_partners(count)):
        if h:
            blocks.append(swap(pack(near[h], False, extra), offset, devices))
    return blocks


def column_of(scalars_ref, shape):
    row = lax.broadcasted_iota(jnp.int32, shape, 0)
    column = jnp.zeros(shape, jnp.int32)
    for k in range(shape[0]):
        column = jnp.where(row == k, scalars_ref[k], column)
    return column


def tables_kernel(
    count, state_ref, allow_ref, table_ref, emission_ref, sums_in_ref,
    route_ref, chooser_ref, sums_ref,
):
    device = lax.axis_index("vocab")
    devices = 1 << count
    states = table_ref.shape[0]
    sums_ref[...] = sums_in_ref[...]
    allow, table = allow_ref[...], table_ref[...]
    hits = [jnp.max((allow == b).astype(jnp.float32), axis=0, keepdims=True) for b in range(devices)]
    shape = (states, states)
    diagonal = [lax.broadcasted_iota(jnp.int32, shape, axis) for axis in (0, 1)]
    diagonal = (diagonal[0] == diagonal[1]).astype(jnp.bfloat16)
    hits = dot_rows(diagonal, jnp.concatenate(hits, axis=0).astype(jnp.bfloat16))
    ids = lax.broadcasted_iota(jnp.int32, shape, 1)
    own_step = jnp.zeros(shape, jnp.float32)
    for b in range(devices):
        step = jnp.where(table[:, b : b + 1] == ids, hits[:, b : b + 1], 0.0)
        own_step = jnp.where(device == b, step, own_step)
        step = step.astype(jnp.bfloat16)
        route_ref[pl.ds(b * states, states)] = jnp.concatenate([step] * 3, axis=1)
    shape = (states, devices)
    prompts = state_ref[...] == lax.broadcasted_iota(jnp.int32, shape, 0)
    chooser = lax.dot_general(
        prompts.astype(jnp.bfloat16),
        own_step.astype(jnp.bfloat16),
        (((0,), (0,)), ((), ())),
        preferred_element_type=jnp.float32,
    ).astype(jnp.bfloat16)
    chooser_ref[...] = jnp.concatenate([chooser] * 3, axis=1)


def tables(state, allow, table, emission, sums, count):
    devices, states = 1 << count, table.shape[0]
    return pl.pallas_call(
        functools.partial(tables_kernel, count),
        out_shape=[
            pltpu.VMEM((devices * states, 3 * states), jnp.bfloat16),
            pltpu.VMEM((devices, 3 * states), jnp.bfloat16),
            jax.ShapeDtypeStruct(sums.shape, sums.dtype),
        ],
        in_specs=[VMEM] * 5,
        out_specs=[VMEM] * 3,
        compiler_params=PARAMS,
        name="tables",
    )(state, allow, table, emission, sums)


def products_kernel(
    count, token_hbm, state_hbm, allow_hbm, table_hbm, start_hbm, emission_ref,
    sums_ref, kept_ref, sent_ref, state_ref, allow_ref, table_ref, messages_ref,
    token_ref, columns_ref, sems,
):
    device = lax.axis_index("vocab")
    devices = 1 << count
    rows = emission_ref.shape[0] >> count
    own = pl.ds(pl.multiple_of(device * rows, rows), rows)
    pairs = [
        (token_hbm, token_ref), (state_hbm, state_ref), (allow_hbm, allow_ref),
        (table_hbm, table_ref), (start_hbm.at[:, own], messages_ref),
    ]
    copies = [
        pltpu.make_async_copy(source, to, sems.at[k]) for k, (source, to) in enumerate(pairs)
    ]
    for copy in copies:
        copy.start()
    shape = (devices * devices // 2, devices * devices)
    to, source = (lax.broadcasted_iota(jnp.int32, shape, axis) for axis in (0, 1))
    same_block = (to & (devices - 1)) == (source >> count)
    orders = []
    for first in range(2):
        prompt = partner_at((to >> count) + first * (devices // 2), count)
        onehot = same_block & ((source & (devices - 1)) == prompt)
        orders.append(onehot.astype(jnp.bfloat16))
    copies[0].wait()
    shape = (devices, BLK)
    tokens = column_of(token_ref, shape) - device * BLK
    onehot = (tokens == lax.broadcasted_iota(jnp.int32, shape, 1)).astype(jnp.bfloat16)
    left = jnp.concatenate([onehot, jnp.ones((16, BLK), jnp.bfloat16)], axis=0)
    for k in range(devices):
        product = dot_rows(left, emission_ref[pl.ds(k * rows, rows)])
        columns_ref[pl.ds(k * devices, devices)] = product[:devices].astype(jnp.bfloat16)
        sums_ref[k] = product[devices : devices + 1]
    for order, out_ref in zip(orders, (kept_ref, sent_ref)):
        ordered = jnp.dot(order, columns_ref[...], preferred_element_type=jnp.float32)
        out_ref[...] = ordered.astype(jnp.bfloat16).reshape(out_ref.shape)
    for copy in copies[1:]:
        copy.wait()


def first_products(last_token, prompt_state, allow_list, trans_table, beta_start, emission, count):
    devices, rows = 1 << count, emission.shape[0] >> count
    half = pltpu.VMEM((4, devices // 8, devices, rows), jnp.bfloat16)
    small = (prompt_state[None], allow_list.T, trans_table)
    operands = (last_token,) + small + (beta_start.T,)
    return pl.pallas_call(
        functools.partial(products_kernel, count),
        out_shape=[jax.ShapeDtypeStruct((devices, 1, rows), jnp.float32), half, half]
        + [pltpu.VMEM(array.shape, array.dtype) for array in small]
        + [pltpu.VMEM((beta_start.shape[1], rows), jnp.float32)],
        in_specs=[ANY] * len(operands) + [VMEM],
        out_specs=[VMEM] * 7,
        scratch_shapes=[
            pltpu.SMEM(last_token.shape, jnp.int32),
            pltpu.VMEM((devices * devices, rows), jnp.bfloat16),
            pltpu.SemaphoreType.DMA((len(operands),)),
        ],
        compiler_params=PARAMS,
        name="first_products",
    )(*(in_hbm(operand) for operand in operands), emission)


def in_hbm(array):
    return pltpu.with_memory_space_constraint(array, pltpu.HBM)


def forward_kernel(prior_ref, *refs):
    blocks, out_ref = refs[:-1], refs[-1]
    devices, rows = out_ref.shape
    columns = blocks[0][-devices:]
    for block in blocks[1:]:
        columns += block[-devices:].astype(jnp.float32)
    prior = jnp.concatenate([prior_ref[:, pl.ds(k * rows, rows)] for k in range(devices)], axis=0)
    unnormal = prior * columns
    out_ref[...] = (unnormal / jnp.sum(unnormal)).astype(jnp.bfloat16)


def forward_messages_here(prior, blocks, devices):
    return pl.pallas_call(
        forward_kernel,
        out_shape=pltpu.VMEM((devices, blocks[0].shape[1]), jnp.bfloat16),
        in_specs=[VMEM] * (1 + len(blocks)),
        out_specs=VMEM,
        compiler_params=PARAMS,
        name="forward_messages",
    )(prior, *blocks)


def partner_at(place, count):
    number = jnp.zeros_like(place)
    for bit, offset in enumerate(basis(count)):
        number = number ^ (((place >> (count - 1 - bit)) & 1) * offset)
    return lax.axis_index("vocab") ^ number


def order_kernel(count, near_ref, far_ref, out_ref):
    size = 1 << count
    shape = (size * size, size * size)
    to, source = (lax.broadcasted_iota(jnp.int32, shape, axis) for axis in (0, 1))
    same_block = partner_at(to >> count, count) == (source & (size - 1))
    same_prompt = (to & (size - 1)) == partner_at(source >> count, count)
    onehot = (same_block & same_prompt).astype(jnp.bfloat16)
    half = size * size // 2
    rows = out_ref.shape[1]
    near = near_ref[...].reshape(half, rows)
    far = far_ref[...].reshape(half, rows)
    ordered = jnp.dot(onehot[:, :half], near, preferred_element_type=jnp.float32)
    ordered += jnp.dot(onehot[:, half:], far, preferred_element_type=jnp.float32)
    out_ref[...] = ordered.astype(jnp.bfloat16)


def order_forward(near, far, count):
    rows = near.shape[-1]
    return pl.pallas_call(
        functools.partial(order_kernel, count),
        out_shape=pltpu.VMEM((1 << (2 * count), rows), jnp.bfloat16),
        in_specs=[VMEM] * 2,
        out_specs=VMEM,
        compiler_params=PARAMS,
        name="order_forward",
    )(near, far)


def last_kernel(near_ref, *refs):
    blocks, out_ref = refs[:-2], refs[-1]
    count, states, _ = out_ref.shape
    for h in range(count):
        messages = near_ref[h]
        for g, block in enumerate(blocks, 1):
            for part in range(2):
                start = (part * count + (h ^ g)) * states
                messages += block[pl.ds(start, states)].astype(jnp.float32)
        out_ref[h] = messages


def last_sum(near, after, devices, count):
    packed = pack(near, True, ())
    blocks = [swap(packed, offset, devices) for offset in far_partners(count)[1:]]
    return pl.pallas_call(
        last_kernel,
        out_shape=pltpu.VMEM(near.shape, jnp.float32),
        in_specs=[VMEM] * (1 + len(blocks)) + [ANY],
        out_specs=VMEM,
        compiler_params=PARAMS,
        name="last_messages",
    )(near, *blocks, after)


def half_products(halves, transition_ref, out_ref, count, first):
    states = halves.shape[0] // 2
    rows = transition_ref.shape[0] >> count
    for place, partner in half_places(count, first):
        product = dot_rows(halves, transition_ref[partner_rows(partner, rows)])
        product = product[:states] + product[states:]
        out_ref[place + (pl.ds(0, states),)] = product.astype(out_ref.dtype)


def add_rows(out_ref, states, extra):
    for ref in extra:
        rows = pl.ds(states, ref.shape[2])
        for place in ((y, k) for y in range(ref.shape[0]) for k in range(ref.shape[1])):
            out_ref[place + (rows,)] = ref[place].astype(out_ref.dtype)


def send_kernel(count, number, transition_ref, route_ref, sums_ref, *refs):
    parts, extra, (halves_ref, out_ref) = refs[:number], refs[number:-2], refs[-2:]
    states = halves_ref.shape[0] // 2
    messages = parts[0][:states].astype(jnp.float32)
    for part in parts[1:]:
        messages += part[:states].astype(jnp.float32)
    selected = jnp.dot(
        route_ref[...],
        jnp.concatenate(split_three(messages), axis=0),
        preferred_element_type=jnp.float32,
    )
    emitted = selected[:states] * sums_ref[0]
    for b in range(1, 1 << count):
        emitted += selected[b * states : (b + 1) * states] * sums_ref[b]
    halves = jnp.concatenate(split_wide(emitted), axis=0)
    halves_ref[...] = halves
    half_products(halves, transition_ref, out_ref, count, 1)
    add_rows(out_ref, states, extra)


def keep_kernel(count, transition_ref, halves_ref, *refs):
    extra, out_ref = refs[:-1], refs[-1]
    half_products(halves_ref[...], transition_ref, out_ref, count, 0)
    add_rows(out_ref, halves_ref.shape[0] // 2, extra)


def step(transition, route, sums, parts, dtype, devices, count, kept_rows=(), sent_rows=()):
    states, rows = route.shape[0] // devices, parts[0].shape[1]
    total = states + sum(block.shape[2] for block in kept_rows)
    shape = (4, devices // 8, total, rows)
    halves, sent = pl.pallas_call(
        functools.partial(send_kernel, count, len(parts)),
        out_shape=[
            pltpu.VMEM((2 * states, rows), jnp.bfloat16),
            pltpu.VMEM(shape, dtype),
        ],
        in_specs=[VMEM] * (3 + len(parts) + len(sent_rows)),
        out_specs=[VMEM] * 2,
        compiler_params=PARAMS,
        name="step_sent_half",
    )(transition, route, sums, *parts, *sent_rows)
    received = swap(sent, 1, devices)
    kept = pl.pallas_call(
        functools.partial(keep_kernel, count),
        out_shape=pltpu.VMEM(shape, jnp.float32),
        in_specs=[VMEM] * (2 + len(kept_rows)),
        out_specs=VMEM,
        compiler_params=PARAMS,
        name="step_kept_half",
    )(transition, halves, *kept_rows)
    return kept, received


def weigh_blocks(emission_ref, forward_ref, chooser, parts_ref, count, first, squares):
    rows = emission_ref.shape[0] >> count
    prompts = chooser.shape[0]
    weights = jnp.zeros((prompts, emission_ref.shape[1]), jnp.float32)
    for order, ((q, h), partner) in enumerate(half_places(count, first)):
        if q not in squares:
            continue
        pieces = jnp.concatenate(split_three(parts_ref[squares.index(q), h]), axis=0)
        chosen = jnp.dot(chooser, pieces, preferred_element_type=jnp.float32)
        block = order + (first << (count - 1))
        forward = forward_ref[pl.ds(block * prompts, prompts)].astype(jnp.float32)
        scaled = (forward * chosen).astype(jnp.bfloat16)
        tile = emission_ref[partner_rows(partner, rows)]
        weights += jnp.dot(scaled, tile, preferred_element_type=jnp.float32)
    return weights


def weigh_kernel(count, groups, emission_ref, forward_ref, chooser_ref, *refs):
    parts, out_ref = refs[:-1], refs[-1]
    chooser = chooser_ref[...]
    out_ref[...] = functools.reduce(jnp.add, [
        weigh_blocks(emission_ref, forward_ref, chooser, part_ref, count, first, squares)
        for part_ref, (first, squares) in zip(parts, groups)
    ])


def last_weigh_kernel(
    count, first, squares, emission_ref, forward_ref, chooser_ref, logits_ref, before_ref,
    parts_ref, raised_ref, pair_ref,
):
    chooser = chooser_ref[...]
    logits = logits_ref[...].astype(jnp.float32)
    top = jnp.max(logits, axis=1, keepdims=True)
    weights = weigh_blocks(
        emission_ref, forward_ref, chooser, parts_ref, count, first, squares
    ) + before_ref[...]
    allowed = jnp.sum(chooser.astype(jnp.float32), axis=1, keepdims=True) > 0
    raised = jnp.where(allowed, jnp.exp(logits - top) * weights, 0.0)
    raised_ref[...] = raised
    total = jnp.sum(raised, axis=1, keepdims=True)
    lane = lax.broadcasted_iota(jnp.int32, pair_ref.shape, 1)
    pair_ref[...] = jnp.where(lane == 0, top, total)


def weigh(emission, forward, chooser, logits, far, devices, count):
    early, late = (0, 1), (2, 3)
    offsets = square_partners(count)
    arrived = [far] + [swap(far, offset, devices) for offset in offsets[1:]]
    near_early = jnp.stack([arrived[q] for q in early])
    near_late = jnp.stack([arrived[q] for q in late])
    far_early, far_late = swap(near_early, 1, devices), swap(near_late, 1, devices)

    def add(parts, groups):
        return pl.pallas_call(
            functools.partial(weigh_kernel, count, groups),
            out_shape=pltpu.VMEM(logits.shape, jnp.float32),
            in_specs=[VMEM] * (3 + len(parts)),
            out_specs=VMEM,
            compiler_params=PARAMS,
            name="weigh_tokens",
        )(emission, forward, chooser, *parts)

    weights = add((near_early, far_early, near_late), ((0, early), (1, early), (0, late)))
    return pl.pallas_call(
        functools.partial(last_weigh_kernel, count, 1, late),
        out_shape=[
            pltpu.VMEM(logits.shape, jnp.float32),
            pltpu.VMEM((logits.shape[0], 128), jnp.float32),
        ],
        in_specs=[VMEM] * 6,
        out_specs=[VMEM] * 2,
        compiler_params=PARAMS,
        name="weigh_last",
    )(emission, forward, chooser, logits, weights, far_late)


def normalise(raised, pair, devices):
    pairs = spread(pair[:, :2].T, devices)
    own_top = pair[:, :1]
    tops, totals = pairs[:, 0], pairs[:, 1]
    top = jnp.max(tops, axis=0)
    total = jnp.sum(totals * jnp.exp(tops - top), axis=0)
    return BLK * devices * (raised * jnp.exp(own_top - top[:, None])) / total[:, None]


def forward_messages(emission, last_token, prior_msg, devices, device):
    hidden = emission.shape[0]
    local_rows = prior_msg.shape[0]
    token_ids = jnp.arange(BLK, dtype=jnp.int32)
    tokens = last_token - device * BLK
    onehot = (tokens[:, None] == token_ids[None, :]).astype(jnp.bfloat16)
    owned = dot_rows(onehot, emission)
    owned = owned.astype(jnp.bfloat16).reshape(devices, local_rows, hidden)
    columns = jnp.sum(exchange(owned), axis=0, dtype=jnp.float32)
    unnormal = prior_msg * columns
    forward_msg = (unnormal / jnp.sum(unnormal, axis=1, keepdims=True)).astype(jnp.bfloat16)
    return spread(forward_msg, devices).reshape(devices * local_rows, hidden)


def per_device(
    emission,
    transition,
    beta_start,
    allow_list,
    trans_table,
    last_token,
    prompt_state,
    prior_msg,
    lm_logits,
):
    devices = lax.axis_size("vocab")
    device = lax.axis_index("vocab")
    hidden = emission.shape[0]
    states = beta_start.shape[1]
    own_rows = transition.shape[1]
    prompts = prompt_state.shape[0]
    count = devices.bit_length() - 1
    if devices == 1 << count and count > 2 and own_rows % 128 == 0 and prompts == devices:
        sums, columns, columns_out, state, allow, table, messages = first_products(
            last_token, prompt_state, allow_list, trans_table, beta_start, emission, count
        )
        route, chooser, sums = tables(state, allow, table, emission, sums, count)
        sums = exchange(sums)
        parts, kept_rows, sent_rows = [messages], (columns,), (columns_out,)
        for window_step in range(STEPS):
            wide = window_step == STEPS - 1
            dtype = jnp.float32 if wide else jnp.bfloat16
            kept, received = step(
                transition, route, sums, parts, dtype, devices, count, kept_rows, sent_rows
            )
            kept_rows, sent_rows, extra = (), (), ()
            if window_step == 1:
                forward = forward_messages_here(prior_msg, parts, devices)
            if window_step == 2:
                extra = (forward,)
            near, extras = reduce_square(kept, received, wide, devices, count, extra)
            if window_step == 0:
                parts = reduce_far(near, devices, count)
            if window_step == 1:
                parts = reduce_far(near, devices, count, (forward,))
                others = [part[-devices:] for part in parts[1:]]
                forward = jnp.concatenate([forward] + others, axis=0)
        forward = jnp.stack(extras).reshape(4, devices // 8, devices, own_rows)
        forward = order_forward(forward, swap(forward, 1, devices), count)
        messages = last_sum(near, forward, devices, count)
        raised, pair = weigh(emission, forward, chooser, lm_logits, messages, devices, count)
        return messages[0].T, normalise(raised, pair, devices)
    state_ids = jnp.arange(states, dtype=jnp.int32)
    block_ids = jnp.arange(devices, dtype=jnp.int32)
    allowed = jnp.any(allow_list[:, :, None] == block_ids, axis=1)
    dest_here = lax.dynamic_index_in_dim(trans_table, device, axis=1, keepdims=False)
    allow_here = jnp.any(allow_list == device, axis=1)
    dest_rows = jnp.sum(jnp.where(prompt_state[:, None] == state_ids, dest_here, 0), axis=1)
    allow_rows = jnp.any((prompt_state[:, None] == state_ids) & allow_here, axis=1)
    chooser = (dest_rows[:, None] == state_ids) & allow_rows[:, None]
    messages = lax.dynamic_slice_in_dim(beta_start, device * own_rows, own_rows, 0).T
    forward_all = forward_messages(emission, last_token, prior_msg, devices, device)
    own_sums = exchange(jnp.sum(emission, axis=1, dtype=jnp.float32).reshape(devices, own_rows))
    route = allowed.T[:, :, None] & (trans_table.T[:, :, None] == state_ids)
    route = route.astype(jnp.float32).reshape(devices * states, states)
    by_owner = transition.reshape(devices, own_rows, own_rows)
    for window_step in range(STEPS):
        selected = jnp.dot(route, messages, precision=lax.Precision.HIGHEST)
        selected = selected.reshape(devices, states, own_rows)
        emitted = jnp.sum(selected * own_sums[:, None, :], axis=0)
        halves = jnp.concatenate(split_outside(emitted), axis=0)
        partial = jnp.einsum("dzy,sy->dsz", by_owner, halves, preferred_element_type=jnp.float32)
        partial = partial[:, :states] + partial[:, states:]
        if window_step < STEPS - 1:
            partial = partial.astype(jnp.bfloat16)
        messages = jnp.sum(exchange(partial), axis=0, dtype=jnp.float32)
    everywhere = spread(messages, devices)
    chosen = jnp.einsum(
        "ps,dsz->pdz", chooser.astype(jnp.float32), everywhere, precision=lax.Precision.HIGHEST
    )
    forward_all = forward_all.reshape(prompts, devices, own_rows).astype(jnp.float32)
    scaled = (forward_all * chosen).astype(jnp.bfloat16).reshape(prompts, hidden)
    weights = jnp.dot(scaled, emission, preferred_element_type=jnp.float32)
    weights = jnp.where(allow_rows[:, None], weights, 0.0)
    logits = lm_logits.astype(jnp.float32)
    top_here = jnp.max(logits, axis=1)
    raised = jnp.exp(logits - top_here[:, None]) * weights
    pairs = spread(jnp.stack([top_here, jnp.sum(raised, axis=1)]), devices)
    tops, totals = pairs[:, 0], pairs[:, 1]
    top = jnp.max(tops, axis=0)
    total = jnp.sum(totals * jnp.exp(tops - top), axis=0)
    raised = raised * jnp.exp(top_here - top)[:, None]
    return (messages.T, BLK * devices * raised / total[:, None])


def solution(mesh):
    return jax.shard_map(
        per_device,
        mesh=mesh,
        in_specs=(
            P(None, "vocab"),
            P(None, "vocab"),
            P(),
            P(),
            P(),
            P("parts"),
            P("parts"),
            P(("parts", "vocab"), None),
            P("parts", "vocab"),
        ),
        out_specs=(P(("parts", "vocab"), None), P("parts", "vocab")),
        check_vma=False,
    )
```

```python
import functools

import jax
import jax.numpy as jnp
from jax import lax
from jax.experimental import pallas as pl
from jax.experimental.pallas import tpu as pltpu
from jax.sharding import PartitionSpec as P

BLK = 256
STEPS = 3
LIMIT = 16 * 1024 * 1024
VMEM = pl.BlockSpec(memory_space=pltpu.VMEM)
SMEM = pl.BlockSpec(memory_space=pltpu.SMEM)
ANY = pl.BlockSpec(memory_space=pl.ANY)
PARAMS = pltpu.CompilerParams(vmem_limit_bytes=LIMIT)


def exchange(blocks):
    return lax.all_to_all(blocks, "vocab", split_axis=0, concat_axis=0, tiled=True)


def spread(own, devices):
    return exchange(jnp.broadcast_to(own[None], (devices,) + own.shape))


def basis(count):
    return [1, 3, 4] + [(1 << bit) | 1 for bit in range(3, count)]


def swap(block, offset, devices):
    pairs = [(i, i ^ offset) for i in range(devices)]
    return lax.ppermute(block, "vocab", pairs)


def split_wide(wide):
    high = wide.astype(jnp.bfloat16)
    low = (wide - high.astype(jnp.float32)).astype(jnp.bfloat16)
    return high, low


def split_outside(wide):
    high = lax.reduce_precision(wide, exponent_bits=8, mantissa_bits=7)
    return high.astype(jnp.bfloat16), (wide - high).astype(jnp.bfloat16)


def split_three(wide):
    high = wide.astype(jnp.bfloat16)
    rest = wide - high.astype(jnp.float32)
    middle = rest.astype(jnp.bfloat16)
    low = (rest - middle.astype(jnp.float32)).astype(jnp.bfloat16)
    return high, middle, low


def dot_rows(left, right):
    return lax.dot_general(left, right, (((1,), (1,)), ((), ())), preferred_element_type=jnp.float32)


def partner_of(bits, count):
    partner = 0
    for bit, offset in zip(bits, basis(count)):
        partner ^= bit * offset
    return partner


def all_bits(count):
    return [tuple((k >> (count - 1 - b)) & 1 for b in range(count)) for k in range(1 << count)]


def square_partners(count):
    return [partner_of((0,) + bits, count) for bits in all_bits(2)]


def far_partners(count):
    return [partner_of((0, 0, 0) + bits, count) for bits in all_bits(count - 3)]


def half_places(count, first):
    return [
        ((q, h), first ^ near ^ far)
        for q, near in enumerate(square_partners(count))
        for h, far in enumerate(far_partners(count))
    ]


def partner_rows(i, rows):
    owner = lax.axis_index("vocab") ^ i
    return pl.ds(pl.multiple_of(owner * rows, rows), rows)


def pack(blocks, wide, extra):
    rows = blocks.reshape(-1, blocks.shape[-1])
    parts = split_outside(rows) if wide else (rows.astype(jnp.bfloat16),)
    return jnp.concatenate(parts + extra, axis=0)


def unpack(packed, shape, wide):
    size = shape[0] * shape[1]
    rows = packed[:size].astype(jnp.float32)
    if wide:
        rows += packed[size : 2 * size].astype(jnp.float32)
    return rows.reshape(shape)


def reduce_square(kept, received, wide, devices, count, extra=()):
    total = kept + received.astype(jnp.float32)
    near, extras = total[0], list(extra)
    for q, offset in enumerate(square_partners(count)):
        if q:
            packed = swap(pack(total[q], wide, extra), offset, devices)
            near += unpack(packed, total.shape[1:], wide)
            for rows in extra:
                extras.append(packed[-rows.shape[0] :])
    return near, extras


def reduce_far(near, devices, count, extra=()):
    blocks = [near[0]]
    for h, offset in enumerate(far_partners(count)):
        if h:
            blocks.append(swap(pack(near[h], False, extra), offset, devices))
    return blocks


def column_of(scalars_ref, shape):
    row = lax.broadcasted_iota(jnp.int32, shape, 0)
    column = jnp.zeros(shape, jnp.int32)
    for k in range(shape[0]):
        column = jnp.where(row == k, scalars_ref[k], column)
    return column


def tables_kernel(
    count, state_ref, allow_ref, table_ref, emission_ref, sums_in_ref,
    route_ref, chooser_ref, sums_ref,
):
    device = lax.axis_index("vocab")
    devices = 1 << count
    states = table_ref.shape[0]
    sums_ref[...] = sums_in_ref[...]
    allow, table = allow_ref[...], table_ref[...]
    hits = [jnp.max((allow == b).astype(jnp.float32), axis=0, keepdims=True) for b in range(devices)]
    shape = (states, states)
    diagonal = [lax.broadcasted_iota(jnp.int32, shape, axis) for axis in (0, 1)]
    diagonal = (diagonal[0] == diagonal[1]).astype(jnp.bfloat16)
    hits = dot_rows(diagonal, jnp.concatenate(hits, axis=0).astype(jnp.bfloat16))
    ids = lax.broadcasted_iota(jnp.int32, shape, 1)
    own_step = jnp.zeros(shape, jnp.float32)
    for b in range(devices):
        step = jnp.where(table[:, b : b + 1] == ids, hits[:, b : b + 1], 0.0)
        own_step = jnp.where(device == b, step, own_step)
        step = step.astype(jnp.bfloat16)
        route_ref[pl.ds(b * states, states)] = jnp.concatenate([step] * 3, axis=1)
    shape = (states, devices)
    prompts = state_ref[...] == lax.broadcasted_iota(jnp.int32, shape, 0)
    chooser = lax.dot_general(
        prompts.astype(jnp.bfloat16),
        own_step.astype(jnp.bfloat16),
        (((0,), (0,)), ((), ())),
        preferred_element_type=jnp.float32,
    ).astype(jnp.bfloat16)
    chooser_ref[...] = jnp.concatenate([chooser] * 3, axis=1)


def tables(state, allow, table, emission, sums, count):
    devices, states = 1 << count, table.shape[0]
    return pl.pallas_call(
        functools.partial(tables_kernel, count),
        out_shape=[
            pltpu.VMEM((devices * states, 3 * states), jnp.bfloat16),
            pltpu.VMEM((devices, 3 * states), jnp.bfloat16),
            jax.ShapeDtypeStruct(sums.shape, sums.dtype),
        ],
        in_specs=[VMEM] * 5,
        out_specs=[VMEM] * 3,
        compiler_params=PARAMS,
        name="tables",
    )(state, allow, table, emission, sums)


def products_kernel(
    count, token_hbm, state_hbm, allow_hbm, table_hbm, start_hbm, emission_ref,
    sums_ref, kept_ref, sent_ref, state_ref, allow_ref, table_ref, messages_ref,
    token_ref, columns_ref, sems,
):
    device = lax.axis_index("vocab")
    devices = 1 << count
    rows = emission_ref.shape[0] >> count
    own = pl.ds(pl.multiple_of(device * rows, rows), rows)
    pairs = [
        (token_hbm, token_ref), (state_hbm, state_ref), (allow_hbm, allow_ref),
        (table_hbm, table_ref), (start_hbm.at[:, own], messages_ref),
    ]
    copies = [
        pltpu.make_async_copy(source, to, sems.at[k]) for k, (source, to) in enumerate(pairs)
    ]
    for copy in copies:
        copy.start()
    shape = (devices * devices // 2, devices * devices)
    to, source = (lax.broadcasted_iota(jnp.int32, shape, axis) for axis in (0, 1))
    same_block = (to & (devices - 1)) == (source >> count)
    orders = []
    for first in range(2):
        prompt = partner_at((to >> count) + first * (devices // 2), count)
        onehot = same_block & ((source & (devices - 1)) == prompt)
        orders.append(onehot.astype(jnp.bfloat16))
    ones = jnp.ones((16, BLK), jnp.bfloat16)
    early = devices * 3 // 8
    for k in range(early):
        sums_ref[k] = dot_rows(ones, emission_ref[pl.ds(k * rows, rows)])[:1]
    copies[0].wait()
    shape = (devices, BLK)
    tokens = column_of(token_ref, shape) - device * BLK
    onehot = (tokens == lax.broadcasted_iota(jnp.int32, shape, 1)).astype(jnp.bfloat16)
    left = jnp.concatenate([onehot, ones], axis=0)
    for k in range(devices):
        product = dot_rows(onehot if k < early else left, emission_ref[pl.ds(k * rows, rows)])
        columns_ref[pl.ds(k * devices, devices)] = product[:devices].astype(jnp.bfloat16)
        if k >= early:
            sums_ref[k] = product[devices : devices + 1]
    for order, out_ref in zip(orders, (kept_ref, sent_ref)):
        ordered = jnp.dot(order, columns_ref[...], preferred_element_type=jnp.float32)
        out_ref[...] = ordered.astype(jnp.bfloat16).reshape(out_ref.shape)
    for copy in copies[1:]:
        copy.wait()


def first_products(last_token, prompt_state, allow_list, trans_table, beta_start, emission, count):
    devices, rows = 1 << count, emission.shape[0] >> count
    half = pltpu.VMEM((4, devices // 8, devices, rows), jnp.bfloat16)
    small = (prompt_state[None], allow_list.T, trans_table)
    operands = (last_token,) + small + (beta_start.T,)
    return pl.pallas_call(
        functools.partial(products_kernel, count),
        out_shape=[jax.ShapeDtypeStruct((devices, 1, rows), jnp.float32), half, half]
        + [pltpu.VMEM(array.shape, array.dtype) for array in small]
        + [pltpu.VMEM((beta_start.shape[1], rows), jnp.float32)],
        in_specs=[ANY] * len(operands) + [VMEM],
        out_specs=[VMEM] * 7,
        scratch_shapes=[
            pltpu.SMEM(last_token.shape, jnp.int32),
            pltpu.VMEM((devices * devices, rows), jnp.bfloat16),
            pltpu.SemaphoreType.DMA((len(operands),)),
        ],
        compiler_params=PARAMS,
        name="first_products",
    )(*(in_hbm(operand) for operand in operands), emission)


def in_hbm(array):
    return pltpu.with_memory_space_constraint(array, pltpu.HBM)


def forward_kernel(prior_ref, *refs):
    blocks, out_ref = refs[:-1], refs[-1]
    devices, rows = out_ref.shape
    columns = blocks[0][-devices:]
    for block in blocks[1:]:
        columns += block[-devices:].astype(jnp.float32)
    prior = jnp.concatenate([prior_ref[:, pl.ds(k * rows, rows)] for k in range(devices)], axis=0)
    unnormal = prior * columns
    out_ref[...] = (unnormal / jnp.sum(unnormal)).astype(jnp.bfloat16)


def forward_messages_here(prior, blocks, devices):
    return pl.pallas_call(
        forward_kernel,
        out_shape=pltpu.VMEM((devices, blocks[0].shape[1]), jnp.bfloat16),
        in_specs=[VMEM] * (1 + len(blocks)),
        out_specs=VMEM,
        compiler_params=PARAMS,
        name="forward_messages",
    )(prior, *blocks)


def partner_at(place, count):
    number = jnp.zeros_like(place)
    for bit, offset in enumerate(basis(count)):
        number = number ^ (((place >> (count - 1 - bit)) & 1) * offset)
    return lax.axis_index("vocab") ^ number


def order_kernel(count, near_ref, far_ref, out_ref):
    size = 1 << count
    shape = (size * size, size * size)
    to, source = (lax.broadcasted_iota(jnp.int32, shape, axis) for axis in (0, 1))
    same_block = partner_at(to >> count, count) == (source & (size - 1))
    same_prompt = (to & (size - 1)) == partner_at(source >> count, count)
    onehot = (same_block & same_prompt).astype(jnp.bfloat16)
    half = size * size // 2
    rows = out_ref.shape[1]
    near = near_ref[...].reshape(half, rows)
    far = far_ref[...].reshape(half, rows)
    ordered = jnp.dot(onehot[:, :half], near, preferred_element_type=jnp.float32)
    ordered += jnp.dot(onehot[:, half:], far, preferred_element_type=jnp.float32)
    out_ref[...] = ordered.astype(jnp.bfloat16)


def order_forward(near, far, count):
    rows = near.shape[-1]
    return pl.pallas_call(
        functools.partial(order_kernel, count),
        out_shape=pltpu.VMEM((1 << (2 * count), rows), jnp.bfloat16),
        in_specs=[VMEM] * 2,
        out_specs=VMEM,
        compiler_params=PARAMS,
        name="order_forward",
    )(near, far)


def last_kernel(near_ref, *refs):
    blocks, out_ref = refs[:-2], refs[-1]
    count, states, _ = out_ref.shape
    for h in range(count):
        messages = near_ref[h]
        for g, block in enumerate(blocks, 1):
            for part in range(2):
                start = (part * count + (h ^ g)) * states
                messages += block[pl.ds(start, states)].astype(jnp.float32)
        out_ref[h] = messages


def last_sum(near, after, devices, count):
    packed = pack(near, True, ())
    blocks = [swap(packed, offset, devices) for offset in far_partners(count)[1:]]
    return pl.pallas_call(
        last_kernel,
        out_shape=pltpu.VMEM(near.shape, jnp.float32),
        in_specs=[VMEM] * (1 + len(blocks)) + [ANY],
        out_specs=VMEM,
        compiler_params=PARAMS,
        name="last_messages",
    )(near, *blocks, after)


def half_products(halves, transition_ref, out_ref, count, first):
    states = halves.shape[0] // 2
    rows = transition_ref.shape[0] >> count
    for place, partner in half_places(count, first):
        product = dot_rows(halves, transition_ref[partner_rows(partner, rows)])
        product = product[:states] + product[states:]
        out_ref[place + (pl.ds(0, states),)] = product.astype(out_ref.dtype)


def add_rows(out_ref, states, extra):
    for ref in extra:
        rows = pl.ds(states, ref.shape[2])
        for place in ((y, k) for y in range(ref.shape[0]) for k in range(ref.shape[1])):
            out_ref[place + (rows,)] = ref[place].astype(out_ref.dtype)


def send_kernel(count, number, transition_ref, route_ref, sums_ref, *refs):
    parts, extra, (halves_ref, out_ref) = refs[:number], refs[number:-2], refs[-2:]
    states = halves_ref.shape[0] // 2
    messages = parts[0][:states].astype(jnp.float32)
    for part in parts[1:]:
        messages += part[:states].astype(jnp.float32)
    selected = jnp.dot(
        route_ref[...],
        jnp.concatenate(split_three(messages), axis=0),
        preferred_element_type=jnp.float32,
    )
    emitted = selected[:states] * sums_ref[0]
    for b in range(1, 1 << count):
        emitted += selected[b * states : (b + 1) * states] * sums_ref[b]
    halves = jnp.concatenate(split_wide(emitted), axis=0)
    halves_ref[...] = halves
    half_products(halves, transition_ref, out_ref, count, 1)
    add_rows(out_ref, states, extra)


def keep_kernel(count, transition_ref, halves_ref, *refs):
    extra, out_ref = refs[:-1], refs[-1]
    half_products(halves_ref[...], transition_ref, out_ref, count, 0)
    add_rows(out_ref, halves_ref.shape[0] // 2, extra)


def step(transition, route, sums, parts, dtype, devices, count, kept_rows=(), sent_rows=()):
    states, rows = route.shape[0] // devices, parts[0].shape[1]
    total = states + sum(block.shape[2] for block in kept_rows)
    shape = (4, devices // 8, total, rows)
    halves, sent = pl.pallas_call(
        functools.partial(send_kernel, count, len(parts)),
        out_shape=[
            pltpu.VMEM((2 * states, rows), jnp.bfloat16),
            pltpu.VMEM(shape, dtype),
        ],
        in_specs=[VMEM] * (3 + len(parts) + len(sent_rows)),
        out_specs=[VMEM] * 2,
        compiler_params=PARAMS,
        name="step_sent_half",
    )(transition, route, sums, *parts, *sent_rows)
    received = swap(sent, 1, devices)
    kept = pl.pallas_call(
        functools.partial(keep_kernel, count),
        out_shape=pltpu.VMEM(shape, jnp.float32),
        in_specs=[VMEM] * (2 + len(kept_rows)),
        out_specs=VMEM,
        compiler_params=PARAMS,
        name="step_kept_half",
    )(transition, halves, *kept_rows)
    return kept, received


def weigh_blocks(emission_ref, forward_ref, chooser, parts_ref, count, first, squares):
    rows = emission_ref.shape[0] >> count
    prompts = chooser.shape[0]
    weights = jnp.zeros((prompts, emission_ref.shape[1]), jnp.float32)
    for order, ((q, h), partner) in enumerate(half_places(count, first)):
        if q not in squares:
            continue
        pieces = jnp.concatenate(split_three(parts_ref[squares.index(q), h]), axis=0)
        chosen = jnp.dot(chooser, pieces, preferred_element_type=jnp.float32)
        block = order + (first << (count - 1))
        forward = forward_ref[pl.ds(block * prompts, prompts)].astype(jnp.float32)
        scaled = (forward * chosen).astype(jnp.bfloat16)
        tile = emission_ref[partner_rows(partner, rows)]
        weights += jnp.dot(scaled, tile, preferred_element_type=jnp.float32)
    return weights


def weigh_kernel(count, groups, emission_ref, forward_ref, chooser_ref, *refs):
    parts, out_ref = refs[:-1], refs[-1]
    chooser = chooser_ref[...]
    out_ref[...] = functools.reduce(jnp.add, [
        weigh_blocks(emission_ref, forward_ref, chooser, part_ref, count, first, squares)
        for part_ref, (first, squares) in zip(parts, groups)
    ])


def last_weigh_kernel(
    count, first, squares, emission_ref, forward_ref, chooser_ref, logits_ref, before_ref,
    parts_ref, raised_ref, pair_ref,
):
    chooser = chooser_ref[...]
    logits = logits_ref[...].astype(jnp.float32)
    top = jnp.max(logits, axis=1, keepdims=True)
    weights = weigh_blocks(
        emission_ref, forward_ref, chooser, parts_ref, count, first, squares
    ) + before_ref[...]
    allowed = jnp.sum(chooser.astype(jnp.float32), axis=1, keepdims=True) > 0
    raised = jnp.where(allowed, jnp.exp(logits - top) * weights, 0.0)
    raised_ref[...] = raised
    total = jnp.sum(raised, axis=1, keepdims=True)
    lane = lax.broadcasted_iota(jnp.int32, pair_ref.shape, 1)
    pair_ref[...] = jnp.where(lane == 0, top, total)


def weigh(emission, forward, chooser, logits, far, devices, count):
    early, late = (0, 1), (2, 3)
    offsets = square_partners(count)
    arrived = [far] + [swap(far, offset, devices) for offset in offsets[1:]]
    near_early = jnp.stack([arrived[q] for q in early])
    near_late = jnp.stack([arrived[q] for q in late])
    far_early, far_late = swap(near_early, 1, devices), swap(near_late, 1, devices)

    def add(parts, groups):
        return pl.pallas_call(
            functools.partial(weigh_kernel, count, groups),
            out_shape=pltpu.VMEM(logits.shape, jnp.float32),
            in_specs=[VMEM] * (3 + len(parts)),
            out_specs=VMEM,
            compiler_params=PARAMS,
            name="weigh_tokens",
        )(emission, forward, chooser, *parts)

    weights = add((near_early, far_early, near_late), ((0, early), (1, early), (0, late)))
    return pl.pallas_call(
        functools.partial(last_weigh_kernel, count, 1, late),
        out_shape=[
            pltpu.VMEM(logits.shape, jnp.float32),
            pltpu.VMEM((logits.shape[0], 128), jnp.float32),
        ],
        in_specs=[VMEM] * 6,
        out_specs=[VMEM] * 2,
        compiler_params=PARAMS,
        name="weigh_last",
    )(emission, forward, chooser, logits, weights, far_late)


def normalise(raised, pair, devices):
    pairs = spread(pair[:, :2].T, devices)
    own_top = pair[:, :1]
    tops, totals = pairs[:, 0], pairs[:, 1]
    top = jnp.max(tops, axis=0)
    total = jnp.sum(totals * jnp.exp(tops - top), axis=0)
    return BLK * devices * (raised * jnp.exp(own_top - top[:, None])) / total[:, None]


def forward_messages(emission, last_token, prior_msg, devices, device):
    hidden = emission.shape[0]
    local_rows = prior_msg.shape[0]
    token_ids = jnp.arange(BLK, dtype=jnp.int32)
    tokens = last_token - device * BLK
    onehot = (tokens[:, None] == token_ids[None, :]).astype(jnp.bfloat16)
    owned = dot_rows(onehot, emission)
    owned = owned.astype(jnp.bfloat16).reshape(devices, local_rows, hidden)
    columns = jnp.sum(exchange(owned), axis=0, dtype=jnp.float32)
    unnormal = prior_msg * columns
    forward_msg = (unnormal / jnp.sum(unnormal, axis=1, keepdims=True)).astype(jnp.bfloat16)
    return spread(forward_msg, devices).reshape(devices * local_rows, hidden)


def per_device(
    emission,
    transition,
    beta_start,
    allow_list,
    trans_table,
    last_token,
    prompt_state,
    prior_msg,
    lm_logits,
):
    devices = lax.axis_size("vocab")
    device = lax.axis_index("vocab")
    hidden = emission.shape[0]
    states = beta_start.shape[1]
    own_rows = transition.shape[1]
    prompts = prompt_state.shape[0]
    count = devices.bit_length() - 1
    if devices == 1 << count and count > 2 and own_rows % 128 == 0 and prompts == devices:
        sums, columns, columns_out, state, allow, table, messages = first_products(
            last_token, prompt_state, allow_list, trans_table, beta_start, emission, count
        )
        route, chooser, sums = tables(state, allow, table, emission, sums, count)
        sums = exchange(sums)
        parts, kept_rows, sent_rows = [messages], (columns,), (columns_out,)
        for window_step in range(STEPS):
            wide = window_step == STEPS - 1
            dtype = jnp.float32 if wide else jnp.bfloat16
            kept, received = step(
                transition, route, sums, parts, dtype, devices, count, kept_rows, sent_rows
            )
            kept_rows, sent_rows, extra = (), (), ()
            if window_step == 1:
                forward = forward_messages_here(prior_msg, parts, devices)
            if window_step == 2:
                extra = (forward,)
            near, extras = reduce_square(kept, received, wide, devices, count, extra)
            if window_step == 0:
                parts = reduce_far(near, devices, count)
            if window_step == 1:
                parts = reduce_far(near, devices, count, (forward,))
                others = [part[-devices:] for part in parts[1:]]
                forward = jnp.concatenate([forward] + others, axis=0)
        forward = jnp.stack(extras).reshape(4, devices // 8, devices, own_rows)
        forward = order_forward(forward, swap(forward, 1, devices), count)
        messages = last_sum(near, forward, devices, count)
        raised, pair = weigh(emission, forward, chooser, lm_logits, messages, devices, count)
        return messages[0].T, normalise(raised, pair, devices)
    state_ids = jnp.arange(states, dtype=jnp.int32)
    block_ids = jnp.arange(devices, dtype=jnp.int32)
    allowed = jnp.any(allow_list[:, :, None] == block_ids, axis=1)
    dest_here = lax.dynamic_index_in_dim(trans_table, device, axis=1, keepdims=False)
    allow_here = jnp.any(allow_list == device, axis=1)
    dest_rows = jnp.sum(jnp.where(prompt_state[:, None] == state_ids, dest_here, 0), axis=1)
    allow_rows = jnp.any((prompt_state[:, None] == state_ids) & allow_here, axis=1)
    chooser = (dest_rows[:, None] == state_ids) & allow_rows[:, None]
    messages = lax.dynamic_slice_in_dim(beta_start, device * own_rows, own_rows, 0).T
    forward_all = forward_messages(emission, last_token, prior_msg, devices, device)
    own_sums = exchange(jnp.sum(emission, axis=1, dtype=jnp.float32).reshape(devices, own_rows))
    route = allowed.T[:, :, None] & (trans_table.T[:, :, None] == state_ids)
    route = route.astype(jnp.float32).reshape(devices * states, states)
    by_owner = transition.reshape(devices, own_rows, own_rows)
    for window_step in range(STEPS):
        selected = jnp.dot(route, messages, precision=lax.Precision.HIGHEST)
        selected = selected.reshape(devices, states, own_rows)
        emitted = jnp.sum(selected * own_sums[:, None, :], axis=0)
        halves = jnp.concatenate(split_outside(emitted), axis=0)
        partial = jnp.einsum("dzy,sy->dsz", by_owner, halves, preferred_element_type=jnp.float32)
        partial = partial[:, :states] + partial[:, states:]
        if window_step < STEPS - 1:
            partial = partial.astype(jnp.bfloat16)
        messages = jnp.sum(exchange(partial), axis=0, dtype=jnp.float32)
    everywhere = spread(messages, devices)
    chosen = jnp.einsum(
        "ps,dsz->pdz", chooser.astype(jnp.float32), everywhere, precision=lax.Precision.HIGHEST
    )
    forward_all = forward_all.reshape(prompts, devices, own_rows).astype(jnp.float32)
    scaled = (forward_all * chosen).astype(jnp.bfloat16).reshape(prompts, hidden)
    weights = jnp.dot(scaled, emission, preferred_element_type=jnp.float32)
    weights = jnp.where(allow_rows[:, None], weights, 0.0)
    logits = lm_logits.astype(jnp.float32)
    top_here = jnp.max(logits, axis=1)
    raised = jnp.exp(logits - top_here[:, None]) * weights
    pairs = spread(jnp.stack([top_here, jnp.sum(raised, axis=1)]), devices)
    tops, totals = pairs[:, 0], pairs[:, 1]
    top = jnp.max(tops, axis=0)
    total = jnp.sum(totals * jnp.exp(tops - top), axis=0)
    raised = raised * jnp.exp(top_here - top)[:, None]
    return (messages.T, BLK * devices * raised / total[:, None])


def solution(mesh):
    return jax.shard_map(
        per_device,
        mesh=mesh,
        in_specs=(
            P(None, "vocab"),
            P(None, "vocab"),
            P(),
            P(),
            P(),
            P("parts"),
            P("parts"),
            P(("parts", "vocab"), None),
            P("parts", "vocab"),
        ),
        out_specs=(P(("parts", "vocab"), None), P("parts", "vocab")),
        check_vma=False,
    )
```

```python
import functools

import jax
import jax.numpy as jnp
from jax import lax
from jax.experimental import pallas as pl
from jax.experimental.pallas import tpu as pltpu
from jax.sharding import PartitionSpec as P

BLK = 256
STEPS = 3
LIMIT = 16 * 1024 * 1024
VMEM = pl.BlockSpec(memory_space=pltpu.VMEM)
SMEM = pl.BlockSpec(memory_space=pltpu.SMEM)
ANY = pl.BlockSpec(memory_space=pl.ANY)
PARAMS = pltpu.CompilerParams(vmem_limit_bytes=LIMIT)


def exchange(blocks):
    return lax.all_to_all(blocks, "vocab", split_axis=0, concat_axis=0, tiled=True)


def spread(own, devices):
    return exchange(jnp.broadcast_to(own[None], (devices,) + own.shape))


def basis(count):
    return [1, 2, 5] + [(1 << bit) | 1 for bit in range(3, count)]


def swap(block, offset, devices):
    pairs = [(i, i ^ offset) for i in range(devices)]
    return lax.ppermute(block, "vocab", pairs)


def split_wide(wide):
    high = wide.astype(jnp.bfloat16)
    low = (wide - high.astype(jnp.float32)).astype(jnp.bfloat16)
    return high, low


def split_outside(wide):
    high = lax.reduce_precision(wide, exponent_bits=8, mantissa_bits=7)
    return high.astype(jnp.bfloat16), (wide - high).astype(jnp.bfloat16)


def split_three(wide):
    high = wide.astype(jnp.bfloat16)
    rest = wide - high.astype(jnp.float32)
    middle = rest.astype(jnp.bfloat16)
    low = (rest - middle.astype(jnp.float32)).astype(jnp.bfloat16)
    return high, middle, low


def dot_rows(left, right):
    return lax.dot_general(left, right, (((1,), (1,)), ((), ())), preferred_element_type=jnp.float32)


def partner_of(bits, count):
    partner = 0
    for bit, offset in zip(bits, basis(count)):
        partner ^= bit * offset
    return partner


def all_bits(count):
    return [tuple((k >> (count - 1 - b)) & 1 for b in range(count)) for k in range(1 << count)]


def square_partners(count):
    return [partner_of((0,) + bits, count) for bits in all_bits(2)]


def far_partners(count):
    return [partner_of((0, 0, 0) + bits, count) for bits in all_bits(count - 3)]


def half_places(count, first):
    return [
        ((q, h), first ^ near ^ far)
        for q, near in enumerate(square_partners(count))
        for h, far in enumerate(far_partners(count))
    ]


def partner_rows(i, rows):
    owner = lax.axis_index("vocab") ^ i
    return pl.ds(pl.multiple_of(owner * rows, rows), rows)


def pack(blocks, wide, extra):
    rows = blocks.reshape(-1, blocks.shape[-1])
    parts = split_outside(rows) if wide else (rows.astype(jnp.bfloat16),)
    return jnp.concatenate(parts + extra, axis=0)


def unpack(packed, shape, wide):
    size = shape[0] * shape[1]
    rows = packed[:size].astype(jnp.float32)
    if wide:
        rows += packed[size : 2 * size].astype(jnp.float32)
    return rows.reshape(shape)


def reduce_square(kept, received, wide, devices, count, extra=()):
    total = kept + received.astype(jnp.float32)
    near, extras = total[0], list(extra)
    for q, offset in enumerate(square_partners(count)):
        if q:
            packed = swap(pack(total[q], wide, extra), offset, devices)
            near += unpack(packed, total.shape[1:], wide)
            for rows in extra:
                extras.append(packed[-rows.shape[0] :])
    return near, extras


def reduce_far(near, devices, count, extra=()):
    blocks = [near[0]]
    for h, offset in enumerate(far_partners(count)):
        if h:
            blocks.append(swap(pack(near[h], False, extra), offset, devices))
    return blocks


def column_of(scalars_ref, shape):
    row = lax.broadcasted_iota(jnp.int32, shape, 0)
    column = jnp.zeros(shape, jnp.int32)
    for k in range(shape[0]):
        column = jnp.where(row == k, scalars_ref[k], column)
    return column


def tables_kernel(
    count, state_ref, allow_ref, table_ref, emission_ref, sums_in_ref,
    route_ref, chooser_ref, sums_ref,
):
    device = lax.axis_index("vocab")
    devices = 1 << count
    states = table_ref.shape[0]
    sums_ref[...] = sums_in_ref[...]
    allow, table = allow_ref[...], table_ref[...]
    hits = [jnp.max((allow == b).astype(jnp.float32), axis=0, keepdims=True) for b in range(devices)]
    shape = (states, states)
    diagonal = [lax.broadcasted_iota(jnp.int32, shape, axis) for axis in (0, 1)]
    diagonal = (diagonal[0] == diagonal[1]).astype(jnp.bfloat16)
    hits = dot_rows(diagonal, jnp.concatenate(hits, axis=0).astype(jnp.bfloat16))
    ids = lax.broadcasted_iota(jnp.int32, shape, 1)
    own_step = jnp.zeros(shape, jnp.float32)
    for b in range(devices):
        step = jnp.where(table[:, b : b + 1] == ids, hits[:, b : b + 1], 0.0)
        own_step = jnp.where(device == b, step, own_step)
        step = step.astype(jnp.bfloat16)
        route_ref[pl.ds(b * states, states)] = jnp.concatenate([step] * 3, axis=1)
    shape = (states, devices)
    prompts = state_ref[...] == lax.broadcasted_iota(jnp.int32, shape, 0)
    chooser = lax.dot_general(
        prompts.astype(jnp.bfloat16),
        own_step.astype(jnp.bfloat16),
        (((0,), (0,)), ((), ())),
        preferred_element_type=jnp.float32,
    ).astype(jnp.bfloat16)
    chooser_ref[...] = jnp.concatenate([chooser] * 3, axis=1)


def tables(state, allow, table, emission, sums, count):
    devices, states = 1 << count, table.shape[0]
    return pl.pallas_call(
        functools.partial(tables_kernel, count),
        out_shape=[
            pltpu.VMEM((devices * states, 3 * states), jnp.bfloat16),
            pltpu.VMEM((devices, 3 * states), jnp.bfloat16),
            jax.ShapeDtypeStruct(sums.shape, sums.dtype),
        ],
        in_specs=[VMEM] * 5,
        out_specs=[VMEM] * 3,
        compiler_params=PARAMS,
        name="tables",
    )(state, allow, table, emission, sums)


def products_kernel(
    count, token_hbm, state_hbm, allow_hbm, table_hbm, start_hbm, emission_ref,
    sums_ref, kept_ref, sent_ref, state_ref, allow_ref, table_ref, messages_ref,
    token_ref, columns_ref, sems,
):
    device = lax.axis_index("vocab")
    devices = 1 << count
    rows = emission_ref.shape[0] >> count
    own = pl.ds(pl.multiple_of(device * rows, rows), rows)
    pairs = [
        (token_hbm, token_ref), (state_hbm, state_ref), (allow_hbm, allow_ref),
        (table_hbm, table_ref), (start_hbm.at[:, own], messages_ref),
    ]
    copies = [
        pltpu.make_async_copy(source, to, sems.at[k]) for k, (source, to) in enumerate(pairs)
    ]
    for copy in copies:
        copy.start()
    shape = (devices * devices // 2, devices * devices)
    to, source = (lax.broadcasted_iota(jnp.int32, shape, axis) for axis in (0, 1))
    same_block = (to & (devices - 1)) == (source >> count)
    orders = []
    for first in range(2):
        prompt = partner_at((to >> count) + first * (devices // 2), count)
        onehot = same_block & ((source & (devices - 1)) == prompt)
        orders.append(onehot.astype(jnp.bfloat16))
    ones = jnp.ones((16, BLK), jnp.bfloat16)
    early = devices * 3 // 8
    for k in range(early):
        sums_ref[k] = dot_rows(ones, emission_ref[pl.ds(k * rows, rows)])[:1]
    copies[0].wait()
    shape = (devices, BLK)
    tokens = column_of(token_ref, shape) - device * BLK
    onehot = (tokens == lax.broadcasted_iota(jnp.int32, shape, 1)).astype(jnp.bfloat16)
    left = jnp.concatenate([onehot, ones], axis=0)
    for k in range(devices):
        product = dot_rows(onehot if k < early else left, emission_ref[pl.ds(k * rows, rows)])
        columns_ref[pl.ds(k * devices, devices)] = product[:devices].astype(jnp.bfloat16)
        if k >= early:
            sums_ref[k] = product[devices : devices + 1]
    for order, out_ref in zip(orders, (kept_ref, sent_ref)):
        ordered = jnp.dot(order, columns_ref[...], preferred_element_type=jnp.float32)
        out_ref[...] = ordered.astype(jnp.bfloat16).reshape(out_ref.shape)
    for copy in copies[1:]:
        copy.wait()


def first_products(last_token, prompt_state, allow_list, trans_table, beta_start, emission, count):
    devices, rows = 1 << count, emission.shape[0] >> count
    half = pltpu.VMEM((4, devices // 8, devices, rows), jnp.bfloat16)
    small = (prompt_state[None], allow_list.T, trans_table)
    operands = (last_token,) + small + (beta_start.T,)
    return pl.pallas_call(
        functools.partial(products_kernel, count),
        out_shape=[jax.ShapeDtypeStruct((devices, 1, rows), jnp.float32), half, half]
        + [pltpu.VMEM(array.shape, array.dtype) for array in small]
        + [pltpu.VMEM((beta_start.shape[1], rows), jnp.float32)],
        in_specs=[ANY] * len(operands) + [VMEM],
        out_specs=[VMEM] * 7,
        scratch_shapes=[
            pltpu.SMEM(last_token.shape, jnp.int32),
            pltpu.VMEM((devices * devices, rows), jnp.bfloat16),
            pltpu.SemaphoreType.DMA((len(operands),)),
        ],
        compiler_params=PARAMS,
        name="first_products",
    )(*(in_hbm(operand) for operand in operands), emission)


def in_hbm(array):
    return pltpu.with_memory_space_constraint(array, pltpu.HBM)


def forward_kernel(prior_ref, *refs):
    blocks, out_ref = refs[:-1], refs[-1]
    devices, rows = out_ref.shape
    columns = blocks[0][-devices:]
    for block in blocks[1:]:
        columns += block[-devices:].astype(jnp.float32)
    prior = jnp.concatenate([prior_ref[:, pl.ds(k * rows, rows)] for k in range(devices)], axis=0)
    unnormal = prior * columns
    out_ref[...] = (unnormal / jnp.sum(unnormal)).astype(jnp.bfloat16)


def forward_messages_here(prior, blocks, devices):
    return pl.pallas_call(
        forward_kernel,
        out_shape=pltpu.VMEM((devices, blocks[0].shape[1]), jnp.bfloat16),
        in_specs=[VMEM] * (1 + len(blocks)),
        out_specs=VMEM,
        compiler_params=PARAMS,
        name="forward_messages",
    )(prior, *blocks)


def partner_at(place, count):
    number = jnp.zeros_like(place)
    for bit, offset in enumerate(basis(count)):
        number = number ^ (((place >> (count - 1 - bit)) & 1) * offset)
    return lax.axis_index("vocab") ^ number


def order_kernel(count, near_ref, far_ref, out_ref):
    size = 1 << count
    shape = (size * size, size * size)
    to, source = (lax.broadcasted_iota(jnp.int32, shape, axis) for axis in (0, 1))
    same_block = partner_at(to >> count, count) == (source & (size - 1))
    same_prompt = (to & (size - 1)) == partner_at(source >> count, count)
    onehot = (same_block & same_prompt).astype(jnp.bfloat16)
    half = size * size // 2
    rows = out_ref.shape[1]
    near = near_ref[...].reshape(half, rows)
    far = far_ref[...].reshape(half, rows)
    ordered = jnp.dot(onehot[:, :half], near, preferred_element_type=jnp.float32)
    ordered += jnp.dot(onehot[:, half:], far, preferred_element_type=jnp.float32)
    out_ref[...] = ordered.astype(jnp.bfloat16)


def order_forward(near, far, count):
    rows = near.shape[-1]
    return pl.pallas_call(
        functools.partial(order_kernel, count),
        out_shape=pltpu.VMEM((1 << (2 * count), rows), jnp.bfloat16),
        in_specs=[VMEM] * 2,
        out_specs=VMEM,
        compiler_params=PARAMS,
        name="order_forward",
    )(near, far)


def last_kernel(near_ref, *refs):
    blocks, out_ref = refs[:-2], refs[-1]
    count, states, _ = out_ref.shape
    for h in range(count):
        messages = near_ref[h]
        for g, block in enumerate(blocks, 1):
            for part in range(2):
                start = (part * count + (h ^ g)) * states
                messages += block[pl.ds(start, states)].astype(jnp.float32)
        out_ref[h] = messages


def last_sum(near, after, devices, count):
    packed = pack(near, True, ())
    blocks = [swap(packed, offset, devices) for offset in far_partners(count)[1:]]
    return pl.pallas_call(
        last_kernel,
        out_shape=pltpu.VMEM(near.shape, jnp.float32),
        in_specs=[VMEM] * (1 + len(blocks)) + [ANY],
        out_specs=VMEM,
        compiler_params=PARAMS,
        name="last_messages",
    )(near, *blocks, after)


def half_products(halves, transition_ref, out_ref, count, first):
    states = halves.shape[0] // 2
    rows = transition_ref.shape[0] >> count
    for place, partner in half_places(count, first):
        product = dot_rows(halves, transition_ref[partner_rows(partner, rows)])
        product = product[:states] + product[states:]
        out_ref[place + (pl.ds(0, states),)] = product.astype(out_ref.dtype)


def add_rows(out_ref, states, extra):
    for ref in extra:
        rows = pl.ds(states, ref.shape[2])
        for place in ((y, k) for y in range(ref.shape[0]) for k in range(ref.shape[1])):
            out_ref[place + (rows,)] = ref[place].astype(out_ref.dtype)


def send_kernel(count, number, transition_ref, route_ref, sums_ref, *refs):
    parts, extra, (halves_ref, out_ref) = refs[:number], refs[number:-2], refs[-2:]
    states = halves_ref.shape[0] // 2
    messages = parts[0][:states].astype(jnp.float32)
    for part in parts[1:]:
        messages += part[:states].astype(jnp.float32)
    selected = jnp.dot(
        route_ref[...],
        jnp.concatenate(split_three(messages), axis=0),
        preferred_element_type=jnp.float32,
    )
    emitted = selected[:states] * sums_ref[0]
    for b in range(1, 1 << count):
        emitted += selected[b * states : (b + 1) * states] * sums_ref[b]
    halves = jnp.concatenate(split_wide(emitted), axis=0)
    halves_ref[...] = halves
    half_products(halves, transition_ref, out_ref, count, 1)
    add_rows(out_ref, states, extra)


def keep_kernel(count, transition_ref, halves_ref, *refs):
    extra, out_ref = refs[:-1], refs[-1]
    half_products(halves_ref[...], transition_ref, out_ref, count, 0)
    add_rows(out_ref, halves_ref.shape[0] // 2, extra)


def step(transition, route, sums, parts, dtype, devices, count, kept_rows=(), sent_rows=()):
    states, rows = route.shape[0] // devices, parts[0].shape[1]
    total = states + sum(block.shape[2] for block in kept_rows)
    shape = (4, devices // 8, total, rows)
    halves, sent = pl.pallas_call(
        functools.partial(send_kernel, count, len(parts)),
        out_shape=[
            pltpu.VMEM((2 * states, rows), jnp.bfloat16),
            pltpu.VMEM(shape, dtype),
        ],
        in_specs=[VMEM] * (3 + len(parts) + len(sent_rows)),
        out_specs=[VMEM] * 2,
        compiler_params=PARAMS,
        name="step_sent_half",
    )(transition, route, sums, *parts, *sent_rows)
    received = swap(sent, 1, devices)
    kept = pl.pallas_call(
        functools.partial(keep_kernel, count),
        out_shape=pltpu.VMEM(shape, jnp.float32),
        in_specs=[VMEM] * (2 + len(kept_rows)),
        out_specs=VMEM,
        compiler_params=PARAMS,
        name="step_kept_half",
    )(transition, halves, *kept_rows)
    return kept, received


def weigh_blocks(emission_ref, forward_ref, chooser, parts_ref, count, first, squares):
    rows = emission_ref.shape[0] >> count
    prompts = chooser.shape[0]
    weights = jnp.zeros((prompts, emission_ref.shape[1]), jnp.float32)
    for order, ((q, h), partner) in enumerate(half_places(count, first)):
        if q not in squares:
            continue
        pieces = jnp.concatenate(split_three(parts_ref[squares.index(q), h]), axis=0)
        chosen = jnp.dot(chooser, pieces, preferred_element_type=jnp.float32)
        block = order + (first << (count - 1))
        forward = forward_ref[pl.ds(block * prompts, prompts)].astype(jnp.float32)
        scaled = (forward * chosen).astype(jnp.bfloat16)
        tile = emission_ref[partner_rows(partner, rows)]
        weights += jnp.dot(scaled, tile, preferred_element_type=jnp.float32)
    return weights


def weigh_kernel(count, groups, emission_ref, forward_ref, chooser_ref, *refs):
    parts, out_ref = refs[:-1], refs[-1]
    chooser = chooser_ref[...]
    out_ref[...] = functools.reduce(jnp.add, [
        weigh_blocks(emission_ref, forward_ref, chooser, part_ref, count, first, squares)
        for part_ref, (first, squares) in zip(parts, groups)
    ])


def last_weigh_kernel(
    count, first, squares, emission_ref, forward_ref, chooser_ref, logits_ref, before_ref,
    parts_ref, raised_ref, pair_ref,
):
    chooser = chooser_ref[...]
    logits = logits_ref[...].astype(jnp.float32)
    top = jnp.max(logits, axis=1, keepdims=True)
    weights = weigh_blocks(
        emission_ref, forward_ref, chooser, parts_ref, count, first, squares
    ) + before_ref[...]
    allowed = jnp.sum(chooser.astype(jnp.float32), axis=1, keepdims=True) > 0
    raised = jnp.where(allowed, jnp.exp(logits - top) * weights, 0.0)
    raised_ref[...] = raised
    total = jnp.sum(raised, axis=1, keepdims=True)
    lane = lax.broadcasted_iota(jnp.int32, pair_ref.shape, 1)
    pair_ref[...] = jnp.where(lane == 0, top, total)


def weigh(emission, forward, chooser, logits, far, devices, count):
    early, late = (0, 1), (2, 3)
    offsets = square_partners(count)
    arrived = [far] + [swap(far, offset, devices) for offset in offsets[1:]]
    near_early = jnp.stack([arrived[q] for q in early])
    near_late = jnp.stack([arrived[q] for q in late])
    far_early, far_late = swap(near_early, 1, devices), swap(near_late, 1, devices)

    def add(parts, groups):
        return pl.pallas_call(
            functools.partial(weigh_kernel, count, groups),
            out_shape=pltpu.VMEM(logits.shape, jnp.float32),
            in_specs=[VMEM] * (3 + len(parts)),
            out_specs=VMEM,
            compiler_params=PARAMS,
            name="weigh_tokens",
        )(emission, forward, chooser, *parts)

    weights = add((near_early, far_early, near_late), ((0, early), (1, early), (0, late)))
    return pl.pallas_call(
        functools.partial(last_weigh_kernel, count, 1, late),
        out_shape=[
            pltpu.VMEM(logits.shape, jnp.float32),
            pltpu.VMEM((logits.shape[0], 128), jnp.float32),
        ],
        in_specs=[VMEM] * 6,
        out_specs=[VMEM] * 2,
        compiler_params=PARAMS,
        name="weigh_last",
    )(emission, forward, chooser, logits, weights, far_late)


def normalise(raised, pair, devices):
    pairs = spread(pair[:, :2].T, devices)
    own_top = pair[:, :1]
    tops, totals = pairs[:, 0], pairs[:, 1]
    top = jnp.max(tops, axis=0)
    total = jnp.sum(totals * jnp.exp(tops - top), axis=0)
    return BLK * devices * (raised * jnp.exp(own_top - top[:, None])) / total[:, None]


def forward_messages(emission, last_token, prior_msg, devices, device):
    hidden = emission.shape[0]
    local_rows = prior_msg.shape[0]
    token_ids = jnp.arange(BLK, dtype=jnp.int32)
    tokens = last_token - device * BLK
    onehot = (tokens[:, None] == token_ids[None, :]).astype(jnp.bfloat16)
    owned = dot_rows(onehot, emission)
    owned = owned.astype(jnp.bfloat16).reshape(devices, local_rows, hidden)
    columns = jnp.sum(exchange(owned), axis=0, dtype=jnp.float32)
    unnormal = prior_msg * columns
    forward_msg = (unnormal / jnp.sum(unnormal, axis=1, keepdims=True)).astype(jnp.bfloat16)
    return spread(forward_msg, devices).reshape(devices * local_rows, hidden)


def per_device(
    emission,
    transition,
    beta_start,
    allow_list,
    trans_table,
    last_token,
    prompt_state,
    prior_msg,
    lm_logits,
):
    devices = lax.axis_size("vocab")
    device = lax.axis_index("vocab")
    hidden = emission.shape[0]
    states = beta_start.shape[1]
    own_rows = transition.shape[1]
    prompts = prompt_state.shape[0]
    count = devices.bit_length() - 1
    if devices == 1 << count and count > 2 and own_rows % 128 == 0 and prompts == devices:
        sums, columns, columns_out, state, allow, table, messages = first_products(
            last_token, prompt_state, allow_list, trans_table, beta_start, emission, count
        )
        route, chooser, sums = tables(state, allow, table, emission, sums, count)
        sums = exchange(sums)
        parts, kept_rows, sent_rows = [messages], (columns,), (columns_out,)
        for window_step in range(STEPS):
            wide = window_step == STEPS - 1
            dtype = jnp.float32 if wide else jnp.bfloat16
            kept, received = step(
                transition, route, sums, parts, dtype, devices, count, kept_rows, sent_rows
            )
            kept_rows, sent_rows, extra = (), (), ()
            if window_step == 1:
                forward = forward_messages_here(prior_msg, parts, devices)
            if window_step == 2:
                extra = (forward,)
            near, extras = reduce_square(kept, received, wide, devices, count, extra)
            if window_step == 0:
                parts = reduce_far(near, devices, count)
            if window_step == 1:
                parts = reduce_far(near, devices, count, (forward,))
                others = [part[-devices:] for part in parts[1:]]
                forward = jnp.concatenate([forward] + others, axis=0)
        forward = jnp.stack(extras).reshape(4, devices // 8, devices, own_rows)
        forward = order_forward(forward, swap(forward, 1, devices), count)
        messages = last_sum(near, forward, devices, count)
        raised, pair = weigh(emission, forward, chooser, lm_logits, messages, devices, count)
        return messages[0].T, normalise(raised, pair, devices)
    state_ids = jnp.arange(states, dtype=jnp.int32)
    block_ids = jnp.arange(devices, dtype=jnp.int32)
    allowed = jnp.any(allow_list[:, :, None] == block_ids, axis=1)
    dest_here = lax.dynamic_index_in_dim(trans_table, device, axis=1, keepdims=False)
    allow_here = jnp.any(allow_list == device, axis=1)
    dest_rows = jnp.sum(jnp.where(prompt_state[:, None] == state_ids, dest_here, 0), axis=1)
    allow_rows = jnp.any((prompt_state[:, None] == state_ids) & allow_here, axis=1)
    chooser = (dest_rows[:, None] == state_ids) & allow_rows[:, None]
    messages = lax.dynamic_slice_in_dim(beta_start, device * own_rows, own_rows, 0).T
    forward_all = forward_messages(emission, last_token, prior_msg, devices, device)
    own_sums = exchange(jnp.sum(emission, axis=1, dtype=jnp.float32).reshape(devices, own_rows))
    route = allowed.T[:, :, None] & (trans_table.T[:, :, None] == state_ids)
    route = route.astype(jnp.float32).reshape(devices * states, states)
    by_owner = transition.reshape(devices, own_rows, own_rows)
    for window_step in range(STEPS):
        selected = jnp.dot(route, messages, precision=lax.Precision.HIGHEST)
        selected = selected.reshape(devices, states, own_rows)
        emitted = jnp.sum(selected * own_sums[:, None, :], axis=0)
        halves = jnp.concatenate(split_outside(emitted), axis=0)
        partial = jnp.einsum("dzy,sy->dsz", by_owner, halves, preferred_element_type=jnp.float32)
        partial = partial[:, :states] + partial[:, states:]
        if window_step < STEPS - 1:
            partial = partial.astype(jnp.bfloat16)
        messages = jnp.sum(exchange(partial), axis=0, dtype=jnp.float32)
    everywhere = spread(messages, devices)
    chosen = jnp.einsum(
        "ps,dsz->pdz", chooser.astype(jnp.float32), everywhere, precision=lax.Precision.HIGHEST
    )
    forward_all = forward_all.reshape(prompts, devices, own_rows).astype(jnp.float32)
    scaled = (forward_all * chosen).astype(jnp.bfloat16).reshape(prompts, hidden)
    weights = jnp.dot(scaled, emission, preferred_element_type=jnp.float32)
    weights = jnp.where(allow_rows[:, None], weights, 0.0)
    logits = lm_logits.astype(jnp.float32)
    top_here = jnp.max(logits, axis=1)
    raised = jnp.exp(logits - top_here[:, None]) * weights
    pairs = spread(jnp.stack([top_here, jnp.sum(raised, axis=1)]), devices)
    tops, totals = pairs[:, 0], pairs[:, 1]
    top = jnp.max(tops, axis=0)
    total = jnp.sum(totals * jnp.exp(tops - top), axis=0)
    raised = raised * jnp.exp(top_here - top)[:, None]
    return (messages.T, BLK * devices * raised / total[:, None])


def solution(mesh):
    return jax.shard_map(
        per_device,
        mesh=mesh,
        in_specs=(
            P(None, "vocab"),
            P(None, "vocab"),
            P(),
            P(),
            P(),
            P("parts"),
            P("parts"),
            P(("parts", "vocab"), None),
            P("parts", "vocab"),
        ),
        out_specs=(P(("parts", "vocab"), None), P("parts", "vocab")),
        check_vma=False,
    )
```

```python
import functools

import jax
import jax.numpy as jnp
from jax import lax
from jax.experimental import pallas as pl
from jax.experimental.pallas import tpu as pltpu
from jax.sharding import PartitionSpec as P

BLK = 256
STEPS = 3
CHUNKS = 4
LIMIT = 16 * 1024 * 1024
VMEM = pl.BlockSpec(memory_space=pltpu.VMEM)
SMEM = pl.BlockSpec(memory_space=pltpu.SMEM)
ANY = pl.BlockSpec(memory_space=pl.ANY)
PARAMS = pltpu.CompilerParams(vmem_limit_bytes=LIMIT)


def exchange(blocks):
    return lax.all_to_all(blocks, "vocab", split_axis=0, concat_axis=0, tiled=True)


def spread(own, devices):
    return exchange(jnp.broadcast_to(own[None], (devices,) + own.shape))


def basis(count):
    return [1] + [(1 << bit) | 1 for bit in range(1, count)]


def swap(block, offset, devices):
    pairs = [(i, i ^ offset) for i in range(devices)]
    return lax.ppermute(block, "vocab", pairs)


def split_wide(wide):
    high = wide.astype(jnp.bfloat16)
    low = (wide - high.astype(jnp.float32)).astype(jnp.bfloat16)
    return high, low


def split_outside(wide):
    high = lax.reduce_precision(wide, exponent_bits=8, mantissa_bits=7)
    return high.astype(jnp.bfloat16), (wide - high).astype(jnp.bfloat16)


def split_three(wide):
    high = wide.astype(jnp.bfloat16)
    rest = wide - high.astype(jnp.float32)
    middle = rest.astype(jnp.bfloat16)
    low = (rest - middle.astype(jnp.float32)).astype(jnp.bfloat16)
    return high, middle, low


def dot_rows(left, right):
    return lax.dot_general(left, right, (((1,), (1,)), ((), ())), preferred_element_type=jnp.float32)


def partner_of(bits, count):
    partner = 0
    for bit, offset in zip(bits, basis(count)):
        partner ^= bit * offset
    return partner


def all_bits(count):
    return [tuple((k >> (count - 1 - b)) & 1 for b in range(count)) for k in range(1 << count)]


def square_partners(count):
    return [partner_of((0,) + bits, count) for bits in all_bits(2)]


def far_partners(count):
    return [partner_of((0, 0, 0) + bits, count) for bits in all_bits(count - 3)]


def half_places(count, first):
    return [
        ((q, h), first ^ near ^ far)
        for q, near in enumerate(square_partners(count))
        for h, far in enumerate(far_partners(count))
    ]


def partner_rows(i, rows):
    owner = lax.axis_index("vocab") ^ i
    return pl.ds(pl.multiple_of(owner * rows, rows), rows)


def pack(blocks, wide, extra):
    rows = blocks.reshape(-1, blocks.shape[-1])
    parts = split_outside(rows) if wide else (rows.astype(jnp.bfloat16),)
    return jnp.concatenate(parts + extra, axis=0)


def unpack(packed, shape, wide):
    size = shape[0] * shape[1]
    rows = packed[:size].astype(jnp.float32)
    if wide:
        rows += packed[size : 2 * size].astype(jnp.float32)
    return rows.reshape(shape)


def reduce_square(kept, received, wide, devices, count, extra=()):
    total = kept + received.astype(jnp.float32)
    near, extras = total[0], list(extra)
    for q, offset in enumerate(square_partners(count)):
        if q:
            packed = swap(pack(total[q], wide, extra), offset, devices)
            near += unpack(packed, total.shape[1:], wide)
            for rows in extra:
                extras.append(packed[-rows.shape[0] :])
    return near, extras


def reduce_far(near, devices, count, extra=()):
    blocks = [near[0]]
    for h, offset in enumerate(far_partners(count)):
        if h:
            blocks.append(swap(pack(near[h], False, extra), offset, devices))
    return blocks


def gather_square(far, devices, count):
    near = jnp.stack([far] + [swap(far, offset, devices) for offset in square_partners(count)[1:]])
    return near, swap(near, 1, devices)


def column_of(scalars_ref, shape):
    row = lax.broadcasted_iota(jnp.int32, shape, 0)
    column = jnp.zeros(shape, jnp.int32)
    for k in range(shape[0]):
        column = jnp.where(row == k, scalars_ref[k], column)
    return column


def tables_kernel(
    count, state_ref, allow_ref, table_ref, emission_ref, sums_in_ref,
    route_ref, chooser_ref, sums_ref,
):
    device = lax.axis_index("vocab")
    devices = 1 << count
    states = table_ref.shape[0]
    sums_ref[...] = sums_in_ref[...]
    allow, table = allow_ref[...], table_ref[...]
    hits = [jnp.max((allow == b).astype(jnp.float32), axis=0, keepdims=True) for b in range(devices)]
    shape = (states, states)
    diagonal = [lax.broadcasted_iota(jnp.int32, shape, axis) for axis in (0, 1)]
    diagonal = (diagonal[0] == diagonal[1]).astype(jnp.bfloat16)
    hits = dot_rows(diagonal, jnp.concatenate(hits, axis=0).astype(jnp.bfloat16))
    ids = lax.broadcasted_iota(jnp.int32, shape, 1)
    own_step = jnp.zeros(shape, jnp.float32)
    for b in range(devices):
        step = jnp.where(table[:, b : b + 1] == ids, hits[:, b : b + 1], 0.0)
        own_step = jnp.where(device == b, step, own_step)
        step = step.astype(jnp.bfloat16)
        route_ref[pl.ds(b * states, states)] = jnp.concatenate([step] * 3, axis=1)
    shape = (states, devices)
    prompts = state_ref[...] == lax.broadcasted_iota(jnp.int32, shape, 0)
    chooser = lax.dot_general(
        prompts.astype(jnp.bfloat16),
        own_step.astype(jnp.bfloat16),
        (((0,), (0,)), ((), ())),
        preferred_element_type=jnp.float32,
    ).astype(jnp.bfloat16)
    chooser_ref[...] = jnp.concatenate([chooser] * 3, axis=1)


def tables(state, allow, table, emission, sums, count):
    devices, states = 1 << count, table.shape[0]
    return pl.pallas_call(
        functools.partial(tables_kernel, count),
        out_shape=[
            pltpu.VMEM((devices * states, 3 * states), jnp.bfloat16),
            pltpu.VMEM((devices, 3 * states), jnp.bfloat16),
            jax.ShapeDtypeStruct(sums.shape, sums.dtype),
        ],
        in_specs=[VMEM] * 5,
        out_specs=[VMEM] * 3,
        compiler_params=PARAMS,
        name="tables",
    )(state, allow, table, emission, sums)


def products_kernel(
    count, token_hbm, state_hbm, allow_hbm, table_hbm, start_hbm, emission_hbm,
    sums_ref, kept_ref, sent_ref, state_ref, allow_ref, table_ref, messages_ref, emission_ref,
    token_ref, columns_ref, sems, chunk_sems,
):
    device = lax.axis_index("vocab")
    devices = 1 << count
    rows = emission_ref.shape[0] >> count
    own = pl.ds(pl.multiple_of(device * rows, rows), rows)
    pairs = [
        (token_hbm, token_ref), (state_hbm, state_ref), (allow_hbm, allow_ref),
        (table_hbm, table_ref), (start_hbm.at[:, own], messages_ref),
    ]
    copies = [
        pltpu.make_async_copy(source, to, sems.at[k]) for k, (source, to) in enumerate(pairs)
    ]
    size = emission_ref.shape[0] // CHUNKS
    chunks = []
    for k in range(CHUNKS):
        span = pl.ds(k * size, size)
        chunks.append(
            pltpu.make_async_copy(emission_hbm.at[span], emission_ref.at[span], chunk_sems.at[k])
        )
    for copy in copies[:1] + chunks + copies[1:]:
        copy.start()
    shape = (devices * devices // 2, devices * devices)
    to, source = (lax.broadcasted_iota(jnp.int32, shape, axis) for axis in (0, 1))
    same_block = (to & (devices - 1)) == (source >> count)
    orders = []
    for first in range(2):
        prompt = partner_at((to >> count) + first * (devices // 2), count)
        onehot = same_block & ((source & (devices - 1)) == prompt)
        orders.append(onehot.astype(jnp.bfloat16))
    copies[0].wait()
    shape = (devices, BLK)
    tokens = column_of(token_ref, shape) - device * BLK
    onehot = (tokens == lax.broadcasted_iota(jnp.int32, shape, 1)).astype(jnp.bfloat16)
    left = jnp.concatenate([onehot, jnp.ones((16, BLK), jnp.bfloat16)], axis=0)
    for k in range(devices):
        if k * rows % size == 0:
            chunks[k * rows // size].wait()
        product = dot_rows(left, emission_ref[pl.ds(k * rows, rows)])
        columns_ref[pl.ds(k * devices, devices)] = product[:devices].astype(jnp.bfloat16)
        sums_ref[k] = product[devices : devices + 1]
    for order, out_ref in zip(orders, (kept_ref, sent_ref)):
        ordered = jnp.dot(order, columns_ref[...], preferred_element_type=jnp.float32)
        out_ref[...] = ordered.astype(jnp.bfloat16).reshape(out_ref.shape)
    for copy in copies[1:]:
        copy.wait()


def first_products(last_token, prompt_state, allow_list, trans_table, beta_start, emission, count):
    devices, rows = 1 << count, emission.shape[0] >> count
    half = pltpu.VMEM((4, devices // 8, devices, rows), jnp.bfloat16)
    small = (prompt_state[None], allow_list.T, trans_table)
    operands = (last_token,) + small + (beta_start.T,)
    return pl.pallas_call(
        functools.partial(products_kernel, count),
        out_shape=[jax.ShapeDtypeStruct((devices, 1, rows), jnp.float32), half, half]
        + [pltpu.VMEM(array.shape, array.dtype) for array in small]
        + [pltpu.VMEM((beta_start.shape[1], rows), jnp.float32)]
        + [pltpu.VMEM(emission.shape, emission.dtype)],
        in_specs=[ANY] * (len(operands) + 1),
        out_specs=[VMEM] * 8,
        scratch_shapes=[
            pltpu.SMEM(last_token.shape, jnp.int32),
            pltpu.VMEM((devices * devices, rows), jnp.bfloat16),
            pltpu.SemaphoreType.DMA((len(operands),)),
            pltpu.SemaphoreType.DMA((CHUNKS,)),
        ],
        compiler_params=PARAMS,
        name="first_products",
    )(*(in_hbm(operand) for operand in operands + (emission,)))


def in_hbm(array):
    return pltpu.with_memory_space_constraint(array, pltpu.HBM)


def forward_kernel(prior_ref, *refs):
    blocks, out_ref = refs[:-1], refs[-1]
    devices, rows = out_ref.shape
    columns = blocks[0][-devices:]
    for block in blocks[1:]:
        columns += block[-devices:].astype(jnp.float32)
    prior = jnp.concatenate([prior_ref[:, pl.ds(k * rows, rows)] for k in range(devices)], axis=0)
    unnormal = prior * columns
    out_ref[...] = (unnormal / jnp.sum(unnormal)).astype(jnp.bfloat16)


def forward_messages_here(prior, blocks, devices):
    return pl.pallas_call(
        forward_kernel,
        out_shape=pltpu.VMEM((devices, blocks[0].shape[1]), jnp.bfloat16),
        in_specs=[VMEM] * (1 + len(blocks)),
        out_specs=VMEM,
        compiler_params=PARAMS,
        name="forward_messages",
    )(prior, *blocks)


def partner_at(place, count):
    number = jnp.zeros_like(place)
    for bit, offset in enumerate(basis(count)):
        number = number ^ (((place >> (count - 1 - bit)) & 1) * offset)
    return lax.axis_index("vocab") ^ number


def order_kernel(count, near_ref, far_ref, out_ref):
    size = 1 << count
    shape = (size * size, size * size)
    to, source = (lax.broadcasted_iota(jnp.int32, shape, axis) for axis in (0, 1))
    same_block = partner_at(to >> count, count) == (source & (size - 1))
    same_prompt = (to & (size - 1)) == partner_at(source >> count, count)
    onehot = (same_block & same_prompt).astype(jnp.bfloat16)
    half = size * size // 2
    rows = out_ref.shape[1]
    near = near_ref[...].reshape(half, rows)
    far = far_ref[...].reshape(half, rows)
    ordered = jnp.dot(onehot[:, :half], near, preferred_element_type=jnp.float32)
    ordered += jnp.dot(onehot[:, half:], far, preferred_element_type=jnp.float32)
    out_ref[...] = ordered.astype(jnp.bfloat16)


def order_forward(near, far, count):
    rows = near.shape[-1]
    return pl.pallas_call(
        functools.partial(order_kernel, count),
        out_shape=pltpu.VMEM((1 << (2 * count), rows), jnp.bfloat16),
        in_specs=[VMEM] * 2,
        out_specs=VMEM,
        compiler_params=PARAMS,
        name="order_forward",
    )(near, far)


def last_kernel(near_ref, *refs):
    blocks, out_ref = refs[:-2], refs[-1]
    count, states, _ = out_ref.shape
    for h in range(count):
        messages = near_ref[h]
        for g, block in enumerate(blocks, 1):
            for part in range(2):
                start = (part * count + (h ^ g)) * states
                messages += block[pl.ds(start, states)].astype(jnp.float32)
        out_ref[h] = messages


def last_sum(near, after, devices, count):
    packed = pack(near, True, ())
    blocks = [swap(packed, offset, devices) for offset in far_partners(count)[1:]]
    return pl.pallas_call(
        last_kernel,
        out_shape=pltpu.VMEM(near.shape, jnp.float32),
        in_specs=[VMEM] * (1 + len(blocks)) + [ANY],
        out_specs=VMEM,
        compiler_params=PARAMS,
        name="last_messages",
    )(near, *blocks, after)


def half_products(halves, transition_ref, out_ref, count, first):
    states = halves.shape[0] // 2
    rows = transition_ref.shape[0] >> count
    for place, partner in half_places(count, first):
        product = dot_rows(halves, transition_ref[partner_rows(partner, rows)])
        product = product[:states] + product[states:]
        out_ref[place + (pl.ds(0, states),)] = product.astype(out_ref.dtype)


def add_rows(out_ref, states, extra):
    for ref in extra:
        rows = pl.ds(states, ref.shape[2])
        for place in ((y, k) for y in range(ref.shape[0]) for k in range(ref.shape[1])):
            out_ref[place + (rows,)] = ref[place].astype(out_ref.dtype)


def send_kernel(count, number, transition_ref, route_ref, sums_ref, *refs):
    parts, extra, (halves_ref, out_ref) = refs[:number], refs[number:-2], refs[-2:]
    states = halves_ref.shape[0] // 2
    messages = parts[0][:states].astype(jnp.float32)
    for part in parts[1:]:
        messages += part[:states].astype(jnp.float32)
    selected = jnp.dot(
        route_ref[...],
        jnp.concatenate(split_three(messages), axis=0),
        preferred_element_type=jnp.float32,
    )
    emitted = selected[:states] * sums_ref[0]
    for b in range(1, 1 << count):
        emitted += selected[b * states : (b + 1) * states] * sums_ref[b]
    halves = jnp.concatenate(split_wide(emitted), axis=0)
    halves_ref[...] = halves
    half_products(halves, transition_ref, out_ref, count, 1)
    add_rows(out_ref, states, extra)


def keep_kernel(count, transition_ref, halves_ref, *refs):
    extra, out_ref = refs[:-1], refs[-1]
    half_products(halves_ref[...], transition_ref, out_ref, count, 0)
    add_rows(out_ref, halves_ref.shape[0] // 2, extra)


def step(transition, route, sums, parts, dtype, devices, count, kept_rows=(), sent_rows=()):
    states, rows = route.shape[0] // devices, parts[0].shape[1]
    total = states + sum(block.shape[2] for block in kept_rows)
    shape = (4, devices // 8, total, rows)
    halves, sent = pl.pallas_call(
        functools.partial(send_kernel, count, len(parts)),
        out_shape=[
            pltpu.VMEM((2 * states, rows), jnp.bfloat16),
            pltpu.VMEM(shape, dtype),
        ],
        in_specs=[VMEM] * (3 + len(parts) + len(sent_rows)),
        out_specs=[VMEM] * 2,
        compiler_params=PARAMS,
        name="step_sent_half",
    )(transition, route, sums, *parts, *sent_rows)
    received = swap(sent, 1, devices)
    kept = pl.pallas_call(
        functools.partial(keep_kernel, count),
        out_shape=pltpu.VMEM(shape, jnp.float32),
        in_specs=[VMEM] * (2 + len(kept_rows)),
        out_specs=VMEM,
        compiler_params=PARAMS,
        name="step_kept_half",
    )(transition, halves, *kept_rows)
    return kept, received


def weigh_half(emission_ref, forward_ref, chooser, parts_ref, count, first):
    rows = emission_ref.shape[0] >> count
    prompts = chooser.shape[0]
    weights = jnp.zeros((prompts, emission_ref.shape[1]), jnp.float32)
    for order, (place, partner) in enumerate(half_places(count, first)):
        pieces = jnp.concatenate(split_three(parts_ref[place]), axis=0)
        chosen = jnp.dot(chooser, pieces, preferred_element_type=jnp.float32)
        block = order + (first << (count - 1))
        forward = forward_ref[pl.ds(block * prompts, prompts)].astype(jnp.float32)
        scaled = (forward * chosen).astype(jnp.bfloat16)
        tile = emission_ref[partner_rows(partner, rows)]
        weights += jnp.dot(scaled, tile, preferred_element_type=jnp.float32)
    return weights


def near_kernel(count, emission_ref, forward_ref, chooser_ref, parts_ref, out_ref):
    out_ref[...] = weigh_half(emission_ref, forward_ref, chooser_ref[...], parts_ref, count, 0)


def far_kernel(count, emission_ref, forward_ref, chooser_ref, logits_ref, near_ref, parts_ref, raised_ref, pair_ref):
    chooser = chooser_ref[...]
    logits = logits_ref[...].astype(jnp.float32)
    top = jnp.max(logits, axis=1, keepdims=True)
    weights = near_ref[...] + weigh_half(emission_ref, forward_ref, chooser, parts_ref, count, 1)
    allowed = jnp.sum(chooser.astype(jnp.float32), axis=1, keepdims=True) > 0
    raised = jnp.where(allowed, jnp.exp(logits - top) * weights, 0.0)
    raised_ref[...] = raised
    total = jnp.sum(raised, axis=1, keepdims=True)
    lane = lax.broadcasted_iota(jnp.int32, pair_ref.shape, 1)
    pair_ref[...] = jnp.where(lane == 0, top, total)


def weigh(emission, forward, chooser, logits, near, far, count):
    half = pl.pallas_call(
        functools.partial(near_kernel, count),
        out_shape=pltpu.VMEM(logits.shape, jnp.float32),
        in_specs=[VMEM] * 4,
        out_specs=VMEM,
        compiler_params=PARAMS,
        name="weigh_near",
    )(emission, forward, chooser, near)
    return pl.pallas_call(
        functools.partial(far_kernel, count),
        out_shape=[
            pltpu.VMEM(logits.shape, jnp.float32),
            pltpu.VMEM((logits.shape[0], 128), jnp.float32),
        ],
        in_specs=[VMEM] * 6,
        out_specs=[VMEM] * 2,
        compiler_params=PARAMS,
        name="weigh_far",
    )(emission, forward, chooser, logits, half, far)


def normalise(raised, pair, devices):
    pairs = spread(pair[:, :2].T, devices)
    own_top = pair[:, :1]
    tops, totals = pairs[:, 0], pairs[:, 1]
    top = jnp.max(tops, axis=0)
    total = jnp.sum(totals * jnp.exp(tops - top), axis=0)
    return BLK * devices * (raised * jnp.exp(own_top - top[:, None])) / total[:, None]


def forward_messages(emission, last_token, prior_msg, devices, device):
    hidden = emission.shape[0]
    local_rows = prior_msg.shape[0]
    token_ids = jnp.arange(BLK, dtype=jnp.int32)
    tokens = last_token - device * BLK
    onehot = (tokens[:, None] == token_ids[None, :]).astype(jnp.bfloat16)
    owned = dot_rows(onehot, emission)
    owned = owned.astype(jnp.bfloat16).reshape(devices, local_rows, hidden)
    columns = jnp.sum(exchange(owned), axis=0, dtype=jnp.float32)
    unnormal = prior_msg * columns
    forward_msg = (unnormal / jnp.sum(unnormal, axis=1, keepdims=True)).astype(jnp.bfloat16)
    return spread(forward_msg, devices).reshape(devices * local_rows, hidden)


def per_device(
    emission,
    transition,
    beta_start,
    allow_list,
    trans_table,
    last_token,
    prompt_state,
    prior_msg,
    lm_logits,
):
    devices = lax.axis_size("vocab")
    device = lax.axis_index("vocab")
    hidden = emission.shape[0]
    states = beta_start.shape[1]
    own_rows = transition.shape[1]
    prompts = prompt_state.shape[0]
    count = devices.bit_length() - 1
    if devices == 1 << count and count > 2 and own_rows % 128 == 0 and prompts == devices:
        sums, columns, columns_out, state, allow, table, messages, held = first_products(
            last_token, prompt_state, allow_list, trans_table, beta_start, emission, count
        )
        route, chooser, sums = tables(state, allow, table, held, sums, count)
        sums = exchange(sums)
        parts, kept_rows, sent_rows = [messages], (columns,), (columns_out,)
        for window_step in range(STEPS):
            wide = window_step == STEPS - 1
            dtype = jnp.float32 if wide else jnp.bfloat16
            kept, received = step(
                transition, route, sums, parts, dtype, devices, count, kept_rows, sent_rows
            )
            kept_rows, sent_rows, extra = (), (), ()
            if window_step == 1:
                forward = forward_messages_here(prior_msg, parts, devices)
            if window_step == 2:
                extra = (forward,)
            near, extras = reduce_square(kept, received, wide, devices, count, extra)
            if window_step == 0:
                parts = reduce_far(near, devices, count)
            if window_step == 1:
                parts = reduce_far(near, devices, count, (forward,))
                others = [part[-devices:] for part in parts[1:]]
                forward = jnp.concatenate([forward] + others, axis=0)
        forward = jnp.stack(extras).reshape(4, devices // 8, devices, own_rows)
        forward = order_forward(forward, swap(forward, 1, devices), count)
        messages = last_sum(near, forward, devices, count)
        near, far = gather_square(messages, devices, count)
        messages = messages[0]
        raised, pair = weigh(emission, forward, chooser, lm_logits, near, far, count)
        return messages.T, normalise(raised, pair, devices)
    state_ids = jnp.arange(states, dtype=jnp.int32)
    block_ids = jnp.arange(devices, dtype=jnp.int32)
    allowed = jnp.any(allow_list[:, :, None] == block_ids, axis=1)
    dest_here = lax.dynamic_index_in_dim(trans_table, device, axis=1, keepdims=False)
    allow_here = jnp.any(allow_list == device, axis=1)
    dest_rows = jnp.sum(jnp.where(prompt_state[:, None] == state_ids, dest_here, 0), axis=1)
    allow_rows = jnp.any((prompt_state[:, None] == state_ids) & allow_here, axis=1)
    chooser = (dest_rows[:, None] == state_ids) & allow_rows[:, None]
    messages = lax.dynamic_slice_in_dim(beta_start, device * own_rows, own_rows, 0).T
    forward_all = forward_messages(emission, last_token, prior_msg, devices, device)
    own_sums = exchange(jnp.sum(emission, axis=1, dtype=jnp.float32).reshape(devices, own_rows))
    route = allowed.T[:, :, None] & (trans_table.T[:, :, None] == state_ids)
    route = route.astype(jnp.float32).reshape(devices * states, states)
    by_owner = transition.reshape(devices, own_rows, own_rows)
    for window_step in range(STEPS):
        selected = jnp.dot(route, messages, precision=lax.Precision.HIGHEST)
        selected = selected.reshape(devices, states, own_rows)
        emitted = jnp.sum(selected * own_sums[:, None, :], axis=0)
        halves = jnp.concatenate(split_outside(emitted), axis=0)
        partial = jnp.einsum("dzy,sy->dsz", by_owner, halves, preferred_element_type=jnp.float32)
        partial = partial[:, :states] + partial[:, states:]
        if window_step < STEPS - 1:
            partial = partial.astype(jnp.bfloat16)
        messages = jnp.sum(exchange(partial), axis=0, dtype=jnp.float32)
    everywhere = spread(messages, devices)
    chosen = jnp.einsum(
        "ps,dsz->pdz", chooser.astype(jnp.float32), everywhere, precision=lax.Precision.HIGHEST
    )
    forward_all = forward_all.reshape(prompts, devices, own_rows).astype(jnp.float32)
    scaled = (forward_all * chosen).astype(jnp.bfloat16).reshape(prompts, hidden)
    weights = jnp.dot(scaled, emission, preferred_element_type=jnp.float32)
    weights = jnp.where(allow_rows[:, None], weights, 0.0)
    logits = lm_logits.astype(jnp.float32)
    top_here = jnp.max(logits, axis=1)
    raised = jnp.exp(logits - top_here[:, None]) * weights
    pairs = spread(jnp.stack([top_here, jnp.sum(raised, axis=1)]), devices)
    tops, totals = pairs[:, 0], pairs[:, 1]
    top = jnp.max(tops, axis=0)
    total = jnp.sum(totals * jnp.exp(tops - top), axis=0)
    raised = raised * jnp.exp(top_here - top)[:, None]
    return (messages.T, BLK * devices * raised / total[:, None])


def solution(mesh):
    return jax.shard_map(
        per_device,
        mesh=mesh,
        in_specs=(
            P(None, "vocab"),
            P(None, "vocab"),
            P(),
            P(),
            P(),
            P("parts"),
            P("parts"),
            P(("parts", "vocab"), None),
            P("parts", "vocab"),
        ),
        out_specs=(P(("parts", "vocab"), None), P("parts", "vocab")),
        check_vma=False,
    )
```

```python
import functools

import jax
import jax.numpy as jnp
from jax import lax
from jax.experimental import pallas as pl
from jax.experimental.pallas import tpu as pltpu
from jax.sharding import PartitionSpec as P

BLK = 256
STEPS = 3
CUTS = (0, 6, 12, 15, 16)
LIMIT = 16 * 1024 * 1024
VMEM = pl.BlockSpec(memory_space=pltpu.VMEM)
SMEM = pl.BlockSpec(memory_space=pltpu.SMEM)
ANY = pl.BlockSpec(memory_space=pl.ANY)
PARAMS = pltpu.CompilerParams(vmem_limit_bytes=LIMIT)


def exchange(blocks):
    return lax.all_to_all(blocks, "vocab", split_axis=0, concat_axis=0, tiled=True)


def spread(own, devices):
    return exchange(jnp.broadcast_to(own[None], (devices,) + own.shape))


def basis(count):
    return [1] + [(1 << bit) | 1 for bit in range(1, count)]


def swap(block, offset, devices):
    pairs = [(i, i ^ offset) for i in range(devices)]
    return lax.ppermute(block, "vocab", pairs)


def split_wide(wide):
    high = wide.astype(jnp.bfloat16)
    low = (wide - high.astype(jnp.float32)).astype(jnp.bfloat16)
    return high, low


def split_outside(wide):
    high = lax.reduce_precision(wide, exponent_bits=8, mantissa_bits=7)
    return high.astype(jnp.bfloat16), (wide - high).astype(jnp.bfloat16)


def split_three(wide):
    high = wide.astype(jnp.bfloat16)
    rest = wide - high.astype(jnp.float32)
    middle = rest.astype(jnp.bfloat16)
    low = (rest - middle.astype(jnp.float32)).astype(jnp.bfloat16)
    return high, middle, low


def dot_rows(left, right):
    return lax.dot_general(left, right, (((1,), (1,)), ((), ())), preferred_element_type=jnp.float32)


def partner_of(bits, count):
    partner = 0
    for bit, offset in zip(bits, basis(count)):
        partner ^= bit * offset
    return partner


def all_bits(count):
    return [tuple((k >> (count - 1 - b)) & 1 for b in range(count)) for k in range(1 << count)]


def square_partners(count):
    return [partner_of((0,) + bits, count) for bits in all_bits(2)]


def far_partners(count):
    return [partner_of((0, 0, 0) + bits, count) for bits in all_bits(count - 3)]


def half_places(count, first):
    return [
        ((q, h), first ^ near ^ far)
        for q, near in enumerate(square_partners(count))
        for h, far in enumerate(far_partners(count))
    ]


def partner_rows(i, rows):
    owner = lax.axis_index("vocab") ^ i
    return pl.ds(pl.multiple_of(owner * rows, rows), rows)


def pack(blocks, wide, extra):
    rows = blocks.reshape(-1, blocks.shape[-1])
    parts = split_outside(rows) if wide else (rows.astype(jnp.bfloat16),)
    return jnp.concatenate(parts + extra, axis=0)


def unpack(packed, shape, wide):
    size = shape[0] * shape[1]
    rows = packed[:size].astype(jnp.float32)
    if wide:
        rows += packed[size : 2 * size].astype(jnp.float32)
    return rows.reshape(shape)


def reduce_square(kept, received, wide, devices, count, extra=()):
    total = kept + received.astype(jnp.float32)
    near, extras = total[0], list(extra)
    for q, offset in enumerate(square_partners(count)):
        if q:
            packed = swap(pack(total[q], wide, extra), offset, devices)
            near += unpack(packed, total.shape[1:], wide)
            for rows in extra:
                extras.append(packed[-rows.shape[0] :])
    return near, extras


def reduce_far(near, devices, count, extra=()):
    blocks = [near[0]]
    for h, offset in enumerate(far_partners(count)):
        if h:
            blocks.append(swap(pack(near[h], False, extra), offset, devices))
    return blocks


def gather_square(far, devices, count):
    near = jnp.stack([far] + [swap(far, offset, devices) for offset in square_partners(count)[1:]])
    return near, swap(near, 1, devices)


def column_of(scalars_ref, shape, order):
    row = lax.broadcasted_iota(jnp.int32, shape, 0)
    column = jnp.zeros(shape, jnp.int32)
    for k, place in enumerate(order):
        column = jnp.where(row == k, scalars_ref[place], column)
    return column


def tables_kernel(
    count, state_ref, allow_ref, table_ref, emission_ref, sums_in_ref,
    route_ref, chooser_ref, sums_ref,
):
    device = lax.axis_index("vocab")
    devices = 1 << count
    states = table_ref.shape[0]
    sums_ref[...] = sums_in_ref[...]
    allow, table = allow_ref[...], table_ref[...]
    hits = [jnp.max((allow == b).astype(jnp.float32), axis=0, keepdims=True) for b in range(devices)]
    shape = (states, states)
    diagonal = [lax.broadcasted_iota(jnp.int32, shape, axis) for axis in (0, 1)]
    diagonal = (diagonal[0] == diagonal[1]).astype(jnp.bfloat16)
    hits = dot_rows(diagonal, jnp.concatenate(hits, axis=0).astype(jnp.bfloat16))
    ids = lax.broadcasted_iota(jnp.int32, shape, 1)
    own_step = jnp.zeros(shape, jnp.float32)
    for b in range(devices):
        step = jnp.where(table[:, b : b + 1] == ids, hits[:, b : b + 1], 0.0)
        own_step = jnp.where(device == b, step, own_step)
        step = step.astype(jnp.bfloat16)
        route_ref[pl.ds(b * states, states)] = jnp.concatenate([step] * 3, axis=1)
    shape = (states, devices)
    prompts = state_ref[...] == lax.broadcasted_iota(jnp.int32, shape, 0)
    chooser = lax.dot_general(
        prompts.astype(jnp.bfloat16),
        own_step.astype(jnp.bfloat16),
        (((0,), (0,)), ((), ())),
        preferred_element_type=jnp.float32,
    ).astype(jnp.bfloat16)
    chooser_ref[...] = jnp.concatenate([chooser] * 3, axis=1)


def tables(state, allow, table, emission, sums, count):
    devices, states = 1 << count, table.shape[0]
    return pl.pallas_call(
        functools.partial(tables_kernel, count),
        out_shape=[
            pltpu.VMEM((devices * states, 3 * states), jnp.bfloat16),
            pltpu.VMEM((devices, 3 * states), jnp.bfloat16),
            jax.ShapeDtypeStruct(sums.shape, sums.dtype),
        ],
        in_specs=[VMEM] * 5,
        out_specs=[VMEM] * 3,
        compiler_params=PARAMS,
        name="tables",
    )(state, allow, table, emission, sums)


def products_kernel(
    count, token_hbm, state_hbm, allow_hbm, table_hbm, start_hbm, emission_hbm,
    sums_ref, kept_ref, sent_ref, state_ref, allow_ref, table_ref, messages_ref, emission_ref,
    token_ref, columns_ref, sems, chunk_sems,
):
    device = lax.axis_index("vocab")
    devices = 1 << count
    rows = emission_ref.shape[0] >> count
    own = pl.ds(pl.multiple_of(device * rows, rows), rows)
    pairs = [
        (token_hbm, token_ref), (state_hbm, state_ref), (allow_hbm, allow_ref),
        (table_hbm, table_ref), (start_hbm.at[:, own], messages_ref),
    ]
    copies = [
        pltpu.make_async_copy(source, to, sems.at[k]) for k, (source, to) in enumerate(pairs)
    ]
    chunks = {}
    cuts = [cut * devices // CUTS[-1] for cut in CUTS]
    for k, (low, high) in enumerate(zip(cuts, cuts[1:])):
        span = pl.ds(low * rows, (high - low) * rows)
        if high > low:
            chunks[low] = pltpu.make_async_copy(
                emission_hbm.at[span], emission_ref.at[span], chunk_sems.at[k]
            )
    for copy in copies[:1] + list(chunks.values()) + copies[1:]:
        copy.start()
    shape = (devices * devices // 2, devices * devices)
    to, source = (lax.broadcasted_iota(jnp.int32, shape, axis) for axis in (0, 1))
    same_block = (to & (devices - 1)) == (source >> count)
    orders = []
    for first in range(2):
        prompt = (to >> count) + first * (devices // 2)
        onehot = same_block & ((source & (devices - 1)) == prompt)
        orders.append(onehot.astype(jnp.bfloat16))
    copies[0].wait()
    shape = (devices, BLK)
    partners = [partner for first in range(2) for _, partner in half_places(count, first)]
    tokens = column_of(token_ref, shape, [device ^ partner for partner in partners]) - device * BLK
    onehot = (tokens == lax.broadcasted_iota(jnp.int32, shape, 1)).astype(jnp.bfloat16)
    left = jnp.concatenate([onehot, jnp.ones((16, BLK), jnp.bfloat16)], axis=0)
    for k in range(devices):
        if k in chunks:
            chunks[k].wait()
        product = dot_rows(left, emission_ref[pl.ds(k * rows, rows)])
        columns_ref[pl.ds(k * devices, devices)] = product[:devices].astype(jnp.bfloat16)
        sums_ref[k] = product[devices : devices + 1]
    for order, out_ref in zip(orders, (kept_ref, sent_ref)):
        ordered = jnp.dot(order, columns_ref[...], preferred_element_type=jnp.float32)
        out_ref[...] = ordered.astype(jnp.bfloat16).reshape(out_ref.shape)
    for copy in copies[1:]:
        copy.wait()


def first_products(last_token, prompt_state, allow_list, trans_table, beta_start, emission, count):
    devices, rows = 1 << count, emission.shape[0] >> count
    half = pltpu.VMEM((4, devices // 8, devices, rows), jnp.bfloat16)
    small = (prompt_state[None], allow_list.T, trans_table)
    operands = (last_token,) + small + (beta_start.T,)
    return pl.pallas_call(
        functools.partial(products_kernel, count),
        out_shape=[jax.ShapeDtypeStruct((devices, 1, rows), jnp.float32), half, half]
        + [pltpu.VMEM(array.shape, array.dtype) for array in small]
        + [pltpu.VMEM((beta_start.shape[1], rows), jnp.float32)]
        + [pltpu.VMEM(emission.shape, emission.dtype)],
        in_specs=[ANY] * (len(operands) + 1),
        out_specs=[VMEM] * 8,
        scratch_shapes=[
            pltpu.SMEM(last_token.shape, jnp.int32),
            pltpu.VMEM((devices * devices, rows), jnp.bfloat16),
            pltpu.SemaphoreType.DMA((len(operands),)),
            pltpu.SemaphoreType.DMA((len(CUTS) - 1,)),
        ],
        compiler_params=PARAMS,
        name="first_products",
    )(*(in_hbm(operand) for operand in operands + (emission,)))


def in_hbm(array):
    return pltpu.with_memory_space_constraint(array, pltpu.HBM)


def forward_kernel(prior_ref, *refs):
    blocks, out_ref = refs[:-1], refs[-1]
    devices, rows = out_ref.shape
    columns = blocks[0][-devices:]
    for block in blocks[1:]:
        columns += block[-devices:].astype(jnp.float32)
    prior = jnp.concatenate([prior_ref[:, pl.ds(k * rows, rows)] for k in range(devices)], axis=0)
    unnormal = prior * columns
    out_ref[...] = (unnormal / jnp.sum(unnormal)).astype(jnp.bfloat16)


def forward_messages_here(prior, blocks, devices):
    return pl.pallas_call(
        forward_kernel,
        out_shape=pltpu.VMEM((devices, blocks[0].shape[1]), jnp.bfloat16),
        in_specs=[VMEM] * (1 + len(blocks)),
        out_specs=VMEM,
        compiler_params=PARAMS,
        name="forward_messages",
    )(prior, *blocks)


def partner_at(place, count):
    number = jnp.zeros_like(place)
    for bit, offset in enumerate(basis(count)):
        number = number ^ (((place >> (count - 1 - bit)) & 1) * offset)
    return lax.axis_index("vocab") ^ number


def order_kernel(count, near_ref, far_ref, out_ref):
    size = 1 << count
    shape = (size * size, size * size)
    to, source = (lax.broadcasted_iota(jnp.int32, shape, axis) for axis in (0, 1))
    same_block = partner_at(to >> count, count) == (source & (size - 1))
    same_prompt = (to & (size - 1)) == partner_at(source >> count, count)
    onehot = (same_block & same_prompt).astype(jnp.bfloat16)
    half = size * size // 2
    rows = out_ref.shape[1]
    near = near_ref[...].reshape(half, rows)
    far = far_ref[...].reshape(half, rows)
    ordered = jnp.dot(onehot[:, :half], near, preferred_element_type=jnp.float32)
    ordered += jnp.dot(onehot[:, half:], far, preferred_element_type=jnp.float32)
    out_ref[...] = ordered.astype(jnp.bfloat16)


def order_forward(near, far, count):
    rows = near.shape[-1]
    return pl.pallas_call(
        functools.partial(order_kernel, count),
        out_shape=pltpu.VMEM((1 << (2 * count), rows), jnp.bfloat16),
        in_specs=[VMEM] * 2,
        out_specs=VMEM,
        compiler_params=PARAMS,
        name="order_forward",
    )(near, far)


def last_kernel(near_ref, *refs):
    blocks, out_ref = refs[:-2], refs[-1]
    count, states, _ = out_ref.shape
    for h in range(count):
        messages = near_ref[h]
        for g, block in enumerate(blocks, 1):
            for part in range(2):
                start = (part * count + (h ^ g)) * states
                messages += block[pl.ds(start, states)].astype(jnp.float32)
        out_ref[h] = messages


def last_sum(near, after, devices, count):
    packed = pack(near, True, ())
    blocks = [swap(packed, offset, devices) for offset in far_partners(count)[1:]]
    return pl.pallas_call(
        last_kernel,
        out_shape=pltpu.VMEM(near.shape, jnp.float32),
        in_specs=[VMEM] * (1 + len(blocks)) + [ANY],
        out_specs=VMEM,
        compiler_params=PARAMS,
        name="last_messages",
    )(near, *blocks, after)


def half_products(halves, transition_ref, out_ref, count, first):
    states = halves.shape[0] // 2
    rows = transition_ref.shape[0] >> count
    for place, partner in half_places(count, first):
        product = dot_rows(halves, transition_ref[partner_rows(partner, rows)])
        product = product[:states] + product[states:]
        out_ref[place + (pl.ds(0, states),)] = product.astype(out_ref.dtype)


def add_rows(out_ref, states, extra):
    for ref in extra:
        rows = pl.ds(states, ref.shape[2])
        for place in ((y, k) for y in range(ref.shape[0]) for k in range(ref.shape[1])):
            out_ref[place + (rows,)] = ref[place].astype(out_ref.dtype)


def send_kernel(count, number, transition_ref, route_ref, sums_ref, *refs):
    parts, extra, (halves_ref, out_ref) = refs[:number], refs[number:-2], refs[-2:]
    states = halves_ref.shape[0] // 2
    messages = parts[0][:states].astype(jnp.float32)
    for part in parts[1:]:
        messages += part[:states].astype(jnp.float32)
    selected = jnp.dot(
        route_ref[...],
        jnp.concatenate(split_three(messages), axis=0),
        preferred_element_type=jnp.float32,
    )
    emitted = selected[:states] * sums_ref[0]
    for b in range(1, 1 << count):
        emitted += selected[b * states : (b + 1) * states] * sums_ref[b]
    halves = jnp.concatenate(split_wide(emitted), axis=0)
    halves_ref[...] = halves
    half_products(halves, transition_ref, out_ref, count, 1)
    add_rows(out_ref, states, extra)


def keep_kernel(count, transition_ref, halves_ref, *refs):
    extra, out_ref = refs[:-1], refs[-1]
    half_products(halves_ref[...], transition_ref, out_ref, count, 0)
    add_rows(out_ref, halves_ref.shape[0] // 2, extra)


def step(transition, route, sums, parts, dtype, devices, count, kept_rows=(), sent_rows=()):
    states, rows = route.shape[0] // devices, parts[0].shape[1]
    total = states + sum(block.shape[2] for block in kept_rows)
    shape = (4, devices // 8, total, rows)
    halves, sent = pl.pallas_call(
        functools.partial(send_kernel, count, len(parts)),
        out_shape=[
            pltpu.VMEM((2 * states, rows), jnp.bfloat16),
            pltpu.VMEM(shape, dtype),
        ],
        in_specs=[VMEM] * (3 + len(parts) + len(sent_rows)),
        out_specs=[VMEM] * 2,
        compiler_params=PARAMS,
        name="step_sent_half",
    )(transition, route, sums, *parts, *sent_rows)
    received = swap(sent, 1, devices)
    kept = pl.pallas_call(
        functools.partial(keep_kernel, count),
        out_shape=pltpu.VMEM(shape, jnp.float32),
        in_specs=[VMEM] * (2 + len(kept_rows)),
        out_specs=VMEM,
        compiler_params=PARAMS,
        name="step_kept_half",
    )(transition, halves, *kept_rows)
    return kept, received


def weigh_half(emission_ref, forward_ref, chooser, parts_ref, count, first):
    rows = emission_ref.shape[0] >> count
    prompts = chooser.shape[0]
    weights = jnp.zeros((prompts, emission_ref.shape[1]), jnp.float32)
    for order, (place, partner) in enumerate(half_places(count, first)):
        pieces = jnp.concatenate(split_three(parts_ref[place]), axis=0)
        chosen = jnp.dot(chooser, pieces, preferred_element_type=jnp.float32)
        block = order + (first << (count - 1))
        forward = forward_ref[pl.ds(block * prompts, prompts)].astype(jnp.float32)
        scaled = (forward * chosen).astype(jnp.bfloat16)
        tile = emission_ref[partner_rows(partner, rows)]
        weights += jnp.dot(scaled, tile, preferred_element_type=jnp.float32)
    return weights


def near_kernel(count, emission_ref, forward_ref, chooser_ref, parts_ref, out_ref):
    out_ref[...] = weigh_half(emission_ref, forward_ref, chooser_ref[...], parts_ref, count, 0)


def far_kernel(count, emission_ref, forward_ref, chooser_ref, logits_ref, near_ref, parts_ref, raised_ref, pair_ref):
    chooser = chooser_ref[...]
    logits = logits_ref[...].astype(jnp.float32)
    top = jnp.max(logits, axis=1, keepdims=True)
    weights = near_ref[...] + weigh_half(emission_ref, forward_ref, chooser, parts_ref, count, 1)
    allowed = jnp.sum(chooser.astype(jnp.float32), axis=1, keepdims=True) > 0
    raised = jnp.where(allowed, jnp.exp(logits - top) * weights, 0.0)
    raised_ref[...] = raised
    total = jnp.sum(raised, axis=1, keepdims=True)
    lane = lax.broadcasted_iota(jnp.int32, pair_ref.shape, 1)
    pair_ref[...] = jnp.where(lane == 0, top, total)


def weigh(emission, forward, chooser, logits, near, far, count):
    half = pl.pallas_call(
        functools.partial(near_kernel, count),
        out_shape=pltpu.VMEM(logits.shape, jnp.float32),
        in_specs=[VMEM] * 4,
        out_specs=VMEM,
        compiler_params=PARAMS,
        name="weigh_near",
    )(emission, forward, chooser, near)
    return pl.pallas_call(
        functools.partial(far_kernel, count),
        out_shape=[
            pltpu.VMEM(logits.shape, jnp.float32),
            pltpu.VMEM((logits.shape[0], 128), jnp.float32),
        ],
        in_specs=[VMEM] * 6,
        out_specs=[VMEM] * 2,
        compiler_params=PARAMS,
        name="weigh_far",
    )(emission, forward, chooser, logits, half, far)


def normalise(raised, pair, devices):
    pairs = spread(pair[:, :2].T, devices)
    own_top = pair[:, :1]
    tops, totals = pairs[:, 0], pairs[:, 1]
    top = jnp.max(tops, axis=0)
    total = jnp.sum(totals * jnp.exp(tops - top), axis=0)
    return BLK * devices * (raised * jnp.exp(own_top - top[:, None])) / total[:, None]


def forward_messages(emission, last_token, prior_msg, devices, device):
    hidden = emission.shape[0]
    local_rows = prior_msg.shape[0]
    token_ids = jnp.arange(BLK, dtype=jnp.int32)
    tokens = last_token - device * BLK
    onehot = (tokens[:, None] == token_ids[None, :]).astype(jnp.bfloat16)
    owned = dot_rows(onehot, emission)
    owned = owned.astype(jnp.bfloat16).reshape(devices, local_rows, hidden)
    columns = jnp.sum(exchange(owned), axis=0, dtype=jnp.float32)
    unnormal = prior_msg * columns
    forward_msg = (unnormal / jnp.sum(unnormal, axis=1, keepdims=True)).astype(jnp.bfloat16)
    return spread(forward_msg, devices).reshape(devices * local_rows, hidden)


def per_device(
    emission,
    transition,
    beta_start,
    allow_list,
    trans_table,
    last_token,
    prompt_state,
    prior_msg,
    lm_logits,
):
    devices = lax.axis_size("vocab")
    device = lax.axis_index("vocab")
    hidden = emission.shape[0]
    states = beta_start.shape[1]
    own_rows = transition.shape[1]
    prompts = prompt_state.shape[0]
    count = devices.bit_length() - 1
    if devices == 1 << count and count > 2 and own_rows % 128 == 0 and prompts == devices:
        sums, columns, columns_out, state, allow, table, messages, held = first_products(
            last_token, prompt_state, allow_list, trans_table, beta_start, emission, count
        )
        route, chooser, sums = tables(state, allow, table, held, sums, count)
        sums = exchange(sums)
        parts, kept_rows, sent_rows = [messages], (columns,), (columns_out,)
        for window_step in range(STEPS):
            wide = window_step == STEPS - 1
            dtype = jnp.float32 if wide else jnp.bfloat16
            kept, received = step(
                transition, route, sums, parts, dtype, devices, count, kept_rows, sent_rows
            )
            kept_rows, sent_rows, extra = (), (), ()
            if window_step == 1:
                forward = forward_messages_here(prior_msg, parts, devices)
            if window_step == 2:
                extra = (forward,)
            near, extras = reduce_square(kept, received, wide, devices, count, extra)
            if window_step == 0:
                parts = reduce_far(near, devices, count)
            if window_step == 1:
                parts = reduce_far(near, devices, count, (forward,))
                others = [part[-devices:] for part in parts[1:]]
                forward = jnp.concatenate([forward] + others, axis=0)
        forward = jnp.stack(extras).reshape(4, devices // 8, devices, own_rows)
        forward = order_forward(forward, swap(forward, 1, devices), count)
        messages = last_sum(near, forward, devices, count)
        near, far = gather_square(messages, devices, count)
        messages = messages[0]
        raised, pair = weigh(emission, forward, chooser, lm_logits, near, far, count)
        return messages.T, normalise(raised, pair, devices)
    state_ids = jnp.arange(states, dtype=jnp.int32)
    block_ids = jnp.arange(devices, dtype=jnp.int32)
    allowed = jnp.any(allow_list[:, :, None] == block_ids, axis=1)
    dest_here = lax.dynamic_index_in_dim(trans_table, device, axis=1, keepdims=False)
    allow_here = jnp.any(allow_list == device, axis=1)
    dest_rows = jnp.sum(jnp.where(prompt_state[:, None] == state_ids, dest_here, 0), axis=1)
    allow_rows = jnp.any((prompt_state[:, None] == state_ids) & allow_here, axis=1)
    chooser = (dest_rows[:, None] == state_ids) & allow_rows[:, None]
    messages = lax.dynamic_slice_in_dim(beta_start, device * own_rows, own_rows, 0).T
    forward_all = forward_messages(emission, last_token, prior_msg, devices, device)
    own_sums = exchange(jnp.sum(emission, axis=1, dtype=jnp.float32).reshape(devices, own_rows))
    route = allowed.T[:, :, None] & (trans_table.T[:, :, None] == state_ids)
    route = route.astype(jnp.float32).reshape(devices * states, states)
    by_owner = transition.reshape(devices, own_rows, own_rows)
    for window_step in range(STEPS):
        selected = jnp.dot(route, messages, precision=lax.Precision.HIGHEST)
        selected = selected.reshape(devices, states, own_rows)
        emitted = jnp.sum(selected * own_sums[:, None, :], axis=0)
        halves = jnp.concatenate(split_outside(emitted), axis=0)
        partial = jnp.einsum("dzy,sy->dsz", by_owner, halves, preferred_element_type=jnp.float32)
        partial = partial[:, :states] + partial[:, states:]
        if window_step < STEPS - 1:
            partial = partial.astype(jnp.bfloat16)
        messages = jnp.sum(exchange(partial), axis=0, dtype=jnp.float32)
    everywhere = spread(messages, devices)
    chosen = jnp.einsum(
        "ps,dsz->pdz", chooser.astype(jnp.float32), everywhere, precision=lax.Precision.HIGHEST
    )
    forward_all = forward_all.reshape(prompts, devices, own_rows).astype(jnp.float32)
    scaled = (forward_all * chosen).astype(jnp.bfloat16).reshape(prompts, hidden)
    weights = jnp.dot(scaled, emission, preferred_element_type=jnp.float32)
    weights = jnp.where(allow_rows[:, None], weights, 0.0)
    logits = lm_logits.astype(jnp.float32)
    top_here = jnp.max(logits, axis=1)
    raised = jnp.exp(logits - top_here[:, None]) * weights
    pairs = spread(jnp.stack([top_here, jnp.sum(raised, axis=1)]), devices)
    tops, totals = pairs[:, 0], pairs[:, 1]
    top = jnp.max(tops, axis=0)
    total = jnp.sum(totals * jnp.exp(tops - top), axis=0)
    raised = raised * jnp.exp(top_here - top)[:, None]
    return (messages.T, BLK * devices * raised / total[:, None])


def solution(mesh):
    return jax.shard_map(
        per_device,
        mesh=mesh,
        in_specs=(
            P(None, "vocab"),
            P(None, "vocab"),
            P(),
            P(),
            P(),
            P("parts"),
            P("parts"),
            P(("parts", "vocab"), None),
            P("parts", "vocab"),
        ),
        out_specs=(P(("parts", "vocab"), None), P("parts", "vocab")),
        check_vma=False,
    )
```

```python
import functools

import jax
import jax.numpy as jnp
from jax import lax
from jax.experimental import pallas as pl
from jax.experimental.pallas import tpu as pltpu
from jax.sharding import PartitionSpec as P

BLK = 256
STEPS = 3
CHUNKS = 4
LIMIT = 16 * 1024 * 1024
VMEM = pl.BlockSpec(memory_space=pltpu.VMEM)
SMEM = pl.BlockSpec(memory_space=pltpu.SMEM)
ANY = pl.BlockSpec(memory_space=pl.ANY)
PARAMS = pltpu.CompilerParams(vmem_limit_bytes=LIMIT)


def exchange(blocks):
    return lax.all_to_all(blocks, "vocab", split_axis=0, concat_axis=0, tiled=True)


def spread(own, devices):
    return exchange(jnp.broadcast_to(own[None], (devices,) + own.shape))


def basis(count):
    return [1] + [(1 << bit) | 1 for bit in range(1, count)]


def swap(block, offset, devices):
    pairs = [(i, i ^ offset) for i in range(devices)]
    return lax.ppermute(block, "vocab", pairs)


def split_wide(wide):
    high = wide.astype(jnp.bfloat16)
    low = (wide - high.astype(jnp.float32)).astype(jnp.bfloat16)
    return high, low


def split_outside(wide):
    high = lax.reduce_precision(wide, exponent_bits=8, mantissa_bits=7)
    return high.astype(jnp.bfloat16), (wide - high).astype(jnp.bfloat16)


def split_three(wide):
    high = wide.astype(jnp.bfloat16)
    rest = wide - high.astype(jnp.float32)
    middle = rest.astype(jnp.bfloat16)
    low = (rest - middle.astype(jnp.float32)).astype(jnp.bfloat16)
    return high, middle, low


def dot_rows(left, right):
    return lax.dot_general(left, right, (((1,), (1,)), ((), ())), preferred_element_type=jnp.float32)


def partner_of(bits, count):
    partner = 0
    for bit, offset in zip(bits, basis(count)):
        partner ^= bit * offset
    return partner


def all_bits(count):
    return [tuple((k >> (count - 1 - b)) & 1 for b in range(count)) for k in range(1 << count)]


def square_partners(count):
    return [partner_of((0,) + bits, count) for bits in all_bits(2)]


def far_partners(count):
    return [partner_of((0, 0, 0) + bits, count) for bits in all_bits(count - 3)]


def half_places(count, first):
    return [
        ((q, h), first ^ near ^ far)
        for q, near in enumerate(square_partners(count))
        for h, far in enumerate(far_partners(count))
    ]


def partner_rows(i, rows):
    owner = lax.axis_index("vocab") ^ i
    return pl.ds(pl.multiple_of(owner * rows, rows), rows)


def pack(blocks, wide, extra):
    rows = blocks.reshape(-1, blocks.shape[-1])
    parts = split_outside(rows) if wide else (rows.astype(jnp.bfloat16),)
    return jnp.concatenate(parts + extra, axis=0)


def unpack(packed, shape, wide):
    size = shape[0] * shape[1]
    rows = packed[:size].astype(jnp.float32)
    if wide:
        rows += packed[size : 2 * size].astype(jnp.float32)
    return rows.reshape(shape)


def reduce_square(kept, received, wide, devices, count, extra=()):
    total = kept + received.astype(jnp.float32)
    near, extras = total[0], list(extra)
    for q, offset in enumerate(square_partners(count)):
        if q:
            packed = swap(pack(total[q], wide, extra), offset, devices)
            near += unpack(packed, total.shape[1:], wide)
            for rows in extra:
                extras.append(packed[-rows.shape[0] :])
    return near, extras


def reduce_far(near, devices, count, extra=()):
    blocks = [near[0]]
    for h, offset in enumerate(far_partners(count)):
        if h:
            blocks.append(swap(pack(near[h], False, extra), offset, devices))
    return blocks


def gather_square(far, devices, count):
    near = jnp.stack([far] + [swap(far, offset, devices) for offset in square_partners(count)[1:]])
    return near, swap(near, 1, devices)


def column_of(scalars_ref, shape):
    row = lax.broadcasted_iota(jnp.int32, shape, 0)
    column = jnp.zeros(shape, jnp.int32)
    for k in range(shape[0]):
        column = jnp.where(row == k, scalars_ref[k], column)
    return column


def tables_kernel(
    count, state_ref, allow_ref, table_ref, emission_ref, sums_in_ref,
    route_ref, chooser_ref, sums_ref,
):
    device = lax.axis_index("vocab")
    devices = 1 << count
    states = table_ref.shape[0]
    sums_ref[...] = sums_in_ref[...]
    allow, table = allow_ref[...], table_ref[...]
    hits = [jnp.max((allow == b).astype(jnp.float32), axis=0, keepdims=True) for b in range(devices)]
    shape = (states, states)
    diagonal = [lax.broadcasted_iota(jnp.int32, shape, axis) for axis in (0, 1)]
    diagonal = (diagonal[0] == diagonal[1]).astype(jnp.bfloat16)
    hits = dot_rows(diagonal, jnp.concatenate(hits, axis=0).astype(jnp.bfloat16))
    ids = lax.broadcasted_iota(jnp.int32, shape, 1)
    own_step = jnp.zeros(shape, jnp.float32)
    for b in range(devices):
        step = jnp.where(table[:, b : b + 1] == ids, hits[:, b : b + 1], 0.0)
        own_step = jnp.where(device == b, step, own_step)
        step = step.astype(jnp.bfloat16)
        route_ref[pl.ds(b * states, states)] = jnp.concatenate([step] * 3, axis=1)
    shape = (states, devices)
    prompts = state_ref[...] == lax.broadcasted_iota(jnp.int32, shape, 0)
    chooser = lax.dot_general(
        prompts.astype(jnp.bfloat16),
        own_step.astype(jnp.bfloat16),
        (((0,), (0,)), ((), ())),
        preferred_element_type=jnp.float32,
    ).astype(jnp.bfloat16)
    chooser_ref[...] = jnp.concatenate([chooser] * 3, axis=1)


def tables(state, allow, table, emission, sums, count):
    devices, states = 1 << count, table.shape[0]
    return pl.pallas_call(
        functools.partial(tables_kernel, count),
        out_shape=[
            pltpu.VMEM((devices * states, 3 * states), jnp.bfloat16),
            pltpu.VMEM((devices, 3 * states), jnp.bfloat16),
            jax.ShapeDtypeStruct(sums.shape, sums.dtype),
        ],
        in_specs=[VMEM] * 5,
        out_specs=[VMEM] * 3,
        compiler_params=PARAMS,
        name="tables",
    )(state, allow, table, emission, sums)


def products_kernel(
    count, token_hbm, state_hbm, allow_hbm, table_hbm, start_hbm, emission_hbm,
    sums_ref, kept_ref, sent_ref, state_ref, allow_ref, table_ref, messages_ref, emission_ref,
    token_ref, columns_ref, sems, chunk_sems,
):
    device = lax.axis_index("vocab")
    devices = 1 << count
    rows = emission_ref.shape[0] >> count
    own = pl.ds(pl.multiple_of(device * rows, rows), rows)
    pairs = [
        (token_hbm, token_ref), (state_hbm, state_ref), (allow_hbm, allow_ref),
        (table_hbm, table_ref), (start_hbm.at[:, own], messages_ref),
    ]
    copies = [
        pltpu.make_async_copy(source, to, sems.at[k]) for k, (source, to) in enumerate(pairs)
    ]
    size = emission_ref.shape[0] // CHUNKS
    chunks = []
    for k in range(CHUNKS):
        span = pl.ds(k * size, size)
        chunks.append(
            pltpu.make_async_copy(emission_hbm.at[span], emission_ref.at[span], chunk_sems.at[k])
        )
    for copy in copies + chunks:
        copy.start()
    shape = (devices * devices // 2, devices * devices)
    to, source = (lax.broadcasted_iota(jnp.int32, shape, axis) for axis in (0, 1))
    same_block = (to & (devices - 1)) == (source >> count)
    orders = []
    for first in range(2):
        prompt = partner_at((to >> count) + first * (devices // 2), count)
        onehot = same_block & ((source & (devices - 1)) == prompt)
        orders.append(onehot.astype(jnp.bfloat16))
    copies[0].wait()
    shape = (devices, BLK)
    tokens = column_of(token_ref, shape) - device * BLK
    onehot = (tokens == lax.broadcasted_iota(jnp.int32, shape, 1)).astype(jnp.bfloat16)
    left = jnp.concatenate([onehot, jnp.ones((16, BLK), jnp.bfloat16)], axis=0)
    for k in range(devices):
        if k * rows % size == 0:
            chunks[k * rows // size].wait()
        product = dot_rows(left, emission_ref[pl.ds(k * rows, rows)])
        columns_ref[pl.ds(k * devices, devices)] = product[:devices].astype(jnp.bfloat16)
        sums_ref[k] = product[devices : devices + 1]
    for order, out_ref in zip(orders, (kept_ref, sent_ref)):
        ordered = jnp.dot(order, columns_ref[...], preferred_element_type=jnp.float32)
        out_ref[...] = ordered.astype(jnp.bfloat16).reshape(out_ref.shape)
    for copy in copies[1:]:
        copy.wait()


def first_products(last_token, prompt_state, allow_list, trans_table, beta_start, emission, count):
    devices, rows = 1 << count, emission.shape[0] >> count
    half = pltpu.VMEM((4, devices // 8, devices, rows), jnp.bfloat16)
    small = (prompt_state[None], allow_list.T, trans_table)
    operands = (last_token,) + small + (beta_start.T,)
    return pl.pallas_call(
        functools.partial(products_kernel, count),
        out_shape=[jax.ShapeDtypeStruct((devices, 1, rows), jnp.float32), half, half]
        + [pltpu.VMEM(array.shape, array.dtype) for array in small]
        + [pltpu.VMEM((beta_start.shape[1], rows), jnp.float32)]
        + [pltpu.VMEM(emission.shape, emission.dtype)],
        in_specs=[ANY] * (len(operands) + 1),
        out_specs=[VMEM] * 8,
        scratch_shapes=[
            pltpu.SMEM(last_token.shape, jnp.int32),
            pltpu.VMEM((devices * devices, rows), jnp.bfloat16),
            pltpu.SemaphoreType.DMA((len(operands),)),
            pltpu.SemaphoreType.DMA((CHUNKS,)),
        ],
        compiler_params=PARAMS,
        name="first_products",
    )(*(in_hbm(operand) for operand in operands + (emission,)))


def in_hbm(array):
    return pltpu.with_memory_space_constraint(array, pltpu.HBM)


def forward_kernel(prior_ref, *refs):
    blocks, out_ref = refs[:-1], refs[-1]
    devices, rows = out_ref.shape
    columns = blocks[0][-devices:]
    for block in blocks[1:]:
        columns += block[-devices:].astype(jnp.float32)
    prior = jnp.concatenate([prior_ref[:, pl.ds(k * rows, rows)] for k in range(devices)], axis=0)
    unnormal = prior * columns
    out_ref[...] = (unnormal / jnp.sum(unnormal)).astype(jnp.bfloat16)


def forward_messages_here(prior, blocks, devices):
    return pl.pallas_call(
        forward_kernel,
        out_shape=pltpu.VMEM((devices, blocks[0].shape[1]), jnp.bfloat16),
        in_specs=[VMEM] * (1 + len(blocks)),
        out_specs=VMEM,
        compiler_params=PARAMS,
        name="forward_messages",
    )(prior, *blocks)


def partner_at(place, count):
    number = jnp.zeros_like(place)
    for bit, offset in enumerate(basis(count)):
        number = number ^ (((place >> (count - 1 - bit)) & 1) * offset)
    return lax.axis_index("vocab") ^ number


def order_kernel(count, near_ref, far_ref, out_ref):
    size = 1 << count
    shape = (size * size, size * size)
    to, source = (lax.broadcasted_iota(jnp.int32, shape, axis) for axis in (0, 1))
    same_block = partner_at(to >> count, count) == (source & (size - 1))
    same_prompt = (to & (size - 1)) == partner_at(source >> count, count)
    onehot = (same_block & same_prompt).astype(jnp.bfloat16)
    half = size * size // 2
    rows = out_ref.shape[1]
    near = near_ref[...].reshape(half, rows)
    far = far_ref[...].reshape(half, rows)
    ordered = jnp.dot(onehot[:, :half], near, preferred_element_type=jnp.float32)
    ordered += jnp.dot(onehot[:, half:], far, preferred_element_type=jnp.float32)
    out_ref[...] = ordered.astype(jnp.bfloat16)


def order_forward(near, far, count):
    rows = near.shape[-1]
    return pl.pallas_call(
        functools.partial(order_kernel, count),
        out_shape=pltpu.VMEM((1 << (2 * count), rows), jnp.bfloat16),
        in_specs=[VMEM] * 2,
        out_specs=VMEM,
        compiler_params=PARAMS,
        name="order_forward",
    )(near, far)


def last_kernel(near_ref, *refs):
    blocks, out_ref = refs[:-2], refs[-1]
    count, states, _ = out_ref.shape
    for h in range(count):
        messages = near_ref[h]
        for g, block in enumerate(blocks, 1):
            for part in range(2):
                start = (part * count + (h ^ g)) * states
                messages += block[pl.ds(start, states)].astype(jnp.float32)
        out_ref[h] = messages


def last_sum(near, after, devices, count):
    packed = pack(near, True, ())
    blocks = [swap(packed, offset, devices) for offset in far_partners(count)[1:]]
    return pl.pallas_call(
        last_kernel,
        out_shape=pltpu.VMEM(near.shape, jnp.float32),
        in_specs=[VMEM] * (1 + len(blocks)) + [ANY],
        out_specs=VMEM,
        compiler_params=PARAMS,
        name="last_messages",
    )(near, *blocks, after)


def half_products(halves, transition_ref, out_ref, count, first):
    states = halves.shape[0] // 2
    rows = transition_ref.shape[0] >> count
    for place, partner in half_places(count, first):
        product = dot_rows(halves, transition_ref[partner_rows(partner, rows)])
        product = product[:states] + product[states:]
        out_ref[place + (pl.ds(0, states),)] = product.astype(out_ref.dtype)


def add_rows(out_ref, states, extra):
    for ref in extra:
        rows = pl.ds(states, ref.shape[2])
        for place in ((y, k) for y in range(ref.shape[0]) for k in range(ref.shape[1])):
            out_ref[place + (rows,)] = ref[place].astype(out_ref.dtype)


def send_kernel(count, number, transition_ref, route_ref, sums_ref, *refs):
    parts, extra, (halves_ref, out_ref) = refs[:number], refs[number:-2], refs[-2:]
    states = halves_ref.shape[0] // 2
    messages = parts[0][:states].astype(jnp.float32)
    for part in parts[1:]:
        messages += part[:states].astype(jnp.float32)
    selected = jnp.dot(
        route_ref[...],
        jnp.concatenate(split_three(messages), axis=0),
        preferred_element_type=jnp.float32,
    )
    emitted = selected[:states] * sums_ref[0]
    for b in range(1, 1 << count):
        emitted += selected[b * states : (b + 1) * states] * sums_ref[b]
    halves = jnp.concatenate(split_wide(emitted), axis=0)
    halves_ref[...] = halves
    half_products(halves, transition_ref, out_ref, count, 1)
    add_rows(out_ref, states, extra)


def keep_kernel(count, transition_ref, halves_ref, *refs):
    extra, out_ref = refs[:-1], refs[-1]
    half_products(halves_ref[...], transition_ref, out_ref, count, 0)
    add_rows(out_ref, halves_ref.shape[0] // 2, extra)


def step(transition, route, sums, parts, dtype, devices, count, kept_rows=(), sent_rows=()):
    states, rows = route.shape[0] // devices, parts[0].shape[1]
    total = states + sum(block.shape[2] for block in kept_rows)
    shape = (4, devices // 8, total, rows)
    halves, sent = pl.pallas_call(
        functools.partial(send_kernel, count, len(parts)),
        out_shape=[
            pltpu.VMEM((2 * states, rows), jnp.bfloat16),
            pltpu.VMEM(shape, dtype),
        ],
        in_specs=[VMEM] * (3 + len(parts) + len(sent_rows)),
        out_specs=[VMEM] * 2,
        compiler_params=PARAMS,
        name="step_sent_half",
    )(transition, route, sums, *parts, *sent_rows)
    received = swap(sent, 1, devices)
    kept = pl.pallas_call(
        functools.partial(keep_kernel, count),
        out_shape=pltpu.VMEM(shape, jnp.float32),
        in_specs=[VMEM] * (2 + len(kept_rows)),
        out_specs=VMEM,
        compiler_params=PARAMS,
        name="step_kept_half",
    )(transition, halves, *kept_rows)
    return kept, received


def weigh_half(emission_ref, forward_ref, chooser, parts_ref, count, first):
    rows = emission_ref.shape[0] >> count
    prompts = chooser.shape[0]
    weights = jnp.zeros((prompts, emission_ref.shape[1]), jnp.float32)
    for order, (place, partner) in enumerate(half_places(count, first)):
        pieces = jnp.concatenate(split_three(parts_ref[place]), axis=0)
        chosen = jnp.dot(chooser, pieces, preferred_element_type=jnp.float32)
        block = order + (first << (count - 1))
        forward = forward_ref[pl.ds(block * prompts, prompts)].astype(jnp.float32)
        scaled = (forward * chosen).astype(jnp.bfloat16)
        tile = emission_ref[partner_rows(partner, rows)]
        weights += jnp.dot(scaled, tile, preferred_element_type=jnp.float32)
    return weights


def near_kernel(count, emission_ref, forward_ref, chooser_ref, parts_ref, out_ref):
    out_ref[...] = weigh_half(emission_ref, forward_ref, chooser_ref[...], parts_ref, count, 0)


def far_kernel(count, emission_ref, forward_ref, chooser_ref, logits_ref, near_ref, parts_ref, raised_ref, pair_ref):
    chooser = chooser_ref[...]
    logits = logits_ref[...].astype(jnp.float32)
    top = jnp.max(logits, axis=1, keepdims=True)
    weights = near_ref[...] + weigh_half(emission_ref, forward_ref, chooser, parts_ref, count, 1)
    allowed = jnp.sum(chooser.astype(jnp.float32), axis=1, keepdims=True) > 0
    raised = jnp.where(allowed, jnp.exp(logits - top) * weights, 0.0)
    raised_ref[...] = raised
    total = jnp.sum(raised, axis=1, keepdims=True)
    lane = lax.broadcasted_iota(jnp.int32, pair_ref.shape, 1)
    pair_ref[...] = jnp.where(lane == 0, top, total)


def weigh(emission, forward, chooser, logits, near, far, count):
    half = pl.pallas_call(
        functools.partial(near_kernel, count),
        out_shape=pltpu.VMEM(logits.shape, jnp.float32),
        in_specs=[VMEM] * 4,
        out_specs=VMEM,
        compiler_params=PARAMS,
        name="weigh_near",
    )(emission, forward, chooser, near)
    return pl.pallas_call(
        functools.partial(far_kernel, count),
        out_shape=[
            pltpu.VMEM(logits.shape, jnp.float32),
            pltpu.VMEM((logits.shape[0], 128), jnp.float32),
        ],
        in_specs=[VMEM] * 6,
        out_specs=[VMEM] * 2,
        compiler_params=PARAMS,
        name="weigh_far",
    )(emission, forward, chooser, logits, half, far)


def normalise(raised, pair, devices):
    pairs = spread(pair[:, :2].T, devices)
    own_top = pair[:, :1]
    tops, totals = pairs[:, 0], pairs[:, 1]
    top = jnp.max(tops, axis=0)
    total = jnp.sum(totals * jnp.exp(tops - top), axis=0)
    return BLK * devices * (raised * jnp.exp(own_top - top[:, None])) / total[:, None]


def forward_messages(emission, last_token, prior_msg, devices, device):
    hidden = emission.shape[0]
    local_rows = prior_msg.shape[0]
    token_ids = jnp.arange(BLK, dtype=jnp.int32)
    tokens = last_token - device * BLK
    onehot = (tokens[:, None] == token_ids[None, :]).astype(jnp.bfloat16)
    owned = dot_rows(onehot, emission)
    owned = owned.astype(jnp.bfloat16).reshape(devices, local_rows, hidden)
    columns = jnp.sum(exchange(owned), axis=0, dtype=jnp.float32)
    unnormal = prior_msg * columns
    forward_msg = (unnormal / jnp.sum(unnormal, axis=1, keepdims=True)).astype(jnp.bfloat16)
    return spread(forward_msg, devices).reshape(devices * local_rows, hidden)


def per_device(
    emission,
    transition,
    beta_start,
    allow_list,
    trans_table,
    last_token,
    prompt_state,
    prior_msg,
    lm_logits,
):
    devices = lax.axis_size("vocab")
    device = lax.axis_index("vocab")
    hidden = emission.shape[0]
    states = beta_start.shape[1]
    own_rows = transition.shape[1]
    prompts = prompt_state.shape[0]
    count = devices.bit_length() - 1
    if devices == 1 << count and count > 2 and own_rows % 128 == 0 and prompts == devices:
        sums, columns, columns_out, state, allow, table, messages, held = first_products(
            last_token, prompt_state, allow_list, trans_table, beta_start, emission, count
        )
        route, chooser, sums = tables(state, allow, table, held, sums, count)
        sums = exchange(sums)
        parts, kept_rows, sent_rows = [messages], (columns,), (columns_out,)
        for window_step in range(STEPS):
            wide = window_step == STEPS - 1
            dtype = jnp.float32 if wide else jnp.bfloat16
            kept, received = step(
                transition, route, sums, parts, dtype, devices, count, kept_rows, sent_rows
            )
            kept_rows, sent_rows, extra = (), (), ()
            if window_step == 1:
                forward = forward_messages_here(prior_msg, parts, devices)
            if window_step == 2:
                extra = (forward,)
            near, extras = reduce_square(kept, received, wide, devices, count, extra)
            if window_step == 0:
                parts = reduce_far(near, devices, count)
            if window_step == 1:
                parts = reduce_far(near, devices, count, (forward,))
                others = [part[-devices:] for part in parts[1:]]
                forward = jnp.concatenate([forward] + others, axis=0)
        forward = jnp.stack(extras).reshape(4, devices // 8, devices, own_rows)
        forward = order_forward(forward, swap(forward, 1, devices), count)
        messages = last_sum(near, forward, devices, count)
        near, far = gather_square(messages, devices, count)
        messages = messages[0]
        raised, pair = weigh(emission, forward, chooser, lm_logits, near, far, count)
        return messages.T, normalise(raised, pair, devices)
    state_ids = jnp.arange(states, dtype=jnp.int32)
    block_ids = jnp.arange(devices, dtype=jnp.int32)
    allowed = jnp.any(allow_list[:, :, None] == block_ids, axis=1)
    dest_here = lax.dynamic_index_in_dim(trans_table, device, axis=1, keepdims=False)
    allow_here = jnp.any(allow_list == device, axis=1)
    dest_rows = jnp.sum(jnp.where(prompt_state[:, None] == state_ids, dest_here, 0), axis=1)
    allow_rows = jnp.any((prompt_state[:, None] == state_ids) & allow_here, axis=1)
    chooser = (dest_rows[:, None] == state_ids) & allow_rows[:, None]
    messages = lax.dynamic_slice_in_dim(beta_start, device * own_rows, own_rows, 0).T
    forward_all = forward_messages(emission, last_token, prior_msg, devices, device)
    own_sums = exchange(jnp.sum(emission, axis=1, dtype=jnp.float32).reshape(devices, own_rows))
    route = allowed.T[:, :, None] & (trans_table.T[:, :, None] == state_ids)
    route = route.astype(jnp.float32).reshape(devices * states, states)
    by_owner = transition.reshape(devices, own_rows, own_rows)
    for window_step in range(STEPS):
        selected = jnp.dot(route, messages, precision=lax.Precision.HIGHEST)
        selected = selected.reshape(devices, states, own_rows)
        emitted = jnp.sum(selected * own_sums[:, None, :], axis=0)
        halves = jnp.concatenate(split_outside(emitted), axis=0)
        partial = jnp.einsum("dzy,sy->dsz", by_owner, halves, preferred_element_type=jnp.float32)
        partial = partial[:, :states] + partial[:, states:]
        if window_step < STEPS - 1:
            partial = partial.astype(jnp.bfloat16)
        messages = jnp.sum(exchange(partial), axis=0, dtype=jnp.float32)
    everywhere = spread(messages, devices)
    chosen = jnp.einsum(
        "ps,dsz->pdz", chooser.astype(jnp.float32), everywhere, precision=lax.Precision.HIGHEST
    )
    forward_all = forward_all.reshape(prompts, devices, own_rows).astype(jnp.float32)
    scaled = (forward_all * chosen).astype(jnp.bfloat16).reshape(prompts, hidden)
    weights = jnp.dot(scaled, emission, preferred_element_type=jnp.float32)
    weights = jnp.where(allow_rows[:, None], weights, 0.0)
    logits = lm_logits.astype(jnp.float32)
    top_here = jnp.max(logits, axis=1)
    raised = jnp.exp(logits - top_here[:, None]) * weights
    pairs = spread(jnp.stack([top_here, jnp.sum(raised, axis=1)]), devices)
    tops, totals = pairs[:, 0], pairs[:, 1]
    top = jnp.max(tops, axis=0)
    total = jnp.sum(totals * jnp.exp(tops - top), axis=0)
    raised = raised * jnp.exp(top_here - top)[:, None]
    return (messages.T, BLK * devices * raised / total[:, None])


def solution(mesh):
    return jax.shard_map(
        per_device,
        mesh=mesh,
        in_specs=(
            P(None, "vocab"),
            P(None, "vocab"),
            P(),
            P(),
            P(),
            P("parts"),
            P("parts"),
            P(("parts", "vocab"), None),
            P("parts", "vocab"),
        ),
        out_specs=(P(("parts", "vocab"), None), P("parts", "vocab")),
        check_vma=False,
    )
```
